32 devices in a mesh: node: 2 (over y), gz: 16 (over z, x, core).
Axes of the slice: x: 2, y: 2, z: 4, core: 2. Of those that a mesh axis runs over, the one named last changes fastest.
Arguments:
- source: float32 [2, 64, 512, 256], P(None, ('node', 'gz')), parts along dimension 1, may hold values from -56 to 56
- layer_ids: int32 [64, 256], P(('node', 'gz')), parts along dimension 0, may hold values from 0 to 15
- conduct_table: float32 [16], replicated, may hold values from 0.35 to 3.75
- shift: float32 [4], P('node'), parts along dimension 0, may hold values from 0.2 to 1
Outputs:
- solution_field: float32 [2, 64, 512, 256], P(None, ('node', 'gz')), parts along dimension 1
- residual_norms: float32 [4], P('node'), parts along dimension 0
The draws below stay inside these ranges and needn't reach their ends.
There are 2 independent parts, one for each index of `node`. The reference program is written for one: setup_inputs(seed, part) draws one part's arguments, and reference() takes and returns one part's arrays. A program takes and returns all parts, laid end to end along the dimension named above; an argument that names none is the same for every part. Nothing has to cross between parts.
All inputs are finite; a program needn't handle non-finite values.
Results may differ from the reference program's by a relative error of at most 0.0003.
Values sent between devices are 32-bit elements; how exact they have to be, the bound alone decides.
No kernel may reach another device: no remote copies, remote signals or barrier semaphores. Data moves between devices by JAX's collectives and lax.ppermute only.
A program may use at most 64 MiB of HBM per device.

```python
import jax
import jax.numpy as jnp
from jax import lax

NX = 512
NY = 256
ITERS = 2
LAYERS = 16
NZ = 32


def draw_source(key, part):
    keys = jax.random.split(key, 5)
    z_ramp = 1.0 + 2.0 * lax.iota(jnp.float32, NZ) / max(NZ - 1, 1)
    z_ramp = z_ramp[None, :, None, None]
    x_pos = lax.iota(jnp.float32, NX)[None, None, :, None] * (2.0 * jnp.pi / NX)
    amp_one = jnp.clip(jax.random.normal(keys[1], (2, NZ, 1, NY), jnp.float32), -2.0, 2.0)
    amp_two = jnp.clip(jax.random.normal(keys[2], (2, NZ, 1, NY), jnp.float32), -2.0, 2.0)
    phase_one = jax.random.uniform(keys[3], (2, NZ, 1, NY), jnp.float32, 0.0, 2.0 * jnp.pi)
    phase_two = jax.random.uniform(keys[4], (2, NZ, 1, NY), jnp.float32, 0.0, 2.0 * jnp.pi)
    smooth = amp_one * jnp.cos(x_pos + phase_one) + 0.5 * amp_two * jnp.cos(2.0 * x_pos + phase_two)
    texture = jnp.clip(jax.random.normal(keys[0], (2, NZ, NX, NY), jnp.float32), -4.0, 4.0)
    values = z_ramp * (texture + smooth)
    return values.astype(jnp.float32)


def draw_layer_ids(key, part):
    depth = lax.iota(jnp.int32, NZ)[:, None]
    base_layer = depth * LAYERS // NZ
    jitter = jax.random.randint(key, (NZ, NY), -2, 3, jnp.int32)
    return jnp.clip(base_layer + jitter, 0, LAYERS - 1).astype(jnp.int32)


def draw_conduct_table(key, part):
    levels = lax.iota(jnp.float32, LAYERS) / (LAYERS - 1)
    base_layer = 0.5 * jnp.exp(jnp.log(6.0) * levels)
    factor = jax.random.uniform(key, (LAYERS,), jnp.float32, 0.8, 1.25)
    return (base_layer * factor).astype(jnp.float32)


def setup_inputs(seed: int = 0, part: int = 0) -> dict:
    seeds = jax.random.split(jax.random.key(seed), 5)
    part_splits = jax.random.split(jax.random.fold_in(seeds[4], part), 5)
    source = draw_source(jax.random.fold_in(jax.random.fold_in(seeds[4], part), 71), part)
    layer_ids = draw_layer_ids(jax.random.fold_in(jax.random.fold_in(seeds[4], part), 71), part)
    conduct_table = draw_conduct_table(jax.random.fold_in(seeds[4], 71), part)
    shift = jnp.clip(jax.random.uniform(part_splits[3], (2,), jnp.float32, 0.2, 1.0), 0.2, 1.0)
    return {"source": source, "layer_ids": layer_ids, "conduct_table": conduct_table, "shift": shift}


relax = 0.6
highest = lax.Precision.HIGHEST

def sine_table(length):
    indices = lax.iota(jnp.int32, length) + 1
    product = indices[:, None] * indices[None, :] % (2 * (length + 1))
    return jnp.sqrt(2.0 / (length + 1)) * jnp.sin(jnp.pi / (length + 1) * product.astype(jnp.float32))

def sine_eigen(length):
    indices = lax.iota(jnp.float32, length) + 1.0
    return 2.0 - 2.0 * jnp.cos(jnp.pi / (length + 1) * indices)

def expand(weights):
    return weights[None, :, None, :]

def yz_part(field, upper, lower, conduct, cond_hi, cond_lo):
    cond_pad = jnp.pad(conduct, ((0, 0), (1, 1)), mode='edge')
    face_yp = 0.5 * (conduct + cond_pad[:, 2:])
    face_ym = 0.5 * (conduct + cond_pad[:, :-2])
    face_zp = 0.5 * (conduct + cond_hi)
    face_zm = 0.5 * (conduct + cond_lo)
    field_pad = jnp.pad(field, ((0, 0), (0, 0), (0, 0), (1, 1)))
    total = expand(face_yp) * (field - field_pad[..., 2:]) + expand(face_ym) * (field - field_pad[..., :-2])
    return total + expand(face_zp) * (field - upper) + expand(face_zm) * (field - lower)

def shift_mult(shift_re, shift_im, field):
    return jnp.stack([shift_re * field[0] - shift_im * field[1], shift_re * field[1] + shift_im * field[0]])

def sine_both(field, sine_y, sine_z):
    field = jnp.einsum('pzxy,yj->pzxj', field, sine_y, precision=highest)
    return jnp.einsum('pzxy,zk->pkxy', field, sine_z, precision=highest)

def precondition(spectra, mode_eig, mean_cond, shift_re, shift_im, sine_y, sine_z, eig_y, eig_z):
    coeffs = sine_both(spectra, sine_y, sine_z)
    eigen = eig_z[:, None, None] + mode_eig[None, :, None] + eig_y[None, None, :]
    real_den = shift_re + mean_cond * eigen
    modulus = real_den * real_den + shift_im * shift_im
    scaled = jnp.stack([(coeffs[0] * real_den + coeffs[1] * shift_im) / modulus, (coeffs[1] * real_den - coeffs[0] * shift_im) / modulus])
    return sine_both(scaled, sine_y, sine_z)

def reference(source, layer_ids, conduct_table, shift):
    conduct = conduct_table[layer_ids]
    shift_re = shift[0]
    shift_im = shift[1]
    mean_cond = jnp.mean(conduct)
    cond_z = jnp.pad(conduct, ((1, 1), (0, 0)), mode='edge')
    cond_hi = cond_z[2:]
    cond_lo = cond_z[:-2]
    sine_y = sine_table(NY)
    sine_z = sine_table(NZ)
    eig_y = sine_eigen(NY)
    eig_z = sine_eigen(NZ)
    mode_ids = lax.iota(jnp.int32, NX).astype(jnp.float32)
    mode_eig = 2.0 - 2.0 * jnp.cos(2.0 * jnp.pi / NX * mode_ids)
    solution = jnp.zeros_like(source)
    norms = []
    for iteration in range(ITERS):
        padded = jnp.pad(solution, ((0, 0), (1, 1), (0, 0), (0, 0)))
        lap = expand(conduct) * (2.0 * solution - jnp.roll(solution, 1, 2) - jnp.roll(solution, -1, 2))
        lap = lap + yz_part(solution, padded[:, 2:], padded[:, :-2], conduct, cond_hi, cond_lo)
        resid = source - (shift_mult(shift_re, shift_im, solution) + lap)
        norms.append(jnp.sqrt(jnp.sum(resid * resid) / (NX * NY * NZ)))
        spectrum = jnp.fft.fft(lax.complex(resid[0], resid[1]), axis=1)
        spectra = jnp.stack([jnp.real(spectrum), jnp.imag(spectrum)])
        update = precondition(spectra, mode_eig, mean_cond, shift_re, shift_im, sine_y, sine_z, eig_y, eig_z)
        inverse = jnp.fft.ifft(lax.complex(update[0], update[1]), axis=1)
        solution = solution + relax * jnp.stack([jnp.real(inverse), jnp.imag(inverse)])
    return (solution, jnp.stack(norms))
```

```python
import jax
import jax.numpy as jnp
import numpy as np
from jax import lax
from jax.sharding import PartitionSpec as P

ITERS = 2
RADIX = 4

relax = 0.6
high = lax.Precision.HIGH


def sine_table(length):
    indices = np.arange(1, length + 1)
    product = indices[:, None] * indices[None, :] % (2 * (length + 1))
    return (np.sqrt(2.0 / (length + 1)) * np.sin(np.pi / (length + 1) * product)).astype(np.float32)


def sine_eigen(length):
    indices = np.arange(1, length + 1)
    return (4.0 * np.sin(np.pi / (2 * (length + 1)) * indices) ** 2).astype(np.float32)


def wave_eigen(length):
    short = length // RADIX
    waves = RADIX * np.arange(short)[None, :] + np.arange(RADIX)[:, None]
    return (4.0 * np.sin(np.pi / length * waves) ** 2).astype(np.float32)


def wave_tables(length):
    short = length // RADIX
    waves = RADIX * np.arange(short)[None, :] + np.arange(RADIX)[:, None]
    product = waves[:, :, None] * np.arange(short)[None, None, :] % length
    angles = 2.0 * np.pi / length * product
    cos_t, sin_t = np.cos(angles), np.sin(angles)
    top = np.concatenate([cos_t, sin_t], axis=2)
    low = np.concatenate([-sin_t, cos_t], axis=2)
    return np.concatenate([top, low], axis=1).astype(np.float32)


def forward(field, wave_t, sine_y):
    _, planes, length_x, length_y = field.shape
    short = length_x // RADIX
    parts = field.reshape(2, planes, RADIX, short, length_y)
    even, odd = parts[:, :, 0] + parts[:, :, 2], parts[:, :, 1] + parts[:, :, 3]
    even_d, odd_d = parts[:, :, 0] - parts[:, :, 2], parts[:, :, 1] - parts[:, :, 3]
    turned = jnp.stack([odd_d[1], -odd_d[0]])
    mixed = jnp.stack([even + odd, even_d + turned, even - odd, even_d - turned], axis=2)
    mixed = mixed.transpose(1, 2, 0, 3, 4).reshape(planes, RADIX, 2 * short, length_y)
    waves = jnp.einsum("qij,nqjy->nqiy", wave_t, mixed, precision=high)
    modes = jnp.einsum("nqiy,ya->nqia", waves, sine_y, precision=high)
    return modes.reshape(planes, RADIX, 2, short, length_y)


def backward(modes, wave_t, sine_y):
    planes, _, _, short, length_y = modes.shape
    waves = jnp.einsum("nqia,ya->nqiy", modes.reshape(planes, RADIX, 2 * short, length_y), sine_y, precision=high)
    mixed = jnp.einsum("qji,nqjy->nqiy", wave_t, waves, precision=high)
    mixed = mixed.reshape(planes, RADIX, 2, short, length_y)
    even, odd = mixed[:, 0] + mixed[:, 2], mixed[:, 1] + mixed[:, 3]
    even_d, odd_d = mixed[:, 0] - mixed[:, 2], mixed[:, 1] - mixed[:, 3]
    turned = jnp.stack([-odd_d[:, 1], odd_d[:, 0]], axis=1)
    parts = jnp.stack([even + odd, even_d + turned, even - odd, even_d - turned], axis=2)
    return parts.reshape(planes, 2, RADIX * short, length_y).transpose(1, 0, 2, 3)


def cmul(a, b):
    return (a[0] * b[0] - a[1] * b[1], a[0] * b[1] + a[1] * b[0])


def cadd(a, b):
    return (a[0] + b[0], a[1] + b[1])


def cmore(total, factor, term):
    return cadd(total, cmul(factor, term))


def cinv(a):
    scale = 1.0 / (a[0] * a[0] + a[1] * a[1])
    return (a[0] * scale, -a[1] * scale)


def cone(a):
    return (1.0 - a[0], -a[1])


def cpick(cond, a, b):
    return (jnp.where(cond, a[0], b[0]), jnp.where(cond, a[1], b[1]))


def cpower(base, count, most):
    result = (jnp.ones_like(base[0]), jnp.zeros_like(base[0]))
    bit = 0
    while (1 << bit) <= most:
        taken = (count >> bit) & 1 == 1
        result = cpick(taken, cmul(result, base), result)
        base = cmul(base, base)
        bit += 1
    return result


def decay_root(h):
    sq = (h[0] + 0.25 * (h[0] * h[0] - h[1] * h[1]), h[1] + 0.5 * h[0] * h[1])
    size = jnp.sqrt(sq[0] * sq[0] + sq[1] * sq[1])
    root_re = jnp.sqrt(0.5 * (size + sq[0]))
    root = (root_re, 0.5 * sq[1] / root_re)
    return cinv((1.0 + 0.5 * h[0] + root[0], 0.5 * h[1] + root[1]))


def expand(weights):
    return weights[None, :, None, :]


def yz_part(field, upper, lower, conduct, cond_hi, cond_lo):
    cond_pad = jnp.pad(conduct, ((0, 0), (1, 1)), mode="edge")
    face_yp = 0.5 * (conduct + cond_pad[:, 2:])
    face_ym = 0.5 * (conduct + cond_pad[:, :-2])
    face_zp = 0.5 * (conduct + cond_hi)
    face_zm = 0.5 * (conduct + cond_lo)
    field_pad = jnp.pad(field, ((0, 0), (0, 0), (0, 0), (1, 1)))
    total = expand(face_yp) * (field - field_pad[..., 2:]) + expand(face_ym) * (
        field - field_pad[..., :-2]
    )
    return total + expand(face_zp) * (field - upper) + expand(face_zm) * (field - lower)


def shift_mult(shift_re, shift_im, field):
    return jnp.stack(
        [shift_re * field[0] - shift_im * field[1], shift_re * field[1] + shift_im * field[0]]
    )


def pair_up(arrays, groups, flip):
    pairs = [(i, i ^ flip) for i in range(groups)]
    return lax.ppermute(arrays, "gz", pairs)


def step_out(arrays, groups, distance):
    pairs = []
    for i in range(groups):
        j = i + distance if i & 1 else i - distance
        if 0 <= j < groups:
            pairs.append((i, j))
    return lax.ppermute(arrays, "gz", pairs)


def packed(a):
    return jnp.stack(a)


def unpacked(a):
    return (a[0], a[1])


def halves(a, first):
    mid = a[0].shape[0] // 2
    low, high_part = (a[0][:mid], a[1][:mid]), (a[0][mid:], a[1][mid:])
    return cpick(first, low, high_part), cpick(first, high_part, low)


def scan_sums(ahead, behind, powers, groups):
    me = lax.axis_index("gz")
    core = me & 1
    side = (me >> 1) & 1
    rho_n, rho_2n, rho_4n = powers
    is_fwd = core == 1
    keep = cpick(is_fwd, ahead, behind)
    give = cpick(is_fwd, behind, ahead)
    beside = unpacked(pair_up(packed(give), groups, 1))
    chip = cmore(keep, rho_n, beside)
    low_half = side == 0
    own, other = halves(chip, low_half)
    far_2n, _ = halves(rho_2n, low_half)
    factor, _ = halves(rho_4n, low_half)
    got = unpacked(pair_up(packed(other), groups, 2))
    leads = side != core
    near = cpick(leads, got, own)
    far = cpick(leads, own, got)
    run = cmore(near, far_2n, far)
    enter = None
    gap = None
    distance = 1
    while 4 * distance < groups:
        came = unpacked(step_out(packed(run), groups, 4 * distance))
        if enter is None:
            enter, gap = came, factor
        else:
            enter = cmore(enter, gap, came)
            gap = cmul(gap, factor)
        run = cmore(run, factor, came)
        factor = cmul(factor, factor)
        distance *= 2
    second = cmore(far, far_2n, enter)
    mine = cpick(leads, enter, second)
    theirs = cpick(leads, second, enter)
    back = unpacked(pair_up(packed(theirs), groups, 2))
    first_half = cpick(low_half, mine, back)
    last_half = cpick(low_half, back, mine)
    whole = tuple(jnp.concatenate([first_half[i], last_half[i]], axis=0) for i in range(2))
    passed = unpacked(pair_up(packed(whole), groups, 1))
    mid = cmore(beside, rho_n, whole)
    return cpick(is_fwd, mid, passed), cpick(is_fwd, passed, mid)


def solve_z(modes, rho, weights, inverse_d, powers, groups):
    planes = len(modes)
    weight_f, weight_b = weights
    fwd = [cmul(weight_f[i + 1], modes[i]) for i in range(planes)]
    bwd = [cmul(weight_b[i + 1], modes[i]) for i in range(planes)]
    ahead = fwd[0]
    for i in range(1, planes):
        ahead = cmore(fwd[i], rho, ahead)
    behind = bwd[-1]
    for i in range(planes - 2, -1, -1):
        behind = cmore(bwd[i], rho, behind)
    enter_f, enter_b = scan_sums(ahead, behind, powers, groups)
    run_f = [enter_f]
    for i in range(planes):
        run_f.append(cmore(fwd[i], rho, run_f[-1]))
    run_b = [enter_b]
    for i in range(planes - 1, -1, -1):
        run_b.append(cmore(bwd[i], rho, run_b[-1]))
    run_b = run_b[::-1]
    out = []
    for i in range(planes + 1):
        total = cadd(cmul(run_f[i], weight_b[i]), cmul(rho, cmul(run_b[i], weight_f[i])))
        out.append(cmul(total, inverse_d))
    total = cadd(cmul(rho, cmul(run_f[planes], weight_b[planes + 1])), cmul(run_b[planes], weight_f[planes + 1]))
    out.append(cmul(total, inverse_d))
    return out


def body(source, layer_ids, conduct_table, shift):
    shift_re = shift[0]
    shift_im = shift[1]
    planes = source.shape[1]
    length_x = source.shape[2]
    length_y = source.shape[3]
    groups = lax.axis_size("gz")
    length_z = planes * groups
    me = lax.axis_index("gz")
    layers = conduct_table.shape[0]
    onehot = layer_ids[:, :, None] == lax.iota(jnp.int32, layers)[None, None, :]
    conduct = jnp.sum(jnp.where(onehot, conduct_table[None, None, :], 0.0), axis=-1)
    everywhere = lax.all_gather(conduct, "gz", axis=0, tiled=True)
    mean_cond = jnp.sum(everywhere) / (length_y * length_z)
    first = me * planes
    cond_below = lax.dynamic_slice_in_dim(everywhere, jnp.maximum(first - 1, 0), 1, axis=0)
    cond_above = lax.dynamic_slice_in_dim(
        everywhere, jnp.minimum(first + planes, length_z - 1), 1, axis=0
    )
    rim = jnp.concatenate([cond_below, conduct, cond_above], axis=0)
    cond_hi, cond_lo = rim[2:], rim[:-2]

    wave_t = jnp.asarray(wave_tables(length_x))
    sine_y = jnp.asarray(sine_table(length_y))
    eig = jnp.asarray(wave_eigen(length_x))[:, :, None] + jnp.asarray(sine_eigen(length_y))[None, None, :]
    inv_cond = 1.0 / mean_cond
    h = (eig + shift_re * inv_cond, jnp.broadcast_to(shift_im * inv_cond, eig.shape))
    rho = decay_root(h)
    rho_2 = cmul(rho, rho)
    lead = cmul(rho_2, cpower(rho_2, first, length_z))
    tail = cmul(rho_2, cpower(rho_2, length_z - first - planes, length_z))
    pow_f = [cpower(rho_2, first, length_z), lead]
    pow_b = [cpower(rho_2, length_z - first - planes, length_z), tail]
    for _ in range(planes):
        pow_f.append(cmul(pow_f[-1], rho_2))
        pow_b.append(cmul(pow_b[-1], rho_2))
    weight_f = [cone(a) for a in pow_f]
    weight_b = [cone(a) for a in pow_b][::-1]
    whole = cmul(pow_f[0], pow_b[-1])
    rho_inv = (1.0 + 0.5 * h[0], 0.5 * h[1])
    gap = (rho_inv[0] - rho[0], rho_inv[1] - rho[1])
    scale = relax / length_x
    inverse_d = cinv(cmul((2.0 * mean_cond * gap[0], 2.0 * mean_cond * gap[1]), cone(whole)))
    inverse_d = (scale * inverse_d[0], scale * inverse_d[1])
    rho_n = rho
    for _ in range(planes - 1):
        rho_n = cmul(rho_n, rho)
    rho_2n = cmul(rho_n, rho_n)
    powers = (rho_n, rho_2n, cmul(rho_2n, rho_2n))

    cells = length_x * length_y * length_z
    partials = []
    solution = jnp.zeros_like(source)
    for iteration in range(ITERS):
        if iteration == 0:
            resid = source
        else:
            lap = expand(conduct) * (
                2.0 * solution - jnp.roll(solution, 1, 2) - jnp.roll(solution, -1, 2)
            )
            lap = lap + yz_part(solution, rims[:, 2:], rims[:, :-2], conduct, cond_hi, cond_lo)
            resid = source - (shift_mult(shift_re, shift_im, solution) + lap)
        partials.append(jnp.sum(resid * resid))
        spectra = forward(resid, wave_t, sine_y)
        modes = [(spectra[i, :, 0], spectra[i, :, 1]) for i in range(planes)]
        solved = solve_z(modes, rho, (weight_f, weight_b), inverse_d, powers, groups)
        if iteration == ITERS - 1:
            solved = solved[1:-1]
        update = backward(jnp.stack([jnp.stack(a, axis=1) for a in solved]), wave_t, sine_y)
        if iteration == ITERS - 1:
            solution = solution + update
        else:
            rims = update
            solution = update[:, 1:-1]
    norms = jnp.sqrt(lax.psum(jnp.stack(partials), "gz") / cells)
    return (solution, norms)


def solution(mesh):
    placed = (P(None, ("node", "gz"), None, None), P(("node", "gz"), None), P(), P("node"))
    return jax.shard_map(
        body,
        mesh=mesh,
        in_specs=placed,
        out_specs=(P(None, ("node", "gz"), None, None), P("node")),
        check_vma=False,
    )
```

```python
import functools

import jax
import jax.numpy as jnp
import ml_dtypes
import numpy as np
from jax import lax
from jax.experimental import pallas as pl
from jax.experimental.pallas import tpu as pltpu
from jax.sharding import PartitionSpec as P

RADIX = 4
CHUNKS = 2
TAG = 8

relax = 0.6


def sine_table(length):
    indices = np.arange(1, length + 1)
    product = indices[:, None] * indices[None, :] % (2 * (length + 1))
    return np.sqrt(2.0 / (length + 1)) * np.sin(np.pi / (length + 1) * product)


def sine_eigen(length):
    indices = np.arange(1, length + 1)
    return 4.0 * np.sin(np.pi / (2 * (length + 1)) * indices) ** 2


def wave_numbers(length):
    return RADIX * np.arange(length // RADIX)[None, :] + np.arange(RADIX)[:, None]


def wave_eigen(length):
    return 4.0 * np.sin(np.pi / length * wave_numbers(length)) ** 2


def wave_tables(length):
    waves = wave_numbers(length)
    product = waves[:, :, None] * np.arange(length // RADIX)[None, None, :] % length
    angles = 2.0 * np.pi / length * product
    cos_t, sin_t = np.cos(angles), np.sin(angles)
    top = np.concatenate([cos_t, sin_t], axis=2)
    low = np.concatenate([-sin_t, cos_t], axis=2)
    return np.concatenate([top, low], axis=1)


def two_terms(table):
    first = table.astype(ml_dtypes.bfloat16)
    return np.stack([first, (table - first.astype(np.float64)).astype(ml_dtypes.bfloat16)])


def split(value):
    first = value.astype(jnp.bfloat16)
    return first, (value - first.astype(jnp.float32)).astype(jnp.bfloat16)


def dot3(a, b):
    def one(x, y):
        return jnp.dot(x, y, preferred_element_type=jnp.float32)

    return one(a[0], b[0]) + (one(a[0], b[1]) + one(a[1], b[0]))


def cmul(a, b):
    return (a[0] * b[0] - a[1] * b[1], a[0] * b[1] + a[1] * b[0])


def csqr(a):
    cross = a[0] * a[1]
    return ((a[0] - a[1]) * (a[0] + a[1]), cross + cross)


def cadd(a, b):
    return (a[0] + b[0], a[1] + b[1])


def cmore(total, factor, term):
    return cadd(total, cmul(factor, term))


def cinv(a):
    scale = 1.0 / (a[0] * a[0] + a[1] * a[1])
    return (a[0] * scale, -a[1] * scale)


def cone(a):
    return (1.0 - a[0], -a[1])


def cpick(cond, a, b):
    return (jnp.where(cond, a[0], b[0]), jnp.where(cond, a[1], b[1]))


def load(ref, base, short, row, rows):
    return (
        ref[pl.ds(pl.multiple_of(base + row, 8), rows), :],
        ref[pl.ds(pl.multiple_of(base + short + row, 8), rows), :],
    )


def store(ref, base, short, row, rows, value):
    ref[pl.ds(pl.multiple_of(base + row, 8), rows), :] = value[0]
    ref[pl.ds(pl.multiple_of(base + short + row, 8), rows), :] = value[1]


def each_strip(count, rows, body, unroll=1):
    def step(i, carry):
        body(pl.multiple_of(i * rows, rows))
        return carry

    lax.fori_loop(0, count // rows, step, 0, unroll=unroll)


def transform_plane(field_ref, plane, chunk, wave_ref, sine_ref, spectra_ref, place):
    parts = [[field_ref[p, plane, j] for j in range(RADIX)] for p in range(2)]
    if chunk == 0:
        even = [parts[p][0] + parts[p][2] for p in range(2)]
        odd = [parts[p][1] + parts[p][3] for p in range(2)]
    else:
        even = [parts[p][0] - parts[p][2] for p in range(2)]
        odd = [parts[1][1] - parts[1][3], parts[0][3] - parts[0][1]]
    sine = (sine_ref[0], sine_ref[1])
    for half in range(2):
        if half == 0:
            mixed = jnp.concatenate([even[0] + odd[0], even[1] + odd[1]], axis=0)
        else:
            mixed = jnp.concatenate([even[0] - odd[0], even[1] - odd[1]], axis=0)
        rows = mixed.shape[0]
        waves = dot3((wave_ref[0, half], wave_ref[1, half]), split(mixed))
        spectra_ref[place, pl.ds(half * rows, rows), :] = dot3(split(waves), sine)


def forward_kernel(chunk, flags_ref, field_ref, wave_ref, sine_ref, spectra_ref):
    core = flags_ref[0]
    for place in range(2):
        transform_plane(field_ref, core ^ place, chunk, wave_ref, sine_ref, spectra_ref, place)


def decay_root(h):
    sq = (h[0] + 0.25 * (h[0] * h[0] - h[1] * h[1]), h[1] + 0.5 * h[0] * h[1])
    size = jnp.sqrt(sq[0] * sq[0] + sq[1] * sq[1])
    root_re = jnp.sqrt(0.5 * (size + sq[0]))
    root = (root_re, 0.5 * sq[1] / root_re)
    return cinv((1.0 + 0.5 * h[0] + root[0], 0.5 * h[1] + root[1])), root


def far_powers(rho_4, gamma, groups):
    near = far = None
    bit = 0
    power = rho_4
    while (1 << bit) < groups:
        taken = ((gamma >> bit) & 1) == 1
        if near is None:
            one = (jnp.ones_like(power[0]), jnp.zeros_like(power[0]))
            near, far = cpick(taken, power, one), cpick(taken, one, power)
        else:
            grown = cmul(cpick(taken, near, far), power)
            near, far = cpick(taken, grown, near), cpick(taken, far, grown)
        power = csqr(power)
        bit += 1
    return near, far


def first_sums_kernel(
    groups, flags_ref, numbers_ref, eigen_ref, spectra_ref, tag_ref,
    keep_ref, give_ref, square_ref, sums_ref, rest_ref,
):
    short = eigen_ref.shape[1]
    gamma = flags_ref[3]
    h_re, h_im = numbers_ref[1], numbers_ref[2]
    for half in range(2):
        base = half * 2 * short

        def strip(row):
            eigen = eigen_ref[half, pl.ds(row, 8), :]
            h = (eigen + h_re, jnp.full_like(eigen, h_im))
            rho, root = decay_root(h)
            square = csqr(rho)
            fourth = csqr(square)
            near, far = far_powers(fourth, gamma, groups)
            near_o = cmul(near, square)
            near_i = cmul(near_o, square)
            far_i = cmul(far, square)
            far_o = cmul(far_i, square)
            coeffs = (cone(far_o), cmul(rho, cone(far_i)), cmul(rho, cone(near_o)), cone(near_i))
            outer = load(spectra_ref.at[0], base, short, row, 8)
            inner = load(spectra_ref.at[1], base, short, row, 8)
            store(keep_ref, base, short, row, 8, cmore(cmul(coeffs[0], outer), coeffs[1], inner))
            store(give_ref, base, short, row, 8, cmore(cmul(coeffs[2], outer), coeffs[3], inner))
            store(square_ref, base, short, row, 8, square)
            for i in range(4):
                store(sums_ref.at[i], base, short, row, 8, coeffs[i])
            for i, value in enumerate((rho, root, near, far)):
                store(rest_ref.at[i], base, short, row, 8, value)

        each_strip(short, 8, strip)
    keep_ref[pl.ds(4 * short, TAG), :] = tag_ref[...]
    give_ref[pl.ds(4 * short, TAG), :] = tag_ref[...]


def solve_coeffs_kernel(numbers_ref, eigen_ref, rest_ref, coeffs_ref):
    short = eigen_ref.shape[1]
    h_re, h_im, scale = numbers_ref[1], numbers_ref[2], numbers_ref[6]
    for half in range(2):
        base = half * 2 * short

        def strip(row):
            rho, root, near, far = [load(rest_ref.at[i], base, short, row, 8) for i in range(4)]
            eigen = eigen_ref[half, pl.ds(row, 8), :]
            cube = cmul(csqr(rho), csqr(csqr(rho)))
            near_3 = cmul(near, cube)
            far_3 = cmul(far, cube)
            whole = cinv(cmul(root, cone(cmul(near, far_3))))
            whole = (scale * whole[0], scale * whole[1])
            turned = cmul(rho, whole)
            store(coeffs_ref.at[0], base, short, row, 8, cmul(cone(far_3), whole))
            store(coeffs_ref.at[1], base, short, row, 8, cmul(cone(near), turned))
            store(coeffs_ref.at[2], base, short, row, 8, cmul(cone(far), turned))
            store(coeffs_ref.at[3], base, short, row, 8, cmul(cone(near_3), whole))
            w = (2.0 + h_re + eigen, jnp.full_like(eigen, h_im))
            square = csqr(w)
            beta = cinv((square[0] - 1.0, square[1]))
            store(coeffs_ref.at[4], base, short, row, 8, cmul(w, beta))
            store(coeffs_ref.at[5], base, short, row, 8, beta)

        each_strip(short, 8, strip)


def chip_kernel(short, flags_ref, keep_ref, beside_ref, square_ref, own_ref, other_ref):
    side = flags_ref[1]
    for out_ref, half in ((own_ref, side), (other_ref, 1 - side)):
        base = half * 2 * short

        def strip(row):
            chip = cmore(
                load(keep_ref, base, short, row, 16),
                load(square_ref, base, short, row, 16),
                load(beside_ref, base, short, row, 16),
            )
            store(out_ref, 0, short, row, 16, chip)

        each_strip(short, 16, strip)
        out_ref[pl.ds(2 * short, TAG), :] = (
            keep_ref[pl.ds(4 * short, TAG), :] + beside_ref[pl.ds(4 * short, TAG), :]
        )


def pair_kernel(short, flags_ref, own_ref, got_ref, square_ref, run_ref):
    base = flags_ref[1] * 2 * short
    leads = flags_ref[2] == 1

    def strip(row):
        own = load(own_ref, 0, short, row, 16)
        got = load(got_ref, 0, short, row, 16)
        fourth = csqr(load(square_ref, base, short, row, 16))
        run = cmore(cpick(leads, got, own), fourth, cpick(leads, own, got))
        store(run_ref, 0, short, row, 16, run)

    each_strip(short, 16, strip)
    tag = pl.ds(2 * short, TAG)
    run_ref[tag, :] = own_ref[tag, :] + got_ref[tag, :]


def step_kernel(short, doublings, flags_ref, run_ref, came_ref, square_ref, next_ref):
    base = flags_ref[1] * 2 * short

    def strip(row):
        factor = csqr(csqr(load(square_ref, base, short, row, 16)))
        for _ in range(doublings):
            factor = csqr(factor)
        run = cmore(load(run_ref, 0, short, row, 16), factor, load(came_ref, 0, short, row, 16))
        store(next_ref, 0, short, row, 16, run)

    each_strip(short, 16, strip)
    tag = pl.ds(2 * short, TAG)
    next_ref[tag, :] = run_ref[tag, :] + came_ref[tag, :]


def enter_kernel(short, steps, flags_ref, own_ref, got_ref, square_ref, *refs):
    came_refs, (mine_ref, theirs_ref) = refs[:steps], refs[steps:]
    base = flags_ref[1] * 2 * short
    leads = flags_ref[2] == 1

    def strip(row):
        fourth = csqr(load(square_ref, base, short, row, 16))
        factor = csqr(fourth)
        enter = load(came_refs[0], 0, short, row, 16)
        gap = factor
        for came_ref in came_refs[1:]:
            enter = cmore(enter, gap, load(came_ref, 0, short, row, 16))
            factor = csqr(factor)
            gap = cmul(gap, factor)
        far = cpick(leads, load(own_ref, 0, short, row, 16), load(got_ref, 0, short, row, 16))
        second = cmore(far, fourth, enter)
        store(mine_ref, 0, short, row, 16, cpick(leads, enter, second))
        store(theirs_ref, 0, short, row, 16, cpick(leads, second, enter))

    each_strip(short, 16, strip)
    tag = pl.ds(2 * short, TAG)
    total = came_refs[0][tag, :]
    for came_ref in came_refs[1:]:
        total = total + came_ref[tag, :]
    mine_ref[tag, :] = total
    theirs_ref[tag, :] = total


def join_kernel(short, flags_ref, mine_ref, back_ref, whole_ref):
    side = flags_ref[1]
    for ref, half in ((mine_ref, side), (back_ref, 1 - side)):
        base = half * 2 * short

        def strip(row):
            store(whole_ref, base, short, row, 16, load(ref, 0, short, row, 16))

        each_strip(short, 16, strip)
    whole_ref[pl.ds(4 * short, TAG), :] = mine_ref[pl.ds(2 * short, TAG), :]


def inverse_kernel(
    short, rims, numbers_ref, spectra_ref, keep_ref, give_ref, beside_ref, whole_ref, passed_ref,
    square_ref, coeffs_ref, wave_ref, sine_ref, out_ref, field_ref,
):
    scale = numbers_ref[3]
    for half in range(2):
        base = half * 2 * short

        def strip(row):
            def get(ref):
                return load(ref, base, short, row, 8)

            square = get(square_ref)
            passed = get(passed_ref)
            mid = cmore(get(beside_ref), square, get(whole_ref))
            toward = cmore(get(keep_ref), square, mid)
            away = cmore(get(give_ref), square, passed)
            beyond_o = cmore(cmul(get(coeffs_ref.at[0]), passed), get(coeffs_ref.at[1]), toward)
            beyond_i = cmore(cmul(get(coeffs_ref.at[3]), mid), get(coeffs_ref.at[2]), away)
            outer = get(spectra_ref.at[0])
            inner = get(spectra_ref.at[1])
            outer = (scale * outer[0] + beyond_o[0], scale * outer[1] + beyond_o[1])
            inner = (scale * inner[0] + beyond_i[0], scale * inner[1] + beyond_i[1])
            alpha, beta = get(coeffs_ref.at[4]), get(coeffs_ref.at[5])
            store(field_ref.at[0], base, short, row, 8, cmore(cmul(alpha, outer), beta, inner))
            store(field_ref.at[1], base, short, row, 8, cmore(cmul(alpha, inner), beta, outer))
            if rims:
                store(field_ref.at[2], base, short, row, 8, beyond_o)
                store(field_ref.at[3], base, short, row, 8, beyond_i)

        each_strip(short, 8, strip)
    sine = (sine_ref[0], sine_ref[1])
    for plane in range(field_ref.shape[0]):
        for half in range(2):
            rows = pl.ds(half * 2 * short, 2 * short)
            waves = dot3(split(field_ref[plane, rows, :]), sine)
            out_ref[plane, rows, :] = dot3((wave_ref[0, half], wave_ref[1, half]), split(waves))


def butterfly(even_ref, odd_ref, plane, short, row, rows):
    zero = load(even_ref.at[plane], 0, short, row, rows)
    two = load(even_ref.at[plane], 2 * short, short, row, rows)
    one = load(odd_ref.at[plane], 0, short, row, rows)
    three = load(odd_ref.at[plane], 2 * short, short, row, rows)
    even, odd = cadd(zero, two), cadd(one, three)
    even_d = (zero[0] - two[0], zero[1] - two[1])
    odd_d = (one[0] - three[0], one[1] - three[1])
    return (
        (even[0] + odd[0], even[1] + odd[1]),
        (even_d[0] - odd_d[1], even_d[1] + odd_d[0]),
        (even[0] - odd[0], even[1] - odd[1]),
        (even_d[0] + odd_d[1], even_d[1] - odd_d[0]),
    )


def residual_kernel(
    short, flags_ref, numbers_ref, source_ref, even_ref, odd_ref, faces_ref,
    resid_ref, iterate_ref, tag_ref, field_ref,
):
    core = flags_ref[0]
    s_re, s_im = numbers_ref[4], numbers_ref[5]
    length_x = RADIX * short
    for plane in range(4):

        def strip(row):
            parts = butterfly(even_ref, odd_ref, plane, short, row, 8)
            for j in range(RADIX):
                for p in range(2):
                    at = pl.ds(pl.multiple_of(8 + j * short + row, 8), 8)
                    field_ref[plane, p, at, :] = parts[j][p]
                    if plane < 2:
                        at = pl.ds(pl.multiple_of(j * short + row, 8), 8)
                        iterate_ref[p, core ^ plane, at, :] = parts[j][p]

        each_strip(short, 8, strip)
        if plane < 2:
            for p in range(2):
                field_ref[plane, p, pl.ds(0, 8), :] = field_ref[plane, p, pl.ds(length_x, 8), :]
                field_ref[plane, p, pl.ds(length_x + 8, 8), :] = field_ref[plane, p, pl.ds(8, 8), :]

    width = resid_ref.shape[-1]
    squares = jnp.zeros((16, width), jnp.float32)
    squares_source = jnp.zeros((16, width), jnp.float32)
    for plane in range(2):
        faces = [faces_ref[pl.ds(8 * plane + i, 1), :] for i in range(6)]
        diag, along, right, left, beyond, between = faces

        def strip(i, carry):
            total, total_source = carry
            row = pl.multiple_of(i * 16, 16)
            here = []
            for p in range(2):
                wide = field_ref[plane, p, pl.ds(row, 32), :]
                cells = wide[8:24]
                value = diag * cells - along * (wide[7:23] + wide[9:25])
                value = value - right * pltpu.roll(cells, width - 1, 1) - left * pltpu.roll(cells, 1, 1)
                at = pl.ds(pl.multiple_of(row + 8, 8), 16)
                value = value - beyond * field_ref[2 + plane, p, at, :]
                value = value - between * field_ref[1 - plane, p, at, :]
                here.append((cells, value))
            (u_re, l_re), (u_im, l_im) = here
            f_re = source_ref[0, core ^ plane, pl.ds(row, 16), :]
            f_im = source_ref[1, core ^ plane, pl.ds(row, 16), :]
            r_re = f_re - (s_re * u_re - s_im * u_im + l_re)
            r_im = f_im - (s_re * u_im + s_im * u_re + l_im)
            resid_ref[0, core ^ plane, pl.ds(row, 16), :] = r_re
            resid_ref[1, core ^ plane, pl.ds(row, 16), :] = r_im
            return (
                total + (r_re * r_re + r_im * r_im),
                total_source + (f_re * f_re + f_im * f_im),
            )

        squares, squares_source = lax.fori_loop(0, length_x // 16, strip, (squares, squares_source))
    tag_ref[...] = jnp.zeros_like(tag_ref)
    tag_ref[pl.ds(0, 1), :] = jnp.sum(squares_source, axis=0, keepdims=True)
    tag_ref[pl.ds(1, 1), :] = jnp.sum(squares, axis=0, keepdims=True)


def next_sums_kernel(
    chunk, short, flags_ref, field_ref, wave_ref, sine_ref, tag_ref, sums_ref,
    spectra_ref, keep_ref, give_ref,
):
    forward_kernel(chunk, flags_ref, field_ref, wave_ref, sine_ref, spectra_ref)
    for half in range(2):
        base = half * 2 * short

        def strip(row):
            coeffs = [load(sums_ref.at[i], base, short, row, 8) for i in range(4)]
            outer = load(spectra_ref.at[0], base, short, row, 8)
            inner = load(spectra_ref.at[1], base, short, row, 8)
            store(keep_ref, base, short, row, 8, cmore(cmul(coeffs[0], outer), coeffs[1], inner))
            store(give_ref, base, short, row, 8, cmore(cmul(coeffs[2], outer), coeffs[3], inner))

        each_strip(short, 8, strip)
    keep_ref[pl.ds(4 * short, TAG), :] = tag_ref[...]
    give_ref[pl.ds(4 * short, TAG), :] = tag_ref[...]


def finish_kernel(
    short, cells, flags_ref, iterate_ref, even_ref, odd_ref, run_ref, whole_ref, passed_ref,
    out_ref, norms_ref,
):
    core = flags_ref[0]
    for plane in range(2):

        def strip(row):
            parts = butterfly(even_ref, odd_ref, plane, short, row, 8)
            for j in range(RADIX):
                for p in range(2):
                    at = pl.ds(pl.multiple_of(j * short + row, 8), 8)
                    before = iterate_ref[p, core ^ plane, at, :]
                    out_ref[p, core ^ plane, at, :] = before + parts[j][p]

        each_strip(short, 8, strip)
    total = run_ref[pl.ds(2 * short, TAG), :] + (
        whole_ref[pl.ds(4 * short, TAG), :] + passed_ref[pl.ds(4 * short, TAG), :]
    )
    norms = jnp.sqrt(jnp.sum(total, axis=1, keepdims=True) * (1.0 / cells))
    norms_ref[...] = jnp.broadcast_to(norms, norms_ref.shape)


smem = pl.BlockSpec(memory_space=pltpu.SMEM)
vmem = pl.BlockSpec(memory_space=pltpu.VMEM)


def call(kernel, scalars, arrays, outs, scratch=(), flops=0):
    out_shape = [jax.ShapeDtypeStruct(shape, jnp.float32) for shape in outs]
    moved = sum(a.size * a.dtype.itemsize for a in arrays) + sum(4 * int(np.prod(s)) for s in outs)
    return pl.pallas_call(
        kernel,
        out_shape=out_shape,
        in_specs=[smem] * len(scalars) + [vmem] * len(arrays),
        out_specs=[vmem] * len(outs),
        scratch_shapes=[pltpu.VMEM(shape, jnp.float32) for shape in scratch],
        compiler_params=pltpu.CompilerParams(vmem_limit_bytes=48 * 2**20),
        cost_estimate=pl.CostEstimate(flops=flops, bytes_accessed=moved, transcendentals=0),
    )(*scalars, *arrays)


def pair_up(array, groups, flip):
    return lax.ppermute(array, "gz", [(i, i ^ flip) for i in range(groups)])


def step_out(array, groups, distance):
    pairs = []
    for i in range(groups):
        j = i + distance if i & 1 else i - distance
        if 0 <= j < groups:
            pairs.append((i, j))
    return lax.ppermute(array, "gz", pairs)


def scan_sums(keep, give, square, flags, groups, short, width):
    half = (2 * short + TAG, width)
    both = (4 * short + TAG, width)
    beside = pair_up(give, groups, 1)
    own, other = call(functools.partial(chip_kernel, short), [flags], [keep, beside, square], [half, half])
    got = pair_up(other, groups, 2)
    (first_run,) = call(functools.partial(pair_kernel, short), [flags], [own, got, square], [half])
    run = first_run
    came = []
    steps = 0
    while 4 << steps < groups:
        came.append(step_out(run, groups, 4 << steps))
        if 8 << steps < groups:
            (run,) = call(
                functools.partial(step_kernel, short, steps), [flags], [run, came[-1], square], [half]
            )
        steps += 1
    mine, theirs = call(
        functools.partial(enter_kernel, short, steps), [flags], [own, got, square, *came], [half, half]
    )
    back = pair_up(theirs, groups, 2)
    (whole,) = call(functools.partial(join_kernel, short), [flags], [mine, back], [both])
    passed = pair_up(whole, groups, 1)
    return beside, whole, passed, first_run


def body(source, layer_ids, conduct_table, shift):
    planes, length_x, length_y = source.shape[1:]
    groups = lax.axis_size("gz")
    length_z = planes * groups
    short = length_x // RADIX
    if planes != 2 or groups < 8 or groups & (groups - 1) or short % 16 or length_x % RADIX:
        raise ValueError("unsupported layout")
    me = lax.axis_index("gz")
    core = me & 1
    side = (me >> 1) & 1
    gamma = jnp.where(core == 0, me, groups - 1 - me)
    flags = jnp.stack([core, side, (side != core).astype(jnp.int32), gamma]).astype(jnp.int32)

    layers = conduct_table.shape[0]
    onehot = layer_ids[:, :, None] == lax.iota(jnp.int32, layers)[None, None, :]
    conduct = jnp.sum(jnp.where(onehot, conduct_table[None, None, :], 0.0), axis=-1)
    total = jnp.sum(conduct)
    flip = 1
    while flip < groups:
        total = total + pair_up(total, groups, flip)
        flip *= 2
    mean_cond = total / (length_y * length_z)
    inv_cond = 1.0 / mean_cond
    scale = relax / length_x * inv_cond
    numbers = jnp.stack(
        [inv_cond, shift[0] * inv_cond, shift[1] * inv_cond, scale, shift[0], shift[1], 0.5 * scale]
    )

    outer = jnp.where(core == 0, conduct[:1], conduct[1:])
    inner = jnp.where(core == 0, conduct[1:], conduct[:1])
    beyond_o = jnp.where(gamma == 0, outer, step_out_rows(outer, groups))
    beyond_i = pair_up(inner, groups, 1)
    lane = lax.broadcasted_iota(jnp.int32, (1, length_y), 1)
    rows = []
    for cells, beyond in ((outer, beyond_o), (inner, beyond_i)):
        right = 0.5 * (cells + jnp.roll(cells, -1, 1))
        left = 0.5 * (cells + jnp.roll(cells, 1, 1))
        far_face = 0.5 * (cells + beyond)
        between = 0.5 * (outer + inner)
        right_edge = lane == length_y - 1
        left_edge = lane == 0
        diag = 2.0 * cells + jnp.where(right_edge, cells, right) + jnp.where(left_edge, cells, left)
        diag = diag + far_face + between
        right = jnp.where(right_edge, 0.0, right)
        left = jnp.where(left_edge, 0.0, left)
        rows += [diag, cells, right, left, far_face, between, cells, cells]
    faces = jnp.concatenate(rows, axis=0)

    waves = two_terms(wave_tables(length_x))
    turned = np.ascontiguousarray(np.swapaxes(waves, 2, 3))
    chunk_rows = [np.arange(chunk, RADIX, CHUNKS) for chunk in range(CHUNKS)]
    wave_f = [jnp.asarray(waves[:, rows]) for rows in chunk_rows]
    wave_b = [jnp.asarray(turned[:, rows]) for rows in chunk_rows]
    sine = jnp.asarray(two_terms(sine_table(length_y)))
    eigen = wave_eigen(length_x)[:, :, None] + sine_eigen(length_y)[None, None, :]
    eigen = [jnp.asarray(eigen[rows].astype(np.float32)) for rows in chunk_rows]

    both = (4 * short + TAG, length_y)
    modes = (4 * short, length_y)
    parted = (2, planes, RADIX, short, length_y)
    plain = (2, planes, length_x, length_y)
    matmul = 2 * 3 * (2 * short) * length_y * (2 * short + length_y)

    chunks = range(CHUNKS)
    blank = jnp.zeros((TAG, length_y), jnp.float32)
    spectra, sums, squares, coeffs, keep, give = [], [], [], [], [], []
    for t in chunks:
        (a,) = call(
            functools.partial(forward_kernel, t), [flags], [source.reshape(parted), wave_f[t], sine],
            [(2, *modes)], flops=4 * matmul,
        )
        spectra.append(a)
    rest = []
    for t in chunks:
        a, b, c, d, e = call(
            functools.partial(first_sums_kernel, groups), [flags, numbers], [eigen[t], spectra[t], blank],
            [both, both, modes, (4, *modes), (4, *modes)],
        )
        keep.append(a)
        give.append(b)
        squares.append(c)
        sums.append(d)
        rest.append(e)
    for t in chunks:
        (a,) = call(solve_coeffs_kernel, [numbers], [eigen[t], rest[t]], [(6, *modes)])
        coeffs.append(a)

    def solve(rims):
        mixed, scans = [], []
        for t in chunks:
            scans.append(scan_sums(keep[t], give[t], squares[t], flags, groups, short, length_y))
        for t in chunks:
            beside, whole, passed, _ = scans[t]
            count = 4 if rims else 2
            (a,) = call(
                functools.partial(inverse_kernel, short, rims), [numbers],
                [spectra[t], keep[t], give[t], beside, whole, passed, squares[t], coeffs[t], wave_b[t], sine],
                [(count, *modes)], scratch=[(count, *modes)], flops=2 * count * matmul,
            )
            mixed.append(a)
        return mixed, scans[0]

    mixed, _ = solve(True)
    resid, iterate, tag = call(
        functools.partial(residual_kernel, short), [flags, numbers], [source, *mixed, faces],
        [plain, plain, (TAG, length_y)], scratch=[(4, 2, length_x + 16, length_y)],
    )
    for t in chunks:
        spectra[t], keep[t], give[t] = call(
            functools.partial(next_sums_kernel, t, short), [flags],
            [resid.reshape(parted), wave_f[t], sine, tag, sums[t]],
            [(2, *modes), both, both], flops=4 * matmul,
        )
    mixed, (_, whole, passed, run) = solve(False)
    solution, norms = call(
        functools.partial(finish_kernel, short, length_x * length_y * length_z), [flags],
        [iterate, *mixed, run, whole, passed], [plain, (TAG, 128)],
    )
    return solution, norms[:2, 0]


def step_out_rows(rows, groups):
    pairs = []
    for i in range(groups):
        j = i + 1 if i & 1 else i - 1
        if 0 <= j < groups:
            pairs.append((i, j))
    return lax.ppermute(rows, "gz", pairs)


def solution(mesh):
    placed = (P(None, ("node", "gz"), None, None), P(("node", "gz"), None), P(), P("node"))
    return jax.shard_map(
        body,
        mesh=mesh,
        in_specs=placed,
        out_specs=(P(None, ("node", "gz"), None, None), P("node")),
        check_vma=False,
    )
```

```python
import functools

import jax
import jax.numpy as jnp
import ml_dtypes
import numpy as np
from jax import lax
from jax.experimental import pallas as pl
from jax.experimental.pallas import tpu as pltpu
from jax.sharding import PartitionSpec as P

RADIX = 4
CHUNKS = 2
TAG = 8

relax = 0.6


def sine_table(length):
    indices = np.arange(1, length + 1)
    product = indices[:, None] * indices[None, :] % (2 * (length + 1))
    return np.sqrt(2.0 / (length + 1)) * np.sin(np.pi / (length + 1) * product)


def sine_eigen(length):
    indices = np.arange(1, length + 1)
    return 4.0 * np.sin(np.pi / (2 * (length + 1)) * indices) ** 2


def wave_numbers(length):
    return RADIX * np.arange(length // RADIX)[None, :] + np.arange(RADIX)[:, None]


def wave_eigen(length):
    return 4.0 * np.sin(np.pi / length * wave_numbers(length)) ** 2


def wave_tables(length):
    waves = wave_numbers(length)
    short = length // RADIX
    product = waves[:, :, None] * np.arange(short)[None, None, :] % length
    angles = 2.0 * np.pi / length * product
    cos_t, sin_t = np.cos(angles), np.sin(angles)
    top = np.concatenate([cos_t, sin_t], axis=2).reshape(RADIX, CHUNKS, short // CHUNKS, 2 * short)
    low = np.concatenate([-sin_t, cos_t], axis=2).reshape(RADIX, CHUNKS, short // CHUNKS, 2 * short)
    return np.concatenate([top, low], axis=2).reshape(RADIX, 2 * short, 2 * short)


def two_terms(table):
    first = table.astype(ml_dtypes.bfloat16)
    return np.stack([first, (table - first.astype(np.float64)).astype(ml_dtypes.bfloat16)])


def split(value):
    first = value.astype(jnp.bfloat16)
    return first, (value - first.astype(jnp.float32)).astype(jnp.bfloat16)


def dot3(a, b):
    def one(x, y):
        return jnp.dot(x, y, preferred_element_type=jnp.float32)

    return one(a[0], b[0]) + (one(a[0], b[1]) + one(a[1], b[0]))


def cmul(a, b):
    return (a[0] * b[0] - a[1] * b[1], a[0] * b[1] + a[1] * b[0])


def csqr(a):
    cross = a[0] * a[1]
    return ((a[0] - a[1]) * (a[0] + a[1]), cross + cross)


def cpow(a, count):
    result = None
    while count:
        if count & 1:
            result = a if result is None else cmul(result, a)
        count >>= 1
        if count:
            a = csqr(a)
    return result


def cadd(a, b):
    return (a[0] + b[0], a[1] + b[1])


def csub(a, b):
    return (a[0] - b[0], a[1] - b[1])


def cscale(a, scale):
    return (a[0] * scale, a[1] * scale)


def cmore(total, factor, term):
    return cadd(total, cmul(factor, term))


def cinv(a):
    scale = 1.0 / (a[0] * a[0] + a[1] * a[1])
    return (a[0] * scale, -a[1] * scale)


def cone(a):
    return (1.0 - a[0], -a[1])


def cpick(cond, a, b):
    return (jnp.where(cond, a[0], b[0]), jnp.where(cond, a[1], b[1]))


def rows_at(start, rows):
    if isinstance(start, int):
        return pl.ds(start, rows)
    return pl.ds(pl.multiple_of(start, 8), rows)


def load(ref, base, short, row, rows):
    return (ref[rows_at(base + row, rows), :], ref[rows_at(base + short + row, rows), :])


def store(ref, base, short, row, rows, value):
    ref[rows_at(base + row, rows), :] = value[0]
    ref[rows_at(base + short + row, rows), :] = value[1]


def each_strip(count, rows, body):
    def step(i, carry):
        body(pl.multiple_of(i * rows, rows))
        return carry

    lax.fori_loop(0, count // rows, step, 0)


def squares_of(a):
    return a[0] * a[0] + a[1] * a[1]


def conduct_kernel(table_ref, ids_ref, out_ref):
    planes = ids_ref.shape[0]
    ids = ids_ref[...]
    cells = jnp.zeros(ids.shape, jnp.float32)
    for layer in range(table_ref.shape[0]):
        cells = jnp.where(ids == layer, table_ref[layer], cells)
    out_ref[...] = jnp.zeros_like(out_ref)
    out_ref[pl.ds(0, planes), :] = cells


def group_kernel(planes, flags_ref, own_ref, one_ref, two_ref, three_ref, cells_ref, edge_ref):
    j = flags_ref[0]
    for d, ref in enumerate((own_ref, one_ref, two_ref, three_ref)):
        for p in range(planes):
            cells_ref[pl.ds((j ^ d) * planes + p, 1), :] = ref[pl.ds(p, 1), :]
    count = cells_ref.shape[0]
    edge_ref[...] = jnp.zeros_like(edge_ref)
    edge_ref[pl.ds(0, 1), :] = jnp.sum(cells_ref[...], axis=0, keepdims=True)
    edge_ref[pl.ds(1, 1), :] = cells_ref[pl.ds(0, 1), :]
    edge_ref[pl.ds(2, 1), :] = cells_ref[pl.ds(count - 1, 1), :]


def total_kernel(cells, shift_ref, *refs):
    part_refs, out_ref = refs[:-1], refs[-1]
    total = part_refs[0][...]
    for ref in part_refs[1:]:
        total = total + ref[...]
    if cells is None:
        out_ref[...] = total
        return
    inv_cond = 1.0 / (jnp.sum(total[0:1, :], axis=1, keepdims=True) * (1.0 / cells))
    inv = inv_cond[0, 0]
    out_ref[0] = shift_ref[0] * inv
    out_ref[1] = shift_ref[1] * inv
    out_ref[2] = relax * inv
    out_ref[3] = 0.5 * relax * inv
    out_ref[4] = shift_ref[0]
    out_ref[5] = shift_ref[1]


def faces_kernel(stacks, flags_ref, cells_ref, below_ref, above_ref, faces_ref, padded_ref):
    z = flags_ref[1]
    count, width = cells_ref.shape
    cells = cells_ref[...]
    padded_ref[pl.ds(8, count), :] = cells
    padded_ref[pl.ds(7, 1), :] = jnp.where(z == 0, cells[0:1], below_ref[pl.ds(2, 1), :])
    padded_ref[pl.ds(8 + count, 1), :] = jnp.where(
        z == stacks - 1, cells[count - 1 : count], above_ref[pl.ds(1, 1), :]
    )
    lane = lax.broadcasted_iota(jnp.int32, cells.shape, 1)
    last, first = lane == width - 1, lane == 0
    right = 0.5 * (cells + pltpu.roll(cells, width - 1, 1))
    left = 0.5 * (cells + pltpu.roll(cells, 1, 1))
    low = 0.5 * (cells + padded_ref[pl.ds(7, count), :])
    high = 0.5 * (cells + padded_ref[pl.ds(9, count), :])
    faces_ref[0] = jnp.where(last, cells, right) + jnp.where(first, cells, left) + (low + high)
    faces_ref[1] = cells
    faces_ref[2] = jnp.where(last, 0.0, right)
    faces_ref[3] = jnp.where(first, 0.0, left)
    faces_ref[4] = low
    faces_ref[5] = high


def forward_kernel(distances, flags_ref, source_ref, wave_ref, *out_refs):
    planes = source_ref.shape[1]
    for n, d in enumerate(distances):
        q = flags_ref[0] ^ d
        sign = (1 - 2 * (q & 1)).astype(jnp.float32)
        turn_re = jnp.where(q == 0, 1.0, jnp.where(q == 2, -1.0, 0.0))
        turn_im = jnp.where(q == 1, 1.0, jnp.where(q == 3, -1.0, 0.0))
        for p in range(planes):
            parts = [[source_ref[c, p, i] for i in range(RADIX)] for c in range(2)]
            even = [parts[c][0] + sign * parts[c][2] for c in range(2)]
            odd = [parts[c][1] + sign * parts[c][3] for c in range(2)]
            mixed = jnp.concatenate(
                [
                    even[0] + (turn_re * odd[0] + turn_im * odd[1]),
                    even[1] + (turn_re * odd[1] - turn_im * odd[0]),
                ],
                axis=0,
            )
            waves = dot3((wave_ref[0, q], wave_ref[1, q]), split(mixed))
            rows = waves.shape[0] // CHUNKS
            for t in range(CHUNKS):
                out_refs[n * CHUNKS + t][pl.ds(p * rows, rows), :] = waves[t * rows : (t + 1) * rows]


def backward_kernel(planes, cells, flags_ref, wave_ref, *refs):
    arrays, (out_ref, norms_ref, mixed_ref) = refs[:-3], refs[-3:]
    rows = (arrays[0].shape[0] - TAG) // planes
    short = rows * CHUNKS // 2
    total = None
    for d in range(RADIX):
        q = flags_ref[0] ^ d
        chunks = arrays[d * CHUNKS : (d + 1) * CHUNKS]
        for ref in chunks:
            tag = ref[pl.ds(planes * rows, TAG), :]
            total = tag if total is None else total + tag
        for p in range(planes):
            waves = jnp.concatenate([ref[pl.ds(p * rows, rows), :] for ref in chunks], axis=0)
            mixed_ref[p, q] = dot3((wave_ref[0, q], wave_ref[1, q]), split(waves))
    for p in range(planes):

        def strip(row):
            zero, one, two, three = [load(mixed_ref.at[p, q], 0, short, row, 8) for q in range(RADIX)]
            even, odd = cadd(zero, two), cadd(one, three)
            even_d, odd_d = csub(zero, two), csub(one, three)
            parts = (
                cadd(even, odd),
                (even_d[0] - odd_d[1], even_d[1] + odd_d[0]),
                csub(even, odd),
                (even_d[0] + odd_d[1], even_d[1] - odd_d[0]),
            )
            for i in range(RADIX):
                for c in range(2):
                    out_ref[c, p, rows_at(i * short + row, 8), :] = parts[i][c]

        each_strip(short, 8, strip)
    norms = jnp.sqrt(jnp.sum(total, axis=1, keepdims=True) * (1.0 / cells))
    norms_ref[...] = jnp.broadcast_to(norms, norms_ref.shape)


def decay_root(h):
    sq = (h[0] + 0.25 * (h[0] * h[0] - h[1] * h[1]), h[1] + 0.5 * h[0] * h[1])
    size = jnp.sqrt(squares_of(sq))
    root_re = jnp.sqrt(0.5 * (size + sq[0]))
    root = (root_re, 0.5 * sq[1] / root_re)
    return cinv((1.0 + 0.5 * h[0] + root[0], 0.5 * h[1] + root[1])), root


def two_powers(power, z, stacks):
    low = high = None
    bit = 0
    while (1 << bit) < stacks:
        taken = ((z >> bit) & 1) == 1
        if low is None:
            one = (jnp.ones_like(power[0]), jnp.zeros_like(power[0]))
            low, high = cpick(taken, power, one), cpick(taken, one, power)
        else:
            grown = cmul(cpick(taken, low, high), power)
            low, high = cpick(taken, grown, low), cpick(taken, high, grown)
        power = csqr(power)
        bit += 1
    return low, high


def sums_of(planes, rho, cross_f, cross_b):
    ahead = planes[0]
    for a in planes[1:]:
        ahead = cmore(a, rho, ahead)
    behind = planes[-1]
    for a in planes[-2::-1]:
        behind = cmore(a, rho, behind)
    return csub(ahead, cmul(cross_f, behind)), csub(behind, cmul(cross_b, ahead))


def sine_rows(source_ref, target_ref, sine_ref, count):
    sine = (sine_ref[0], sine_ref[1])
    rows = 256 if count % 256 == 0 else count
    for i in range(0, count, rows):
        target_ref[pl.ds(i, rows), :] = dot3(split(source_ref[pl.ds(i, rows), :]), sine)


def start_kernel(
    chunk, planes, stacks, flags_ref, numbers_ref, wave_eig_ref, sine_eig_ref, sine_ref,
    own_ref, one_ref, two_ref, three_ref, field_ref, modes_ref, sums_ref, base_ref,
):
    j, z = flags_ref[0], flags_ref[1]
    rows = own_ref.shape[0] // planes
    short = rows // 2
    count = RADIX * planes
    for d, ref in enumerate((own_ref, one_ref, two_ref, three_ref)):
        part = planes * rows
        field_ref[rows_at((j ^ d) * part, part), :] = ref[...]
    sine_rows(field_ref, modes_ref, sine_ref, count * rows)
    h_re, h_im = numbers_ref[0], numbers_ref[1]
    sine_eig = sine_eig_ref[...]

    def strip(i, total):
        row = pl.multiple_of(i * 8, 8)
        eigen = wave_eig_ref[j, rows_at(chunk * short + row, 8), :] + sine_eig
        rho, root = decay_root((eigen + h_re, jnp.full_like(eigen, h_im)))
        block = cpow(rho, count)
        next_one = cmul(block, rho)
        low, high = two_powers(csqr(block), z, stacks)
        cross_f, cross_b = cmul(next_one, low), cmul(next_one, high)
        for n, value in enumerate((rho, cross_f, cross_b, block, low, high)):
            store(base_ref.at[n], 0, short, row, 8, value)
        found = [load(modes_ref, l * rows, short, row, 8) for l in range(count)]
        ahead, behind = sums_of(found, rho, cross_f, cross_b)
        store(sums_ref, 0, short, row, 8, ahead)
        store(sums_ref, rows, short, row, 8, behind)
        for l in range(count):
            total = total + squares_of(load(field_ref, l * rows, short, row, 8))
        return total

    total = lax.fori_loop(0, short // 8, strip, jnp.zeros((8, field_ref.shape[1]), jnp.float32))
    sums_ref[pl.ds(2 * rows, TAG), :] = jnp.zeros((TAG, field_ref.shape[1]), jnp.float32)
    sums_ref[pl.ds(2 * rows, 1), :] = jnp.sum(total, axis=0, keepdims=True)


def factors_kernel(
    chunk, count, levels, flags_ref, numbers_ref, wave_eig_ref, sine_eig_ref, base_ref, out_ref,
):
    j, z = flags_ref[0], flags_ref[1]
    short = base_ref.shape[1] // 2
    h_re, h_im, scale = numbers_ref[0], numbers_ref[1], numbers_ref[3]
    sine_eig = sine_eig_ref[...]

    def strip(row):
        eigen = wave_eig_ref[j, rows_at(chunk * short + row, 8), :] + sine_eig
        h = (eigen + h_re, jnp.full_like(eigen, h_im))
        rho, _, _, block, low, high = [load(base_ref.at[n], 0, short, row, 8) for n in range(6)]
        half_gap = csub((1.0 + 0.5 * h[0], 0.5 * h[1]), rho)
        wide = cmul(csqr(block), csqr(rho))
        low_w, high_w = cmul(low, wide), cmul(high, wide)
        whole = cscale(cinv(cmul(half_gap, cone(cmul(low, high_w)))), scale)
        turned = cmul(rho, whole)
        values = [
            cmul(cone(high_w), whole), cmul(cone(low), turned),
            cmul(cone(high), turned), cmul(cone(low_w), whole),
        ]
        pivot = (2.0 + h[0], h[1])
        inverse = cinv(pivot)
        values.append(inverse)
        for _ in range(count - 1):
            inverse = cinv(csub(pivot, inverse))
            values.append(inverse)
        near = far = None
        power = block
        for level in range(1, levels):
            taken = ((z >> (level - 1)) & 1) == 1
            if near is None:
                one = (jnp.ones_like(power[0]), jnp.zeros_like(power[0]))
                near, far = cpick(taken, power, one), cpick(taken, one, power)
            else:
                grown = cmul(cpick(taken, near, far), power)
                near, far = cpick(taken, grown, near), cpick(taken, far, grown)
            power = csqr(power)
            values.append(cpick(((z >> level) & 1) == 1, near, far))
        for n, value in enumerate(values):
            store(out_ref.at[n], 0, short, row, 8, value)

    each_strip(short, 8, strip)


def join_kernel(level, levels, flags_ref, sums_ref, came_ref, base_ref, out_ref):
    z = flags_ref[1]
    short = base_ref.shape[1] // 2
    rows = 2 * short
    above = ((z >> level) & 1) == 1
    last = level + 2 == levels
    upper = ((z >> (level + 1)) & 1) == 1

    def strip(row):
        block = load(base_ref.at[3], 0, short, row, 8)
        for _ in range(level):
            block = csqr(block)
        ahead, behind = load(sums_ref, 0, short, row, 8), load(sums_ref, rows, short, row, 8)
        ahead_c, behind_c = load(came_ref, 0, short, row, 8), load(came_ref, rows, short, row, 8)
        joined = cmore(cpick(above, ahead, ahead_c), block, cpick(above, ahead_c, ahead))
        joined_b = cmore(cpick(above, behind_c, behind), block, cpick(above, behind, behind_c))
        if last:
            store(out_ref, 0, short, row, 8, cpick(upper, joined_b, joined))
        else:
            store(out_ref, 0, short, row, 8, joined)
            store(out_ref, rows, short, row, 8, joined_b)

    each_strip(short, 8, strip)
    out_ref[pl.ds(out_ref.shape[0] - TAG, TAG), :] = (
        sums_ref[pl.ds(2 * rows, TAG), :] + came_ref[pl.ds(2 * rows, TAG), :]
    )


def solved(count, levels, z, scale, modes_ref, sums_ref, came_refs, base_ref, factors_ref, row):
    short = base_ref.shape[1] // 2
    rows = 2 * short

    def factor(n):
        return load(factors_ref.at[n], 0, short, row, 8)

    enter_f = enter_b = None
    for level, ref in enumerate(came_refs):
        above = ((z >> level) & 1) == 1
        base = 0 if level == levels - 1 else jnp.where(above, 0, rows)
        came = load(ref, base, short, row, 8)
        if level:
            came = cmul(factor(4 + count + level - 1), came)
        nought = (jnp.zeros_like(came[0]), jnp.zeros_like(came[0]))
        now_f, now_b = cpick(above, came, nought), cpick(above, nought, came)
        enter_f = now_f if enter_f is None else cadd(enter_f, now_f)
        enter_b = now_b if enter_b is None else cadd(enter_b, now_b)
    block = load(base_ref.at[3], 0, short, row, 8)
    all_f = cmore(load(sums_ref, 0, short, row, 8), block, enter_f)
    all_b = cmore(load(sums_ref, rows, short, row, 8), block, enter_b)
    below = cmore(cmul(factor(0), enter_f), factor(1), all_b)
    above = cmore(cmul(factor(3), enter_b), factor(2), all_f)
    planes = [cscale(load(modes_ref, l * rows, short, row, 8), scale) for l in range(count)]
    planes[0] = cadd(planes[0], below)
    planes[-1] = cadd(planes[-1], above)
    for l in range(1, count):
        planes[l] = cmore(planes[l], factor(4 + l - 1), planes[l - 1])
    planes[-1] = cmul(factor(4 + count - 1), planes[-1])
    for l in range(count - 2, -1, -1):
        planes[l] = cmul(factor(4 + l), cadd(planes[l], planes[l + 1]))
    return below, planes, above


def middle_kernel(
    chunk, count, levels, flags_ref, numbers_ref, wave_eig_ref, sine_ref, faces_ref, field_ref,
    modes_ref, base_ref, factors_ref, sums_ref, *refs,
):
    came_refs = refs[:levels]
    found_ref, next_ref, next_sums_ref, work_ref = refs[levels:]
    j, z = flags_ref[0], flags_ref[1]
    scale, s_re, s_im = numbers_ref[2], numbers_ref[4], numbers_ref[5]
    short = base_ref.shape[1] // 2
    rows = 2 * short
    width = base_ref.shape[2]

    def solve(row):
        below, planes, above = solved(
            count, levels, z, scale, modes_ref, sums_ref, came_refs, base_ref, factors_ref, row
        )
        store(work_ref, 0, short, row, 8, below)
        store(work_ref, (count + 1) * rows, short, row, 8, above)
        for l in range(count):
            store(work_ref, (l + 1) * rows, short, row, 8, planes[l])
            store(found_ref, l * rows, short, row, 8, planes[l])

    each_strip(short, 8, solve)
    sine_rows(work_ref, work_ref, sine_ref, (count + 2) * rows)

    def residual(i, total):
        row = pl.multiple_of(i * 8, 8)
        eigen = wave_eig_ref[j, rows_at(chunk * short + row, 8), :]
        under = load(work_ref, 0, short, row, 8)
        here = load(work_ref, rows, short, row, 8)
        for l in range(count):
            over = load(work_ref, (l + 2) * rows, short, row, 8)
            diag, cell, right, left, low, high = [faces_ref[n, pl.ds(l, 1), :] for n in range(6)]
            diag = s_re + (diag + cell * eigen)
            value = []
            for c in range(2):
                v = diag * here[c] - right * pltpu.roll(here[c], width - 1, 1)
                v = v - left * pltpu.roll(here[c], 1, 1)
                value.append(v - (low * under[c] + high * over[c]))
            value = (value[0] - s_im * here[1], value[1] + s_im * here[0])
            value = csub(load(field_ref, l * rows, short, row, 8), value)
            total = total + squares_of(value)
            store(work_ref, l * rows, short, row, 8, value)
            under, here = here, over
        return total

    total = lax.fori_loop(0, short // 8, residual, jnp.zeros((8, width), jnp.float32))
    sine_rows(work_ref, next_ref, sine_ref, count * rows)

    def sums(row):
        rho, cross_f, cross_b = [load(base_ref.at[n], 0, short, row, 8) for n in range(3)]
        planes = [load(next_ref, l * rows, short, row, 8) for l in range(count)]
        ahead, behind = sums_of(planes, rho, cross_f, cross_b)
        store(next_sums_ref, 0, short, row, 8, ahead)
        store(next_sums_ref, rows, short, row, 8, behind)

    each_strip(short, 8, sums)
    next_sums_ref[pl.ds(2 * rows, TAG), :] = sums_ref[pl.ds(2 * rows, TAG), :]
    next_sums_ref[pl.ds(2 * rows + 1, 1), :] = jnp.sum(total, axis=0, keepdims=True)


def end_kernel(
    count, levels, flags_ref, numbers_ref, sine_ref, found_ref, modes_ref, base_ref, factors_ref,
    sums_ref, *refs,
):
    came_refs = refs[:levels]
    out_refs, work_ref = refs[levels : levels + RADIX], refs[-1]
    j, z = flags_ref[0], flags_ref[1]
    scale = numbers_ref[2]
    short = base_ref.shape[1] // 2
    rows = 2 * short

    def solve(row):
        _, planes, _ = solved(
            count, levels, z, scale, modes_ref, sums_ref, came_refs, base_ref, factors_ref, row
        )
        for l in range(count):
            before = load(found_ref, l * rows, short, row, 8)
            store(work_ref, l * rows, short, row, 8, cadd(before, planes[l]))

    each_strip(short, 8, solve)
    sine_rows(work_ref, work_ref, sine_ref, count * rows)
    part = count // RADIX * rows
    if levels > 1:
        tag = refs[levels + RADIX][...]
    else:
        tag = sums_ref[pl.ds(2 * rows, TAG), :]
    last_ref = came_refs[-1]
    tag = tag + last_ref[pl.ds(last_ref.shape[0] - TAG, TAG), :]
    for d in range(RADIX):
        out_refs[d][pl.ds(0, part), :] = work_ref[rows_at((j ^ d) * part, part), :]
        out_refs[d][pl.ds(part, TAG), :] = tag


smem = pl.BlockSpec(memory_space=pltpu.SMEM)
vmem = pl.BlockSpec(memory_space=pltpu.VMEM)


def call(kernel, scalars, arrays, outs, scratch=(), flops=0, scalar_out=False):
    out_shape = [jax.ShapeDtypeStruct(shape, jnp.float32) for shape in outs]
    moved = sum(a.size * a.dtype.itemsize for a in arrays) + sum(4 * int(np.prod(s)) for s in outs)
    held = moved + sum(4 * int(np.prod(s)) for s in scratch)
    return pl.pallas_call(
        kernel,
        out_shape=out_shape,
        in_specs=[smem] * len(scalars) + [vmem] * len(arrays),
        out_specs=[smem if scalar_out else vmem] * len(outs),
        scratch_shapes=[pltpu.VMEM(shape, jnp.float32) for shape in scratch],
        compiler_params=pltpu.CompilerParams(vmem_limit_bytes=held + 4 * 2**20),
        cost_estimate=pl.CostEstimate(flops=flops, bytes_accessed=moved, transcendentals=0),
    )(*scalars, *arrays)


def pair_up(array, groups, flip):
    return lax.ppermute(array, "gz", [(i, i ^ flip) for i in range(groups)])


def step_by(array, groups, distance):
    return lax.ppermute(
        array, "gz", [(i, i + distance) for i in range(groups) if 0 <= i + distance < groups]
    )


def body(source, layer_ids, conduct_table, shift):
    planes, length_x, length_y = source.shape[1:]
    groups = lax.axis_size("gz")
    stacks = groups // RADIX
    levels = stacks.bit_length() - 1
    count = RADIX * planes
    length_z = planes * groups
    short = length_x // RADIX // CHUNKS
    rows = 2 * short
    if stacks < 2 or groups != RADIX << levels or planes > 8 or short % 8 or length_x % (RADIX * CHUNKS):
        raise ValueError("unsupported layout")
    me = lax.axis_index("gz")
    flags = jnp.stack([me % RADIX, me // RADIX]).astype(jnp.int32)

    wave = wave_tables(length_x)
    wave_f = jnp.asarray(two_terms(wave))
    wave_b = jnp.asarray(two_terms(np.ascontiguousarray(np.swapaxes(wave, 1, 2)) / length_x))
    sine = jnp.asarray(two_terms(sine_table(length_y)))
    wave_eig = np.broadcast_to(wave_eigen(length_x)[:, :, None], (RADIX, length_x // RADIX, length_y))
    wave_eig = jnp.asarray(np.ascontiguousarray(wave_eig).astype(np.float32))
    sine_eig = jnp.asarray(np.tile(sine_eigen(length_y)[None, :], (8, 1)).astype(np.float32))

    row_block = (8, length_y)
    (cells,) = call(conduct_kernel, [conduct_table], [layer_ids], [row_block])
    others = [pair_up(cells, groups, d) for d in range(1, RADIX)]
    cells, edge = call(
        functools.partial(group_kernel, planes), [flags], [cells, *others], [(count, length_y), row_block]
    )
    below = step_by(edge, groups, RADIX)
    above = step_by(edge, groups, -RADIX)
    flip = RADIX
    total = edge
    while flip < groups:
        wide = 4 * flip <= groups
        parts = [pair_up(total, groups, flip * n) for n in range(1, 4 if wide else 2)]
        flip *= 4 if wide else 2
        if flip < groups:
            (total,) = call(functools.partial(total_kernel, None), [shift], [total, *parts], [row_block])
        else:
            (numbers,) = call(
                functools.partial(total_kernel, length_y * length_z), [shift], [total, *parts], [(6,)],
                scalar_out=True,
            )
    (faces,) = call(
        functools.partial(faces_kernel, stacks), [flags], [cells, below, above], [(6, count, length_y)],
        scratch=[(count + 16, length_y)],
    )

    chunks = range(CHUNKS)
    parted = source.reshape(2, planes, RADIX, length_x // RADIX, length_y)
    piece = (planes * rows, length_y)
    dots = 6 * length_y * length_y
    spectra = {}
    for distances in ((2,), (3,), (1, 0)):
        made = call(
            functools.partial(forward_kernel, distances), [flags], [parted, wave_f],
            [piece] * (len(distances) * CHUNKS), flops=len(distances) * planes * rows * CHUNKS * dots,
        )
        for n, d in enumerate(distances):
            for t in chunks:
                spectra[d, t] = made[n * CHUNKS + t]
    for t in chunks:
        for d in (2, 3, 1):
            spectra[d, t] = pair_up(spectra[d, t], groups, d)

    block = (count * rows, length_y)
    sums_block = (2 * rows + TAG, length_y)
    single = (rows + TAG, length_y)
    part = (planes * rows + TAG, length_y)

    def exchange(sums, base):
        came, joined = [], [sums]
        for level in range(levels):
            came.append(pair_up(joined[-1], groups, RADIX << level))
            if level + 1 < levels:
                shape = single if level + 2 == levels else sums_block
                (a,) = call(
                    functools.partial(join_kernel, level, levels), [flags], [joined[-1], came[-1], base], [shape]
                )
                joined.append(a)
        return came, joined[1:]

    answers = {}
    for t in chunks:
        field, modes, sums, base = call(
            functools.partial(start_kernel, t, planes, stacks), [flags, numbers],
            [wave_eig, sine_eig, sine] + [spectra[d, t] for d in range(RADIX)],
            [block, block, sums_block, (6, rows, length_y)], flops=count * rows * dots,
        )
        (factors,) = call(
            functools.partial(factors_kernel, t, count, levels), [flags, numbers],
            [wave_eig, sine_eig, base], [(4 + count + levels - 1, rows, length_y)],
        )
        came, _ = exchange(sums, base)
        found, modes, sums = call(
            functools.partial(middle_kernel, t, count, levels), [flags, numbers],
            [wave_eig, sine, faces, field, modes, base, factors, sums, *came],
            [block, block, sums_block], scratch=[((count + 2) * rows, length_y)],
            flops=(2 * count + 2) * rows * dots,
        )
        came, joined = exchange(sums, base)
        tags = [joined[-1][-TAG:]] if joined else []
        made = call(
            functools.partial(end_kernel_with_tag if tags else end_kernel, count, levels), [flags, numbers],
            [sine, found, modes, base, factors, sums, *came, *tags],
            [part] * RADIX, scratch=[block], flops=count * rows * dots,
        )
        for d in range(RADIX):
            answers[d, t] = pair_up(made[d], groups, d) if d else made[d]
    solution, norms = call(
        functools.partial(backward_kernel, planes, length_x * length_x * length_y * length_z),
        [flags], [wave_b] + [answers[d, t] for d in range(RADIX) for t in chunks],
        [(2, planes, length_x, length_y), (TAG, 128)],
        scratch=[(planes, RADIX, length_x // RADIX * 2, length_y)],
        flops=planes * RADIX * rows * CHUNKS * dots,
    )
    return solution, norms[:2, 0]


def end_kernel_with_tag(count, levels, *refs):
    head = 2 + 6 + levels
    tag_ref = refs[head]
    rest = refs[head + 1 :]
    end_kernel(count, levels, *refs[:head], *rest[:RADIX], tag_ref, rest[RADIX])


def solution(mesh):
    placed = (P(None, ("node", "gz"), None, None), P(("node", "gz"), None), P(), P("node"))
    return jax.shard_map(
        body,
        mesh=mesh,
        in_specs=placed,
        out_specs=(P(None, ("node", "gz"), None, None), P("node")),
        check_vma=False,
    )
```

```python
import functools

import jax
import jax.numpy as jnp
import ml_dtypes
import numpy as np
from jax import lax
from jax.experimental import pallas as pl
from jax.experimental.pallas import tpu as pltpu
from jax.sharding import PartitionSpec as P

RADIX = 4
CHUNKS = 2
TAG = 8

relax = 0.6


def sine_table(length):
    indices = np.arange(1, length + 1)
    product = indices[:, None] * indices[None, :] % (2 * (length + 1))
    return np.sqrt(2.0 / (length + 1)) * np.sin(np.pi / (length + 1) * product)


def sine_eigen(length):
    indices = np.arange(1, length + 1)
    return 4.0 * np.sin(np.pi / (2 * (length + 1)) * indices) ** 2


def wave_numbers(length):
    return RADIX * np.arange(length // RADIX)[None, :] + np.arange(RADIX)[:, None]


def wave_eigen(length):
    return 4.0 * np.sin(np.pi / length * wave_numbers(length)) ** 2


def wave_tables(length):
    waves = wave_numbers(length)
    short = length // RADIX
    product = waves[:, :, None] * np.arange(short)[None, None, :] % length
    angles = 2.0 * np.pi / length * product
    cos_t, sin_t = np.cos(angles), np.sin(angles)
    top = np.concatenate([cos_t, sin_t], axis=2).reshape(RADIX, CHUNKS, short // CHUNKS, 2 * short)
    low = np.concatenate([-sin_t, cos_t], axis=2).reshape(RADIX, CHUNKS, short // CHUNKS, 2 * short)
    return np.concatenate([top, low], axis=2).reshape(RADIX, 2 * short, 2 * short)


def two_terms(table):
    first = table.astype(ml_dtypes.bfloat16)
    return np.stack([first, (table - first.astype(np.float64)).astype(ml_dtypes.bfloat16)])


def split(value):
    first = value.astype(jnp.bfloat16)
    return first, (value - first.astype(jnp.float32)).astype(jnp.bfloat16)


def dot3(a, b):
    def one(x, y):
        return jnp.dot(x, y, preferred_element_type=jnp.float32)

    return one(a[0], b[0]) + (one(a[0], b[1]) + one(a[1], b[0]))


def cmul(a, b):
    return (a[0] * b[0] - a[1] * b[1], a[0] * b[1] + a[1] * b[0])


def csqr(a):
    cross = a[0] * a[1]
    return ((a[0] - a[1]) * (a[0] + a[1]), cross + cross)


def cpow(a, count):
    result = None
    while count:
        if count & 1:
            result = a if result is None else cmul(result, a)
        count >>= 1
        if count:
            a = csqr(a)
    return result


def cadd(a, b):
    return (a[0] + b[0], a[1] + b[1])


def csub(a, b):
    return (a[0] - b[0], a[1] - b[1])


def cscale(a, scale):
    return (a[0] * scale, a[1] * scale)


def cmore(total, factor, term):
    return cadd(total, cmul(factor, term))


def cinv(a):
    scale = 1.0 / (a[0] * a[0] + a[1] * a[1])
    return (a[0] * scale, -a[1] * scale)


def cone(a):
    return (1.0 - a[0], -a[1])


def cpick(cond, a, b):
    return (jnp.where(cond, a[0], b[0]), jnp.where(cond, a[1], b[1]))


def rows_at(start, rows):
    if isinstance(start, int):
        return pl.ds(start, rows)
    return pl.ds(pl.multiple_of(start, 8), rows)


def load(ref, base, short, row, rows):
    return (ref[rows_at(base + row, rows), :], ref[rows_at(base + short + row, rows), :])


def store(ref, base, short, row, rows, value):
    ref[rows_at(base + row, rows), :] = value[0]
    ref[rows_at(base + short + row, rows), :] = value[1]


def each_strip(count, rows, body):
    def step(i, carry):
        body(pl.multiple_of(i * rows, rows))
        return carry

    lax.fori_loop(0, count // rows, step, 0)


def squares_of(a):
    return a[0] * a[0] + a[1] * a[1]


def conduct_kernel(table_ref, ids_ref, out_ref):
    planes = ids_ref.shape[0]
    ids = ids_ref[...]
    cells = jnp.zeros(ids.shape, jnp.float32)
    for layer in range(table_ref.shape[0]):
        cells = jnp.where(ids == layer, table_ref[layer], cells)
    out_ref[...] = jnp.zeros_like(out_ref)
    out_ref[pl.ds(0, planes), :] = cells


def group_kernel(planes, flags_ref, own_ref, one_ref, two_ref, three_ref, cells_ref, edge_ref):
    j = flags_ref[0]
    for d, ref in enumerate((own_ref, one_ref, two_ref, three_ref)):
        for p in range(planes):
            cells_ref[pl.ds((j ^ d) * planes + p, 1), :] = ref[pl.ds(p, 1), :]
    count = cells_ref.shape[0]
    edge_ref[...] = jnp.zeros_like(edge_ref)
    edge_ref[pl.ds(0, 1), :] = jnp.sum(cells_ref[...], axis=0, keepdims=True)
    edge_ref[pl.ds(1, 1), :] = cells_ref[pl.ds(0, 1), :]
    edge_ref[pl.ds(2, 1), :] = cells_ref[pl.ds(count - 1, 1), :]


def total_kernel(cells, shift_ref, *refs):
    part_refs, out_ref = refs[:-1], refs[-1]
    total = part_refs[0][...]
    for ref in part_refs[1:]:
        total = total + ref[...]
    if cells is None:
        out_ref[...] = total
        return
    inv_cond = 1.0 / (jnp.sum(total[0:1, :], axis=1, keepdims=True) * (1.0 / cells))
    inv = inv_cond[0, 0]
    out_ref[0] = shift_ref[0] * inv
    out_ref[1] = shift_ref[1] * inv
    out_ref[2] = relax * inv
    out_ref[3] = 0.5 * relax * inv
    out_ref[4] = shift_ref[0]
    out_ref[5] = shift_ref[1]


def faces_kernel(stacks, crossed, flags_ref, cells_ref, below_ref, above_ref, faces_ref, padded_ref):
    z = flags_ref[1]
    count, width = cells_ref.shape
    cells = cells_ref[...]
    below, above = below_ref[...], above_ref[...]
    if crossed:
        odd = (z & 1) == 1
        below, above = jnp.where(odd, above, below), jnp.where(odd, below, above)
    padded_ref[pl.ds(8, count), :] = cells
    padded_ref[pl.ds(7, 1), :] = jnp.where(z == 0, cells[0:1], below[2:3])
    padded_ref[pl.ds(8 + count, 1), :] = jnp.where(z == stacks - 1, cells[count - 1 : count], above[1:2])
    lane = lax.broadcasted_iota(jnp.int32, cells.shape, 1)
    last, first = lane == width - 1, lane == 0
    right = 0.5 * (cells + pltpu.roll(cells, width - 1, 1))
    left = 0.5 * (cells + pltpu.roll(cells, 1, 1))
    low = 0.5 * (cells + padded_ref[pl.ds(7, count), :])
    high = 0.5 * (cells + padded_ref[pl.ds(9, count), :])
    faces_ref[0] = jnp.where(last, cells, right) + jnp.where(first, cells, left) + (low + high)
    faces_ref[1] = cells
    faces_ref[2] = jnp.where(last, 0.0, right)
    faces_ref[3] = jnp.where(first, 0.0, left)
    faces_ref[4] = low
    faces_ref[5] = high


def forward_kernel(distances, flags_ref, source_ref, wave_ref, *out_refs):
    planes = source_ref.shape[1]
    for n, d in enumerate(distances):
        q = flags_ref[0] ^ d
        sign = (1 - 2 * (q & 1)).astype(jnp.float32)
        turn_re = jnp.where(q == 0, 1.0, jnp.where(q == 2, -1.0, 0.0))
        turn_im = jnp.where(q == 1, 1.0, jnp.where(q == 3, -1.0, 0.0))
        for p in range(planes):
            parts = [[source_ref[c, p, i] for i in range(RADIX)] for c in range(2)]
            even = [parts[c][0] + sign * parts[c][2] for c in range(2)]
            odd = [parts[c][1] + sign * parts[c][3] for c in range(2)]
            mixed = jnp.concatenate(
                [
                    even[0] + (turn_re * odd[0] + turn_im * odd[1]),
                    even[1] + (turn_re * odd[1] - turn_im * odd[0]),
                ],
                axis=0,
            )
            waves = dot3((wave_ref[0, q], wave_ref[1, q]), split(mixed))
            rows = waves.shape[0] // CHUNKS
            for t in range(CHUNKS):
                out_refs[n * CHUNKS + t][pl.ds(p * rows, rows), :] = waves[t * rows : (t + 1) * rows]


def backward_kernel(planes, cells, flags_ref, wave_ref, *refs):
    arrays, (out_ref, norms_ref, mixed_ref) = refs[:-3], refs[-3:]
    rows = (arrays[0].shape[0] - TAG) // planes
    short = rows * CHUNKS // 2
    total = None
    for d in range(RADIX):
        q = flags_ref[0] ^ d
        chunks = arrays[d * CHUNKS : (d + 1) * CHUNKS]
        for ref in chunks:
            tag = ref[pl.ds(planes * rows, TAG), :]
            total = tag if total is None else total + tag
        for p in range(planes):
            waves = jnp.concatenate([ref[pl.ds(p * rows, rows), :] for ref in chunks], axis=0)
            mixed_ref[p, q] = dot3((wave_ref[0, q], wave_ref[1, q]), split(waves))
    for p in range(planes):

        def strip(row):
            zero, one, two, three = [load(mixed_ref.at[p, q], 0, short, row, 8) for q in range(RADIX)]
            even, odd = cadd(zero, two), cadd(one, three)
            even_d, odd_d = csub(zero, two), csub(one, three)
            parts = (
                cadd(even, odd),
                (even_d[0] - odd_d[1], even_d[1] + odd_d[0]),
                csub(even, odd),
                (even_d[0] + odd_d[1], even_d[1] - odd_d[0]),
            )
            for i in range(RADIX):
                for c in range(2):
                    out_ref[c, p, rows_at(i * short + row, 8), :] = parts[i][c]

        each_strip(short, 8, strip)
    norms = jnp.sqrt(jnp.sum(total, axis=1, keepdims=True) * (1.0 / cells))
    for n in range(norms_ref.shape[0]):
        norms_ref[n] = norms[n, 0]


def decay_root(h):
    sq = (h[0] + 0.25 * (h[0] * h[0] - h[1] * h[1]), h[1] + 0.5 * h[0] * h[1])
    size = jnp.sqrt(squares_of(sq))
    root_re = jnp.sqrt(0.5 * (size + sq[0]))
    root = (root_re, 0.5 * sq[1] / root_re)
    return cinv((1.0 + 0.5 * h[0] + root[0], 0.5 * h[1] + root[1])), root


def two_powers(power, z, stacks):
    low = high = None
    bit = 0
    while (1 << bit) < stacks:
        taken = ((z >> bit) & 1) == 1
        if low is None:
            one = (jnp.ones_like(power[0]), jnp.zeros_like(power[0]))
            low, high = cpick(taken, power, one), cpick(taken, one, power)
        else:
            grown = cmul(cpick(taken, low, high), power)
            low, high = cpick(taken, grown, low), cpick(taken, high, grown)
        power = csqr(power)
        bit += 1
    return low, high


def sums_of(planes, rho, cross_f, cross_b):
    ahead = planes[0]
    for a in planes[1:]:
        ahead = cmore(a, rho, ahead)
    behind = planes[-1]
    for a in planes[-2::-1]:
        behind = cmore(a, rho, behind)
    return csub(ahead, cmul(cross_f, behind)), csub(behind, cmul(cross_b, ahead))


def sine_rows(source_ref, target_ref, sine_ref, count):
    sine = (sine_ref[0], sine_ref[1])
    rows = 256 if count % 256 == 0 else count
    for i in range(0, count, rows):
        target_ref[pl.ds(i, rows), :] = dot3(split(source_ref[pl.ds(i, rows), :]), sine)


def fill_give(z, rows, sums_ref, give_refs):
    for ref in give_refs:
        ref[pl.ds(0, rows), :] = sums_ref[rows_at((z & 1) * rows, rows), :]
        ref[pl.ds(rows, TAG), :] = sums_ref[pl.ds(2 * rows, TAG), :]


def start_kernel(
    chunk, planes, stacks, flags_ref, numbers_ref, wave_eig_ref, sine_eig_ref, sine_ref,
    own_ref, one_ref, two_ref, three_ref, field_ref, modes_ref, base_ref, sums_ref, *give_refs,
):
    j, z = flags_ref[0], flags_ref[1]
    rows = own_ref.shape[0] // planes
    short = rows // 2
    count = RADIX * planes
    for d, ref in enumerate((own_ref, one_ref, two_ref, three_ref)):
        part = planes * rows
        field_ref[rows_at((j ^ d) * part, part), :] = ref[...]
    sine_rows(field_ref, modes_ref, sine_ref, count * rows)
    h_re, h_im = numbers_ref[0], numbers_ref[1]
    sine_eig = sine_eig_ref[...]

    def strip(i, total):
        row = pl.multiple_of(i * 8, 8)
        eigen = wave_eig_ref[j, rows_at(chunk * short + row, 8), :] + sine_eig
        rho, root = decay_root((eigen + h_re, jnp.full_like(eigen, h_im)))
        block = cpow(rho, count)
        next_one = cmul(block, rho)
        low, high = two_powers(csqr(block), z, stacks)
        cross_f, cross_b = cmul(next_one, low), cmul(next_one, high)
        for n, value in enumerate((rho, cross_f, cross_b, block, low, high)):
            store(base_ref.at[n], 0, short, row, 8, value)
        found = [load(modes_ref, l * rows, short, row, 8) for l in range(count)]
        ahead, behind = sums_of(found, rho, cross_f, cross_b)
        store(sums_ref, 0, short, row, 8, ahead)
        store(sums_ref, rows, short, row, 8, behind)
        for l in range(count):
            total = total + squares_of(load(field_ref, l * rows, short, row, 8))
        return total

    total = lax.fori_loop(0, short // 8, strip, jnp.zeros((8, field_ref.shape[1]), jnp.float32))
    sums_ref[pl.ds(2 * rows, TAG), :] = jnp.zeros((TAG, field_ref.shape[1]), jnp.float32)
    sums_ref[pl.ds(2 * rows, 1), :] = jnp.sum(total, axis=0, keepdims=True)
    fill_give(z, rows, sums_ref, give_refs)


def factors_kernel(
    chunk, count, levels, flags_ref, numbers_ref, wave_eig_ref, sine_eig_ref, base_ref, out_ref,
):
    j, z = flags_ref[0], flags_ref[1]
    short = base_ref.shape[1] // 2
    h_re, h_im, scale = numbers_ref[0], numbers_ref[1], numbers_ref[3]
    sine_eig = sine_eig_ref[...]

    def strip(row):
        eigen = wave_eig_ref[j, rows_at(chunk * short + row, 8), :] + sine_eig
        h = (eigen + h_re, jnp.full_like(eigen, h_im))
        rho, _, _, block, low, high = [load(base_ref.at[n], 0, short, row, 8) for n in range(6)]
        half_gap = csub((1.0 + 0.5 * h[0], 0.5 * h[1]), rho)
        wide = cmul(csqr(block), csqr(rho))
        low_w, high_w = cmul(low, wide), cmul(high, wide)
        whole = cscale(cinv(cmul(half_gap, cone(cmul(low, high_w)))), scale)
        turned = cmul(rho, whole)
        values = [
            cmul(cone(high_w), whole), cmul(cone(low), turned),
            cmul(cone(high), turned), cmul(cone(low_w), whole),
        ]
        pivot = (2.0 + h[0], h[1])
        inverse = cinv(pivot)
        values.append(inverse)
        for _ in range(count - 1):
            inverse = cinv(csub(pivot, inverse))
            values.append(inverse)
        near = far = None
        power = block
        for level in range(1, levels):
            taken = ((z >> (level - 1)) & 1) == 1
            if near is None:
                one = (jnp.ones_like(power[0]), jnp.zeros_like(power[0]))
                near, far = cpick(taken, power, one), cpick(taken, one, power)
            else:
                grown = cmul(cpick(taken, near, far), power)
                near, far = cpick(taken, grown, near), cpick(taken, far, grown)
            power = csqr(power)
            values.append(cpick(((z >> level) & 1) == 1, near, far))
        for n, value in enumerate(values):
            store(out_ref.at[n], 0, short, row, 8, value)

    each_strip(short, 8, strip)


def join_two_kernel(flags_ref, sums_ref, came_ref, base_ref, out_ref):
    z = flags_ref[1]
    short = base_ref.shape[1] // 2
    rows = 2 * short
    side = (z >> 1) * rows

    def strip(row):
        block = load(base_ref.at[3], 0, short, row, 8)
        came = load(came_ref, 0, short, row, 8)
        store(out_ref, 0, short, row, 8, cmore(load(sums_ref, side, short, row, 8), block, came))

    each_strip(short, 8, strip)
    out_ref[pl.ds(rows, TAG), :] = sums_ref[pl.ds(2 * rows, TAG), :] + came_ref[pl.ds(rows, TAG), :]


def join_kernel(level, levels, flags_ref, sums_ref, came_ref, base_ref, out_ref):
    z = flags_ref[1]
    short = base_ref.shape[1] // 2
    rows = 2 * short
    above = ((z >> level) & 1) == 1
    last = level + 2 == levels
    upper = ((z >> (level + 1)) & 1) == 1

    def strip(row):
        block = load(base_ref.at[3], 0, short, row, 8)
        for _ in range(level):
            block = csqr(block)
        ahead, behind = load(sums_ref, 0, short, row, 8), load(sums_ref, rows, short, row, 8)
        ahead_c, behind_c = load(came_ref, 0, short, row, 8), load(came_ref, rows, short, row, 8)
        joined = cmore(cpick(above, ahead, ahead_c), block, cpick(above, ahead_c, ahead))
        joined_b = cmore(cpick(above, behind_c, behind), block, cpick(above, behind, behind_c))
        if last:
            store(out_ref, 0, short, row, 8, cpick(upper, joined_b, joined))
        else:
            store(out_ref, 0, short, row, 8, joined)
            store(out_ref, rows, short, row, 8, joined_b)

    each_strip(short, 8, strip)
    out_ref[pl.ds(out_ref.shape[0] - TAG, TAG), :] = (
        sums_ref[pl.ds(2 * rows, TAG), :] + came_ref[pl.ds(2 * rows, TAG), :]
    )


def solved(count, levels, z, scale, modes_ref, sums_ref, came_refs, base_ref, factors_ref, row):
    short = base_ref.shape[1] // 2
    rows = 2 * short

    def factor(n):
        return load(factors_ref.at[n], 0, short, row, 8)

    enter_f = enter_b = None
    for level in range(levels):
        above = ((z >> level) & 1) == 1
        if len(came_refs) > levels:
            came = load(came_refs[level], 0, short, row, 8)
            for ref in came_refs[level + 1 :] if level else ():
                came = cadd(came, load(ref, 0, short, row, 8))
        else:
            base = 0 if level == levels - 1 else jnp.where(above, 0, rows)
            came = load(came_refs[level], base, short, row, 8)
        if level:
            came = cmul(factor(4 + count + level - 1), came)
        nought = (jnp.zeros_like(came[0]), jnp.zeros_like(came[0]))
        now_f, now_b = cpick(above, came, nought), cpick(above, nought, came)
        enter_f = now_f if enter_f is None else cadd(enter_f, now_f)
        enter_b = now_b if enter_b is None else cadd(enter_b, now_b)
    block = load(base_ref.at[3], 0, short, row, 8)
    all_f = cmore(load(sums_ref, 0, short, row, 8), block, enter_f)
    all_b = cmore(load(sums_ref, rows, short, row, 8), block, enter_b)
    below = cmore(cmul(factor(0), enter_f), factor(1), all_b)
    above = cmore(cmul(factor(3), enter_b), factor(2), all_f)
    planes = [cscale(load(modes_ref, l * rows, short, row, 8), scale) for l in range(count)]
    planes[0] = cadd(planes[0], below)
    planes[-1] = cadd(planes[-1], above)
    for l in range(1, count):
        planes[l] = cmore(planes[l], factor(4 + l - 1), planes[l - 1])
    planes[-1] = cmul(factor(4 + count - 1), planes[-1])
    for l in range(count - 2, -1, -1):
        planes[l] = cmul(factor(4 + l), cadd(planes[l], planes[l + 1]))
    return below, planes, above


def middle_kernel(
    chunk, count, levels, arrivals, flags_ref, numbers_ref, wave_eig_ref, sine_ref, faces_ref, field_ref,
    modes_ref, base_ref, factors_ref, sums_ref, *refs,
):
    came_refs, (found_ref, next_ref, next_sums_ref) = refs[:arrivals], refs[arrivals : arrivals + 3]
    give_refs, work_ref = refs[arrivals + 3 : -1], refs[-1]
    j, z = flags_ref[0], flags_ref[1]
    scale, s_re, s_im = numbers_ref[2], numbers_ref[4], numbers_ref[5]
    short = base_ref.shape[1] // 2
    rows = 2 * short
    width = base_ref.shape[2]

    def solve(row):
        below, planes, above = solved(
            count, levels, z, scale, modes_ref, sums_ref, came_refs, base_ref, factors_ref, row
        )
        store(work_ref, 0, short, row, 8, below)
        store(work_ref, (count + 1) * rows, short, row, 8, above)
        for l in range(count):
            store(work_ref, (l + 1) * rows, short, row, 8, planes[l])
            store(found_ref, l * rows, short, row, 8, planes[l])

    each_strip(short, 8, solve)
    sine_rows(work_ref, work_ref, sine_ref, (count + 2) * rows)

    def residual(i, total):
        row = pl.multiple_of(i * 8, 8)
        eigen = wave_eig_ref[j, rows_at(chunk * short + row, 8), :]
        under = load(work_ref, 0, short, row, 8)
        here = load(work_ref, rows, short, row, 8)
        for l in range(count):
            over = load(work_ref, (l + 2) * rows, short, row, 8)
            diag, cell, right, left, low, high = [faces_ref[n, pl.ds(l, 1), :] for n in range(6)]
            diag = s_re + (diag + cell * eigen)
            value = []
            for c in range(2):
                v = diag * here[c] - right * pltpu.roll(here[c], width - 1, 1)
                v = v - left * pltpu.roll(here[c], 1, 1)
                value.append(v - (low * under[c] + high * over[c]))
            value = (value[0] - s_im * here[1], value[1] + s_im * here[0])
            value = csub(load(field_ref, l * rows, short, row, 8), value)
            total = total + squares_of(value)
            store(work_ref, l * rows, short, row, 8, value)
            under, here = here, over
        return total

    total = lax.fori_loop(0, short // 8, residual, jnp.zeros((8, width), jnp.float32))
    sine_rows(work_ref, next_ref, sine_ref, count * rows)

    def sums(row):
        rho, cross_f, cross_b = [load(base_ref.at[n], 0, short, row, 8) for n in range(3)]
        planes = [load(next_ref, l * rows, short, row, 8) for l in range(count)]
        ahead, behind = sums_of(planes, rho, cross_f, cross_b)
        store(next_sums_ref, 0, short, row, 8, ahead)
        store(next_sums_ref, rows, short, row, 8, behind)

    each_strip(short, 8, sums)
    next_sums_ref[pl.ds(2 * rows, TAG), :] = sums_ref[pl.ds(2 * rows, TAG), :]
    next_sums_ref[pl.ds(2 * rows + 1, 1), :] = jnp.sum(total, axis=0, keepdims=True)
    fill_give(z, rows, next_sums_ref, give_refs)


def end_kernel(
    count, levels, arrivals, flags_ref, numbers_ref, sine_ref, found_ref, modes_ref, base_ref,
    factors_ref, sums_ref, *refs,
):
    came_refs, out_refs, work_ref = refs[:arrivals], refs[-1 - RADIX : -1], refs[-1]
    j, z = flags_ref[0], flags_ref[1]
    scale = numbers_ref[2]
    short = base_ref.shape[1] // 2
    rows = 2 * short

    def solve(row):
        _, planes, _ = solved(
            count, levels, z, scale, modes_ref, sums_ref, came_refs, base_ref, factors_ref, row
        )
        for l in range(count):
            before = load(found_ref, l * rows, short, row, 8)
            store(work_ref, l * rows, short, row, 8, cadd(before, planes[l]))

    each_strip(short, 8, solve)
    sine_rows(work_ref, work_ref, sine_ref, count * rows)
    part = count // RADIX * rows
    if arrivals > levels:
        tag_refs = (sums_ref, *came_refs)
    elif levels > 1:
        tag_refs = (refs[arrivals], came_refs[-1])
    else:
        tag_refs = (sums_ref, came_refs[-1])
    tag = None
    for ref in tag_refs:
        part_tag = ref[pl.ds(ref.shape[0] - TAG, TAG), :]
        tag = part_tag if tag is None else tag + part_tag
    for d in range(RADIX):
        out_refs[d][pl.ds(0, part), :] = work_ref[rows_at((j ^ d) * part, part), :]
        out_refs[d][pl.ds(part, TAG), :] = tag


smem = pl.BlockSpec(memory_space=pltpu.SMEM)
vmem = pl.BlockSpec(memory_space=pltpu.VMEM)
unread = pl.BlockSpec(memory_space=pl.ANY)


def call(kernel, scalars, arrays, outs, scratch=(), flops=0, after=()):
    out_shape = [jax.ShapeDtypeStruct(shape, jnp.float32) for shape in outs]
    head = len(scalars) + len(arrays)

    def run(*refs):
        kernel(*refs[:head], *refs[head + len(after) :])

    moved = sum(a.size * a.dtype.itemsize for a in arrays) + sum(4 * int(np.prod(s)) for s in outs)
    held = moved + sum(4 * int(np.prod(s)) for s in scratch)
    return pl.pallas_call(
        run,
        out_shape=out_shape,
        in_specs=[smem] * len(scalars) + [vmem] * len(arrays) + [unread] * len(after),
        out_specs=[smem if len(shape) == 1 else vmem for shape in outs],
        scratch_shapes=[pltpu.VMEM(shape, jnp.float32) for shape in scratch],
        compiler_params=pltpu.CompilerParams(vmem_limit_bytes=held + 4 * 2**20),
        cost_estimate=pl.CostEstimate(flops=flops, bytes_accessed=moved, transcendentals=0),
    )(*scalars, *arrays, *after)


def pair_up(array, groups, flip):
    return lax.ppermute(array, "gz", [(i, i ^ flip) for i in range(groups)])


def step_by(array, groups, distance):
    return lax.ppermute(
        array, "gz", [(i, i + distance) for i in range(groups) if 0 <= i + distance < groups]
    )


def body(source, layer_ids, conduct_table, shift):
    planes, length_x, length_y = source.shape[1:]
    groups = lax.axis_size("gz")
    stacks = groups // RADIX
    levels = stacks.bit_length() - 1
    count = RADIX * planes
    length_z = planes * groups
    short = length_x // RADIX // CHUNKS
    rows = 2 * short
    if stacks < 2 or groups != RADIX << levels or planes > 8 or short % 8 or length_x % (RADIX * CHUNKS):
        raise ValueError("unsupported layout")
    me = lax.axis_index("gz")
    flags = jnp.stack([me % RADIX, me // RADIX]).astype(jnp.int32)

    wave = wave_tables(length_x)
    wave_f = jnp.asarray(two_terms(wave))
    wave_b = jnp.asarray(two_terms(np.ascontiguousarray(np.swapaxes(wave, 1, 2)) / length_x))
    sine = jnp.asarray(two_terms(sine_table(length_y)))
    wave_eig = np.broadcast_to(wave_eigen(length_x)[:, :, None], (RADIX, length_x // RADIX, length_y))
    wave_eig = jnp.asarray(np.ascontiguousarray(wave_eig).astype(np.float32))
    sine_eig = jnp.asarray(np.tile(sine_eigen(length_y)[None, :], (8, 1)).astype(np.float32))

    row_block = (8, length_y)
    (cells,) = call(conduct_kernel, [conduct_table], [layer_ids], [row_block])
    others = [pair_up(cells, groups, d) for d in range(1, RADIX)]

    chunks = range(CHUNKS)
    parted = source.reshape(2, planes, RADIX, length_x // RADIX, length_y)
    piece = (planes * rows, length_y)
    dots = 6 * length_y * length_y
    spectra = {}

    def transform(distances, after):
        made = call(
            functools.partial(forward_kernel, distances), [flags], [parted, wave_f],
            [piece] * (len(distances) * CHUNKS), flops=len(distances) * planes * rows * CHUNKS * dots,
            after=after,
        )
        for n, d in enumerate(distances):
            for t in chunks:
                spectra[d, t] = made[n * CHUNKS + t]
        return made[:1]

    placed = transform((2,), others)
    placed = transform((3,), placed)
    cells, edge = call(
        functools.partial(group_kernel, planes), [flags], [cells, *others], [(count, length_y), row_block],
        after=placed,
    )
    placed = transform((1, 0), [edge])
    for t in chunks:
        for d in (2, 3, 1):
            spectra[d, t] = pair_up(spectra[d, t], groups, d)

    crossed = stacks == 4
    flip = RADIX
    total = edge
    while flip < groups:
        wide = 4 * flip <= groups
        parts = [pair_up(total, groups, flip * n) for n in range(1, 4 if wide else 2)]
        flip *= 4 if wide else 2
        if crossed:
            below, above = parts[2], parts[0]
        if flip < groups:
            (total,) = call(functools.partial(total_kernel, None), [shift], [total, *parts], [row_block])
        else:
            (numbers,) = call(
                functools.partial(total_kernel, length_y * length_z), [shift], [total, *parts], [(6,)],
                after=placed,
            )
    if not crossed:
        below = step_by(edge, groups, RADIX)
        above = step_by(edge, groups, -RADIX)

    block = (count * rows, length_y)
    sums_block = (2 * rows + TAG, length_y)
    single = (rows + TAG, length_y)
    part = (planes * rows + TAG, length_y)
    four = stacks == 4
    arrivals = 3 if four else levels
    gives = [single] if four else []

    def exchange(sums, base, after):
        if four:
            sums, give = sums
            came = pair_up(give, groups, RADIX)
            (joined,) = call(join_two_kernel, [flags], [sums, came, base], [single], after=after)
            near = [(RADIX * a + i, RADIX * b + i) for a, b in ((1, 2), (2, 1)) for i in range(RADIX)]
            far = [(RADIX * a + i, RADIX * b + i) for a, b in ((1, 3), (2, 0)) for i in range(RADIX)]
            return [came, lax.ppermute(joined, "gz", near), lax.ppermute(joined, "gz", far)], [], joined
        came, joined = [], [sums[0]]
        for level in range(levels):
            came.append(pair_up(joined[-1], groups, RADIX << level))
            if level + 1 < levels:
                shape = single if level + 2 == levels else sums_block
                (a,) = call(
                    functools.partial(join_kernel, level, levels), [flags], [joined[-1], came[-1], base], [shape],
                    after=after,
                )
                joined.append(a)
        return came, [joined[-1][-TAG:]] if levels > 1 else [], joined[-1]

    state = [{} for _ in chunks]

    def start(t, after):
        st = state[t]
        st["field"], st["modes"], st["base"], *st["sums"] = call(
            functools.partial(start_kernel, t, planes, stacks), [flags, numbers],
            [wave_eig, sine_eig, sine] + [spectra[d, t] for d in range(RADIX)],
            [block, block, (6, rows, length_y), sums_block, *gives], flops=count * rows * dots, after=after,
        )
        return [st["sums"][-1]]

    def factors(t, after):
        st = state[t]
        (st["factors"],) = call(
            functools.partial(factors_kernel, t, count, levels), [flags, numbers],
            [wave_eig, sine_eig, st["base"]], [(4 + count + levels - 1, rows, length_y)], after=after,
        )
        return [st["factors"]]

    def join(t, after):
        st = state[t]
        st["came"], st["tags"], joined = exchange(st["sums"], st["base"], after)
        return [joined]

    def middle(t, after):
        st = state[t]
        st["found"], st["modes"], *st["sums"] = call(
            functools.partial(middle_kernel, t, count, levels, arrivals), [flags, numbers],
            [wave_eig, sine, faces, st["field"], st["modes"], st["base"], st["factors"], st["sums"][0], *st["came"]],
            [block, block, sums_block, *gives], scratch=[((count + 2) * rows, length_y)],
            flops=(2 * count + 2) * rows * dots, after=after,
        )
        return [st["sums"][-1]]

    def end(t, after):
        st = state[t]
        made = call(
            functools.partial(end_kernel, count, levels, arrivals), [flags, numbers],
            [sine, st["found"], st["modes"], st["base"], st["factors"], st["sums"][0], *st["came"], *st["tags"]],
            [part] * RADIX, scratch=[block], flops=count * rows * dots, after=after,
        )
        st["answers"] = [made[0]] + [None] * (RADIX - 1)
        for d in (2, 3, 1):
            st["answers"][d] = pair_up(made[d], groups, d)
        return made[:1]

    def edges(after):
        return call(
            functools.partial(faces_kernel, stacks, crossed), [flags], [cells, below, above],
            [(6, count, length_y)], scratch=[(count + 16, length_y)], after=after,
        )

    placed = start(0, [])
    placed = join(0, placed)
    placed = start(1, placed)
    (faces,) = placed = edges(placed)
    for t in chunks:
        placed = factors(t, placed)
    placed = middle(0, placed)
    placed = join(1, placed)
    placed = join(0, placed)
    placed = middle(1, placed)
    placed = end(0, placed)
    placed = join(1, placed)
    placed = end(1, placed)
    solution, norms = call(
        functools.partial(backward_kernel, planes, length_x * length_x * length_y * length_z),
        [flags], [wave_b] + [state[t]["answers"][d] for d in range(RADIX) for t in chunks],
        [(2, planes, length_x, length_y), (2,)],
        scratch=[(planes, RADIX, length_x // RADIX * 2, length_y)],
        flops=planes * RADIX * rows * CHUNKS * dots,
    )
    return solution, norms


def solution(mesh):
    placed = (P(None, ("node", "gz"), None, None), P(("node", "gz"), None), P(), P("node"))
    return jax.shard_map(
        body,
        mesh=mesh,
        in_specs=placed,
        out_specs=(P(None, ("node", "gz"), None, None), P("node")),
        check_vma=False,
    )
```

```python
import functools

import jax
import jax.numpy as jnp
import ml_dtypes
import numpy as np
from jax import lax
from jax.experimental import pallas as pl
from jax.experimental.pallas import tpu as pltpu
from jax.sharding import PartitionSpec as P

RADIX = 4
HALVES = 2
GROUP = RADIX * HALVES
CHUNKS = 2
TAG = 8

relax = 0.6


def sine_table(length):
    indices = np.arange(1, length + 1)
    product = indices[:, None] * indices[None, :] % (2 * (length + 1))
    return np.sqrt(2.0 / (length + 1)) * np.sin(np.pi / (length + 1) * product)


def sine_eigen(length):
    indices = np.arange(1, length + 1)
    return 4.0 * np.sin(np.pi / (2 * (length + 1)) * indices) ** 2


def wave_numbers(length):
    return RADIX * np.arange(length // RADIX)[None, :] + np.arange(RADIX)[:, None]


def wave_eigen(length):
    return 4.0 * np.sin(np.pi / length * wave_numbers(length)) ** 2


def wave_tables(length):
    waves = wave_numbers(length)
    short = length // RADIX
    product = waves[:, :, None] * np.arange(short)[None, None, :] % length
    angles = 2.0 * np.pi / length * product
    cos_t, sin_t = np.cos(angles), np.sin(angles)
    pieces = HALVES * CHUNKS
    top = np.concatenate([cos_t, sin_t], axis=2).reshape(RADIX, pieces, short // pieces, 2 * short)
    low = np.concatenate([-sin_t, cos_t], axis=2).reshape(RADIX, pieces, short // pieces, 2 * short)
    return np.concatenate([top, low], axis=2).reshape(RADIX, 2 * short, 2 * short)


def two_terms(table):
    first = table.astype(ml_dtypes.bfloat16)
    return np.stack([first, (table - first.astype(np.float64)).astype(ml_dtypes.bfloat16)])


def split(value):
    first = value.astype(jnp.bfloat16)
    return first, (value - first.astype(jnp.float32)).astype(jnp.bfloat16)


def dot3(a, b):
    def one(x, y):
        return jnp.dot(x, y, preferred_element_type=jnp.float32)

    return one(a[0], b[0]) + (one(a[0], b[1]) + one(a[1], b[0]))


def cmul(a, b):
    return (a[0] * b[0] - a[1] * b[1], a[0] * b[1] + a[1] * b[0])


def csqr(a):
    cross = a[0] * a[1]
    return ((a[0] - a[1]) * (a[0] + a[1]), cross + cross)


def cpow(a, count):
    result = None
    while count:
        if count & 1:
            result = a if result is None else cmul(result, a)
        count >>= 1
        if count:
            a = csqr(a)
    return result


def cadd(a, b):
    return (a[0] + b[0], a[1] + b[1])


def csub(a, b):
    return (a[0] - b[0], a[1] - b[1])


def cscale(a, scale):
    return (a[0] * scale, a[1] * scale)


def cmore(total, factor, term):
    return cadd(total, cmul(factor, term))


def cinv(a):
    scale = 1.0 / (a[0] * a[0] + a[1] * a[1])
    return (a[0] * scale, -a[1] * scale)


def cone(a):
    return (1.0 - a[0], -a[1])


def cpick(cond, a, b):
    return (jnp.where(cond, a[0], b[0]), jnp.where(cond, a[1], b[1]))


def rows_at(start, rows):
    if isinstance(start, int):
        return pl.ds(start, rows)
    return pl.ds(pl.multiple_of(start, 8), rows)


def load(ref, base, short, row, rows):
    return (ref[rows_at(base + row, rows), :], ref[rows_at(base + short + row, rows), :])


def store(ref, base, short, row, rows, value):
    ref[rows_at(base + row, rows), :] = value[0]
    ref[rows_at(base + short + row, rows), :] = value[1]


def each_strip(count, rows, body):
    def step(i, carry):
        body(pl.multiple_of(i * rows, rows))
        return carry

    lax.fori_loop(0, count // rows, step, 0)


def squares_of(a):
    return a[0] * a[0] + a[1] * a[1]


def conduct_kernel(table_ref, ids_ref, out_ref):
    planes = ids_ref.shape[0]
    ids = ids_ref[...]
    cells = jnp.zeros(ids.shape, jnp.float32)
    for layer in range(table_ref.shape[0]):
        cells = jnp.where(ids == layer, table_ref[layer], cells)
    out_ref[...] = jnp.zeros_like(out_ref)
    out_ref[pl.ds(0, planes), :] = cells
    out_ref[pl.ds(TAG - 1, 1), :] = jnp.sum(cells, axis=0, keepdims=True)


def add_kernel(one_ref, two_ref, out_ref):
    out_ref[...] = one_ref[...] + two_ref[...]


def fill_tag(out_ref, planes, own_ref, below_ref, above_ref, part_refs):
    start = out_ref.shape[0] - TAG
    for n, ref in enumerate((own_ref, below_ref, above_ref)):
        out_ref[pl.ds(start + n * planes, planes), :] = ref[pl.ds(0, planes), :]
    total = part_refs[0][pl.ds(TAG - 1, 1), :]
    for ref in part_refs[1:]:
        total = total + ref[pl.ds(TAG - 1, 1), :]
    out_ref[pl.ds(start + TAG - 1, 1), :] = total


def group_kernel(planes, blocks, cells_total, flags_ref, shift_ref, *refs):
    part_refs, (faces_ref, numbers_ref, padded_ref, below_ref, above_ref) = refs[:GROUP], refs[GROUP:]
    z, member = flags_ref[2], flags_ref[3]
    _, count, width = faces_ref.shape
    total = None
    for d, ref in enumerate(part_refs):
        tag = ref[pl.ds(ref.shape[0] - TAG, TAG), :]
        place = member ^ d
        for p in range(planes):
            padded_ref[pl.ds(8 + place * planes + p, 1), :] = tag[p : p + 1]
        below_ref[pl.ds(place, 1), :] = tag[2 * planes - 1 : 2 * planes]
        above_ref[pl.ds(place, 1), :] = tag[2 * planes : 2 * planes + 1]
        total = tag[TAG - 1 :] if total is None else total + tag[TAG - 1 :]
    inv = (1.0 / (jnp.sum(total, axis=1, keepdims=True) * (1.0 / cells_total)))[0, 0]
    numbers_ref[0] = shift_ref[0] * inv
    numbers_ref[1] = shift_ref[1] * inv
    numbers_ref[2] = relax * inv
    numbers_ref[3] = 0.5 * relax * inv
    numbers_ref[4] = shift_ref[0]
    numbers_ref[5] = shift_ref[1]
    cells = padded_ref[pl.ds(8, count), :]
    padded_ref[pl.ds(7, 1), :] = jnp.where(z == 0, cells[0:1], below_ref[pl.ds(GROUP - 1, 1), :])
    padded_ref[pl.ds(8 + count, 1), :] = jnp.where(
        z == blocks - 1, cells[count - 1 : count], above_ref[pl.ds(0, 1), :]
    )
    lane = lax.broadcasted_iota(jnp.int32, cells.shape, 1)
    last, first = lane == width - 1, lane == 0
    right = 0.5 * (cells + pltpu.roll(cells, width - 1, 1))
    left = 0.5 * (cells + pltpu.roll(cells, 1, 1))
    low = 0.5 * (cells + padded_ref[pl.ds(7, count), :])
    high = 0.5 * (cells + padded_ref[pl.ds(9, count), :])
    faces_ref[0] = jnp.where(last, cells, right) + jnp.where(first, cells, left) + (low + high)
    faces_ref[1] = cells
    faces_ref[2] = jnp.where(last, 0.0, right)
    faces_ref[3] = jnp.where(first, 0.0, left)
    faces_ref[4] = low
    faces_ref[5] = high


def forward_kernel(distance, parts_count, flags_ref, source_ref, wave_ref, own_ref, below_ref, above_ref, *refs):
    part_refs, out_refs, stage_ref = refs[:parts_count], refs[parts_count:-1], refs[-1]
    planes = source_ref.shape[1]
    q = flags_ref[0] ^ distance
    sign = (1 - 2 * (q & 1)).astype(jnp.float32)
    turn_re = jnp.where(q == 0, 1.0, jnp.where(q == 2, -1.0, 0.0))
    turn_im = jnp.where(q == 1, 1.0, jnp.where(q == 3, -1.0, 0.0))
    rows = stage_ref.shape[1] // (HALVES * CHUNKS)
    for p in range(planes):
        parts = [[source_ref[c, p, i] for i in range(RADIX)] for c in range(2)]
        even = [parts[c][0] + sign * parts[c][2] for c in range(2)]
        odd = [parts[c][1] + sign * parts[c][3] for c in range(2)]
        mixed = jnp.concatenate(
            [
                even[0] + (turn_re * odd[0] + turn_im * odd[1]),
                even[1] + (turn_re * odd[1] - turn_im * odd[0]),
            ],
            axis=0,
        )
        stage_ref[p] = dot3((wave_ref[0, q], wave_ref[1, q]), split(mixed))
        for n in range(HALVES):
            h = flags_ref[1] ^ n
            for t in range(CHUNKS):
                out_refs[n * CHUNKS + t][pl.ds(p * rows, rows), :] = stage_ref[
                    p, rows_at((h * CHUNKS + t) * rows, rows), :
                ]
    for ref in out_refs:
        fill_tag(ref, planes, own_ref, below_ref, above_ref, part_refs)


def backward_kernel(planes, cells, flags_ref, wave_ref, *refs):
    arrays, (out_ref, norms_ref, mixed_ref, stage_ref) = refs[:-4], refs[-4:]
    rows = (arrays[0].shape[0] - TAG) // planes
    short = rows * CHUNKS * HALVES // 2
    total = None
    for ref in arrays:
        tag = ref[pl.ds(planes * rows, TAG), :]
        total = tag if total is None else total + tag
    for d in range(RADIX):
        q = flags_ref[0] ^ d
        for p in range(planes):
            for n in range(HALVES):
                h = flags_ref[1] ^ n
                for t in range(CHUNKS):
                    stage_ref[d, p, rows_at((h * CHUNKS + t) * rows, rows), :] = arrays[
                        (d + RADIX * n) * CHUNKS + t
                    ][pl.ds(p * rows, rows), :]
            mixed_ref[p, q] = dot3((wave_ref[0, q], wave_ref[1, q]), split(stage_ref[d, p]))
    for p in range(planes):

        def strip(row):
            zero, one, two, three = [load(mixed_ref.at[p, q], 0, short, row, 8) for q in range(RADIX)]
            even, odd = cadd(zero, two), cadd(one, three)
            even_d, odd_d = csub(zero, two), csub(one, three)
            parts = (
                cadd(even, odd),
                (even_d[0] - odd_d[1], even_d[1] + odd_d[0]),
                csub(even, odd),
                (even_d[0] + odd_d[1], even_d[1] - odd_d[0]),
            )
            for i in range(RADIX):
                for c in range(2):
                    out_ref[c, p, rows_at(i * short + row, 8), :] = parts[i][c]

        each_strip(short, 8, strip)
    norms = jnp.sqrt(jnp.sum(total, axis=1, keepdims=True) * (1.0 / cells))
    for n in range(norms_ref.shape[0]):
        norms_ref[n] = norms[n, 0]


def decay_root(h):
    sq = (h[0] + 0.25 * (h[0] * h[0] - h[1] * h[1]), h[1] + 0.5 * h[0] * h[1])
    size = jnp.sqrt(squares_of(sq))
    root_re = jnp.sqrt(0.5 * (size + sq[0]))
    root = (root_re, 0.5 * sq[1] / root_re)
    return cinv((1.0 + 0.5 * h[0] + root[0], 0.5 * h[1] + root[1])), root


def two_powers(power, z, stacks):
    low = high = None
    bit = 0
    while (1 << bit) < stacks:
        taken = ((z >> bit) & 1) == 1
        if low is None:
            one = (jnp.ones_like(power[0]), jnp.zeros_like(power[0]))
            low, high = cpick(taken, power, one), cpick(taken, one, power)
        else:
            grown = cmul(cpick(taken, low, high), power)
            low, high = cpick(taken, grown, low), cpick(taken, high, grown)
        power = csqr(power)
        bit += 1
    return low, high


def sums_of(planes, rho, cross_f, cross_b):
    ahead = planes[0]
    for a in planes[1:]:
        ahead = cmore(a, rho, ahead)
    behind = planes[-1]
    for a in planes[-2::-1]:
        behind = cmore(a, rho, behind)
    return csub(ahead, cmul(cross_f, behind)), csub(behind, cmul(cross_b, ahead))


def sine_rows(source_ref, target_ref, sine_ref, count):
    sine = (sine_ref[0], sine_ref[1])
    rows = 256 if count % 256 == 0 else count
    for i in range(0, count, rows):
        target_ref[pl.ds(i, rows), :] = dot3(split(source_ref[pl.ds(i, rows), :]), sine)


def fill_give(z, rows, sums_ref, give_refs):
    for ref in give_refs:
        ref[pl.ds(0, rows), :] = sums_ref[rows_at((z & 1) * rows, rows), :]
        ref[pl.ds(rows, TAG), :] = sums_ref[pl.ds(2 * rows, TAG), :]


def start_kernel(
    chunk, planes, blocks, flags_ref, numbers_ref, wave_eig_ref, sine_eig_ref, sine_ref,
    *refs,
):
    part_refs, (field_ref, modes_ref, base_ref, sums_ref), give_refs = refs[:GROUP], refs[GROUP : GROUP + 4], refs[GROUP + 4 :]
    q, h, z, member = [flags_ref[n] for n in range(4)]
    part = part_refs[0].shape[0] - TAG
    rows = part // planes
    short = rows // 2
    count = GROUP * planes
    first_row = (h * CHUNKS + chunk) * short
    for d, ref in enumerate(part_refs):
        field_ref[rows_at((member ^ d) * part, part), :] = ref[pl.ds(0, part), :]
    sine_rows(field_ref, modes_ref, sine_ref, count * rows)
    h_re, h_im = numbers_ref[0], numbers_ref[1]
    sine_eig = sine_eig_ref[...]

    def strip(i, total):
        row = pl.multiple_of(i * 8, 8)
        eigen = wave_eig_ref[q, rows_at(first_row + row, 8), :] + sine_eig
        rho, _ = decay_root((eigen + h_re, jnp.full_like(eigen, h_im)))
        block = cpow(rho, count)
        next_one = cmul(block, rho)
        low, high = two_powers(csqr(block), z, blocks)
        cross_f, cross_b = cmul(next_one, low), cmul(next_one, high)
        for n, value in enumerate((rho, cross_f, cross_b, block, low, high)):
            store(base_ref.at[n], 0, short, row, 8, value)
        found = [load(modes_ref, l * rows, short, row, 8) for l in range(count)]
        ahead, behind = sums_of(found, rho, cross_f, cross_b)
        store(sums_ref, 0, short, row, 8, ahead)
        store(sums_ref, rows, short, row, 8, behind)
        for l in range(count):
            total = total + squares_of(load(field_ref, l * rows, short, row, 8))
        return total

    total = lax.fori_loop(0, short // 8, strip, jnp.zeros((8, field_ref.shape[1]), jnp.float32))
    sums_ref[pl.ds(2 * rows, TAG), :] = jnp.zeros((TAG, field_ref.shape[1]), jnp.float32)
    sums_ref[pl.ds(2 * rows, 1), :] = jnp.sum(total, axis=0, keepdims=True)
    fill_give(z, rows, sums_ref, give_refs)


def factors_kernel(
    chunk, count, levels, flags_ref, numbers_ref, wave_eig_ref, sine_eig_ref, base_ref, out_ref,
):
    q, h_part, z = flags_ref[0], flags_ref[1], flags_ref[2]
    short = base_ref.shape[1] // 2
    h_re, h_im, scale = numbers_ref[0], numbers_ref[1], numbers_ref[3]
    sine_eig = sine_eig_ref[...]

    def strip(row):
        eigen = wave_eig_ref[q, rows_at((h_part * CHUNKS + chunk) * short + row, 8), :] + sine_eig
        h = (eigen + h_re, jnp.full_like(eigen, h_im))
        rho, _, _, block, low, high = [load(base_ref.at[n], 0, short, row, 8) for n in range(6)]
        half_gap = csub((1.0 + 0.5 * h[0], 0.5 * h[1]), rho)
        wide = cmul(csqr(block), csqr(rho))
        low_w, high_w = cmul(low, wide), cmul(high, wide)
        whole = cscale(cinv(cmul(half_gap, cone(cmul(low, high_w)))), scale)
        turned = cmul(rho, whole)
        values = [
            cmul(cone(high_w), whole), cmul(cone(low), turned),
            cmul(cone(high), turned), cmul(cone(low_w), whole),
        ]
        pivot = (2.0 + h[0], h[1])
        inverse = cinv(pivot)
        values.append(inverse)
        for _ in range(count - 1):
            inverse = cinv(csub(pivot, inverse))
            values.append(inverse)
        near = far = None
        power = block
        for level in range(1, levels):
            taken = ((z >> (level - 1)) & 1) == 1
            if near is None:
                one = (jnp.ones_like(power[0]), jnp.zeros_like(power[0]))
                near, far = cpick(taken, power, one), cpick(taken, one, power)
            else:
                grown = cmul(cpick(taken, near, far), power)
                near, far = cpick(taken, grown, near), cpick(taken, far, grown)
            power = csqr(power)
            values.append(cpick(((z >> level) & 1) == 1, near, far))
        for n, value in enumerate(values):
            store(out_ref.at[n], 0, short, row, 8, value)

    each_strip(short, 8, strip)


def join_kernel(level, levels, flags_ref, sums_ref, came_ref, base_ref, out_ref):
    z = flags_ref[2]
    short = base_ref.shape[1] // 2
    rows = 2 * short
    above = ((z >> level) & 1) == 1
    last = level + 2 == levels
    upper = ((z >> (level + 1)) & 1) == 1

    def strip(row):
        block = load(base_ref.at[3], 0, short, row, 8)
        for _ in range(level):
            block = csqr(block)
        ahead, behind = load(sums_ref, 0, short, row, 8), load(sums_ref, rows, short, row, 8)
        ahead_c, behind_c = load(came_ref, 0, short, row, 8), load(came_ref, rows, short, row, 8)
        joined = cmore(cpick(above, ahead, ahead_c), block, cpick(above, ahead_c, ahead))
        joined_b = cmore(cpick(above, behind_c, behind), block, cpick(above, behind, behind_c))
        if last:
            store(out_ref, 0, short, row, 8, cpick(upper, joined_b, joined))
        else:
            store(out_ref, 0, short, row, 8, joined)
            store(out_ref, rows, short, row, 8, joined_b)

    each_strip(short, 8, strip)
    out_ref[pl.ds(out_ref.shape[0] - TAG, TAG), :] = (
        sums_ref[pl.ds(2 * rows, TAG), :] + came_ref[pl.ds(2 * rows, TAG), :]
    )


def solved(count, levels, z, scale, modes_ref, sums_ref, came_refs, base_ref, factors_ref, row):
    short = base_ref.shape[1] // 2
    rows = 2 * short

    def factor(n):
        return load(factors_ref.at[n], 0, short, row, 8)

    enter_f = enter_b = None
    for level in range(levels):
        above = ((z >> level) & 1) == 1
        base = 0 if level == levels - 1 else jnp.where(above, 0, rows)
        came = load(came_refs[level], base, short, row, 8)
        if level:
            came = cmul(factor(4 + count + level - 1), came)
        nought = (jnp.zeros_like(came[0]), jnp.zeros_like(came[0]))
        now_f, now_b = cpick(above, came, nought), cpick(above, nought, came)
        enter_f = now_f if enter_f is None else cadd(enter_f, now_f)
        enter_b = now_b if enter_b is None else cadd(enter_b, now_b)
    block = load(base_ref.at[3], 0, short, row, 8)
    all_f = cmore(load(sums_ref, 0, short, row, 8), block, enter_f)
    all_b = cmore(load(sums_ref, rows, short, row, 8), block, enter_b)
    below = cmore(cmul(factor(0), enter_f), factor(1), all_b)
    above = cmore(cmul(factor(3), enter_b), factor(2), all_f)
    planes = [cscale(load(modes_ref, l * rows, short, row, 8), scale) for l in range(count)]
    planes[0] = cadd(planes[0], below)
    planes[-1] = cadd(planes[-1], above)
    for l in range(1, count):
        planes[l] = cmore(planes[l], factor(4 + l - 1), planes[l - 1])
    planes[-1] = cmul(factor(4 + count - 1), planes[-1])
    for l in range(count - 2, -1, -1):
        planes[l] = cmul(factor(4 + l), cadd(planes[l], planes[l + 1]))
    return below, planes, above


def middle_kernel(
    chunk, count, levels, flags_ref, numbers_ref, wave_eig_ref, sine_ref, faces_ref, field_ref,
    modes_ref, base_ref, factors_ref, sums_ref, *refs,
):
    came_refs, (found_ref, next_ref, next_sums_ref) = refs[:levels], refs[levels : levels + 3]
    give_refs, work_ref = refs[levels + 3 : -1], refs[-1]
    q, h, z = flags_ref[0], flags_ref[1], flags_ref[2]
    scale, s_re, s_im = numbers_ref[2], numbers_ref[4], numbers_ref[5]
    short = base_ref.shape[1] // 2
    rows = 2 * short
    width = base_ref.shape[2]

    def solve(row):
        below, planes, above = solved(
            count, levels, z, scale, modes_ref, sums_ref, came_refs, base_ref, factors_ref, row
        )
        store(work_ref, 0, short, row, 8, below)
        store(work_ref, (count + 1) * rows, short, row, 8, above)
        for l in range(count):
            store(work_ref, (l + 1) * rows, short, row, 8, planes[l])
            store(found_ref, l * rows, short, row, 8, planes[l])

    each_strip(short, 8, solve)
    sine_rows(work_ref, work_ref, sine_ref, (count + 2) * rows)

    def residual(i, total):
        row = pl.multiple_of(i * 8, 8)
        eigen = wave_eig_ref[q, rows_at((h * CHUNKS + chunk) * short + row, 8), :]
        under = load(work_ref, 0, short, row, 8)
        here = load(work_ref, rows, short, row, 8)
        for l in range(count):
            over = load(work_ref, (l + 2) * rows, short, row, 8)
            diag, cell, right, left, low, high = [faces_ref[n, pl.ds(l, 1), :] for n in range(6)]
            diag = s_re + (diag + cell * eigen)
            value = []
            for c in range(2):
                v = diag * here[c] - right * pltpu.roll(here[c], width - 1, 1)
                v = v - left * pltpu.roll(here[c], 1, 1)
                value.append(v - (low * under[c] + high * over[c]))
            value = (value[0] - s_im * here[1], value[1] + s_im * here[0])
            value = csub(load(field_ref, l * rows, short, row, 8), value)
            total = total + squares_of(value)
            store(work_ref, l * rows, short, row, 8, value)
            under, here = here, over
        return total

    total = lax.fori_loop(0, short // 8, residual, jnp.zeros((8, width), jnp.float32))
    sine_rows(work_ref, next_ref, sine_ref, count * rows)

    def sums(row):
        rho, cross_f, cross_b = [load(base_ref.at[n], 0, short, row, 8) for n in range(3)]
        planes = [load(next_ref, l * rows, short, row, 8) for l in range(count)]
        ahead, behind = sums_of(planes, rho, cross_f, cross_b)
        store(next_sums_ref, 0, short, row, 8, ahead)
        store(next_sums_ref, rows, short, row, 8, behind)

    each_strip(short, 8, sums)
    next_sums_ref[pl.ds(2 * rows, TAG), :] = sums_ref[pl.ds(2 * rows, TAG), :]
    next_sums_ref[pl.ds(2 * rows + 1, 1), :] = jnp.sum(total, axis=0, keepdims=True)
    fill_give(z, rows, next_sums_ref, give_refs)


def end_kernel(
    count, levels, flags_ref, numbers_ref, sine_ref, found_ref, modes_ref, base_ref,
    factors_ref, sums_ref, *refs,
):
    came_refs, out_refs, work_ref = refs[:levels], refs[-1 - GROUP : -1], refs[-1]
    z, member = flags_ref[2], flags_ref[3]
    scale = numbers_ref[2]
    short = base_ref.shape[1] // 2
    rows = 2 * short

    def solve(row):
        _, planes, _ = solved(
            count, levels, z, scale, modes_ref, sums_ref, came_refs, base_ref, factors_ref, row
        )
        for l in range(count):
            before = load(found_ref, l * rows, short, row, 8)
            store(work_ref, l * rows, short, row, 8, cadd(before, planes[l]))

    each_strip(short, 8, solve)
    sine_rows(work_ref, work_ref, sine_ref, count * rows)
    part = count // GROUP * rows
    tag_refs = (refs[levels] if levels > 1 else sums_ref, came_refs[-1])
    tag = None
    for ref in tag_refs:
        part_tag = ref[pl.ds(ref.shape[0] - TAG, TAG), :]
        tag = part_tag if tag is None else tag + part_tag
    for d in range(GROUP):
        out_refs[d][pl.ds(0, part), :] = work_ref[rows_at((member ^ d) * part, part), :]
        out_refs[d][pl.ds(part, TAG), :] = tag


smem = pl.BlockSpec(memory_space=pltpu.SMEM)
vmem = pl.BlockSpec(memory_space=pltpu.VMEM)
unread = pl.BlockSpec(memory_space=pl.ANY)


def call(kernel, scalars, arrays, outs, scratch=(), flops=0, after=()):
    out_shape = [jax.ShapeDtypeStruct(shape, jnp.float32) for shape in outs]
    head = len(scalars) + len(arrays)

    def run(*refs):
        kernel(*refs[:head], *refs[head + len(after) :])

    moved = sum(a.size * a.dtype.itemsize for a in arrays) + sum(4 * int(np.prod(s)) for s in outs)
    held = moved + sum(4 * int(np.prod(s)) for s in scratch)
    return pl.pallas_call(
        run,
        out_shape=out_shape,
        in_specs=[smem] * len(scalars) + [vmem] * len(arrays) + [unread] * len(after),
        out_specs=[smem if len(shape) == 1 else vmem for shape in outs],
        scratch_shapes=[pltpu.VMEM(shape, jnp.float32) for shape in scratch],
        compiler_params=pltpu.CompilerParams(vmem_limit_bytes=held + 4 * 2**20),
        cost_estimate=pl.CostEstimate(flops=flops, bytes_accessed=moved, transcendentals=0),
    )(*scalars, *arrays, *after)


def pair_up(array, groups, flip):
    return lax.ppermute(array, "gz", [(i, i ^ flip) for i in range(groups)])


def step_by(array, groups, distance):
    return lax.ppermute(
        array, "gz", [(i, i + distance) for i in range(groups) if 0 <= i + distance < groups]
    )


def body(source, layer_ids, conduct_table, shift):
    planes, length_x, length_y = source.shape[1:]
    groups = lax.axis_size("gz")
    blocks = groups // GROUP
    levels = blocks.bit_length() - 1
    count = GROUP * planes
    length_z = planes * groups
    full = length_x // RADIX
    short = full // (HALVES * CHUNKS)
    rows = 2 * short
    if blocks < 2 or groups != GROUP << levels or planes > 2 or short % 8 or length_x != RADIX * full:
        raise ValueError("unsupported layout")
    me = lax.axis_index("gz")
    member = me % GROUP
    flags = jnp.stack([member % RADIX, member // RADIX, me // GROUP, member]).astype(jnp.int32)

    wave = wave_tables(length_x)
    wave_f = jnp.asarray(two_terms(wave))
    wave_b = jnp.asarray(two_terms(np.ascontiguousarray(np.swapaxes(wave, 1, 2)) / length_x))
    sine = jnp.asarray(two_terms(sine_table(length_y)))
    wave_eig = np.broadcast_to(wave_eigen(length_x)[:, :, None], (RADIX, full, length_y))
    wave_eig = jnp.asarray(np.ascontiguousarray(wave_eig).astype(np.float32))
    sine_eig = jnp.asarray(np.tile(sine_eigen(length_y)[None, :], (8, 1)).astype(np.float32))

    chunks = range(CHUNKS)
    row_block = (TAG, length_y)
    block = (count * rows, length_y)
    sums_block = (2 * rows + TAG, length_y)
    single = (rows + TAG, length_y)
    part = (planes * rows + TAG, length_y)
    gives = [single] if levels == 1 else []
    dots = 6 * length_y * length_y

    (cells,) = call(conduct_kernel, [conduct_table], [layer_ids], [row_block])
    if levels == 1:
        below = above = pair_up(cells, groups, GROUP)
        totals = [cells, below]
    else:
        below = step_by(cells, groups, GROUP)
        above = step_by(cells, groups, -GROUP)
        total = cells
        for level in range(levels):
            (total,) = call(add_kernel, [], [total, pair_up(total, groups, GROUP << level)], [row_block])
        totals = [total]

    parted = source.reshape(2, planes, RADIX, full, length_y)
    spectra = {}
    placed = []
    for d in (2, 0, 3, 1):
        made = call(
            functools.partial(forward_kernel, d, len(totals)), [flags],
            [parted, wave_f, cells, below, above, *totals], [part] * (HALVES * CHUNKS),
            scratch=[(planes, 2 * full, length_y)], flops=planes * 2 * full * dots, after=placed,
        )
        placed = made[:1]
        for n in range(HALVES):
            for t in chunks:
                spectra[d + RADIX * n, t] = made[n * CHUNKS + t]
    for t in chunks:
        for d in (6, 2, 4, 7, 3, 5, 1):
            spectra[d, t] = pair_up(spectra[d, t], groups, d)
    faces, numbers = call(
        functools.partial(group_kernel, planes, blocks, length_y * length_z), [flags, shift],
        [spectra[d, 0] for d in range(GROUP)], [(6, count, length_y), (6,)],
        scratch=[(count + 16, length_y), row_block, row_block],
    )

    state = [{} for _ in chunks]

    def exchange(st, after):
        sums, give = st["sums"][0], st["sums"][-1]
        st["came"], st["tags"] = [], []
        for level in range(levels):
            st["came"].append(pair_up(give, groups, GROUP << level))
            if level + 1 < levels:
                shape = single if level + 2 == levels else sums_block
                (give,) = call(
                    functools.partial(join_kernel, level, levels), [flags], [sums, st["came"][-1], st["base"]],
                    [shape], after=after,
                )
                sums = give
                st["tags"] = [give[-TAG:]]

    def start(t, after):
        st = state[t]
        st["field"], st["modes"], st["base"], *st["sums"] = call(
            functools.partial(start_kernel, t, planes, blocks), [flags, numbers],
            [wave_eig, sine_eig, sine] + [spectra[d, t] for d in range(GROUP)],
            [block, block, (6, rows, length_y), sums_block, *gives], flops=count * rows * dots, after=after,
        )
        exchange(st, [])
        (st["factors"],) = call(
            functools.partial(factors_kernel, t, count, levels), [flags, numbers],
            [wave_eig, sine_eig, st["base"]], [(4 + count + levels - 1, rows, length_y)],
        )
        return [st["factors"]]

    def middle(t, after):
        st = state[t]
        st["found"], st["modes"], *st["sums"] = call(
            functools.partial(middle_kernel, t, count, levels), [flags, numbers],
            [wave_eig, sine, faces, st["field"], st["modes"], st["base"], st["factors"], st["sums"][0], *st["came"]],
            [block, block, sums_block, *gives], scratch=[((count + 2) * rows, length_y)],
            flops=(2 * count + 2) * rows * dots, after=after,
        )
        exchange(st, [])
        return [st["sums"][-1]]

    def end(t, after):
        st = state[t]
        made = call(
            functools.partial(end_kernel, count, levels), [flags, numbers],
            [sine, st["found"], st["modes"], st["base"], st["factors"], st["sums"][0], *st["came"], *st["tags"]],
            [part] * GROUP, scratch=[block], flops=count * rows * dots, after=after,
        )
        st["answers"] = list(made)
        for d in (6, 7, 2, 3, 4, 5, 1):
            st["answers"][d] = pair_up(made[d], groups, d)
        return made[:1]

    placed = start(0, [])
    placed = middle(0, placed)
    placed = start(1, placed)
    placed = end(0, placed)
    placed = middle(1, placed)
    placed = end(1, placed)
    return call(
        functools.partial(backward_kernel, planes, length_x * length_x * length_y * length_z),
        [flags], [wave_b] + [state[t]["answers"][d] for d in range(GROUP) for t in chunks],
        [(2, planes, length_x, length_y), (2,)],
        scratch=[(planes, RADIX, 2 * full, length_y), (RADIX, planes, 2 * full, length_y)],
        flops=planes * RADIX * 2 * full * dots,
    )


def solution(mesh):
    placed = (P(None, ("node", "gz"), None, None), P(("node", "gz"), None), P(), P("node"))
    return jax.shard_map(
        body,
        mesh=mesh,
        in_specs=placed,
        out_specs=(P(None, ("node", "gz"), None, None), P("node")),
        check_vma=False,
    )
```

```python
import functools

import jax
import jax.numpy as jnp
import ml_dtypes
import numpy as np
from jax import lax
from jax.experimental import pallas as pl
from jax.experimental.pallas import tpu as pltpu
from jax.sharding import PartitionSpec as P

RADIX = 4
HALVES = 2
GROUP = RADIX * HALVES
CHUNKS = 2
SENDS = (6, 7, 2, 3, 4, 5, 1, 0)
TAG = 8

relax = 0.6


def sine_table(length):
    indices = np.arange(1, length + 1)
    product = indices[:, None] * indices[None, :] % (2 * (length + 1))
    return np.sqrt(2.0 / (length + 1)) * np.sin(np.pi / (length + 1) * product)


def sine_eigen(length):
    indices = np.arange(1, length + 1)
    return 4.0 * np.sin(np.pi / (2 * (length + 1)) * indices) ** 2


def wave_numbers(length):
    return RADIX * np.arange(length // RADIX)[None, :] + np.arange(RADIX)[:, None]


def wave_eigen(length):
    return 4.0 * np.sin(np.pi / length * wave_numbers(length)) ** 2


def wave_tables(length):
    waves = wave_numbers(length)
    short = length // RADIX
    product = waves[:, :, None] * np.arange(short)[None, None, :] % length
    angles = 2.0 * np.pi / length * product
    cos_t, sin_t = np.cos(angles), np.sin(angles)
    pieces = HALVES * CHUNKS
    top = np.concatenate([cos_t, sin_t], axis=2).reshape(RADIX, pieces, short // pieces, 2 * short)
    low = np.concatenate([-sin_t, cos_t], axis=2).reshape(RADIX, pieces, short // pieces, 2 * short)
    return np.concatenate([top, low], axis=2).reshape(RADIX, 2 * short, 2 * short)


def two_terms(table):
    first = table.astype(ml_dtypes.bfloat16)
    return np.stack([first, (table - first.astype(np.float64)).astype(ml_dtypes.bfloat16)])


def split(value):
    first = value.astype(jnp.bfloat16)
    return first, (value - first.astype(jnp.float32)).astype(jnp.bfloat16)


def dot3(a, b):
    def one(x, y):
        return jnp.dot(x, y, preferred_element_type=jnp.float32)

    return one(a[0], b[0]) + (one(a[0], b[1]) + one(a[1], b[0]))


def cmul(a, b):
    return (a[0] * b[0] - a[1] * b[1], a[0] * b[1] + a[1] * b[0])


def csqr(a):
    cross = a[0] * a[1]
    return ((a[0] - a[1]) * (a[0] + a[1]), cross + cross)


def cpow(a, count):
    result = None
    while count:
        if count & 1:
            result = a if result is None else cmul(result, a)
        count >>= 1
        if count:
            a = csqr(a)
    return result


def cadd(a, b):
    return (a[0] + b[0], a[1] + b[1])


def csub(a, b):
    return (a[0] - b[0], a[1] - b[1])


def cscale(a, scale):
    return (a[0] * scale, a[1] * scale)


def cmore(total, factor, term):
    return cadd(total, cmul(factor, term))


def cinv(a):
    scale = 1.0 / (a[0] * a[0] + a[1] * a[1])
    return (a[0] * scale, -a[1] * scale)


def cone(a):
    return (1.0 - a[0], -a[1])


def cpick(cond, a, b):
    return (jnp.where(cond, a[0], b[0]), jnp.where(cond, a[1], b[1]))


def rows_at(start, rows):
    if isinstance(start, int):
        return pl.ds(start, rows)
    return pl.ds(pl.multiple_of(start, 8), rows)


def load(ref, base, short, row, rows):
    return (ref[rows_at(base + row, rows), :], ref[rows_at(base + short + row, rows), :])


def store(ref, base, short, row, rows, value):
    ref[rows_at(base + row, rows), :] = value[0]
    ref[rows_at(base + short + row, rows), :] = value[1]


def each_strip(count, rows, body):
    def step(i, carry):
        body(pl.multiple_of(i * rows, rows))
        return carry

    lax.fori_loop(0, count // rows, step, 0)


def squares_of(a):
    return a[0] * a[0] + a[1] * a[1]


def conduct_kernel(table_ref, ids_ref, source_ref, wave_ref, out_ref):
    planes = ids_ref.shape[0]
    ids = ids_ref[...]
    cells = jnp.zeros(ids.shape, jnp.float32)
    for layer in range(table_ref.shape[0]):
        cells = jnp.where(ids == layer, table_ref[layer], cells)
    out_ref[...] = jnp.zeros_like(out_ref)
    out_ref[pl.ds(0, planes), :] = cells
    out_ref[pl.ds(TAG - 1, 1), :] = jnp.sum(cells, axis=0, keepdims=True)


def add_kernel(one_ref, two_ref, out_ref):
    out_ref[...] = one_ref[...] + two_ref[...]


def fill_tag(out_ref, planes, own_ref, below_ref, above_ref, part_refs):
    start = out_ref.shape[0] - TAG
    for n, ref in enumerate((own_ref, below_ref, above_ref)):
        out_ref[pl.ds(start + n * planes, planes), :] = ref[pl.ds(0, planes), :]
    total = part_refs[0][pl.ds(TAG - 1, 1), :]
    for ref in part_refs[1:]:
        total = total + ref[pl.ds(TAG - 1, 1), :]
    out_ref[pl.ds(start + TAG - 1, 1), :] = total


def group_kernel(planes, blocks, cells_total, flags_ref, shift_ref, *refs):
    part_refs, (faces_ref, numbers_ref, padded_ref, below_ref, above_ref) = refs[:GROUP], refs[GROUP:]
    z, member = flags_ref[2], flags_ref[3]
    _, count, width = faces_ref.shape
    total = None
    for d, ref in zip(SENDS, part_refs):
        tag = ref[pl.ds(ref.shape[0] - TAG, TAG), :]
        place = member ^ d
        for p in range(planes):
            padded_ref[pl.ds(8 + place * planes + p, 1), :] = tag[p : p + 1]
        below_ref[pl.ds(place, 1), :] = tag[2 * planes - 1 : 2 * planes]
        above_ref[pl.ds(place, 1), :] = tag[2 * planes : 2 * planes + 1]
        total = tag[TAG - 1 :] if total is None else total + tag[TAG - 1 :]
    inv = (1.0 / (jnp.sum(total, axis=1, keepdims=True) * (1.0 / cells_total)))[0, 0]
    numbers_ref[0] = shift_ref[0] * inv
    numbers_ref[1] = shift_ref[1] * inv
    numbers_ref[2] = relax * inv
    numbers_ref[3] = 0.5 * relax * inv
    numbers_ref[4] = shift_ref[0]
    numbers_ref[5] = shift_ref[1]
    cells = padded_ref[pl.ds(8, count), :]
    padded_ref[pl.ds(7, 1), :] = jnp.where(z == 0, cells[0:1], below_ref[pl.ds(GROUP - 1, 1), :])
    padded_ref[pl.ds(8 + count, 1), :] = jnp.where(
        z == blocks - 1, cells[count - 1 : count], above_ref[pl.ds(0, 1), :]
    )
    lane = lax.broadcasted_iota(jnp.int32, cells.shape, 1)
    last, first = lane == width - 1, lane == 0
    right = 0.5 * (cells + pltpu.roll(cells, width - 1, 1))
    left = 0.5 * (cells + pltpu.roll(cells, 1, 1))
    low = 0.5 * (cells + padded_ref[pl.ds(7, count), :])
    high = 0.5 * (cells + padded_ref[pl.ds(9, count), :])
    faces_ref[0] = jnp.where(last, cells, right) + jnp.where(first, cells, left) + (low + high)
    faces_ref[1] = cells
    faces_ref[2] = jnp.where(last, 0.0, right)
    faces_ref[3] = jnp.where(first, 0.0, left)
    faces_ref[4] = low
    faces_ref[5] = high


def forward_kernel(distance, parts_count, flags_ref, source_ref, wave_ref, own_ref, below_ref, above_ref, *refs):
    part_refs, out_refs, stage_ref = refs[:parts_count], refs[parts_count:-1], refs[-1]
    planes = source_ref.shape[1]
    q = flags_ref[0] ^ distance
    sign = (1 - 2 * (q & 1)).astype(jnp.float32)
    turn_re = jnp.where(q == 0, 1.0, jnp.where(q == 2, -1.0, 0.0))
    turn_im = jnp.where(q == 1, 1.0, jnp.where(q == 3, -1.0, 0.0))
    rows = stage_ref.shape[1] // (HALVES * CHUNKS)
    for p in range(planes):
        parts = [[source_ref[c, p, i] for i in range(RADIX)] for c in range(2)]
        even = [parts[c][0] + sign * parts[c][2] for c in range(2)]
        odd = [parts[c][1] + sign * parts[c][3] for c in range(2)]
        mixed = jnp.concatenate(
            [
                even[0] + (turn_re * odd[0] + turn_im * odd[1]),
                even[1] + (turn_re * odd[1] - turn_im * odd[0]),
            ],
            axis=0,
        )
        stage_ref[p] = dot3((wave_ref[0, q], wave_ref[1, q]), split(mixed))
        for n in range(HALVES):
            h = flags_ref[1] ^ n
            for t in range(CHUNKS):
                out_refs[n][pl.ds((t * planes + p) * rows, rows), :] = stage_ref[
                    p, rows_at((h * CHUNKS + t) * rows, rows), :
                ]
    for ref in out_refs:
        fill_tag(ref, planes, own_ref, below_ref, above_ref, part_refs)


def backward_kernel(planes, cells, flags_ref, wave_ref, *refs):
    arrays, (out_ref, norms_ref, mixed_ref, stage_ref) = refs[:-4], refs[-4:]
    came = {(d, t): arrays[t * GROUP + n] for t in range(CHUNKS) for n, d in enumerate(SENDS)}
    rows = (arrays[0].shape[0] - TAG) // planes
    short = rows * CHUNKS * HALVES // 2
    total = None
    for ref in arrays:
        tag = ref[pl.ds(planes * rows, TAG), :]
        total = tag if total is None else total + tag
    for d in range(RADIX):
        q = flags_ref[0] ^ d
        for p in range(planes):
            for n in range(HALVES):
                h = flags_ref[1] ^ n
                for t in range(CHUNKS):
                    stage_ref[d, p, rows_at((h * CHUNKS + t) * rows, rows), :] = came[d + RADIX * n, t][
                        pl.ds(p * rows, rows), :
                    ]
            mixed_ref[p, q] = dot3((wave_ref[0, q], wave_ref[1, q]), split(stage_ref[d, p]))
    for p in range(planes):

        def strip(row):
            zero, one, two, three = [load(mixed_ref.at[p, q], 0, short, row, 8) for q in range(RADIX)]
            even, odd = cadd(zero, two), cadd(one, three)
            even_d, odd_d = csub(zero, two), csub(one, three)
            parts = (
                cadd(even, odd),
                (even_d[0] - odd_d[1], even_d[1] + odd_d[0]),
                csub(even, odd),
                (even_d[0] + odd_d[1], even_d[1] - odd_d[0]),
            )
            for i in range(RADIX):
                for c in range(2):
                    out_ref[c, p, rows_at(i * short + row, 8), :] = parts[i][c]

        each_strip(short, 8, strip)
    norms = jnp.sqrt(jnp.sum(total, axis=1, keepdims=True) * (1.0 / cells))
    for n in range(norms_ref.shape[0]):
        norms_ref[n] = norms[n, 0]


def decay_root(h):
    sq = (h[0] + 0.25 * (h[0] * h[0] - h[1] * h[1]), h[1] + 0.5 * h[0] * h[1])
    size = jnp.sqrt(squares_of(sq))
    root_re = jnp.sqrt(0.5 * (size + sq[0]))
    root = (root_re, 0.5 * sq[1] / root_re)
    return cinv((1.0 + 0.5 * h[0] + root[0], 0.5 * h[1] + root[1])), root


def two_powers(power, z, stacks):
    low = high = None
    bit = 0
    while (1 << bit) < stacks:
        taken = ((z >> bit) & 1) == 1
        if low is None:
            one = (jnp.ones_like(power[0]), jnp.zeros_like(power[0]))
            low, high = cpick(taken, power, one), cpick(taken, one, power)
        else:
            grown = cmul(cpick(taken, low, high), power)
            low, high = cpick(taken, grown, low), cpick(taken, high, grown)
        power = csqr(power)
        bit += 1
    return low, high


def sums_of(planes, rho, cross_f, cross_b):
    ahead = planes[0]
    for a in planes[1:]:
        ahead = cmore(a, rho, ahead)
    behind = planes[-1]
    for a in planes[-2::-1]:
        behind = cmore(a, rho, behind)
    return csub(ahead, cmul(cross_f, behind)), csub(behind, cmul(cross_b, ahead))


def sine_rows(source_ref, target_ref, sine_ref, count):
    sine = (sine_ref[0], sine_ref[1])
    rows = max(n for n in range(16, 257, 16) if count % n == 0)
    for i in range(0, count, rows):
        target_ref[pl.ds(i, rows), :] = dot3(split(source_ref[pl.ds(i, rows), :]), sine)


def fill_give(z, rows, sums_ref, give_refs):
    for ref in give_refs:
        ref[pl.ds(0, rows), :] = sums_ref[rows_at((z & 1) * rows, rows), :]
        ref[pl.ds(rows, TAG), :] = sums_ref[pl.ds(2 * rows, TAG), :]


def start_kernel(
    chunk, planes, blocks, flags_ref, numbers_ref, wave_eig_ref, sine_eig_ref, sine_ref,
    *refs,
):
    part_refs, (field_ref, modes_ref, base_ref, sums_ref), give_refs = refs[:GROUP], refs[GROUP : GROUP + 4], refs[GROUP + 4 :]
    q, h, z, member = [flags_ref[n] for n in range(4)]
    part = (part_refs[0].shape[0] - TAG) // CHUNKS
    rows = part // planes
    short = rows // 2
    count = GROUP * planes
    first_row = (h * CHUNKS + chunk) * short
    for d, ref in zip(SENDS, part_refs):
        field_ref[rows_at((member ^ d) * part, part), :] = ref[pl.ds(chunk * part, part), :]
    sine_rows(field_ref, modes_ref, sine_ref, count * rows)
    h_re, h_im = numbers_ref[0], numbers_ref[1]
    sine_eig = sine_eig_ref[...]

    def strip(i, total):
        row = pl.multiple_of(i * 8, 8)
        eigen = wave_eig_ref[q, rows_at(first_row + row, 8), :] + sine_eig
        rho, _ = decay_root((eigen + h_re, jnp.full_like(eigen, h_im)))
        block = cpow(rho, count)
        next_one = cmul(block, rho)
        low, high = two_powers(csqr(block), z, blocks)
        cross_f, cross_b = cmul(next_one, low), cmul(next_one, high)
        for n, value in enumerate((rho, cross_f, cross_b, block, low, high)):
            store(base_ref.at[n], 0, short, row, 8, value)
        found = [load(modes_ref, l * rows, short, row, 8) for l in range(count)]
        ahead, behind = sums_of(found, rho, cross_f, cross_b)
        store(sums_ref, 0, short, row, 8, ahead)
        store(sums_ref, rows, short, row, 8, behind)
        for l in range(count):
            total = total + squares_of(load(field_ref, l * rows, short, row, 8))
        return total

    total = lax.fori_loop(0, short // 8, strip, jnp.zeros((8, field_ref.shape[1]), jnp.float32))
    sums_ref[pl.ds(2 * rows, TAG), :] = jnp.zeros((TAG, field_ref.shape[1]), jnp.float32)
    sums_ref[pl.ds(2 * rows, 1), :] = jnp.sum(total, axis=0, keepdims=True)
    fill_give(z, rows, sums_ref, give_refs)


def factors_kernel(
    chunk, count, levels, flags_ref, numbers_ref, wave_eig_ref, sine_eig_ref, base_ref, out_ref,
):
    q, h_part, z = flags_ref[0], flags_ref[1], flags_ref[2]
    short = base_ref.shape[1] // 2
    h_re, h_im, scale = numbers_ref[0], numbers_ref[1], numbers_ref[3]
    sine_eig = sine_eig_ref[...]

    def strip(row):
        eigen = wave_eig_ref[q, rows_at((h_part * CHUNKS + chunk) * short + row, 8), :] + sine_eig
        h = (eigen + h_re, jnp.full_like(eigen, h_im))
        rho, _, _, block, low, high = [load(base_ref.at[n], 0, short, row, 8) for n in range(6)]
        half_gap = csub((1.0 + 0.5 * h[0], 0.5 * h[1]), rho)
        wide = cmul(csqr(block), csqr(rho))
        low_w, high_w = cmul(low, wide), cmul(high, wide)
        whole = cscale(cinv(cmul(half_gap, cone(cmul(low, high_w)))), scale)
        turned = cmul(rho, whole)
        values = [
            cmul(cone(high_w), whole), cmul(cone(low), turned),
            cmul(cone(high), turned), cmul(cone(low_w), whole),
        ]
        pivot = (2.0 + h[0], h[1])
        inverse = cinv(pivot)
        values.append(inverse)
        for _ in range(count - 1):
            inverse = cinv(csub(pivot, inverse))
            values.append(inverse)
        near = far = None
        power = block
        for level in range(1, levels):
            taken = ((z >> (level - 1)) & 1) == 1
            if near is None:
                one = (jnp.ones_like(power[0]), jnp.zeros_like(power[0]))
                near, far = cpick(taken, power, one), cpick(taken, one, power)
            else:
                grown = cmul(cpick(taken, near, far), power)
                near, far = cpick(taken, grown, near), cpick(taken, far, grown)
            power = csqr(power)
            values.append(cpick(((z >> level) & 1) == 1, near, far))
        for n, value in enumerate(values):
            store(out_ref.at[n], 0, short, row, 8, value)

    each_strip(short, 8, strip)


def join_kernel(level, levels, flags_ref, sums_ref, came_ref, base_ref, out_ref):
    z = flags_ref[2]
    short = base_ref.shape[1] // 2
    rows = 2 * short
    above = ((z >> level) & 1) == 1
    last = level + 2 == levels
    upper = ((z >> (level + 1)) & 1) == 1

    def strip(row):
        block = load(base_ref.at[3], 0, short, row, 8)
        for _ in range(level):
            block = csqr(block)
        ahead, behind = load(sums_ref, 0, short, row, 8), load(sums_ref, rows, short, row, 8)
        ahead_c, behind_c = load(came_ref, 0, short, row, 8), load(came_ref, rows, short, row, 8)
        joined = cmore(cpick(above, ahead, ahead_c), block, cpick(above, ahead_c, ahead))
        joined_b = cmore(cpick(above, behind_c, behind), block, cpick(above, behind, behind_c))
        if last:
            store(out_ref, 0, short, row, 8, cpick(upper, joined_b, joined))
        else:
            store(out_ref, 0, short, row, 8, joined)
            store(out_ref, rows, short, row, 8, joined_b)

    each_strip(short, 8, strip)
    out_ref[pl.ds(out_ref.shape[0] - TAG, TAG), :] = (
        sums_ref[pl.ds(2 * rows, TAG), :] + came_ref[pl.ds(2 * rows, TAG), :]
    )


def solved(count, levels, z, scale, modes_ref, sums_ref, came_refs, base_ref, factors_ref, row):
    short = base_ref.shape[1] // 2
    rows = 2 * short

    def factor(n):
        return load(factors_ref.at[n], 0, short, row, 8)

    enter_f = enter_b = None
    for level in range(levels):
        above = ((z >> level) & 1) == 1
        base = 0 if level == levels - 1 else jnp.where(above, 0, rows)
        came = load(came_refs[level], base, short, row, 8)
        if level:
            came = cmul(factor(4 + count + level - 1), came)
        nought = (jnp.zeros_like(came[0]), jnp.zeros_like(came[0]))
        now_f, now_b = cpick(above, came, nought), cpick(above, nought, came)
        enter_f = now_f if enter_f is None else cadd(enter_f, now_f)
        enter_b = now_b if enter_b is None else cadd(enter_b, now_b)
    block = load(base_ref.at[3], 0, short, row, 8)
    all_f = cmore(load(sums_ref, 0, short, row, 8), block, enter_f)
    all_b = cmore(load(sums_ref, rows, short, row, 8), block, enter_b)
    below = cmore(cmul(factor(0), enter_f), factor(1), all_b)
    above = cmore(cmul(factor(3), enter_b), factor(2), all_f)
    planes = [cscale(load(modes_ref, l * rows, short, row, 8), scale) for l in range(count)]
    planes[0] = cadd(planes[0], below)
    planes[-1] = cadd(planes[-1], above)
    for l in range(1, count):
        planes[l] = cmore(planes[l], factor(4 + l - 1), planes[l - 1])
    planes[-1] = cmul(factor(4 + count - 1), planes[-1])
    for l in range(count - 2, -1, -1):
        planes[l] = cmul(factor(4 + l), cadd(planes[l], planes[l + 1]))
    return below, planes, above


def middle_kernel(
    chunk, count, levels, flags_ref, numbers_ref, wave_eig_ref, sine_ref, faces_ref, field_ref,
    modes_ref, base_ref, factors_ref, sums_ref, *refs,
):
    came_refs, (found_ref, next_ref, next_sums_ref) = refs[:levels], refs[levels : levels + 3]
    give_refs, work_ref = refs[levels + 3 : -1], refs[-1]
    q, h, z = flags_ref[0], flags_ref[1], flags_ref[2]
    scale, s_re, s_im = numbers_ref[2], numbers_ref[4], numbers_ref[5]
    short = base_ref.shape[1] // 2
    rows = 2 * short
    width = base_ref.shape[2]

    def solve(row):
        below, planes, above = solved(
            count, levels, z, scale, modes_ref, sums_ref, came_refs, base_ref, factors_ref, row
        )
        store(work_ref, 0, short, row, 8, below)
        store(work_ref, (count + 1) * rows, short, row, 8, above)
        for l in range(count):
            store(work_ref, (l + 1) * rows, short, row, 8, planes[l])
            store(found_ref, l * rows, short, row, 8, planes[l])

    each_strip(short, 8, solve)
    sine_rows(work_ref, work_ref, sine_ref, (count + 2) * rows)

    def residual(i, total):
        row = pl.multiple_of(i * 8, 8)
        eigen = wave_eig_ref[q, rows_at((h * CHUNKS + chunk) * short + row, 8), :]
        under = load(work_ref, 0, short, row, 8)
        here = load(work_ref, rows, short, row, 8)
        for l in range(count):
            over = load(work_ref, (l + 2) * rows, short, row, 8)
            diag, cell, right, left, low, high = [faces_ref[n, pl.ds(l, 1), :] for n in range(6)]
            diag = s_re + (diag + cell * eigen)
            value = []
            for c in range(2):
                v = diag * here[c] - right * pltpu.roll(here[c], width - 1, 1)
                v = v - left * pltpu.roll(here[c], 1, 1)
                value.append(v - (low * under[c] + high * over[c]))
            value = (value[0] - s_im * here[1], value[1] + s_im * here[0])
            value = csub(load(field_ref, l * rows, short, row, 8), value)
            total = total + squares_of(value)
            store(work_ref, l * rows, short, row, 8, value)
            under, here = here, over
        return total

    total = lax.fori_loop(0, short // 8, residual, jnp.zeros((8, width), jnp.float32))
    sine_rows(work_ref, next_ref, sine_ref, count * rows)

    def sums(row):
        rho, cross_f, cross_b = [load(base_ref.at[n], 0, short, row, 8) for n in range(3)]
        planes = [load(next_ref, l * rows, short, row, 8) for l in range(count)]
        ahead, behind = sums_of(planes, rho, cross_f, cross_b)
        store(next_sums_ref, 0, short, row, 8, ahead)
        store(next_sums_ref, rows, short, row, 8, behind)

    each_strip(short, 8, sums)
    next_sums_ref[pl.ds(2 * rows, TAG), :] = sums_ref[pl.ds(2 * rows, TAG), :]
    next_sums_ref[pl.ds(2 * rows + 1, 1), :] = jnp.sum(total, axis=0, keepdims=True)
    fill_give(z, rows, next_sums_ref, give_refs)


def end_kernel(
    count, levels, flags_ref, numbers_ref, sine_ref, found_ref, modes_ref, base_ref,
    factors_ref, sums_ref, *refs,
):
    came_refs, out_refs, work_ref = refs[:levels], refs[-1 - GROUP : -1], refs[-1]
    z, member = flags_ref[2], flags_ref[3]
    scale = numbers_ref[2]
    short = base_ref.shape[1] // 2
    rows = 2 * short

    def solve(row):
        _, planes, _ = solved(
            count, levels, z, scale, modes_ref, sums_ref, came_refs, base_ref, factors_ref, row
        )
        for l in range(count):
            before = load(found_ref, l * rows, short, row, 8)
            store(work_ref, l * rows, short, row, 8, cadd(before, planes[l]))

    each_strip(short, 8, solve)
    sine_rows(work_ref, work_ref, sine_ref, count * rows)
    part = count // GROUP * rows
    tag_refs = (refs[levels] if levels > 1 else sums_ref, came_refs[-1])
    tag = None
    for ref in tag_refs:
        part_tag = ref[pl.ds(ref.shape[0] - TAG, TAG), :]
        tag = part_tag if tag is None else tag + part_tag
    for d in range(GROUP):
        out_refs[d][pl.ds(0, part), :] = work_ref[rows_at((member ^ d) * part, part), :]
        out_refs[d][pl.ds(part, TAG), :] = tag


smem = pl.BlockSpec(memory_space=pltpu.SMEM)
vmem = pl.BlockSpec(memory_space=pltpu.VMEM)
unread = pl.BlockSpec(memory_space=pl.ANY)


def call(kernel, scalars, arrays, outs, scratch=(), flops=0, after=()):
    out_shape = [jax.ShapeDtypeStruct(shape, jnp.float32) for shape in outs]
    head = len(scalars) + len(arrays)

    def run(*refs):
        kernel(*refs[:head], *refs[head + len(after) :])

    moved = sum(a.size * a.dtype.itemsize for a in arrays) + sum(4 * int(np.prod(s)) for s in outs)
    held = moved + sum(4 * int(np.prod(s)) for s in scratch)
    return pl.pallas_call(
        run,
        out_shape=out_shape,
        in_specs=[smem] * len(scalars) + [vmem] * len(arrays) + [unread] * len(after),
        out_specs=[smem if len(shape) == 1 else vmem for shape in outs],
        scratch_shapes=[pltpu.VMEM(shape, jnp.float32) for shape in scratch],
        compiler_params=pltpu.CompilerParams(vmem_limit_bytes=held + 4 * 2**20),
        cost_estimate=pl.CostEstimate(flops=flops, bytes_accessed=moved, transcendentals=0),
    )(*scalars, *arrays, *after)


def pair_up(array, groups, flip):
    return lax.ppermute(array, "gz", [(i, i ^ flip) for i in range(groups)])


def step_by(array, groups, distance):
    return lax.ppermute(
        array, "gz", [(i, i + distance) for i in range(groups) if 0 <= i + distance < groups]
    )


def body(source, layer_ids, conduct_table, shift):
    planes, length_x, length_y = source.shape[1:]
    groups = lax.axis_size("gz")
    blocks = groups // GROUP
    levels = blocks.bit_length() - 1
    count = GROUP * planes
    length_z = planes * groups
    full = length_x // RADIX
    short = full // (HALVES * CHUNKS)
    rows = 2 * short
    if blocks < 2 or groups != GROUP << levels or planes > 2 or short % 8 or length_x != RADIX * full:
        raise ValueError("unsupported layout")
    me = lax.axis_index("gz")
    member = me % GROUP
    flags = jnp.stack([member % RADIX, member // RADIX, me // GROUP, member]).astype(jnp.int32)

    wave = wave_tables(length_x)
    wave_f = jnp.asarray(two_terms(wave))
    wave_b = jnp.asarray(two_terms(np.ascontiguousarray(np.swapaxes(wave, 1, 2)) / length_x))
    sine = jnp.asarray(two_terms(sine_table(length_y)))
    wave_eig = np.broadcast_to(wave_eigen(length_x)[:, :, None], (RADIX, full, length_y))
    wave_eig = jnp.asarray(np.ascontiguousarray(wave_eig).astype(np.float32))
    sine_eig = jnp.asarray(np.tile(sine_eigen(length_y)[None, :], (8, 1)).astype(np.float32))

    chunks = range(CHUNKS)
    row_block = (TAG, length_y)
    block = (count * rows, length_y)
    sums_block = (2 * rows + TAG, length_y)
    single = (rows + TAG, length_y)
    part = (planes * rows + TAG, length_y)
    parts = (CHUNKS * planes * rows + TAG, length_y)
    gives = [single] if levels == 1 else []
    dots = 6 * length_y * length_y

    parted = source.reshape(2, planes, RADIX, full, length_y)
    (cells,) = call(conduct_kernel, [conduct_table], [layer_ids, parted, wave_f], [row_block])
    if levels == 1:
        below = above = pair_up(cells, groups, GROUP)
        totals = [cells, below]
    else:
        below = step_by(cells, groups, GROUP)
        above = step_by(cells, groups, -GROUP)
        total = cells
        for level in range(levels):
            (total,) = call(add_kernel, [], [total, pair_up(total, groups, GROUP << level)], [row_block])
        totals = [total]

    spectra = {}
    placed = []
    for d in (2, 3, 0, 1):
        made = call(
            functools.partial(forward_kernel, d, len(totals)), [flags],
            [parted, wave_f, cells, below, above, *totals], [parts] * HALVES,
            scratch=[(planes, 2 * full, length_y)], flops=planes * 2 * full * dots, after=placed,
        )
        placed = made[:1]
        for n in range(HALVES):
            spectra[d + RADIX * n] = made[n]
    for d in SENDS[:-1]:
        spectra[d] = pair_up(spectra[d], groups, d)
    faces, numbers = call(
        functools.partial(group_kernel, planes, blocks, length_y * length_z), [flags, shift],
        [spectra[d] for d in SENDS], [(6, count, length_y), (6,)],
        scratch=[(count + 16, length_y), row_block, row_block],
    )

    state = [{} for _ in chunks]

    def exchange(st, after):
        sums, give = st["sums"][0], st["sums"][-1]
        st["came"], st["tags"] = [], []
        for level in range(levels):
            st["came"].append(pair_up(give, groups, GROUP << level))
            if level + 1 < levels:
                shape = single if level + 2 == levels else sums_block
                (give,) = call(
                    functools.partial(join_kernel, level, levels), [flags], [sums, st["came"][-1], st["base"]],
                    [shape], after=after,
                )
                sums = give
                st["tags"] = [give[-TAG:]]

    def start(t, after):
        st = state[t]
        st["field"], st["modes"], st["base"], *st["sums"] = call(
            functools.partial(start_kernel, t, planes, blocks), [flags, numbers],
            [wave_eig, sine_eig, sine] + [spectra[d] for d in SENDS],
            [block, block, (6, rows, length_y), sums_block, *gives], flops=count * rows * dots, after=after,
        )
        exchange(st, [])
        return [st["sums"][-1]]

    def factors(t, after):
        st = state[t]
        (st["factors"],) = call(
            functools.partial(factors_kernel, t, count, levels), [flags, numbers],
            [wave_eig, sine_eig, st["base"]], [(4 + count + levels - 1, rows, length_y)], after=after,
        )
        return [st["factors"]]

    def middle(t, after):
        st = state[t]
        st["found"], st["modes"], *st["sums"] = call(
            functools.partial(middle_kernel, t, count, levels), [flags, numbers],
            [wave_eig, sine, faces, st["field"], st["modes"], st["base"], st["factors"], st["sums"][0], *st["came"]],
            [block, block, sums_block, *gives], scratch=[((count + 2) * rows, length_y)],
            flops=(2 * count + 2) * rows * dots, after=after,
        )
        exchange(st, [])
        return [st["sums"][-1]]

    def end(t, after):
        st = state[t]
        made = call(
            functools.partial(end_kernel, count, levels), [flags, numbers],
            [sine, st["found"], st["modes"], st["base"], st["factors"], st["sums"][0], *st["came"], *st["tags"]],
            [part] * GROUP, scratch=[block], flops=count * rows * dots, after=after,
        )
        st["answers"] = list(made)
        for d in SENDS[:-1]:
            st["answers"][d] = pair_up(made[d], groups, d)
        return [st["answers"][d] for d in SENDS[:2]]

    placed = []
    for step in (start, factors, middle, end):
        for t in chunks:
            placed = step(t, placed)
    return call(
        functools.partial(backward_kernel, planes, length_x * length_x * length_y * length_z),
        [flags], [wave_b] + [state[t]["answers"][d] for t in chunks for d in SENDS],
        [(2, planes, length_x, length_y), (2,)],
        scratch=[(planes, RADIX, 2 * full, length_y), (RADIX, planes, 2 * full, length_y)],
        flops=planes * RADIX * 2 * full * dots,
    )


def solution(mesh):
    placed = (P(None, ("node", "gz"), None, None), P(("node", "gz"), None), P(), P("node"))
    return jax.shard_map(
        body,
        mesh=mesh,
        in_specs=placed,
        out_specs=(P(None, ("node", "gz"), None, None), P("node")),
        check_vma=False,
    )
```

```python
import functools

import jax
import jax.numpy as jnp
import ml_dtypes
import numpy as np
from jax import lax
from jax.experimental import pallas as pl
from jax.experimental.pallas import tpu as pltpu
from jax.sharding import PartitionSpec as P

RADIX = 4
HALVES = 2
GROUP = RADIX * HALVES
CHUNKS = 2
TAG = 8

relax = 0.6


def sine_table(length):
    indices = np.arange(1, length + 1)
    product = indices[:, None] * indices[None, :] % (2 * (length + 1))
    return np.sqrt(2.0 / (length + 1)) * np.sin(np.pi / (length + 1) * product)


def sine_eigen(length):
    indices = np.arange(1, length + 1)
    return 4.0 * np.sin(np.pi / (2 * (length + 1)) * indices) ** 2


def wave_numbers(length):
    return RADIX * np.arange(length // RADIX)[None, :] + np.arange(RADIX)[:, None]


def wave_eigen(length):
    return 4.0 * np.sin(np.pi / length * wave_numbers(length)) ** 2


def wave_tables(length):
    waves = wave_numbers(length)
    short = length // RADIX
    product = waves[:, :, None] * np.arange(short)[None, None, :] % length
    angles = 2.0 * np.pi / length * product
    cos_t, sin_t = np.cos(angles), np.sin(angles)
    shape = (RADIX, HALVES, CHUNKS, short // (HALVES * CHUNKS), 2 * short)
    top = np.concatenate([cos_t, sin_t], axis=2).reshape(shape)
    low = np.concatenate([-sin_t, cos_t], axis=2).reshape(shape)
    table = np.concatenate([top, low], axis=3).swapaxes(1, 2)
    return table.reshape(RADIX, 2 * short, 2 * short)


def two_terms(table):
    first = table.astype(ml_dtypes.bfloat16)
    return np.stack([first, (table - first.astype(np.float64)).astype(ml_dtypes.bfloat16)])


def split(value):
    first = value.astype(jnp.bfloat16)
    return first, (value - first.astype(jnp.float32)).astype(jnp.bfloat16)


def dot3(a, b):
    def one(x, y):
        return jnp.dot(x, y, preferred_element_type=jnp.float32)

    return one(a[0], b[0]) + (one(a[0], b[1]) + one(a[1], b[0]))


def cmul(a, b):
    return (a[0] * b[0] - a[1] * b[1], a[0] * b[1] + a[1] * b[0])


def csqr(a):
    cross = a[0] * a[1]
    return ((a[0] - a[1]) * (a[0] + a[1]), cross + cross)


def cpow(a, count):
    result = None
    while count:
        if count & 1:
            result = a if result is None else cmul(result, a)
        count >>= 1
        if count:
            a = csqr(a)
    return result


def cadd(a, b):
    return (a[0] + b[0], a[1] + b[1])


def csub(a, b):
    return (a[0] - b[0], a[1] - b[1])


def cscale(a, scale):
    return (a[0] * scale, a[1] * scale)


def cmore(total, factor, term):
    return cadd(total, cmul(factor, term))


def cinv(a):
    scale = 1.0 / (a[0] * a[0] + a[1] * a[1])
    return (a[0] * scale, -a[1] * scale)


def cone(a):
    return (1.0 - a[0], -a[1])


def cpick(cond, a, b):
    return (jnp.where(cond, a[0], b[0]), jnp.where(cond, a[1], b[1]))


def rows_at(start, rows):
    if isinstance(start, int):
        return pl.ds(start, rows)
    return pl.ds(pl.multiple_of(start, 8), rows)


def load(ref, base, short, row, rows):
    return (ref[rows_at(base + row, rows), :], ref[rows_at(base + short + row, rows), :])


def store(ref, base, short, row, rows, value):
    ref[rows_at(base + row, rows), :] = value[0]
    ref[rows_at(base + short + row, rows), :] = value[1]


def each_strip(count, rows, body):
    def step(i, carry):
        body(pl.multiple_of(i * rows, rows))
        return carry

    lax.fori_loop(0, count // rows, step, 0)


def squares_of(a):
    return a[0] * a[0] + a[1] * a[1]


def conduct_kernel(table_ref, ids_ref, source_ref, wave_ref, out_ref, source_out_ref, wave_out_ref, held_ref, arrived):
    fetches = [
        pltpu.make_async_copy(ids_ref, held_ref, arrived.at[0]),
        pltpu.make_async_copy(source_ref, source_out_ref, arrived.at[1]),
        pltpu.make_async_copy(wave_ref, wave_out_ref, arrived.at[2]),
    ]
    for fetch in fetches:
        fetch.start()
    fetches[0].wait()
    planes = ids_ref.shape[0]
    ids = held_ref[...]
    cells = jnp.zeros(ids.shape, jnp.float32)
    for layer in range(table_ref.shape[0]):
        cells = jnp.where(ids == layer, table_ref[layer], cells)
    out_ref[...] = jnp.zeros_like(out_ref)
    out_ref[pl.ds(0, planes), :] = cells
    out_ref[pl.ds(TAG - 1, 1), :] = jnp.sum(cells, axis=0, keepdims=True)
    for fetch in fetches[1:]:
        fetch.wait()


def add_kernel(one_ref, two_ref, out_ref):
    out_ref[...] = one_ref[...] + two_ref[...]


def fill_tag(out_ref, start, planes, own_ref, below_ref, above_ref, part_refs):
    for n, ref in enumerate((own_ref, below_ref, above_ref)):
        out_ref[pl.ds(start + n * planes, planes), :] = ref[pl.ds(0, planes), :]
    total = part_refs[0][pl.ds(TAG - 1, 1), :]
    for ref in part_refs[1:]:
        total = total + ref[pl.ds(TAG - 1, 1), :]
    out_ref[pl.ds(start + TAG - 1, 1), :] = total


def group_kernel(
    planes, blocks, cells_total, flags_ref, shift_ref, field_ref, faces_ref, numbers_ref, padded_ref,
):
    z = flags_ref[2]
    _, count, width = faces_ref.shape
    stride = field_ref.shape[0] // GROUP
    total = None
    for n in range(GROUP):
        tag = field_ref[pl.ds((n + 1) * stride - TAG, TAG), :]
        padded_ref[pl.ds(8 + n * planes, planes), :] = tag[:planes]
        total = tag[TAG - 1 :] if total is None else total + tag[TAG - 1 :]
    below = field_ref[pl.ds(GROUP * stride - TAG + 2 * planes - 1, 1), :]
    above = field_ref[pl.ds(stride - TAG + 2 * planes, 1), :]
    inv = (1.0 / (jnp.sum(total, axis=1, keepdims=True) * (1.0 / cells_total)))[0, 0]
    numbers_ref[0] = shift_ref[0] * inv
    numbers_ref[1] = shift_ref[1] * inv
    numbers_ref[2] = relax * inv
    numbers_ref[3] = 0.5 * relax * inv
    numbers_ref[4] = shift_ref[0]
    numbers_ref[5] = shift_ref[1]
    cells = padded_ref[pl.ds(8, count), :]
    padded_ref[pl.ds(7, 1), :] = jnp.where(z == 0, cells[0:1], below)
    padded_ref[pl.ds(8 + count, 1), :] = jnp.where(z == blocks - 1, cells[count - 1 : count], above)
    lane = lax.broadcasted_iota(jnp.int32, cells.shape, 1)
    last, first = lane == width - 1, lane == 0
    right = 0.5 * (cells + pltpu.roll(cells, width - 1, 1))
    left = 0.5 * (cells + pltpu.roll(cells, 1, 1))
    low = 0.5 * (cells + padded_ref[pl.ds(7, count), :])
    high = 0.5 * (cells + padded_ref[pl.ds(9, count), :])
    faces_ref[0] = jnp.where(last, cells, right) + jnp.where(first, cells, left) + (low + high)
    faces_ref[1] = cells
    faces_ref[2] = jnp.where(last, 0.0, right)
    faces_ref[3] = jnp.where(first, 0.0, left)
    faces_ref[4] = low
    faces_ref[5] = high


def forward_kernel(chunk, source_ref, wave_ref, own_ref, below_ref, above_ref, *refs):
    part_refs, out_ref = refs[:-1], refs[-1]
    planes = source_ref.shape[1]
    stride = out_ref.shape[0] // GROUP
    rows = (stride - TAG) // planes
    for p in range(planes):
        parts = [[source_ref[c, p, i] for i in range(RADIX)] for c in range(2)]
        even = [parts[c][0] + parts[c][2] for c in range(2)]
        odd = [parts[c][1] + parts[c][3] for c in range(2)]
        even_d = [parts[c][0] - parts[c][2] for c in range(2)]
        odd_d = [parts[c][1] - parts[c][3] for c in range(2)]
        mixed = (
            [even[0] + odd[0], even[1] + odd[1]],
            [even_d[0] + odd_d[1], even_d[1] - odd_d[0]],
            [even[0] - odd[0], even[1] - odd[1]],
            [even_d[0] - odd_d[1], even_d[1] + odd_d[0]],
        )
        for q in range(RADIX):
            table = [wave_ref[n, q, pl.ds(chunk * HALVES * rows, HALVES * rows), :] for n in range(2)]
            waves = dot3(table, split(jnp.concatenate(mixed[q], axis=0)))
            for h in range(HALVES):
                out_ref[pl.ds((q + RADIX * h) * stride + p * rows, rows), :] = waves[h * rows : (h + 1) * rows]
    for n in range(GROUP):
        fill_tag(out_ref, (n + 1) * stride - TAG, planes, own_ref, below_ref, above_ref, part_refs)


def backward_kernel(planes, cells, wave_ref, *refs):
    arrays, (out_ref, norms_ref, mixed_ref) = refs[:CHUNKS], refs[CHUNKS:]
    stride = arrays[0].shape[0] // GROUP
    rows = (stride - TAG) // planes
    short = rows * CHUNKS * HALVES // 2
    total = None
    for ref in arrays:
        for n in range(GROUP):
            tag = ref[pl.ds((n + 1) * stride - TAG, TAG), :]
            total = tag if total is None else total + tag
    for q in range(RADIX):
        for p in range(planes):
            waves = jnp.concatenate(
                [
                    ref[pl.ds((q + RADIX * h) * stride + p * rows, rows), :]
                    for ref in arrays
                    for h in range(HALVES)
                ],
                axis=0,
            )
            mixed_ref[p, q] = dot3((wave_ref[0, q], wave_ref[1, q]), split(waves))
    for p in range(planes):

        def strip(row):
            zero, one, two, three = [load(mixed_ref.at[p, q], 0, short, row, 8) for q in range(RADIX)]
            even, odd = cadd(zero, two), cadd(one, three)
            even_d, odd_d = csub(zero, two), csub(one, three)
            parts = (
                cadd(even, odd),
                (even_d[0] - odd_d[1], even_d[1] + odd_d[0]),
                csub(even, odd),
                (even_d[0] + odd_d[1], even_d[1] - odd_d[0]),
            )
            for i in range(RADIX):
                for c in range(2):
                    out_ref[c, p, rows_at(i * short + row, 8), :] = parts[i][c]

        each_strip(short, 8, strip)
    norms = jnp.sqrt(jnp.sum(total, axis=1, keepdims=True) * (1.0 / cells))
    for n in range(norms_ref.shape[0]):
        norms_ref[n] = norms[n, 0]


def decay_root(h):
    sq = (h[0] + 0.25 * (h[0] * h[0] - h[1] * h[1]), h[1] + 0.5 * h[0] * h[1])
    size = jnp.sqrt(squares_of(sq))
    root_re = jnp.sqrt(0.5 * (size + sq[0]))
    root = (root_re, 0.5 * sq[1] / root_re)
    return cinv((1.0 + 0.5 * h[0] + root[0], 0.5 * h[1] + root[1])), root


def two_powers(power, z, stacks):
    low = high = None
    bit = 0
    while (1 << bit) < stacks:
        taken = ((z >> bit) & 1) == 1
        if low is None:
            one = (jnp.ones_like(power[0]), jnp.zeros_like(power[0]))
            low, high = cpick(taken, power, one), cpick(taken, one, power)
        else:
            grown = cmul(cpick(taken, low, high), power)
            low, high = cpick(taken, grown, low), cpick(taken, high, grown)
        power = csqr(power)
        bit += 1
    return low, high


def sums_of(planes, rho, cross_f, cross_b):
    ahead = planes[0]
    for a in planes[1:]:
        ahead = cmore(a, rho, ahead)
    behind = planes[-1]
    for a in planes[-2::-1]:
        behind = cmore(a, rho, behind)
    return csub(ahead, cmul(cross_f, behind)), csub(behind, cmul(cross_b, ahead))


def sine_rows(source_ref, target_ref, sine_ref, count):
    sine = (sine_ref[0], sine_ref[1])
    rows = max(n for n in range(16, 257, 16) if count % n == 0)
    for i in range(0, count, rows):
        target_ref[pl.ds(i, rows), :] = dot3(split(source_ref[pl.ds(i, rows), :]), sine)


def sine_members(source_ref, target_ref, sine_ref):
    sine = (sine_ref[0], sine_ref[1])
    stride = source_ref.shape[0] // GROUP
    part = stride - TAG
    for n in range(0, GROUP, 2):
        pair = [source_ref[pl.ds((n + i) * stride, part), :] for i in range(2)]
        target_ref[pl.ds(n * part, 2 * part), :] = dot3(split(jnp.concatenate(pair, axis=0)), sine)


def plane_start(ref, planes, rows, plane):
    return plane // planes * (ref.shape[0] // GROUP) + plane % planes * rows


def fill_give(z, rows, sums_ref, give_refs):
    for ref in give_refs:
        ref[pl.ds(0, rows), :] = sums_ref[rows_at((z & 1) * rows, rows), :]
        ref[pl.ds(rows, TAG), :] = sums_ref[pl.ds(2 * rows, TAG), :]


def start_kernel(
    chunk, planes, blocks, flags_ref, numbers_ref, wave_eig_ref, sine_eig_ref, sine_ref,
    field_ref, modes_ref, base_ref, sums_ref, *give_refs,
):
    q, h, z = flags_ref[0], flags_ref[1], flags_ref[2]
    rows = base_ref.shape[1]
    short = rows // 2
    count = GROUP * planes
    first_row = (h * CHUNKS + chunk) * short
    sine_members(field_ref, modes_ref, sine_ref)
    h_re, h_im = numbers_ref[0], numbers_ref[1]
    sine_eig = sine_eig_ref[...]

    def strip(i, total):
        row = pl.multiple_of(i * 8, 8)
        eigen = wave_eig_ref[q, rows_at(first_row + row, 8), :] + sine_eig
        rho, _ = decay_root((eigen + h_re, jnp.full_like(eigen, h_im)))
        block = cpow(rho, count)
        next_one = cmul(block, rho)
        low, high = two_powers(csqr(block), z, blocks)
        cross_f, cross_b = cmul(next_one, low), cmul(next_one, high)
        for n, value in enumerate((rho, cross_f, cross_b, block, low, high)):
            store(base_ref.at[n], 0, short, row, 8, value)
        found = [load(modes_ref, l * rows, short, row, 8) for l in range(count)]
        ahead, behind = sums_of(found, rho, cross_f, cross_b)
        store(sums_ref, 0, short, row, 8, ahead)
        store(sums_ref, rows, short, row, 8, behind)
        for l in range(count):
            total = total + squares_of(load(field_ref, plane_start(field_ref, planes, rows, l), short, row, 8))
        return total

    total = lax.fori_loop(0, short // 8, strip, jnp.zeros((8, field_ref.shape[1]), jnp.float32))
    sums_ref[pl.ds(2 * rows, TAG), :] = jnp.zeros((TAG, field_ref.shape[1]), jnp.float32)
    sums_ref[pl.ds(2 * rows, 1), :] = jnp.sum(total, axis=0, keepdims=True)
    fill_give(z, rows, sums_ref, give_refs)


def factors_kernel(
    chunk, count, levels, flags_ref, numbers_ref, wave_eig_ref, sine_eig_ref, base_ref, out_ref,
):
    q, h_part, z = flags_ref[0], flags_ref[1], flags_ref[2]
    short = base_ref.shape[1] // 2
    h_re, h_im, scale = numbers_ref[0], numbers_ref[1], numbers_ref[3]
    sine_eig = sine_eig_ref[...]

    def strip(row):
        eigen = wave_eig_ref[q, rows_at((h_part * CHUNKS + chunk) * short + row, 8), :] + sine_eig
        h = (eigen + h_re, jnp.full_like(eigen, h_im))
        rho, _, _, block, low, high = [load(base_ref.at[n], 0, short, row, 8) for n in range(6)]
        half_gap = csub((1.0 + 0.5 * h[0], 0.5 * h[1]), rho)
        wide = cmul(csqr(block), csqr(rho))
        low_w, high_w = cmul(low, wide), cmul(high, wide)
        whole = cscale(cinv(cmul(half_gap, cone(cmul(low, high_w)))), scale)
        turned = cmul(rho, whole)
        values = [
            cmul(cone(high_w), whole), cmul(cone(low), turned),
            cmul(cone(high), turned), cmul(cone(low_w), whole),
        ]
        pivot = (2.0 + h[0], h[1])
        inverse = cinv(pivot)
        values.append(inverse)
        for _ in range(count - 1):
            inverse = cinv(csub(pivot, inverse))
            values.append(inverse)
        near = far = None
        power = block
        for level in range(1, levels):
            taken = ((z >> (level - 1)) & 1) == 1
            if near is None:
                one = (jnp.ones_like(power[0]), jnp.zeros_like(power[0]))
                near, far = cpick(taken, power, one), cpick(taken, one, power)
            else:
                grown = cmul(cpick(taken, near, far), power)
                near, far = cpick(taken, grown, near), cpick(taken, far, grown)
            power = csqr(power)
            values.append(cpick(((z >> level) & 1) == 1, near, far))
        for n, value in enumerate(values):
            store(out_ref.at[n], 0, short, row, 8, value)

    each_strip(short, 8, strip)


def join_kernel(level, levels, flags_ref, sums_ref, came_ref, base_ref, out_ref):
    z = flags_ref[2]
    short = base_ref.shape[1] // 2
    rows = 2 * short
    above = ((z >> level) & 1) == 1
    last = level + 2 == levels
    upper = ((z >> (level + 1)) & 1) == 1

    def strip(row):
        block = load(base_ref.at[3], 0, short, row, 8)
        for _ in range(level):
            block = csqr(block)
        ahead, behind = load(sums_ref, 0, short, row, 8), load(sums_ref, rows, short, row, 8)
        ahead_c, behind_c = load(came_ref, 0, short, row, 8), load(came_ref, rows, short, row, 8)
        joined = cmore(cpick(above, ahead, ahead_c), block, cpick(above, ahead_c, ahead))
        joined_b = cmore(cpick(above, behind_c, behind), block, cpick(above, behind, behind_c))
        if last:
            store(out_ref, 0, short, row, 8, cpick(upper, joined_b, joined))
        else:
            store(out_ref, 0, short, row, 8, joined)
            store(out_ref, rows, short, row, 8, joined_b)

    each_strip(short, 8, strip)
    out_ref[pl.ds(out_ref.shape[0] - TAG, TAG), :] = (
        sums_ref[pl.ds(2 * rows, TAG), :] + came_ref[pl.ds(2 * rows, TAG), :]
    )


def solved(count, levels, z, scale, modes_ref, sums_ref, came_refs, base_ref, factors_ref, row):
    short = base_ref.shape[1] // 2
    rows = 2 * short

    def factor(n):
        return load(factors_ref.at[n], 0, short, row, 8)

    enter_f = enter_b = None
    for level in range(levels):
        above = ((z >> level) & 1) == 1
        base = 0 if level == levels - 1 else jnp.where(above, 0, rows)
        came = load(came_refs[level], base, short, row, 8)
        if level:
            came = cmul(factor(4 + count + level - 1), came)
        nought = (jnp.zeros_like(came[0]), jnp.zeros_like(came[0]))
        now_f, now_b = cpick(above, came, nought), cpick(above, nought, came)
        enter_f = now_f if enter_f is None else cadd(enter_f, now_f)
        enter_b = now_b if enter_b is None else cadd(enter_b, now_b)
    block = load(base_ref.at[3], 0, short, row, 8)
    all_f = cmore(load(sums_ref, 0, short, row, 8), block, enter_f)
    all_b = cmore(load(sums_ref, rows, short, row, 8), block, enter_b)
    below = cmore(cmul(factor(0), enter_f), factor(1), all_b)
    above = cmore(cmul(factor(3), enter_b), factor(2), all_f)
    planes = [cscale(load(modes_ref, l * rows, short, row, 8), scale) for l in range(count)]
    planes[0] = cadd(planes[0], below)
    planes[-1] = cadd(planes[-1], above)
    for l in range(1, count):
        planes[l] = cmore(planes[l], factor(4 + l - 1), planes[l - 1])
    planes[-1] = cmul(factor(4 + count - 1), planes[-1])
    for l in range(count - 2, -1, -1):
        planes[l] = cmul(factor(4 + l), cadd(planes[l], planes[l + 1]))
    return below, planes, above


def middle_kernel(
    chunk, planes_each, levels, flags_ref, numbers_ref, wave_eig_ref, sine_ref, faces_ref, field_ref,
    modes_ref, base_ref, factors_ref, sums_ref, *refs,
):
    came_refs, (found_ref, next_ref, next_sums_ref) = refs[:levels], refs[levels : levels + 3]
    give_refs, work_ref = refs[levels + 3 : -1], refs[-1]
    q, h, z = flags_ref[0], flags_ref[1], flags_ref[2]
    scale, s_re, s_im = numbers_ref[2], numbers_ref[4], numbers_ref[5]
    count = GROUP * planes_each
    short = base_ref.shape[1] // 2
    rows = 2 * short
    width = base_ref.shape[2]

    def solve(row):
        below, planes, above = solved(
            count, levels, z, scale, modes_ref, sums_ref, came_refs, base_ref, factors_ref, row
        )
        store(work_ref, 0, short, row, 8, below)
        store(work_ref, (count + 1) * rows, short, row, 8, above)
        for l in range(count):
            store(work_ref, (l + 1) * rows, short, row, 8, planes[l])
            store(found_ref, l * rows, short, row, 8, planes[l])

    each_strip(short, 8, solve)
    sine_rows(work_ref, work_ref, sine_ref, (count + 2) * rows)

    def residual(i, total):
        row = pl.multiple_of(i * 8, 8)
        eigen = wave_eig_ref[q, rows_at((h * CHUNKS + chunk) * short + row, 8), :]
        under = load(work_ref, 0, short, row, 8)
        here = load(work_ref, rows, short, row, 8)
        for l in range(count):
            over = load(work_ref, (l + 2) * rows, short, row, 8)
            diag, cell, right, left, low, high = [faces_ref[n, pl.ds(l, 1), :] for n in range(6)]
            diag = s_re + (diag + cell * eigen)
            value = []
            for c in range(2):
                v = diag * here[c] - right * pltpu.roll(here[c], width - 1, 1)
                v = v - left * pltpu.roll(here[c], 1, 1)
                value.append(v - (low * under[c] + high * over[c]))
            value = (value[0] - s_im * here[1], value[1] + s_im * here[0])
            value = csub(load(field_ref, plane_start(field_ref, planes_each, rows, l), short, row, 8), value)
            total = total + squares_of(value)
            store(work_ref, l * rows, short, row, 8, value)
            under, here = here, over
        return total

    total = lax.fori_loop(0, short // 8, residual, jnp.zeros((8, width), jnp.float32))
    sine_rows(work_ref, next_ref, sine_ref, count * rows)

    def sums(row):
        rho, cross_f, cross_b = [load(base_ref.at[n], 0, short, row, 8) for n in range(3)]
        planes = [load(next_ref, l * rows, short, row, 8) for l in range(count)]
        ahead, behind = sums_of(planes, rho, cross_f, cross_b)
        store(next_sums_ref, 0, short, row, 8, ahead)
        store(next_sums_ref, rows, short, row, 8, behind)

    each_strip(short, 8, sums)
    next_sums_ref[pl.ds(2 * rows, TAG), :] = sums_ref[pl.ds(2 * rows, TAG), :]
    next_sums_ref[pl.ds(2 * rows + 1, 1), :] = jnp.sum(total, axis=0, keepdims=True)
    fill_give(z, rows, next_sums_ref, give_refs)


def end_kernel(
    count, levels, flags_ref, numbers_ref, sine_ref, found_ref, modes_ref, base_ref,
    factors_ref, sums_ref, *refs,
):
    came_refs, out_ref, work_ref = refs[:levels], refs[-2], refs[-1]
    z = flags_ref[2]
    scale = numbers_ref[2]
    short = base_ref.shape[1] // 2
    rows = 2 * short

    def solve(row):
        _, planes, _ = solved(
            count, levels, z, scale, modes_ref, sums_ref, came_refs, base_ref, factors_ref, row
        )
        for l in range(count):
            before = load(found_ref, l * rows, short, row, 8)
            store(work_ref, l * rows, short, row, 8, cadd(before, planes[l]))

    each_strip(short, 8, solve)
    part = count // GROUP * rows
    stride = part + TAG
    sine = (sine_ref[0], sine_ref[1])
    for n in range(0, GROUP, 2):
        pair = dot3(split(work_ref[pl.ds(n * part, 2 * part), :]), sine)
        out_ref[pl.ds(n * stride, part), :] = pair[:part]
        out_ref[pl.ds((n + 1) * stride, part), :] = pair[part:]
    tag_refs = (refs[levels] if levels > 1 else sums_ref, came_refs[-1])
    tag = None
    for ref in tag_refs:
        part_tag = ref[pl.ds(ref.shape[0] - TAG, TAG), :]
        tag = part_tag if tag is None else tag + part_tag
    for n in range(GROUP):
        out_ref[pl.ds((n + 1) * stride - TAG, TAG), :] = tag


smem = pl.BlockSpec(memory_space=pltpu.SMEM)
vmem = pl.BlockSpec(memory_space=pltpu.VMEM)
unread = pl.BlockSpec(memory_space=pl.ANY)
far = pl.BlockSpec(memory_space=pltpu.HBM)


def call(kernel, scalars, arrays, outs, scratch=(), flops=0, after=(), fetched=0):
    out_shape = [a if hasattr(a, "dtype") else jax.ShapeDtypeStruct(a, jnp.float32) for a in outs]
    head = len(scalars) + len(arrays)

    def run(*refs):
        kernel(*refs[:head], *refs[head + len(after) :])

    held = sum(a.size * a.dtype.itemsize for a in [*arrays, *out_shape])
    moved = held
    held += sum(int(np.prod(a.shape)) * 4 for a in scratch if hasattr(a, "shape"))
    ready = len(arrays) - fetched
    return pl.pallas_call(
        run,
        out_shape=out_shape,
        in_specs=[smem] * len(scalars) + [vmem] * ready + [far] * fetched + [unread] * len(after),
        out_specs=[smem if len(a.shape) == 1 else vmem for a in out_shape],
        scratch_shapes=list(scratch),
        compiler_params=pltpu.CompilerParams(vmem_limit_bytes=held + 4 * 2**20),
        cost_estimate=pl.CostEstimate(flops=flops, bytes_accessed=moved, transcendentals=0),
    )(*scalars, *arrays, *after)


def scratch_of(*shapes):
    return [pltpu.VMEM(shape, jnp.float32) for shape in shapes]


def swap_members(array, groups):
    members = [list(range(i, i + GROUP)) for i in range(0, groups, GROUP)]
    return lax.all_to_all(array, "gz", 0, 0, axis_index_groups=members, tiled=True)


def pair_up(array, groups, flip):
    return lax.ppermute(array, "gz", [(i, i ^ flip) for i in range(groups)])


def step_by(array, groups, distance):
    return lax.ppermute(
        array, "gz", [(i, i + distance) for i in range(groups) if 0 <= i + distance < groups]
    )


def body(source, layer_ids, conduct_table, shift):
    planes, length_x, length_y = source.shape[1:]
    groups = lax.axis_size("gz")
    blocks = groups // GROUP
    levels = blocks.bit_length() - 1
    count = GROUP * planes
    length_z = planes * groups
    full = length_x // RADIX
    short = full // (HALVES * CHUNKS)
    rows = 2 * short
    if blocks < 2 or groups != GROUP << levels or planes > 2 or short % 8 or length_x != RADIX * full:
        raise ValueError("unsupported layout")
    me = lax.axis_index("gz")
    member = me % GROUP
    flags = jnp.stack([member % RADIX, member // RADIX, me // GROUP]).astype(jnp.int32)

    wave = wave_tables(length_x)
    wave_f = jnp.asarray(two_terms(wave))
    wave_b = jnp.asarray(two_terms(np.ascontiguousarray(np.swapaxes(wave, 1, 2)) / length_x))
    sine = jnp.asarray(two_terms(sine_table(length_y)))
    wave_eig = np.broadcast_to(wave_eigen(length_x)[:, :, None], (RADIX, full, length_y))
    wave_eig = jnp.asarray(np.ascontiguousarray(wave_eig).astype(np.float32))
    sine_eig = jnp.asarray(np.tile(sine_eigen(length_y)[None, :], (8, 1)).astype(np.float32))

    chunks = range(CHUNKS)
    row_block = (TAG, length_y)
    block = (count * rows, length_y)
    sums_block = (2 * rows + TAG, length_y)
    single = (rows + TAG, length_y)
    parts = (GROUP * (planes * rows + TAG), length_y)
    gives = [single] if levels == 1 else []
    dots = 6 * length_y * length_y

    parted = source.reshape(2, planes, RADIX, full, length_y)
    cells, parted, wave_f = call(
        conduct_kernel, [conduct_table], [layer_ids, parted, wave_f],
        [row_block, jax.ShapeDtypeStruct(parted.shape, parted.dtype), jax.ShapeDtypeStruct(wave_f.shape, wave_f.dtype)],
        scratch=[pltpu.VMEM(layer_ids.shape, layer_ids.dtype), pltpu.SemaphoreType.DMA((3,))], fetched=3,
    )
    if levels == 1:
        below = above = pair_up(cells, groups, GROUP)
        totals = [cells, below]
    else:
        below = step_by(cells, groups, GROUP)
        above = step_by(cells, groups, -GROUP)
        total = cells
        for level in range(levels):
            (total,) = call(add_kernel, [], [total, pair_up(total, groups, GROUP << level)], [row_block])
        totals = [total]

    spectra = []
    for t in chunks:
        (made,) = call(
            functools.partial(forward_kernel, t), [], [parted, wave_f, cells, below, above, *totals], [parts],
            flops=planes * RADIX * HALVES * rows * dots, after=spectra,
        )
        spectra.append(made)
    spectra = [swap_members(a, groups) for a in spectra]
    faces, numbers = call(
        functools.partial(group_kernel, planes, blocks, length_y * length_z), [flags, shift], spectra[:1],
        [(6, count, length_y), (6,)], scratch=scratch_of((count + 16, length_y)),
    )

    state = [{} for _ in chunks]

    def exchange(st, after):
        sums, give = st["sums"][0], st["sums"][-1]
        st["came"], st["tags"] = [], []
        for level in range(levels):
            st["came"].append(pair_up(give, groups, GROUP << level))
            if level + 1 < levels:
                shape = single if level + 2 == levels else sums_block
                (give,) = call(
                    functools.partial(join_kernel, level, levels), [flags], [sums, st["came"][-1], st["base"]],
                    [shape], after=after,
                )
                sums = give
                st["tags"] = [give[-TAG:]]

    def start(t, after):
        st = state[t]
        st["modes"], st["base"], *st["sums"] = call(
            functools.partial(start_kernel, t, planes, blocks), [flags, numbers],
            [wave_eig, sine_eig, sine, spectra[t]],
            [block, (6, rows, length_y), sums_block, *gives], flops=count * rows * dots, after=after,
        )
        exchange(st, [])
        return [st["sums"][-1]]

    def factors(t, after):
        st = state[t]
        (st["factors"],) = call(
            functools.partial(factors_kernel, t, count, levels), [flags, numbers],
            [wave_eig, sine_eig, st["base"]], [(4 + count + levels - 1, rows, length_y)], after=after,
        )
        return [st["factors"]]

    def middle(t, after):
        st = state[t]
        st["found"], st["modes"], *st["sums"] = call(
            functools.partial(middle_kernel, t, planes, levels), [flags, numbers],
            [wave_eig, sine, faces, spectra[t], st["modes"], st["base"], st["factors"], st["sums"][0], *st["came"]],
            [block, block, sums_block, *gives], scratch=scratch_of(((count + 2) * rows, length_y)),
            flops=(2 * count + 2) * rows * dots, after=after,
        )
        exchange(st, [])
        return [st["sums"][-1]]

    def end(t, after):
        st = state[t]
        (made,) = call(
            functools.partial(end_kernel, count, levels), [flags, numbers],
            [sine, st["found"], st["modes"], st["base"], st["factors"], st["sums"][0], *st["came"], *st["tags"]],
            [parts], scratch=scratch_of(block), flops=count * rows * dots, after=after,
        )
        st["answer"] = swap_members(made, groups)
        return [made]

    placed = []
    for step, t in (
        (start, 0), (factors, 0), (middle, 0), (start, 1), (factors, 1), (end, 0), (middle, 1), (end, 1),
    ):
        placed = step(t, placed)
    return call(
        functools.partial(backward_kernel, planes, length_x * length_x * length_y * length_z), [],
        [wave_b, *[st["answer"] for st in state]], [(2, planes, length_x, length_y), (2,)],
        scratch=scratch_of((planes, RADIX, 2 * full, length_y)), flops=planes * RADIX * 2 * full * dots,
    )


def solution(mesh):
    placed = (P(None, ("node", "gz"), None, None), P(("node", "gz"), None), P(), P("node"))
    return jax.shard_map(
        body,
        mesh=mesh,
        in_specs=placed,
        out_specs=(P(None, ("node", "gz"), None, None), P("node")),
        check_vma=False,
    )
```

```python
import functools

import jax
import jax.numpy as jnp
import ml_dtypes
import numpy as np
from jax import lax
from jax.experimental import pallas as pl
from jax.experimental.pallas import tpu as pltpu
from jax.sharding import PartitionSpec as P

RADIX = 4
HALVES = 2
GROUP = RADIX * HALVES
CHUNKS = 2
SENDS = (6, 7, 2, 3, 4, 5, 1, 0)
TAG = 8

relax = 0.6


def sine_table(length):
    indices = np.arange(1, length + 1)
    product = indices[:, None] * indices[None, :] % (2 * (length + 1))
    return np.sqrt(2.0 / (length + 1)) * np.sin(np.pi / (length + 1) * product)


def sine_eigen(length):
    indices = np.arange(1, length + 1)
    return 4.0 * np.sin(np.pi / (2 * (length + 1)) * indices) ** 2


def wave_numbers(length):
    return RADIX * np.arange(length // RADIX)[None, :] + np.arange(RADIX)[:, None]


def wave_eigen(length):
    return 4.0 * np.sin(np.pi / length * wave_numbers(length)) ** 2


def wave_tables(length):
    waves = wave_numbers(length)
    short = length // RADIX
    product = waves[:, :, None] * np.arange(short)[None, None, :] % length
    angles = 2.0 * np.pi / length * product
    cos_t, sin_t = np.cos(angles), np.sin(angles)
    pieces = HALVES * CHUNKS
    top = np.concatenate([cos_t, sin_t], axis=2).reshape(RADIX, pieces, short // pieces, 2 * short)
    low = np.concatenate([-sin_t, cos_t], axis=2).reshape(RADIX, pieces, short // pieces, 2 * short)
    return np.concatenate([top, low], axis=2).reshape(RADIX, 2 * short, 2 * short)


def two_terms(table):
    first = table.astype(ml_dtypes.bfloat16)
    return np.stack([first, (table - first.astype(np.float64)).astype(ml_dtypes.bfloat16)])


def split(value):
    first = value.astype(jnp.bfloat16)
    return first, (value - first.astype(jnp.float32)).astype(jnp.bfloat16)


def dot3(a, b):
    def one(x, y):
        return jnp.dot(x, y, preferred_element_type=jnp.float32)

    return one(a[0], b[0]) + (one(a[0], b[1]) + one(a[1], b[0]))


def cmul(a, b):
    return (a[0] * b[0] - a[1] * b[1], a[0] * b[1] + a[1] * b[0])


def csqr(a):
    cross = a[0] * a[1]
    return ((a[0] - a[1]) * (a[0] + a[1]), cross + cross)


def cpow(a, count):
    result = None
    while count:
        if count & 1:
            result = a if result is None else cmul(result, a)
        count >>= 1
        if count:
            a = csqr(a)
    return result


def cadd(a, b):
    return (a[0] + b[0], a[1] + b[1])


def csub(a, b):
    return (a[0] - b[0], a[1] - b[1])


def cscale(a, scale):
    return (a[0] * scale, a[1] * scale)


def cmore(total, factor, term):
    return cadd(total, cmul(factor, term))


def cinv(a):
    scale = 1.0 / (a[0] * a[0] + a[1] * a[1])
    return (a[0] * scale, -a[1] * scale)


def cone(a):
    return (1.0 - a[0], -a[1])


def cpick(cond, a, b):
    return (jnp.where(cond, a[0], b[0]), jnp.where(cond, a[1], b[1]))


def rows_at(start, rows):
    if isinstance(start, int):
        return pl.ds(start, rows)
    return pl.ds(pl.multiple_of(start, 8), rows)


def load(ref, base, short, row, rows):
    return (ref[rows_at(base + row, rows), :], ref[rows_at(base + short + row, rows), :])


def store(ref, base, short, row, rows, value):
    ref[rows_at(base + row, rows), :] = value[0]
    ref[rows_at(base + short + row, rows), :] = value[1]


def each_strip(count, rows, body):
    def step(i, carry):
        body(pl.multiple_of(i * rows, rows))
        return carry

    lax.fori_loop(0, count // rows, step, 0)


def squares_of(a):
    return a[0] * a[0] + a[1] * a[1]


def conduct_kernel(table_ref, ids_ref, out_ref):
    planes = ids_ref.shape[0]
    ids = ids_ref[...]
    cells = jnp.zeros(ids.shape, jnp.float32)
    for layer in range(table_ref.shape[0]):
        cells = jnp.where(ids == layer, table_ref[layer], cells)
    out_ref[...] = jnp.zeros_like(out_ref)
    out_ref[pl.ds(0, planes), :] = cells
    out_ref[pl.ds(TAG - 1, 1), :] = jnp.sum(cells, axis=0, keepdims=True)


def add_kernel(one_ref, two_ref, out_ref):
    out_ref[...] = one_ref[...] + two_ref[...]


def fill_tag(out_ref, planes, own_ref, below_ref, above_ref, part_refs):
    start = out_ref.shape[0] - TAG
    for n, ref in enumerate((own_ref, below_ref, above_ref)):
        out_ref[pl.ds(start + n * planes, planes), :] = ref[pl.ds(0, planes), :]
    total = part_refs[0][pl.ds(TAG - 1, 1), :]
    for ref in part_refs[1:]:
        total = total + ref[pl.ds(TAG - 1, 1), :]
    out_ref[pl.ds(start + TAG - 1, 1), :] = total


def group_kernel(planes, blocks, cells_total, flags_ref, shift_ref, *refs):
    part_refs, (faces_ref, numbers_ref, padded_ref, below_ref, above_ref) = refs[:GROUP], refs[GROUP:]
    z, member = flags_ref[2], flags_ref[3]
    _, count, width = faces_ref.shape
    total = None
    for d, ref in zip(SENDS, part_refs):
        tag = ref[pl.ds(ref.shape[0] - TAG, TAG), :]
        place = member ^ d
        for p in range(planes):
            padded_ref[pl.ds(8 + place * planes + p, 1), :] = tag[p : p + 1]
        below_ref[pl.ds(place, 1), :] = tag[2 * planes - 1 : 2 * planes]
        above_ref[pl.ds(place, 1), :] = tag[2 * planes : 2 * planes + 1]
        total = tag[TAG - 1 :] if total is None else total + tag[TAG - 1 :]
    inv = (1.0 / (jnp.sum(total, axis=1, keepdims=True) * (1.0 / cells_total)))[0, 0]
    numbers_ref[0] = shift_ref[0] * inv
    numbers_ref[1] = shift_ref[1] * inv
    numbers_ref[2] = relax * inv
    numbers_ref[3] = 0.5 * relax * inv
    numbers_ref[4] = shift_ref[0]
    numbers_ref[5] = shift_ref[1]
    cells = padded_ref[pl.ds(8, count), :]
    padded_ref[pl.ds(7, 1), :] = jnp.where(z == 0, cells[0:1], below_ref[pl.ds(GROUP - 1, 1), :])
    padded_ref[pl.ds(8 + count, 1), :] = jnp.where(
        z == blocks - 1, cells[count - 1 : count], above_ref[pl.ds(0, 1), :]
    )
    lane = lax.broadcasted_iota(jnp.int32, cells.shape, 1)
    last, first = lane == width - 1, lane == 0
    right = 0.5 * (cells + pltpu.roll(cells, width - 1, 1))
    left = 0.5 * (cells + pltpu.roll(cells, 1, 1))
    low = 0.5 * (cells + padded_ref[pl.ds(7, count), :])
    high = 0.5 * (cells + padded_ref[pl.ds(9, count), :])
    faces_ref[0] = jnp.where(last, cells, right) + jnp.where(first, cells, left) + (low + high)
    faces_ref[1] = cells
    faces_ref[2] = jnp.where(last, 0.0, right)
    faces_ref[3] = jnp.where(first, 0.0, left)
    faces_ref[4] = low
    faces_ref[5] = high


def forward_kernel(distance, parts_count, flags_ref, source_ref, wave_ref, own_ref, below_ref, above_ref, *refs):
    part_refs, out_refs, stage_ref = refs[:parts_count], refs[parts_count:-1], refs[-1]
    planes = source_ref.shape[1]
    q = flags_ref[0] ^ distance
    sign = (1 - 2 * (q & 1)).astype(jnp.float32)
    turn_re = jnp.where(q == 0, 1.0, jnp.where(q == 2, -1.0, 0.0))
    turn_im = jnp.where(q == 1, 1.0, jnp.where(q == 3, -1.0, 0.0))
    rows = stage_ref.shape[1] // (HALVES * CHUNKS)
    for p in range(planes):
        parts = [[source_ref[c, p, i] for i in range(RADIX)] for c in range(2)]
        even = [parts[c][0] + sign * parts[c][2] for c in range(2)]
        odd = [parts[c][1] + sign * parts[c][3] for c in range(2)]
        mixed = jnp.concatenate(
            [
                even[0] + (turn_re * odd[0] + turn_im * odd[1]),
                even[1] + (turn_re * odd[1] - turn_im * odd[0]),
            ],
            axis=0,
        )
        stage_ref[p] = dot3((wave_ref[0, q], wave_ref[1, q]), split(mixed))
        for n in range(HALVES):
            h = flags_ref[1] ^ n
            for t in range(CHUNKS):
                out_refs[n * CHUNKS + t][pl.ds(p * rows, rows), :] = stage_ref[
                    p, rows_at((h * CHUNKS + t) * rows, rows), :
                ]
    for ref in out_refs:
        fill_tag(ref, planes, own_ref, below_ref, above_ref, part_refs)


def backward_kernel(planes, cells, flags_ref, wave_ref, *refs):
    arrays, (out_ref, norms_ref, mixed_ref, stage_ref) = refs[:-4], refs[-4:]
    came = {(d, t): arrays[t * GROUP + n] for t in range(CHUNKS) for n, d in enumerate(SENDS)}
    rows = (arrays[0].shape[0] - TAG) // planes
    short = rows * CHUNKS * HALVES // 2
    total = None
    for ref in arrays:
        tag = ref[pl.ds(planes * rows, TAG), :]
        total = tag if total is None else total + tag
    for d in range(RADIX):
        q = flags_ref[0] ^ d
        for p in range(planes):
            for n in range(HALVES):
                h = flags_ref[1] ^ n
                for t in range(CHUNKS):
                    stage_ref[d, p, rows_at((h * CHUNKS + t) * rows, rows), :] = came[d + RADIX * n, t][
                        pl.ds(p * rows, rows), :
                    ]
            mixed_ref[p, q] = dot3((wave_ref[0, q], wave_ref[1, q]), split(stage_ref[d, p]))
    for p in range(planes):

        def strip(row):
            zero, one, two, three = [load(mixed_ref.at[p, q], 0, short, row, 8) for q in range(RADIX)]
            even, odd = cadd(zero, two), cadd(one, three)
            even_d, odd_d = csub(zero, two), csub(one, three)
            parts = (
                cadd(even, odd),
                (even_d[0] - odd_d[1], even_d[1] + odd_d[0]),
                csub(even, odd),
                (even_d[0] + odd_d[1], even_d[1] - odd_d[0]),
            )
            for i in range(RADIX):
                for c in range(2):
                    out_ref[c, p, rows_at(i * short + row, 8), :] = parts[i][c]

        each_strip(short, 8, strip)
    norms = jnp.sqrt(jnp.sum(total, axis=1, keepdims=True) * (1.0 / cells))
    for n in range(norms_ref.shape[0]):
        norms_ref[n] = norms[n, 0]


def decay_root(h):
    sq = (h[0] + 0.25 * (h[0] * h[0] - h[1] * h[1]), h[1] + 0.5 * h[0] * h[1])
    size = jnp.sqrt(squares_of(sq))
    root_re = jnp.sqrt(0.5 * (size + sq[0]))
    root = (root_re, 0.5 * sq[1] / root_re)
    return cinv((1.0 + 0.5 * h[0] + root[0], 0.5 * h[1] + root[1])), root


def two_powers(power, z, stacks):
    low = high = None
    bit = 0
    while (1 << bit) < stacks:
        taken = ((z >> bit) & 1) == 1
        if low is None:
            one = (jnp.ones_like(power[0]), jnp.zeros_like(power[0]))
            low, high = cpick(taken, power, one), cpick(taken, one, power)
        else:
            grown = cmul(cpick(taken, low, high), power)
            low, high = cpick(taken, grown, low), cpick(taken, high, grown)
        power = csqr(power)
        bit += 1
    return low, high


def sums_of(planes, rho, cross_f, cross_b):
    ahead = planes[0]
    for a in planes[1:]:
        ahead = cmore(a, rho, ahead)
    behind = planes[-1]
    for a in planes[-2::-1]:
        behind = cmore(a, rho, behind)
    return csub(ahead, cmul(cross_f, behind)), csub(behind, cmul(cross_b, ahead))


def sine_rows(source_ref, target_ref, sine_ref, count):
    sine = (sine_ref[0], sine_ref[1])
    rows = max(n for n in range(16, 257, 16) if count % n == 0)
    for i in range(0, count, rows):
        target_ref[pl.ds(i, rows), :] = dot3(split(source_ref[pl.ds(i, rows), :]), sine)


def fill_give(z, rows, sums_ref, give_refs):
    for ref in give_refs:
        ref[pl.ds(0, rows), :] = sums_ref[rows_at((z & 1) * rows, rows), :]
        ref[pl.ds(rows, TAG), :] = sums_ref[pl.ds(2 * rows, TAG), :]


def start_kernel(
    chunk, planes, blocks, flags_ref, numbers_ref, wave_eig_ref, sine_eig_ref, sine_ref,
    *refs,
):
    part_refs, (field_ref, modes_ref, base_ref, sums_ref), give_refs = refs[:GROUP], refs[GROUP : GROUP + 4], refs[GROUP + 4 :]
    q, h, z, member = [flags_ref[n] for n in range(4)]
    part = part_refs[0].shape[0] - TAG
    rows = part // planes
    short = rows // 2
    count = GROUP * planes
    first_row = (h * CHUNKS + chunk) * short
    for d, ref in zip(SENDS, part_refs):
        field_ref[rows_at((member ^ d) * part, part), :] = ref[pl.ds(0, part), :]
    sine_rows(field_ref, modes_ref, sine_ref, count * rows)
    h_re, h_im = numbers_ref[0], numbers_ref[1]
    sine_eig = sine_eig_ref[...]

    def strip(i, total):
        row = pl.multiple_of(i * 8, 8)
        eigen = wave_eig_ref[q, rows_at(first_row + row, 8), :] + sine_eig
        rho, _ = decay_root((eigen + h_re, jnp.full_like(eigen, h_im)))
        block = cpow(rho, count)
        next_one = cmul(block, rho)
        low, high = two_powers(csqr(block), z, blocks)
        cross_f, cross_b = cmul(next_one, low), cmul(next_one, high)
        for n, value in enumerate((rho, cross_f, cross_b, block, low, high)):
            store(base_ref.at[n], 0, short, row, 8, value)
        found = [load(modes_ref, l * rows, short, row, 8) for l in range(count)]
        ahead, behind = sums_of(found, rho, cross_f, cross_b)
        store(sums_ref, 0, short, row, 8, ahead)
        store(sums_ref, rows, short, row, 8, behind)
        for l in range(count):
            total = total + squares_of(load(field_ref, l * rows, short, row, 8))
        return total

    total = lax.fori_loop(0, short // 8, strip, jnp.zeros((8, field_ref.shape[1]), jnp.float32))
    sums_ref[pl.ds(2 * rows, TAG), :] = jnp.zeros((TAG, field_ref.shape[1]), jnp.float32)
    sums_ref[pl.ds(2 * rows, 1), :] = jnp.sum(total, axis=0, keepdims=True)
    fill_give(z, rows, sums_ref, give_refs)


def factors_kernel(
    chunk, count, levels, flags_ref, numbers_ref, wave_eig_ref, sine_eig_ref, base_ref, out_ref,
):
    q, h_part, z = flags_ref[0], flags_ref[1], flags_ref[2]
    short = base_ref.shape[1] // 2
    h_re, h_im, scale = numbers_ref[0], numbers_ref[1], numbers_ref[3]
    sine_eig = sine_eig_ref[...]

    def strip(row):
        eigen = wave_eig_ref[q, rows_at((h_part * CHUNKS + chunk) * short + row, 8), :] + sine_eig
        h = (eigen + h_re, jnp.full_like(eigen, h_im))
        rho, _, _, block, low, high = [load(base_ref.at[n], 0, short, row, 8) for n in range(6)]
        half_gap = csub((1.0 + 0.5 * h[0], 0.5 * h[1]), rho)
        wide = cmul(csqr(block), csqr(rho))
        low_w, high_w = cmul(low, wide), cmul(high, wide)
        whole = cscale(cinv(cmul(half_gap, cone(cmul(low, high_w)))), scale)
        turned = cmul(rho, whole)
        values = [
            cmul(cone(high_w), whole), cmul(cone(low), turned),
            cmul(cone(high), turned), cmul(cone(low_w), whole),
        ]
        pivot = (2.0 + h[0], h[1])
        inverse = cinv(pivot)
        values.append(inverse)
        for _ in range(count - 1):
            inverse = cinv(csub(pivot, inverse))
            values.append(inverse)
        near = far = None
        power = block
        for level in range(1, levels):
            taken = ((z >> (level - 1)) & 1) == 1
            if near is None:
                one = (jnp.ones_like(power[0]), jnp.zeros_like(power[0]))
                near, far = cpick(taken, power, one), cpick(taken, one, power)
            else:
                grown = cmul(cpick(taken, near, far), power)
                near, far = cpick(taken, grown, near), cpick(taken, far, grown)
            power = csqr(power)
            values.append(cpick(((z >> level) & 1) == 1, near, far))
        for n, value in enumerate(values):
            store(out_ref.at[n], 0, short, row, 8, value)

    each_strip(short, 8, strip)


def join_kernel(level, levels, flags_ref, sums_ref, came_ref, base_ref, out_ref):
    z = flags_ref[2]
    short = base_ref.shape[1] // 2
    rows = 2 * short
    above = ((z >> level) & 1) == 1
    last = level + 2 == levels
    upper = ((z >> (level + 1)) & 1) == 1

    def strip(row):
        block = load(base_ref.at[3], 0, short, row, 8)
        for _ in range(level):
            block = csqr(block)
        ahead, behind = load(sums_ref, 0, short, row, 8), load(sums_ref, rows, short, row, 8)
        ahead_c, behind_c = load(came_ref, 0, short, row, 8), load(came_ref, rows, short, row, 8)
        joined = cmore(cpick(above, ahead, ahead_c), block, cpick(above, ahead_c, ahead))
        joined_b = cmore(cpick(above, behind_c, behind), block, cpick(above, behind, behind_c))
        if last:
            store(out_ref, 0, short, row, 8, cpick(upper, joined_b, joined))
        else:
            store(out_ref, 0, short, row, 8, joined)
            store(out_ref, rows, short, row, 8, joined_b)

    each_strip(short, 8, strip)
    out_ref[pl.ds(out_ref.shape[0] - TAG, TAG), :] = (
        sums_ref[pl.ds(2 * rows, TAG), :] + came_ref[pl.ds(2 * rows, TAG), :]
    )


def solved(count, levels, z, scale, modes_ref, sums_ref, came_refs, base_ref, factors_ref, row):
    short = base_ref.shape[1] // 2
    rows = 2 * short

    def factor(n):
        return load(factors_ref.at[n], 0, short, row, 8)

    enter_f = enter_b = None
    for level in range(levels):
        above = ((z >> level) & 1) == 1
        base = 0 if level == levels - 1 else jnp.where(above, 0, rows)
        came = load(came_refs[level], base, short, row, 8)
        if level:
            came = cmul(factor(4 + count + level - 1), came)
        nought = (jnp.zeros_like(came[0]), jnp.zeros_like(came[0]))
        now_f, now_b = cpick(above, came, nought), cpick(above, nought, came)
        enter_f = now_f if enter_f is None else cadd(enter_f, now_f)
        enter_b = now_b if enter_b is None else cadd(enter_b, now_b)
    block = load(base_ref.at[3], 0, short, row, 8)
    all_f = cmore(load(sums_ref, 0, short, row, 8), block, enter_f)
    all_b = cmore(load(sums_ref, rows, short, row, 8), block, enter_b)
    below = cmore(cmul(factor(0), enter_f), factor(1), all_b)
    above = cmore(cmul(factor(3), enter_b), factor(2), all_f)
    planes = [cscale(load(modes_ref, l * rows, short, row, 8), scale) for l in range(count)]
    planes[0] = cadd(planes[0], below)
    planes[-1] = cadd(planes[-1], above)
    for l in range(1, count):
        planes[l] = cmore(planes[l], factor(4 + l - 1), planes[l - 1])
    planes[-1] = cmul(factor(4 + count - 1), planes[-1])
    for l in range(count - 2, -1, -1):
        planes[l] = cmul(factor(4 + l), cadd(planes[l], planes[l + 1]))
    return below, planes, above


def middle_kernel(
    chunk, count, levels, flags_ref, numbers_ref, wave_eig_ref, sine_ref, faces_ref, field_ref,
    modes_ref, base_ref, factors_ref, sums_ref, *refs,
):
    came_refs, (found_ref, next_ref, next_sums_ref) = refs[:levels], refs[levels : levels + 3]
    give_refs, work_ref = refs[levels + 3 : -1], refs[-1]
    q, h, z = flags_ref[0], flags_ref[1], flags_ref[2]
    scale, s_re, s_im = numbers_ref[2], numbers_ref[4], numbers_ref[5]
    short = base_ref.shape[1] // 2
    rows = 2 * short
    width = base_ref.shape[2]

    def solve(row):
        below, planes, above = solved(
            count, levels, z, scale, modes_ref, sums_ref, came_refs, base_ref, factors_ref, row
        )
        store(work_ref, 0, short, row, 8, below)
        store(work_ref, (count + 1) * rows, short, row, 8, above)
        for l in range(count):
            store(work_ref, (l + 1) * rows, short, row, 8, planes[l])
            store(found_ref, l * rows, short, row, 8, planes[l])

    each_strip(short, 8, solve)
    sine_rows(work_ref, work_ref, sine_ref, (count + 2) * rows)

    def residual(i, total):
        row = pl.multiple_of(i * 8, 8)
        eigen = wave_eig_ref[q, rows_at((h * CHUNKS + chunk) * short + row, 8), :]
        under = load(work_ref, 0, short, row, 8)
        here = load(work_ref, rows, short, row, 8)
        for l in range(count):
            over = load(work_ref, (l + 2) * rows, short, row, 8)
            diag, cell, right, left, low, high = [faces_ref[n, pl.ds(l, 1), :] for n in range(6)]
            diag = s_re + (diag + cell * eigen)
            value = []
            for c in range(2):
                v = diag * here[c] - right * pltpu.roll(here[c], width - 1, 1)
                v = v - left * pltpu.roll(here[c], 1, 1)
                value.append(v - (low * under[c] + high * over[c]))
            value = (value[0] - s_im * here[1], value[1] + s_im * here[0])
            value = csub(load(field_ref, l * rows, short, row, 8), value)
            total = total + squares_of(value)
            store(work_ref, l * rows, short, row, 8, value)
            under, here = here, over
        return total

    total = lax.fori_loop(0, short // 8, residual, jnp.zeros((8, width), jnp.float32))
    sine_rows(work_ref, next_ref, sine_ref, count * rows)

    def sums(row):
        rho, cross_f, cross_b = [load(base_ref.at[n], 0, short, row, 8) for n in range(3)]
        planes = [load(next_ref, l * rows, short, row, 8) for l in range(count)]
        ahead, behind = sums_of(planes, rho, cross_f, cross_b)
        store(next_sums_ref, 0, short, row, 8, ahead)
        store(next_sums_ref, rows, short, row, 8, behind)

    each_strip(short, 8, sums)
    next_sums_ref[pl.ds(2 * rows, TAG), :] = sums_ref[pl.ds(2 * rows, TAG), :]
    next_sums_ref[pl.ds(2 * rows + 1, 1), :] = jnp.sum(total, axis=0, keepdims=True)
    fill_give(z, rows, next_sums_ref, give_refs)


def end_kernel(
    count, levels, flags_ref, numbers_ref, sine_ref, found_ref, modes_ref, base_ref,
    factors_ref, sums_ref, *refs,
):
    came_refs, out_refs, work_ref = refs[:levels], refs[-1 - GROUP : -1], refs[-1]
    z, member = flags_ref[2], flags_ref[3]
    scale = numbers_ref[2]
    short = base_ref.shape[1] // 2
    rows = 2 * short

    def solve(row):
        _, planes, _ = solved(
            count, levels, z, scale, modes_ref, sums_ref, came_refs, base_ref, factors_ref, row
        )
        for l in range(count):
            before = load(found_ref, l * rows, short, row, 8)
            store(work_ref, l * rows, short, row, 8, cadd(before, planes[l]))

    each_strip(short, 8, solve)
    sine_rows(work_ref, work_ref, sine_ref, count * rows)
    part = count // GROUP * rows
    tag_refs = (refs[levels] if levels > 1 else sums_ref, came_refs[-1])
    tag = None
    for ref in tag_refs:
        part_tag = ref[pl.ds(ref.shape[0] - TAG, TAG), :]
        tag = part_tag if tag is None else tag + part_tag
    for d in range(GROUP):
        out_refs[d][pl.ds(0, part), :] = work_ref[rows_at((member ^ d) * part, part), :]
        out_refs[d][pl.ds(part, TAG), :] = tag


smem = pl.BlockSpec(memory_space=pltpu.SMEM)
vmem = pl.BlockSpec(memory_space=pltpu.VMEM)
unread = pl.BlockSpec(memory_space=pl.ANY)


def call(kernel, scalars, arrays, outs, scratch=(), flops=0, after=()):
    out_shape = [jax.ShapeDtypeStruct(shape, jnp.float32) for shape in outs]
    head = len(scalars) + len(arrays)

    def run(*refs):
        kernel(*refs[:head], *refs[head + len(after) :])

    moved = sum(a.size * a.dtype.itemsize for a in arrays) + sum(4 * int(np.prod(s)) for s in outs)
    held = moved + sum(4 * int(np.prod(s)) for s in scratch)
    return pl.pallas_call(
        run,
        out_shape=out_shape,
        in_specs=[smem] * len(scalars) + [vmem] * len(arrays) + [unread] * len(after),
        out_specs=[smem if len(shape) == 1 else vmem for shape in outs],
        scratch_shapes=[pltpu.VMEM(shape, jnp.float32) for shape in scratch],
        compiler_params=pltpu.CompilerParams(vmem_limit_bytes=held + 4 * 2**20),
        cost_estimate=pl.CostEstimate(flops=flops, bytes_accessed=moved, transcendentals=0),
    )(*scalars, *arrays, *after)


def pair_up(array, groups, flip):
    return lax.ppermute(array, "gz", [(i, i ^ flip) for i in range(groups)])


def step_by(array, groups, distance):
    return lax.ppermute(
        array, "gz", [(i, i + distance) for i in range(groups) if 0 <= i + distance < groups]
    )


def body(source, layer_ids, conduct_table, shift):
    planes, length_x, length_y = source.shape[1:]
    groups = lax.axis_size("gz")
    blocks = groups // GROUP
    levels = blocks.bit_length() - 1
    count = GROUP * planes
    length_z = planes * groups
    full = length_x // RADIX
    short = full // (HALVES * CHUNKS)
    rows = 2 * short
    if blocks < 2 or groups != GROUP << levels or planes > 2 or short % 8 or length_x != RADIX * full:
        raise ValueError("unsupported layout")
    me = lax.axis_index("gz")
    member = me % GROUP
    flags = jnp.stack([member % RADIX, member // RADIX, me // GROUP, member]).astype(jnp.int32)

    wave = wave_tables(length_x)
    wave_f = jnp.asarray(two_terms(wave))
    wave_b = jnp.asarray(two_terms(np.ascontiguousarray(np.swapaxes(wave, 1, 2)) / length_x))
    sine = jnp.asarray(two_terms(sine_table(length_y)))
    wave_eig = np.broadcast_to(wave_eigen(length_x)[:, :, None], (RADIX, full, length_y))
    wave_eig = jnp.asarray(np.ascontiguousarray(wave_eig).astype(np.float32))
    sine_eig = jnp.asarray(np.tile(sine_eigen(length_y)[None, :], (8, 1)).astype(np.float32))

    chunks = range(CHUNKS)
    row_block = (TAG, length_y)
    block = (count * rows, length_y)
    sums_block = (2 * rows + TAG, length_y)
    single = (rows + TAG, length_y)
    part = (planes * rows + TAG, length_y)
    gives = [single] if levels == 1 else []
    dots = 6 * length_y * length_y

    (cells,) = call(conduct_kernel, [conduct_table], [layer_ids], [row_block])
    if levels == 1:
        below = above = pair_up(cells, groups, GROUP)
        totals = [cells, below]
    else:
        below = step_by(cells, groups, GROUP)
        above = step_by(cells, groups, -GROUP)
        total = cells
        for level in range(levels):
            (total,) = call(add_kernel, [], [total, pair_up(total, groups, GROUP << level)], [row_block])
        totals = [total]

    parted = source.reshape(2, planes, RADIX, full, length_y)
    spectra = {}
    placed = []
    for d in (2, 0, 3, 1):
        made = call(
            functools.partial(forward_kernel, d, len(totals)), [flags],
            [parted, wave_f, cells, below, above, *totals], [part] * (HALVES * CHUNKS),
            scratch=[(planes, 2 * full, length_y)], flops=planes * 2 * full * dots, after=placed,
        )
        placed = made[:1]
        for n in range(HALVES):
            for t in chunks:
                spectra[d + RADIX * n, t] = made[n * CHUNKS + t]
    for t in chunks:
        for d in SENDS[:-1] if t == 0 else SENDS[:4]:
            spectra[d, t] = pair_up(spectra[d, t], groups, d)
    faces, numbers = call(
        functools.partial(group_kernel, planes, blocks, length_y * length_z), [flags, shift],
        [spectra[d, 0] for d in SENDS], [(6, count, length_y), (6,)],
        scratch=[(count + 16, length_y), row_block, row_block],
    )

    state = [{} for _ in chunks]

    def exchange(st, after):
        sums, give = st["sums"][0], st["sums"][-1]
        st["came"], st["tags"] = [], []
        for level in range(levels):
            st["came"].append(pair_up(give, groups, GROUP << level))
            if level + 1 < levels:
                shape = single if level + 2 == levels else sums_block
                (give,) = call(
                    functools.partial(join_kernel, level, levels), [flags], [sums, st["came"][-1], st["base"]],
                    [shape], after=after,
                )
                sums = give
                st["tags"] = [give[-TAG:]]

    def start(t, after):
        st = state[t]
        if t:
            for d in SENDS[4:-1]:
                held, _ = lax.optimization_barrier((spectra[d, t], after[0]))
                spectra[d, t] = pair_up(held, groups, d)
        st["field"], st["modes"], st["base"], *st["sums"] = call(
            functools.partial(start_kernel, t, planes, blocks), [flags, numbers],
            [wave_eig, sine_eig, sine] + [spectra[d, t] for d in SENDS],
            [block, block, (6, rows, length_y), sums_block, *gives], flops=count * rows * dots, after=after,
        )
        exchange(st, [])
        (st["factors"],) = call(
            functools.partial(factors_kernel, t, count, levels), [flags, numbers],
            [wave_eig, sine_eig, st["base"]], [(4 + count + levels - 1, rows, length_y)],
        )
        return [st["factors"]]

    def middle(t, after):
        st = state[t]
        st["found"], st["modes"], *st["sums"] = call(
            functools.partial(middle_kernel, t, count, levels), [flags, numbers],
            [wave_eig, sine, faces, st["field"], st["modes"], st["base"], st["factors"], st["sums"][0], *st["came"]],
            [block, block, sums_block, *gives], scratch=[((count + 2) * rows, length_y)],
            flops=(2 * count + 2) * rows * dots, after=after,
        )
        exchange(st, [])
        return [st["sums"][-1]]

    def end(t, after):
        st = state[t]
        made = call(
            functools.partial(end_kernel, count, levels), [flags, numbers],
            [sine, st["found"], st["modes"], st["base"], st["factors"], st["sums"][0], *st["came"], *st["tags"]],
            [part] * GROUP, scratch=[block], flops=count * rows * dots, after=after,
        )
        st["answers"] = list(made)
        for d in SENDS[:-1]:
            st["answers"][d] = pair_up(made[d], groups, d)
        return made[:1]

    placed = start(0, [])
    placed = middle(0, placed)
    placed = start(1, placed)
    placed = end(0, placed)
    placed = middle(1, placed)
    placed = end(1, placed)
    return call(
        functools.partial(backward_kernel, planes, length_x * length_x * length_y * length_z),
        [flags], [wave_b] + [state[t]["answers"][d] for t in chunks for d in SENDS],
        [(2, planes, length_x, length_y), (2,)],
        scratch=[(planes, RADIX, 2 * full, length_y), (RADIX, planes, 2 * full, length_y)],
        flops=planes * RADIX * 2 * full * dots,
    )


def solution(mesh):
    placed = (P(None, ("node", "gz"), None, None), P(("node", "gz"), None), P(), P("node"))
    return jax.shard_map(
        body,
        mesh=mesh,
        in_specs=placed,
        out_specs=(P(None, ("node", "gz"), None, None), P("node")),
        check_vma=False,
    )
```

```python
import functools

import jax
import jax.numpy as jnp
import ml_dtypes
import numpy as np
from jax import lax
from jax.experimental import pallas as pl
from jax.experimental.pallas import tpu as pltpu
from jax.sharding import PartitionSpec as P

RADIX = 4
HALVES = 2
GROUP = RADIX * HALVES
CHUNKS = 2
LONG = (6, 7, 2, 3)
SHORT = (4, 5, 1, 0)
SENDS = LONG + SHORT
TAG = 8

relax = 0.6


def sine_table(length):
    indices = np.arange(1, length + 1)
    product = indices[:, None] * indices[None, :] % (2 * (length + 1))
    return np.sqrt(2.0 / (length + 1)) * np.sin(np.pi / (length + 1) * product)


def sine_eigen(length):
    indices = np.arange(1, length + 1)
    return 4.0 * np.sin(np.pi / (2 * (length + 1)) * indices) ** 2


def wave_numbers(length):
    return RADIX * np.arange(length // RADIX)[None, :] + np.arange(RADIX)[:, None]


def wave_eigen(length):
    return 4.0 * np.sin(np.pi / length * wave_numbers(length)) ** 2


def wave_tables(length):
    waves = wave_numbers(length)
    short = length // RADIX
    product = waves[:, :, None] * np.arange(short)[None, None, :] % length
    angles = 2.0 * np.pi / length * product
    cos_t, sin_t = np.cos(angles), np.sin(angles)
    pieces = HALVES * CHUNKS
    top = np.concatenate([cos_t, sin_t], axis=2).reshape(RADIX, pieces, short // pieces, 2 * short)
    low = np.concatenate([-sin_t, cos_t], axis=2).reshape(RADIX, pieces, short // pieces, 2 * short)
    return np.concatenate([top, low], axis=2).reshape(RADIX, 2 * short, 2 * short)


def two_terms(table):
    first = table.astype(ml_dtypes.bfloat16)
    return np.stack([first, (table - first.astype(np.float64)).astype(ml_dtypes.bfloat16)])


def split(value):
    first = value.astype(jnp.bfloat16)
    return first, (value - first.astype(jnp.float32)).astype(jnp.bfloat16)


def dot3(a, b):
    def one(x, y):
        return jnp.dot(x, y, preferred_element_type=jnp.float32)

    return one(a[0], b[0]) + (one(a[0], b[1]) + one(a[1], b[0]))


def cmul(a, b):
    return (a[0] * b[0] - a[1] * b[1], a[0] * b[1] + a[1] * b[0])


def csqr(a):
    cross = a[0] * a[1]
    return ((a[0] - a[1]) * (a[0] + a[1]), cross + cross)


def cpow(a, count):
    result = None
    while count:
        if count & 1:
            result = a if result is None else cmul(result, a)
        count >>= 1
        if count:
            a = csqr(a)
    return result


def cadd(a, b):
    return (a[0] + b[0], a[1] + b[1])


def csub(a, b):
    return (a[0] - b[0], a[1] - b[1])


def cscale(a, scale):
    return (a[0] * scale, a[1] * scale)


def cmore(total, factor, term):
    return cadd(total, cmul(factor, term))


def cinv(a):
    scale = 1.0 / (a[0] * a[0] + a[1] * a[1])
    return (a[0] * scale, -a[1] * scale)


def cone(a):
    return (1.0 - a[0], -a[1])


def cpick(cond, a, b):
    return (jnp.where(cond, a[0], b[0]), jnp.where(cond, a[1], b[1]))


def rows_at(start, rows):
    if isinstance(start, int):
        return pl.ds(start, rows)
    return pl.ds(pl.multiple_of(start, 8), rows)


def load(ref, base, short, row, rows):
    return (ref[rows_at(base + row, rows), :], ref[rows_at(base + short + row, rows), :])


def store(ref, base, short, row, rows, value):
    ref[rows_at(base + row, rows), :] = value[0]
    ref[rows_at(base + short + row, rows), :] = value[1]


def each_strip(count, rows, body):
    def step(i, carry):
        body(pl.multiple_of(i * rows, rows))
        return carry

    lax.fori_loop(0, count // rows, step, 0)


def squares_of(a):
    return a[0] * a[0] + a[1] * a[1]


def conduct_kernel(table_ref, ids_ref, out_ref):
    planes = ids_ref.shape[0]
    ids = ids_ref[...]
    cells = jnp.zeros(ids.shape, jnp.float32)
    for layer in range(table_ref.shape[0]):
        cells = jnp.where(ids == layer, table_ref[layer], cells)
    out_ref[...] = jnp.zeros_like(out_ref)
    out_ref[pl.ds(0, planes), :] = cells
    out_ref[pl.ds(TAG - 1, 1), :] = jnp.sum(cells, axis=0, keepdims=True)


def add_kernel(one_ref, two_ref, out_ref):
    out_ref[...] = one_ref[...] + two_ref[...]


def fill_tag(out_ref, planes, own_ref, below_ref, above_ref, part_refs):
    start = out_ref.shape[0] - TAG
    for n, ref in enumerate((own_ref, below_ref, above_ref)):
        out_ref[pl.ds(start + n * planes, planes), :] = ref[pl.ds(0, planes), :]
    total = part_refs[0][pl.ds(TAG - 1, 1), :]
    for ref in part_refs[1:]:
        total = total + ref[pl.ds(TAG - 1, 1), :]
    out_ref[pl.ds(start + TAG - 1, 1), :] = total


def tag_of(ref):
    return ref[pl.ds(ref.shape[0] - TAG, TAG), :]


def find_numbers(cells_total, shift_ref, part_refs, numbers_ref):
    total = None
    for ref in part_refs:
        row = ref[pl.ds(ref.shape[0] - 1, 1), :]
        total = row if total is None else total + row
    inv = (1.0 / (jnp.sum(total, axis=1, keepdims=True) * (1.0 / cells_total)))[0, 0]
    numbers_ref[0] = shift_ref[0] * inv
    numbers_ref[1] = shift_ref[1] * inv
    numbers_ref[2] = relax * inv
    numbers_ref[3] = 0.5 * relax * inv
    numbers_ref[4] = shift_ref[0]
    numbers_ref[5] = shift_ref[1]


def faces_kernel(planes, blocks, flags_ref, *refs):
    part_refs, (faces_ref, padded_ref, below_ref, above_ref) = refs[:GROUP], refs[GROUP:]
    z, member = flags_ref[2], flags_ref[3]
    _, count, width = faces_ref.shape
    for d, ref in zip(SENDS, part_refs):
        tag = tag_of(ref)
        place = member ^ d
        for p in range(planes):
            padded_ref[pl.ds(8 + place * planes + p, 1), :] = tag[p : p + 1]
        below_ref[pl.ds(place, 1), :] = tag[2 * planes - 1 : 2 * planes]
        above_ref[pl.ds(place, 1), :] = tag[2 * planes : 2 * planes + 1]
    cells = padded_ref[pl.ds(8, count), :]
    padded_ref[pl.ds(7, 1), :] = jnp.where(z == 0, cells[0:1], below_ref[pl.ds(GROUP - 1, 1), :])
    padded_ref[pl.ds(8 + count, 1), :] = jnp.where(
        z == blocks - 1, cells[count - 1 : count], above_ref[pl.ds(0, 1), :]
    )
    lane = lax.broadcasted_iota(jnp.int32, cells.shape, 1)
    last, first = lane == width - 1, lane == 0
    right = 0.5 * (cells + pltpu.roll(cells, width - 1, 1))
    left = 0.5 * (cells + pltpu.roll(cells, 1, 1))
    low = 0.5 * (cells + padded_ref[pl.ds(7, count), :])
    high = 0.5 * (cells + padded_ref[pl.ds(9, count), :])
    faces_ref[0] = jnp.where(last, cells, right) + jnp.where(first, cells, left) + (low + high)
    faces_ref[1] = cells
    faces_ref[2] = jnp.where(last, 0.0, right)
    faces_ref[3] = jnp.where(first, 0.0, left)
    faces_ref[4] = low
    faces_ref[5] = high


def forward_kernel(distance, parts_count, flags_ref, source_ref, wave_ref, own_ref, below_ref, above_ref, *refs):
    part_refs, out_refs, stage_ref = refs[:parts_count], refs[parts_count:-1], refs[-1]
    planes = source_ref.shape[1]
    q = flags_ref[0] ^ distance
    sign = (1 - 2 * (q & 1)).astype(jnp.float32)
    turn_re = jnp.where(q == 0, 1.0, jnp.where(q == 2, -1.0, 0.0))
    turn_im = jnp.where(q == 1, 1.0, jnp.where(q == 3, -1.0, 0.0))
    rows = stage_ref.shape[1] // (HALVES * CHUNKS)
    for p in range(planes):
        parts = [[source_ref[c, p, i] for i in range(RADIX)] for c in range(2)]
        even = [parts[c][0] + sign * parts[c][2] for c in range(2)]
        odd = [parts[c][1] + sign * parts[c][3] for c in range(2)]
        mixed = jnp.concatenate(
            [
                even[0] + (turn_re * odd[0] + turn_im * odd[1]),
                even[1] + (turn_re * odd[1] - turn_im * odd[0]),
            ],
            axis=0,
        )
        stage_ref[p] = dot3((wave_ref[0, q], wave_ref[1, q]), split(mixed))
        for n in range(HALVES):
            h = flags_ref[1] ^ n
            for t in range(CHUNKS):
                if distance in LONG:
                    ref, start = out_refs[n * CHUNKS + t], p * rows
                else:
                    ref, start = out_refs[n], (t * planes + p) * rows
                ref[pl.ds(start, rows), :] = stage_ref[p, rows_at((h * CHUNKS + t) * rows, rows), :]
    for ref in out_refs:
        fill_tag(ref, planes, own_ref, below_ref, above_ref, part_refs)


def backward_kernel(planes, cells, flags_ref, wave_ref, *refs):
    arrays, (out_ref, norms_ref, mixed_ref, stage_ref) = refs[:-4], refs[-4:]
    came = {(d, t): arrays[t * GROUP + n] for t in range(CHUNKS) for n, d in enumerate(SENDS)}
    rows = (arrays[0].shape[0] - TAG) // planes
    short = rows * CHUNKS * HALVES // 2
    total = None
    for ref in arrays:
        tag = ref[pl.ds(planes * rows, TAG), :]
        total = tag if total is None else total + tag
    for d in range(RADIX):
        q = flags_ref[0] ^ d
        for p in range(planes):
            for n in range(HALVES):
                h = flags_ref[1] ^ n
                for t in range(CHUNKS):
                    stage_ref[d, p, rows_at((h * CHUNKS + t) * rows, rows), :] = came[d + RADIX * n, t][
                        pl.ds(p * rows, rows), :
                    ]
            mixed_ref[p, q] = dot3((wave_ref[0, q], wave_ref[1, q]), split(stage_ref[d, p]))
    for p in range(planes):

        def strip(row):
            zero, one, two, three = [load(mixed_ref.at[p, q], 0, short, row, 8) for q in range(RADIX)]
            even, odd = cadd(zero, two), cadd(one, three)
            even_d, odd_d = csub(zero, two), csub(one, three)
            parts = (
                cadd(even, odd),
                (even_d[0] - odd_d[1], even_d[1] + odd_d[0]),
                csub(even, odd),
                (even_d[0] + odd_d[1], even_d[1] - odd_d[0]),
            )
            for i in range(RADIX):
                for c in range(2):
                    out_ref[c, p, rows_at(i * short + row, 8), :] = parts[i][c]

        each_strip(short, 8, strip)
    norms = jnp.sqrt(jnp.sum(total, axis=1, keepdims=True) * (1.0 / cells))
    for n in range(norms_ref.shape[0]):
        norms_ref[n] = norms[n, 0]


def decay_root(h):
    sq = (h[0] + 0.25 * (h[0] * h[0] - h[1] * h[1]), h[1] + 0.5 * h[0] * h[1])
    size = jnp.sqrt(squares_of(sq))
    root_re = jnp.sqrt(0.5 * (size + sq[0]))
    root = (root_re, 0.5 * sq[1] / root_re)
    return cinv((1.0 + 0.5 * h[0] + root[0], 0.5 * h[1] + root[1])), root


def two_powers(power, z, stacks):
    low = high = None
    bit = 0
    while (1 << bit) < stacks:
        taken = ((z >> bit) & 1) == 1
        if low is None:
            one = (jnp.ones_like(power[0]), jnp.zeros_like(power[0]))
            low, high = cpick(taken, power, one), cpick(taken, one, power)
        else:
            grown = cmul(cpick(taken, low, high), power)
            low, high = cpick(taken, grown, low), cpick(taken, high, grown)
        power = csqr(power)
        bit += 1
    return low, high


def sums_of(planes, rho, cross_f, cross_b):
    ahead = planes[0]
    for a in planes[1:]:
        ahead = cmore(a, rho, ahead)
    behind = planes[-1]
    for a in planes[-2::-1]:
        behind = cmore(a, rho, behind)
    return csub(ahead, cmul(cross_f, behind)), csub(behind, cmul(cross_b, ahead))


def sine_rows(source_ref, target_ref, sine_ref, count):
    sine = (sine_ref[0], sine_ref[1])
    rows = max(n for n in range(16, 257, 16) if count % n == 0)
    for i in range(0, count, rows):
        target_ref[pl.ds(i, rows), :] = dot3(split(source_ref[pl.ds(i, rows), :]), sine)


def fill_give(z, rows, sums_ref, give_refs):
    for ref in give_refs:
        ref[pl.ds(0, rows), :] = sums_ref[rows_at((z & 1) * rows, rows), :]
        ref[pl.ds(rows, TAG), :] = sums_ref[pl.ds(2 * rows, TAG), :]


def start_kernel(
    chunk, planes, blocks, cells_total, flags_ref, numbers_ref, wave_eig_ref, sine_eig_ref, sine_ref, *refs,
):
    part_refs, (field_ref, modes_ref, base_ref, sums_ref), give_refs = refs[:GROUP], refs[GROUP : GROUP + 4], refs[GROUP + 4 :]
    if chunk == 0:
        shift_ref, numbers_ref, give_refs = numbers_ref, give_refs[-1], give_refs[:-1]
        find_numbers(cells_total, shift_ref, part_refs, numbers_ref)
    q, h, z, member = [flags_ref[n] for n in range(4)]
    rows = base_ref.shape[1]
    part = rows * planes
    short = rows // 2
    count = GROUP * planes
    first_row = (h * CHUNKS + chunk) * short
    for d, ref in zip(SENDS, part_refs):
        field_ref[rows_at((member ^ d) * part, part), :] = ref[pl.ds(0 if d in LONG else chunk * part, part), :]
    sine_rows(field_ref, modes_ref, sine_ref, count * rows)
    h_re, h_im = numbers_ref[0], numbers_ref[1]
    sine_eig = sine_eig_ref[...]

    def strip(i, total):
        row = pl.multiple_of(i * 8, 8)
        eigen = wave_eig_ref[q, rows_at(first_row + row, 8), :] + sine_eig
        rho, _ = decay_root((eigen + h_re, jnp.full_like(eigen, h_im)))
        block = cpow(rho, count)
        next_one = cmul(block, rho)
        low, high = two_powers(csqr(block), z, blocks)
        cross_f, cross_b = cmul(next_one, low), cmul(next_one, high)
        for n, value in enumerate((rho, cross_f, cross_b, block, low, high)):
            store(base_ref.at[n], 0, short, row, 8, value)
        found = [load(modes_ref, l * rows, short, row, 8) for l in range(count)]
        ahead, behind = sums_of(found, rho, cross_f, cross_b)
        store(sums_ref, 0, short, row, 8, ahead)
        store(sums_ref, rows, short, row, 8, behind)
        for l in range(count):
            total = total + squares_of(load(field_ref, l * rows, short, row, 8))
        return total

    total = lax.fori_loop(0, short // 8, strip, jnp.zeros((8, field_ref.shape[1]), jnp.float32))
    sums_ref[pl.ds(2 * rows, TAG), :] = jnp.zeros((TAG, field_ref.shape[1]), jnp.float32)
    sums_ref[pl.ds(2 * rows, 1), :] = jnp.sum(total, axis=0, keepdims=True)
    fill_give(z, rows, sums_ref, give_refs)


def factors_kernel(
    chunk, count, levels, flags_ref, numbers_ref, wave_eig_ref, sine_eig_ref, base_ref, out_ref,
):
    q, h_part, z = flags_ref[0], flags_ref[1], flags_ref[2]
    short = base_ref.shape[1] // 2
    h_re, h_im, scale = numbers_ref[0], numbers_ref[1], numbers_ref[3]
    sine_eig = sine_eig_ref[...]

    def strip(row):
        eigen = wave_eig_ref[q, rows_at((h_part * CHUNKS + chunk) * short + row, 8), :] + sine_eig
        h = (eigen + h_re, jnp.full_like(eigen, h_im))
        rho, _, _, block, low, high = [load(base_ref.at[n], 0, short, row, 8) for n in range(6)]
        half_gap = csub((1.0 + 0.5 * h[0], 0.5 * h[1]), rho)
        wide = cmul(csqr(block), csqr(rho))
        low_w, high_w = cmul(low, wide), cmul(high, wide)
        whole = cscale(cinv(cmul(half_gap, cone(cmul(low, high_w)))), scale)
        turned = cmul(rho, whole)
        values = [
            cmul(cone(high_w), whole), cmul(cone(low), turned),
            cmul(cone(high), turned), cmul(cone(low_w), whole),
        ]
        pivot = (2.0 + h[0], h[1])
        inverse = cinv(pivot)
        values.append(inverse)
        for _ in range(count - 1):
            inverse = cinv(csub(pivot, inverse))
            values.append(inverse)
        near = far = None
        power = block
        for level in range(1, levels):
            taken = ((z >> (level - 1)) & 1) == 1
            if near is None:
                one = (jnp.ones_like(power[0]), jnp.zeros_like(power[0]))
                near, far = cpick(taken, power, one), cpick(taken, one, power)
            else:
                grown = cmul(cpick(taken, near, far), power)
                near, far = cpick(taken, grown, near), cpick(taken, far, grown)
            power = csqr(power)
            values.append(cpick(((z >> level) & 1) == 1, near, far))
        for n, value in enumerate(values):
            store(out_ref.at[n], 0, short, row, 8, value)

    each_strip(short, 8, strip)


def join_kernel(level, levels, flags_ref, sums_ref, came_ref, base_ref, out_ref):
    z = flags_ref[2]
    short = base_ref.shape[1] // 2
    rows = 2 * short
    above = ((z >> level) & 1) == 1
    last = level + 2 == levels
    upper = ((z >> (level + 1)) & 1) == 1

    def strip(row):
        block = load(base_ref.at[3], 0, short, row, 8)
        for _ in range(level):
            block = csqr(block)
        ahead, behind = load(sums_ref, 0, short, row, 8), load(sums_ref, rows, short, row, 8)
        ahead_c, behind_c = load(came_ref, 0, short, row, 8), load(came_ref, rows, short, row, 8)
        joined = cmore(cpick(above, ahead, ahead_c), block, cpick(above, ahead_c, ahead))
        joined_b = cmore(cpick(above, behind_c, behind), block, cpick(above, behind, behind_c))
        if last:
            store(out_ref, 0, short, row, 8, cpick(upper, joined_b, joined))
        else:
            store(out_ref, 0, short, row, 8, joined)
            store(out_ref, rows, short, row, 8, joined_b)

    each_strip(short, 8, strip)
    out_ref[pl.ds(out_ref.shape[0] - TAG, TAG), :] = (
        sums_ref[pl.ds(2 * rows, TAG), :] + came_ref[pl.ds(2 * rows, TAG), :]
    )


def solved(count, levels, z, scale, modes_ref, sums_ref, came_refs, base_ref, factors_ref, row):
    short = base_ref.shape[1] // 2
    rows = 2 * short

    def factor(n):
        return load(factors_ref.at[n], 0, short, row, 8)

    enter_f = enter_b = None
    for level in range(levels):
        above = ((z >> level) & 1) == 1
        base = 0 if level == levels - 1 else jnp.where(above, 0, rows)
        came = load(came_refs[level], base, short, row, 8)
        if level:
            came = cmul(factor(4 + count + level - 1), came)
        nought = (jnp.zeros_like(came[0]), jnp.zeros_like(came[0]))
        now_f, now_b = cpick(above, came, nought), cpick(above, nought, came)
        enter_f = now_f if enter_f is None else cadd(enter_f, now_f)
        enter_b = now_b if enter_b is None else cadd(enter_b, now_b)
    block = load(base_ref.at[3], 0, short, row, 8)
    all_f = cmore(load(sums_ref, 0, short, row, 8), block, enter_f)
    all_b = cmore(load(sums_ref, rows, short, row, 8), block, enter_b)
    below = cmore(cmul(factor(0), enter_f), factor(1), all_b)
    above = cmore(cmul(factor(3), enter_b), factor(2), all_f)
    planes = [cscale(load(modes_ref, l * rows, short, row, 8), scale) for l in range(count)]
    planes[0] = cadd(planes[0], below)
    planes[-1] = cadd(planes[-1], above)
    for l in range(1, count):
        planes[l] = cmore(planes[l], factor(4 + l - 1), planes[l - 1])
    planes[-1] = cmul(factor(4 + count - 1), planes[-1])
    for l in range(count - 2, -1, -1):
        planes[l] = cmul(factor(4 + l), cadd(planes[l], planes[l + 1]))
    return below, planes, above


def middle_kernel(
    chunk, count, levels, flags_ref, numbers_ref, wave_eig_ref, sine_ref, faces_ref, field_ref,
    modes_ref, base_ref, factors_ref, sums_ref, *refs,
):
    came_refs, (found_ref, next_ref, next_sums_ref) = refs[:levels], refs[levels : levels + 3]
    give_refs, work_ref = refs[levels + 3 : -1], refs[-1]
    q, h, z = flags_ref[0], flags_ref[1], flags_ref[2]
    scale, s_re, s_im = numbers_ref[2], numbers_ref[4], numbers_ref[5]
    short = base_ref.shape[1] // 2
    rows = 2 * short
    width = base_ref.shape[2]

    def solve(row):
        below, planes, above = solved(
            count, levels, z, scale, modes_ref, sums_ref, came_refs, base_ref, factors_ref, row
        )
        store(work_ref, 0, short, row, 8, below)
        store(work_ref, (count + 1) * rows, short, row, 8, above)
        for l in range(count):
            store(work_ref, (l + 1) * rows, short, row, 8, planes[l])
            store(found_ref, l * rows, short, row, 8, planes[l])

    each_strip(short, 8, solve)
    sine_rows(work_ref, work_ref, sine_ref, (count + 2) * rows)

    def residual(i, total):
        row = pl.multiple_of(i * 8, 8)
        eigen = wave_eig_ref[q, rows_at((h * CHUNKS + chunk) * short + row, 8), :]
        under = load(work_ref, 0, short, row, 8)
        here = load(work_ref, rows, short, row, 8)
        for l in range(count):
            over = load(work_ref, (l + 2) * rows, short, row, 8)
            diag, cell, right, left, low, high = [faces_ref[n, pl.ds(l, 1), :] for n in range(6)]
            diag = s_re + (diag + cell * eigen)
            value = []
            for c in range(2):
                v = diag * here[c] - right * pltpu.roll(here[c], width - 1, 1)
                v = v - left * pltpu.roll(here[c], 1, 1)
                value.append(v - (low * under[c] + high * over[c]))
            value = (value[0] - s_im * here[1], value[1] + s_im * here[0])
            value = csub(load(field_ref, l * rows, short, row, 8), value)
            total = total + squares_of(value)
            store(work_ref, l * rows, short, row, 8, value)
            under, here = here, over
        return total

    total = lax.fori_loop(0, short // 8, residual, jnp.zeros((8, width), jnp.float32))
    sine_rows(work_ref, next_ref, sine_ref, count * rows)

    def sums(row):
        rho, cross_f, cross_b = [load(base_ref.at[n], 0, short, row, 8) for n in range(3)]
        planes = [load(next_ref, l * rows, short, row, 8) for l in range(count)]
        ahead, behind = sums_of(planes, rho, cross_f, cross_b)
        store(next_sums_ref, 0, short, row, 8, ahead)
        store(next_sums_ref, rows, short, row, 8, behind)

    each_strip(short, 8, sums)
    next_sums_ref[pl.ds(2 * rows, TAG), :] = sums_ref[pl.ds(2 * rows, TAG), :]
    next_sums_ref[pl.ds(2 * rows + 1, 1), :] = jnp.sum(total, axis=0, keepdims=True)
    fill_give(z, rows, next_sums_ref, give_refs)


def end_kernel(
    count, levels, flags_ref, numbers_ref, sine_ref, found_ref, modes_ref, base_ref,
    factors_ref, sums_ref, *refs,
):
    came_refs, out_refs, work_ref = refs[:levels], refs[-1 - GROUP : -1], refs[-1]
    z, member = flags_ref[2], flags_ref[3]
    scale = numbers_ref[2]
    short = base_ref.shape[1] // 2
    rows = 2 * short

    def solve(row):
        _, planes, _ = solved(
            count, levels, z, scale, modes_ref, sums_ref, came_refs, base_ref, factors_ref, row
        )
        for l in range(count):
            before = load(found_ref, l * rows, short, row, 8)
            store(work_ref, l * rows, short, row, 8, cadd(before, planes[l]))

    each_strip(short, 8, solve)
    sine_rows(work_ref, work_ref, sine_ref, count * rows)
    part = count // GROUP * rows
    tag_refs = (refs[levels] if levels > 1 else sums_ref, came_refs[-1])
    tag = None
    for ref in tag_refs:
        part_tag = ref[pl.ds(ref.shape[0] - TAG, TAG), :]
        tag = part_tag if tag is None else tag + part_tag
    for d in range(GROUP):
        out_refs[d][pl.ds(0, part), :] = work_ref[rows_at((member ^ d) * part, part), :]
        out_refs[d][pl.ds(part, TAG), :] = tag


smem = pl.BlockSpec(memory_space=pltpu.SMEM)
vmem = pl.BlockSpec(memory_space=pltpu.VMEM)
unread = pl.BlockSpec(memory_space=pl.ANY)


def call(kernel, scalars, arrays, outs, scratch=(), flops=0, after=()):
    out_shape = [jax.ShapeDtypeStruct(shape, jnp.float32) for shape in outs]
    head = len(scalars) + len(arrays)

    def run(*refs):
        kernel(*refs[:head], *refs[head + len(after) :])

    moved = sum(a.size * a.dtype.itemsize for a in arrays) + sum(4 * int(np.prod(s)) for s in outs)
    held = moved + sum(4 * int(np.prod(s)) for s in scratch)
    return pl.pallas_call(
        run,
        out_shape=out_shape,
        in_specs=[smem] * len(scalars) + [vmem] * len(arrays) + [unread] * len(after),
        out_specs=[smem if len(shape) == 1 else vmem for shape in outs],
        scratch_shapes=[pltpu.VMEM(shape, jnp.float32) for shape in scratch],
        compiler_params=pltpu.CompilerParams(vmem_limit_bytes=held + 4 * 2**20),
        cost_estimate=pl.CostEstimate(flops=flops, bytes_accessed=moved, transcendentals=0),
    )(*scalars, *arrays, *after)


def pair_up(array, groups, flip):
    return lax.ppermute(array, "gz", [(i, i ^ flip) for i in range(groups)])


def step_by(array, groups, distance):
    return lax.ppermute(
        array, "gz", [(i, i + distance) for i in range(groups) if 0 <= i + distance < groups]
    )


def body(source, layer_ids, conduct_table, shift):
    planes, length_x, length_y = source.shape[1:]
    groups = lax.axis_size("gz")
    blocks = groups // GROUP
    levels = blocks.bit_length() - 1
    count = GROUP * planes
    length_z = planes * groups
    full = length_x // RADIX
    short = full // (HALVES * CHUNKS)
    rows = 2 * short
    if blocks < 2 or groups != GROUP << levels or planes > 2 or short % 8 or length_x != RADIX * full:
        raise ValueError("unsupported layout")
    me = lax.axis_index("gz")
    member = me % GROUP
    flags = jnp.stack([member % RADIX, member // RADIX, me // GROUP, member]).astype(jnp.int32)

    wave = wave_tables(length_x)
    wave_f = jnp.asarray(two_terms(wave))
    wave_b = jnp.asarray(two_terms(np.ascontiguousarray(np.swapaxes(wave, 1, 2)) / length_x))
    sine = jnp.asarray(two_terms(sine_table(length_y)))
    wave_eig = np.broadcast_to(wave_eigen(length_x)[:, :, None], (RADIX, full, length_y))
    wave_eig = jnp.asarray(np.ascontiguousarray(wave_eig).astype(np.float32))
    sine_eig = jnp.asarray(np.tile(sine_eigen(length_y)[None, :], (8, 1)).astype(np.float32))

    chunks = range(CHUNKS)
    row_block = (TAG, length_y)
    block = (count * rows, length_y)
    sums_block = (2 * rows + TAG, length_y)
    single = (rows + TAG, length_y)
    part = (planes * rows + TAG, length_y)
    parts = (CHUNKS * planes * rows + TAG, length_y)
    gives = [single] if levels == 1 else []
    dots = 6 * length_y * length_y

    (cells,) = call(conduct_kernel, [conduct_table], [layer_ids], [row_block])
    if levels == 1:
        below = above = pair_up(cells, groups, GROUP)
        totals = [cells, below]
    else:
        below = step_by(cells, groups, GROUP)
        above = step_by(cells, groups, -GROUP)
        total = cells
        for level in range(levels):
            (total,) = call(add_kernel, [], [total, pair_up(total, groups, GROUP << level)], [row_block])
        totals = [total]

    parted = source.reshape(2, planes, RADIX, full, length_y)
    spectra = {}
    placed = []
    for d in (2, 0, 3, 1):
        shapes = [part] * (HALVES * CHUNKS) if d in LONG else [parts] * HALVES
        made = call(
            functools.partial(forward_kernel, d, len(totals)), [flags],
            [parted, wave_f, cells, below, above, *totals], shapes,
            scratch=[(planes, 2 * full, length_y)], flops=planes * 2 * full * dots, after=placed,
        )
        placed = made[:1]
        for n in range(HALVES):
            for t in chunks:
                spectra[d + RADIX * n, t] = made[n * CHUNKS + t] if d in LONG else made[n]
    for d in SENDS[:-1]:
        spectra[d, 0] = pair_up(spectra[d, 0], groups, d)
    for t in chunks[1:]:
        for d in SHORT:
            spectra[d, t] = spectra[d, 0]
        for d in LONG:
            spectra[d, t] = pair_up(spectra[d, t], groups, d)

    state = [{} for _ in chunks]

    def exchange(st, after):
        sums, give = st["sums"][0], st["sums"][-1]
        st["came"], st["tags"] = [], []
        for level in range(levels):
            st["came"].append(pair_up(give, groups, GROUP << level))
            if level + 1 < levels:
                shape = single if level + 2 == levels else sums_block
                (give,) = call(
                    functools.partial(join_kernel, level, levels), [flags], [sums, st["came"][-1], st["base"]],
                    [shape], after=after,
                )
                sums = give
                st["tags"] = [give[-TAG:]]

    def start(t, after):
        st = state[t]
        outs = [block, block, (6, rows, length_y), sums_block, *gives]
        made = call(
            functools.partial(start_kernel, t, planes, blocks, length_y * length_z),
            [flags, state[0]["numbers"] if t else shift],
            [wave_eig, sine_eig, sine] + [spectra[d, t] for d in SENDS],
            outs if t else [*outs, (6,)], flops=count * rows * dots, after=after,
        )
        if not t:
            *made, st["numbers"] = made
        st["field"], st["modes"], st["base"], *st["sums"] = made
        exchange(st, [])
        return [st["sums"][-1]]

    def faces(t, after):
        state[t]["faces"] = call(
            functools.partial(faces_kernel, planes, blocks), [flags], [spectra[d, 0] for d in SENDS],
            [(6, count, length_y)], scratch=[(count + 16, length_y), row_block, row_block], after=after,
        )[0]
        return [state[t]["faces"]]

    def factors(t, after):
        st = state[t]
        (st["factors"],) = call(
            functools.partial(factors_kernel, t, count, levels), [flags, state[0]["numbers"]],
            [wave_eig, sine_eig, st["base"]], [(4 + count + levels - 1, rows, length_y)], after=after,
        )
        return [st["factors"]]

    def middle(t, after):
        st = state[t]
        st["found"], st["modes"], *st["sums"] = call(
            functools.partial(middle_kernel, t, count, levels), [flags, state[0]["numbers"]],
            [wave_eig, sine, state[0]["faces"], st["field"], st["modes"], st["base"], st["factors"], st["sums"][0], *st["came"]],
            [block, block, sums_block, *gives], scratch=[((count + 2) * rows, length_y)],
            flops=(2 * count + 2) * rows * dots, after=after,
        )
        exchange(st, [])
        return [st["sums"][-1]]

    def end(t, after):
        st = state[t]
        after = [*after, *[state[u]["answers"][SHORT[0]] for u in range(t)]]
        made = call(
            functools.partial(end_kernel, count, levels), [flags, state[0]["numbers"]],
            [sine, st["found"], st["modes"], st["base"], st["factors"], st["sums"][0], *st["came"], *st["tags"]],
            [part] * GROUP, scratch=[block], flops=count * rows * dots, after=after,
        )
        st["answers"] = list(made)
        for d in SENDS[:-1]:
            st["answers"][d] = pair_up(made[d], groups, d)
        return made[:1]

    placed = []
    for step, t in (
        (start, 0), (factors, 0), (faces, 0), (middle, 0), (start, 1), (factors, 1), (end, 0), (middle, 1), (end, 1),
    ):
        placed = step(t, placed)
    return call(
        functools.partial(backward_kernel, planes, length_x * length_x * length_y * length_z),
        [flags], [wave_b] + [state[t]["answers"][d] for t in chunks for d in SENDS],
        [(2, planes, length_x, length_y), (2,)],
        scratch=[(planes, RADIX, 2 * full, length_y), (RADIX, planes, 2 * full, length_y)],
        flops=planes * RADIX * 2 * full * dots,
    )


def solution(mesh):
    placed = (P(None, ("node", "gz"), None, None), P(("node", "gz"), None), P(), P("node"))
    return jax.shard_map(
        body,
        mesh=mesh,
        in_specs=placed,
        out_specs=(P(None, ("node", "gz"), None, None), P("node")),
        check_vma=False,
    )
```

```python
import functools

import jax
import jax.numpy as jnp
import ml_dtypes
import numpy as np
from jax import lax
from jax.experimental import pallas as pl
from jax.experimental.pallas import tpu as pltpu
from jax.sharding import PartitionSpec as P

RADIX = 4
HALVES = 2
GROUP = RADIX * HALVES
CHUNKS = 2
LONG = (6, 7, 2, 3)
SHORT = (4, 5, 1, 0)
SENDS = LONG + SHORT
EARLY = (6, 2)
NEAR = (1, 0)
JOINT = (5, 1)
TAG = 8

relax = 0.6


def sine_table(length):
    indices = np.arange(1, length + 1)
    product = indices[:, None] * indices[None, :] % (2 * (length + 1))
    return np.sqrt(2.0 / (length + 1)) * np.sin(np.pi / (length + 1) * product)


def sine_eigen(length):
    indices = np.arange(1, length + 1)
    return 4.0 * np.sin(np.pi / (2 * (length + 1)) * indices) ** 2


def wave_numbers(length):
    return RADIX * np.arange(length // RADIX)[None, :] + np.arange(RADIX)[:, None]


def wave_eigen(length):
    return 4.0 * np.sin(np.pi / length * wave_numbers(length)) ** 2


def wave_tables(length):
    waves = wave_numbers(length)
    short = length // RADIX
    product = waves[:, :, None] * np.arange(short)[None, None, :] % length
    angles = 2.0 * np.pi / length * product
    cos_t, sin_t = np.cos(angles), np.sin(angles)
    pieces = HALVES * CHUNKS
    top = np.concatenate([cos_t, sin_t], axis=2).reshape(RADIX, pieces, short // pieces, 2 * short)
    low = np.concatenate([-sin_t, cos_t], axis=2).reshape(RADIX, pieces, short // pieces, 2 * short)
    return np.concatenate([top, low], axis=2).reshape(RADIX, 2 * short, 2 * short)


def two_terms(table):
    first = table.astype(ml_dtypes.bfloat16)
    return np.stack([first, (table - first.astype(np.float64)).astype(ml_dtypes.bfloat16)])


def split(value):
    first = value.astype(jnp.bfloat16)
    return first, (value - first.astype(jnp.float32)).astype(jnp.bfloat16)


def dot3(a, b):
    def one(x, y):
        return jnp.dot(x, y, preferred_element_type=jnp.float32)

    return one(a[0], b[0]) + (one(a[0], b[1]) + one(a[1], b[0]))


def cmul(a, b):
    return (a[0] * b[0] - a[1] * b[1], a[0] * b[1] + a[1] * b[0])


def csqr(a):
    cross = a[0] * a[1]
    return ((a[0] - a[1]) * (a[0] + a[1]), cross + cross)


def cpow(a, count):
    result = None
    while count:
        if count & 1:
            result = a if result is None else cmul(result, a)
        count >>= 1
        if count:
            a = csqr(a)
    return result


def cadd(a, b):
    return (a[0] + b[0], a[1] + b[1])


def csub(a, b):
    return (a[0] - b[0], a[1] - b[1])


def cscale(a, scale):
    return (a[0] * scale, a[1] * scale)


def cmore(total, factor, term):
    return cadd(total, cmul(factor, term))


def cinv(a):
    scale = 1.0 / (a[0] * a[0] + a[1] * a[1])
    return (a[0] * scale, -a[1] * scale)


def cone(a):
    return (1.0 - a[0], -a[1])


def cpick(cond, a, b):
    return (jnp.where(cond, a[0], b[0]), jnp.where(cond, a[1], b[1]))


def rows_at(start, rows):
    if isinstance(start, int):
        return pl.ds(start, rows)
    return pl.ds(pl.multiple_of(start, 8), rows)


def load(ref, base, short, row, rows):
    return (ref[rows_at(base + row, rows), :], ref[rows_at(base + short + row, rows), :])


def store(ref, base, short, row, rows, value):
    ref[rows_at(base + row, rows), :] = value[0]
    ref[rows_at(base + short + row, rows), :] = value[1]


def each_strip(count, rows, body):
    def step(i, carry):
        body(pl.multiple_of(i * rows, rows))
        return carry

    lax.fori_loop(0, count // rows, step, 0)


def squares_of(a):
    return a[0] * a[0] + a[1] * a[1]


def conduct_kernel(table_ref, ids_ref, out_ref):
    planes = ids_ref.shape[0]
    ids = ids_ref[...]
    cells = jnp.zeros(ids.shape, jnp.float32)
    for layer in range(table_ref.shape[0]):
        cells = jnp.where(ids == layer, table_ref[layer], cells)
    out_ref[...] = jnp.zeros_like(out_ref)
    out_ref[pl.ds(0, planes), :] = cells
    out_ref[pl.ds(TAG - 1, 1), :] = jnp.sum(cells, axis=0, keepdims=True)


def add_kernel(one_ref, two_ref, out_ref):
    out_ref[...] = one_ref[...] + two_ref[...]


def fill_tag(out_ref, planes, own_ref, below_ref, above_ref, *part_refs):
    start = out_ref.shape[0] - TAG
    for n, ref in enumerate((own_ref, below_ref, above_ref)):
        out_ref[pl.ds(start + n * planes, planes), :] = ref[pl.ds(0, planes), :]
    total = part_refs[0][pl.ds(TAG - 1, 1), :]
    for ref in part_refs[1:]:
        total = total + ref[pl.ds(TAG - 1, 1), :]
    out_ref[pl.ds(start + TAG - 1, 1), :] = total


def tag_of(ref):
    return ref[pl.ds(ref.shape[0] - TAG, TAG), :]


def find_numbers(cells_total, shift_ref, part_refs, numbers_ref):
    total = None
    for ref in part_refs:
        row = ref[pl.ds(ref.shape[0] - 1, 1), :]
        total = row if total is None else total + row
    inv = (1.0 / (jnp.sum(total, axis=1, keepdims=True) * (1.0 / cells_total)))[0, 0]
    numbers_ref[0] = shift_ref[0] * inv
    numbers_ref[1] = shift_ref[1] * inv
    numbers_ref[2] = relax * inv
    numbers_ref[3] = 0.5 * relax * inv
    numbers_ref[4] = shift_ref[0]
    numbers_ref[5] = shift_ref[1]


def faces_kernel(planes, blocks, flags_ref, *refs):
    part_refs, (faces_ref, padded_ref, below_ref, above_ref) = refs[:GROUP], refs[GROUP:]
    z, member = flags_ref[2], flags_ref[3]
    _, count, width = faces_ref.shape
    for d, ref in zip(SENDS, part_refs):
        tag = tag_of(ref)
        place = member ^ d
        for p in range(planes):
            padded_ref[pl.ds(8 + place * planes + p, 1), :] = tag[p : p + 1]
        below_ref[pl.ds(place, 1), :] = tag[2 * planes - 1 : 2 * planes]
        above_ref[pl.ds(place, 1), :] = tag[2 * planes : 2 * planes + 1]
    cells = padded_ref[pl.ds(8, count), :]
    padded_ref[pl.ds(7, 1), :] = jnp.where(z == 0, cells[0:1], below_ref[pl.ds(GROUP - 1, 1), :])
    padded_ref[pl.ds(8 + count, 1), :] = jnp.where(
        z == blocks - 1, cells[count - 1 : count], above_ref[pl.ds(0, 1), :]
    )
    lane = lax.broadcasted_iota(jnp.int32, cells.shape, 1)
    last, first = lane == width - 1, lane == 0
    right = 0.5 * (cells + pltpu.roll(cells, width - 1, 1))
    left = 0.5 * (cells + pltpu.roll(cells, 1, 1))
    low = 0.5 * (cells + padded_ref[pl.ds(7, count), :])
    high = 0.5 * (cells + padded_ref[pl.ds(9, count), :])
    faces_ref[0] = jnp.where(last, cells, right) + jnp.where(first, cells, left) + (low + high)
    faces_ref[1] = cells
    faces_ref[2] = jnp.where(last, 0.0, right)
    faces_ref[3] = jnp.where(first, 0.0, left)
    faces_ref[4] = low
    faces_ref[5] = high


def forward_kernel(distance, tags_count, flags_ref, source_ref, wave_ref, *refs):
    tag_refs, out_refs, stage_ref = refs[:tags_count], refs[tags_count:-1], refs[-1]
    planes = source_ref.shape[1]
    q = flags_ref[0] ^ distance
    sign = (1 - 2 * (q & 1)).astype(jnp.float32)
    turn_re = jnp.where(q == 0, 1.0, jnp.where(q == 2, -1.0, 0.0))
    turn_im = jnp.where(q == 1, 1.0, jnp.where(q == 3, -1.0, 0.0))
    rows = stage_ref.shape[1] // (HALVES * CHUNKS)
    for p in range(planes):
        parts = [[source_ref[c, p, i] for i in range(RADIX)] for c in range(2)]
        even = [parts[c][0] + sign * parts[c][2] for c in range(2)]
        odd = [parts[c][1] + sign * parts[c][3] for c in range(2)]
        mixed = jnp.concatenate(
            [
                even[0] + (turn_re * odd[0] + turn_im * odd[1]),
                even[1] + (turn_re * odd[1] - turn_im * odd[0]),
            ],
            axis=0,
        )
        stage_ref[p] = dot3((wave_ref[0, q], wave_ref[1, q]), split(mixed))
        outs = iter(out_refs)
        for n in range(HALVES):
            h = flags_ref[1] ^ n
            near = distance + RADIX * n in NEAR
            for t in range(CHUNKS):
                if t == 0 or not near:
                    ref = next(outs)
                start = ((t * planes if near else 0) + p) * rows
                ref[pl.ds(start, rows), :] = stage_ref[p, rows_at((h * CHUNKS + t) * rows, rows), :]
    for ref in out_refs if tags_count else ():
        fill_tag(ref, planes, *tag_refs)


def tag_kernel(planes, *refs):
    fill_tag(refs[-1], planes, *refs[:-1])


def answers_of():
    return [(d, t) for t in range(CHUNKS) for d in SENDS if d not in JOINT or t == CHUNKS - 1]


def backward_kernel(planes, cells, flags_ref, wave_ref, *refs):
    arrays, (out_ref, norms_ref, mixed_ref, stage_ref) = refs[:-4], refs[-4:]
    rows = (arrays[0].shape[0] - TAG) // planes
    came = {}
    for (d, t), ref in zip(answers_of(), arrays):
        for n in range(CHUNKS if d in JOINT else 1):
            came[d, n if d in JOINT else t] = ref.at[pl.ds(n * planes * rows, planes * rows)]
    short = rows * CHUNKS * HALVES // 2
    total = None
    for ref in arrays:
        tag = tag_of(ref)
        total = tag if total is None else total + tag
    for d in range(RADIX):
        q = flags_ref[0] ^ d
        for p in range(planes):
            for n in range(HALVES):
                h = flags_ref[1] ^ n
                for t in range(CHUNKS):
                    stage_ref[d, p, rows_at((h * CHUNKS + t) * rows, rows), :] = came[d + RADIX * n, t][
                        pl.ds(p * rows, rows), :
                    ]
            mixed_ref[p, q] = dot3((wave_ref[0, q], wave_ref[1, q]), split(stage_ref[d, p]))
    for p in range(planes):

        def strip(row):
            zero, one, two, three = [load(mixed_ref.at[p, q], 0, short, row, 8) for q in range(RADIX)]
            even, odd = cadd(zero, two), cadd(one, three)
            even_d, odd_d = csub(zero, two), csub(one, three)
            parts = (
                cadd(even, odd),
                (even_d[0] - odd_d[1], even_d[1] + odd_d[0]),
                csub(even, odd),
                (even_d[0] + odd_d[1], even_d[1] - odd_d[0]),
            )
            for i in range(RADIX):
                for c in range(2):
                    out_ref[c, p, rows_at(i * short + row, 8), :] = parts[i][c]

        each_strip(short, 8, strip)
    norms = jnp.sqrt(jnp.sum(total, axis=1, keepdims=True) * (1.0 / cells))
    for n in range(norms_ref.shape[0]):
        norms_ref[n] = norms[n, 0]


def decay_root(h):
    sq = (h[0] + 0.25 * (h[0] * h[0] - h[1] * h[1]), h[1] + 0.5 * h[0] * h[1])
    size = jnp.sqrt(squares_of(sq))
    root_re = jnp.sqrt(0.5 * (size + sq[0]))
    root = (root_re, 0.5 * sq[1] / root_re)
    return cinv((1.0 + 0.5 * h[0] + root[0], 0.5 * h[1] + root[1])), root


def two_powers(power, z, stacks):
    low = high = None
    bit = 0
    while (1 << bit) < stacks:
        taken = ((z >> bit) & 1) == 1
        if low is None:
            one = (jnp.ones_like(power[0]), jnp.zeros_like(power[0]))
            low, high = cpick(taken, power, one), cpick(taken, one, power)
        else:
            grown = cmul(cpick(taken, low, high), power)
            low, high = cpick(taken, grown, low), cpick(taken, high, grown)
        power = csqr(power)
        bit += 1
    return low, high


def sums_of(planes, rho, cross_f, cross_b):
    ahead = planes[0]
    for a in planes[1:]:
        ahead = cmore(a, rho, ahead)
    behind = planes[-1]
    for a in planes[-2::-1]:
        behind = cmore(a, rho, behind)
    return csub(ahead, cmul(cross_f, behind)), csub(behind, cmul(cross_b, ahead))


def sine_rows(source_ref, target_ref, sine_ref, count):
    sine = (sine_ref[0], sine_ref[1])
    rows = max(n for n in range(16, 257, 16) if count % n == 0)
    for i in range(0, count, rows):
        target_ref[pl.ds(i, rows), :] = dot3(split(source_ref[pl.ds(i, rows), :]), sine)


def fill_give(z, rows, sums_ref, give_refs):
    for ref in give_refs:
        ref[pl.ds(0, rows), :] = sums_ref[rows_at((z & 1) * rows, rows), :]
        ref[pl.ds(rows, TAG), :] = sums_ref[pl.ds(2 * rows, TAG), :]


def start_kernel(
    chunk, planes, blocks, cells_total, flags_ref, numbers_ref, wave_eig_ref, sine_eig_ref, sine_ref, *refs,
):
    part_refs, refs = refs[:GROUP], refs[GROUP:]
    if chunk == 0:
        tag_refs, refs = refs[:GROUP], refs[GROUP:]
    (field_ref, modes_ref, base_ref, sums_ref), give_refs = refs[:4], refs[4:]
    if chunk == 0:
        shift_ref, numbers_ref, give_refs = numbers_ref, give_refs[-1], give_refs[:-1]
        find_numbers(cells_total, shift_ref, tag_refs, numbers_ref)
    q, h, z, member = [flags_ref[n] for n in range(4)]
    rows = base_ref.shape[1]
    part = rows * planes
    short = rows // 2
    count = GROUP * planes
    first_row = (h * CHUNKS + chunk) * short
    for d, ref in zip(SENDS, part_refs):
        field_ref[rows_at((member ^ d) * part, part), :] = ref[pl.ds(chunk * part if d in NEAR else 0, part), :]
    sine_rows(field_ref, modes_ref, sine_ref, count * rows)
    h_re, h_im = numbers_ref[0], numbers_ref[1]
    sine_eig = sine_eig_ref[...]

    def strip(i, total):
        row = pl.multiple_of(i * 8, 8)
        eigen = wave_eig_ref[q, rows_at(first_row + row, 8), :] + sine_eig
        rho, _ = decay_root((eigen + h_re, jnp.full_like(eigen, h_im)))
        block = cpow(rho, count)
        next_one = cmul(block, rho)
        low, high = two_powers(csqr(block), z, blocks)
        cross_f, cross_b = cmul(next_one, low), cmul(next_one, high)
        for n, value in enumerate((rho, cross_f, cross_b, block, low, high)):
            store(base_ref.at[n], 0, short, row, 8, value)
        found = [load(modes_ref, l * rows, short, row, 8) for l in range(count)]
        ahead, behind = sums_of(found, rho, cross_f, cross_b)
        store(sums_ref, 0, short, row, 8, ahead)
        store(sums_ref, rows, short, row, 8, behind)
        for l in range(count):
            total = total + squares_of(load(field_ref, l * rows, short, row, 8))
        return total

    total = lax.fori_loop(0, short // 8, strip, jnp.zeros((8, field_ref.shape[1]), jnp.float32))
    sums_ref[pl.ds(2 * rows, TAG), :] = jnp.zeros((TAG, field_ref.shape[1]), jnp.float32)
    sums_ref[pl.ds(2 * rows, 1), :] = jnp.sum(total, axis=0, keepdims=True)
    fill_give(z, rows, sums_ref, give_refs)


def factors_kernel(
    chunk, count, levels, flags_ref, numbers_ref, wave_eig_ref, sine_eig_ref, base_ref, out_ref,
):
    q, h_part, z = flags_ref[0], flags_ref[1], flags_ref[2]
    short = base_ref.shape[1] // 2
    h_re, h_im, scale = numbers_ref[0], numbers_ref[1], numbers_ref[3]
    sine_eig = sine_eig_ref[...]

    def strip(row):
        eigen = wave_eig_ref[q, rows_at((h_part * CHUNKS + chunk) * short + row, 8), :] + sine_eig
        h = (eigen + h_re, jnp.full_like(eigen, h_im))
        rho, _, _, block, low, high = [load(base_ref.at[n], 0, short, row, 8) for n in range(6)]
        half_gap = csub((1.0 + 0.5 * h[0], 0.5 * h[1]), rho)
        wide = cmul(csqr(block), csqr(rho))
        low_w, high_w = cmul(low, wide), cmul(high, wide)
        whole = cscale(cinv(cmul(half_gap, cone(cmul(low, high_w)))), scale)
        turned = cmul(rho, whole)
        values = [
            cmul(cone(high_w), whole), cmul(cone(low), turned),
            cmul(cone(high), turned), cmul(cone(low_w), whole),
        ]
        pivot = (2.0 + h[0], h[1])
        inverse = cinv(pivot)
        values.append(inverse)
        for _ in range(count - 1):
            inverse = cinv(csub(pivot, inverse))
            values.append(inverse)
        near = far = None
        power = block
        for level in range(1, levels):
            taken = ((z >> (level - 1)) & 1) == 1
            if near is None:
                one = (jnp.ones_like(power[0]), jnp.zeros_like(power[0]))
                near, far = cpick(taken, power, one), cpick(taken, one, power)
            else:
                grown = cmul(cpick(taken, near, far), power)
                near, far = cpick(taken, grown, near), cpick(taken, far, grown)
            power = csqr(power)
            values.append(cpick(((z >> level) & 1) == 1, near, far))
        for n, value in enumerate(values):
            store(out_ref.at[n], 0, short, row, 8, value)

    each_strip(short, 8, strip)


def join_kernel(level, levels, flags_ref, sums_ref, came_ref, base_ref, out_ref):
    z = flags_ref[2]
    short = base_ref.shape[1] // 2
    rows = 2 * short
    above = ((z >> level) & 1) == 1
    last = level + 2 == levels
    upper = ((z >> (level + 1)) & 1) == 1

    def strip(row):
        block = load(base_ref.at[3], 0, short, row, 8)
        for _ in range(level):
            block = csqr(block)
        ahead, behind = load(sums_ref, 0, short, row, 8), load(sums_ref, rows, short, row, 8)
        ahead_c, behind_c = load(came_ref, 0, short, row, 8), load(came_ref, rows, short, row, 8)
        joined = cmore(cpick(above, ahead, ahead_c), block, cpick(above, ahead_c, ahead))
        joined_b = cmore(cpick(above, behind_c, behind), block, cpick(above, behind, behind_c))
        if last:
            store(out_ref, 0, short, row, 8, cpick(upper, joined_b, joined))
        else:
            store(out_ref, 0, short, row, 8, joined)
            store(out_ref, rows, short, row, 8, joined_b)

    each_strip(short, 8, strip)
    out_ref[pl.ds(out_ref.shape[0] - TAG, TAG), :] = (
        sums_ref[pl.ds(2 * rows, TAG), :] + came_ref[pl.ds(2 * rows, TAG), :]
    )


def solved(count, levels, z, scale, modes_ref, sums_ref, came_refs, base_ref, factors_ref, row):
    short = base_ref.shape[1] // 2
    rows = 2 * short

    def factor(n):
        return load(factors_ref.at[n], 0, short, row, 8)

    enter_f = enter_b = None
    for level in range(levels):
        above = ((z >> level) & 1) == 1
        base = 0 if level == levels - 1 else jnp.where(above, 0, rows)
        came = load(came_refs[level], base, short, row, 8)
        if level:
            came = cmul(factor(4 + count + level - 1), came)
        nought = (jnp.zeros_like(came[0]), jnp.zeros_like(came[0]))
        now_f, now_b = cpick(above, came, nought), cpick(above, nought, came)
        enter_f = now_f if enter_f is None else cadd(enter_f, now_f)
        enter_b = now_b if enter_b is None else cadd(enter_b, now_b)
    block = load(base_ref.at[3], 0, short, row, 8)
    all_f = cmore(load(sums_ref, 0, short, row, 8), block, enter_f)
    all_b = cmore(load(sums_ref, rows, short, row, 8), block, enter_b)
    below = cmore(cmul(factor(0), enter_f), factor(1), all_b)
    above = cmore(cmul(factor(3), enter_b), factor(2), all_f)
    planes = [cscale(load(modes_ref, l * rows, short, row, 8), scale) for l in range(count)]
    planes[0] = cadd(planes[0], below)
    planes[-1] = cadd(planes[-1], above)
    for l in range(1, count):
        planes[l] = cmore(planes[l], factor(4 + l - 1), planes[l - 1])
    planes[-1] = cmul(factor(4 + count - 1), planes[-1])
    for l in range(count - 2, -1, -1):
        planes[l] = cmul(factor(4 + l), cadd(planes[l], planes[l + 1]))
    return below, planes, above


def middle_kernel(
    chunk, count, levels, flags_ref, numbers_ref, wave_eig_ref, sine_ref, faces_ref, field_ref,
    modes_ref, base_ref, factors_ref, sums_ref, *refs,
):
    came_refs, (found_ref, next_ref, next_sums_ref) = refs[:levels], refs[levels : levels + 3]
    give_refs, work_ref = refs[levels + 3 : -1], refs[-1]
    q, h, z = flags_ref[0], flags_ref[1], flags_ref[2]
    scale, s_re, s_im = numbers_ref[2], numbers_ref[4], numbers_ref[5]
    short = base_ref.shape[1] // 2
    rows = 2 * short
    width = base_ref.shape[2]

    def solve(row):
        below, planes, above = solved(
            count, levels, z, scale, modes_ref, sums_ref, came_refs, base_ref, factors_ref, row
        )
        store(work_ref, 0, short, row, 8, below)
        store(work_ref, (count + 1) * rows, short, row, 8, above)
        for l in range(count):
            store(work_ref, (l + 1) * rows, short, row, 8, planes[l])
            store(found_ref, l * rows, short, row, 8, planes[l])

    each_strip(short, 8, solve)
    sine_rows(work_ref, work_ref, sine_ref, (count + 2) * rows)

    def residual(i, total):
        row = pl.multiple_of(i * 8, 8)
        eigen = wave_eig_ref[q, rows_at((h * CHUNKS + chunk) * short + row, 8), :]
        under = load(work_ref, 0, short, row, 8)
        here = load(work_ref, rows, short, row, 8)
        for l in range(count):
            over = load(work_ref, (l + 2) * rows, short, row, 8)
            diag, cell, right, left, low, high = [faces_ref[n, pl.ds(l, 1), :] for n in range(6)]
            diag = s_re + (diag + cell * eigen)
            value = []
            for c in range(2):
                v = diag * here[c] - right * pltpu.roll(here[c], width - 1, 1)
                v = v - left * pltpu.roll(here[c], 1, 1)
                value.append(v - (low * under[c] + high * over[c]))
            value = (value[0] - s_im * here[1], value[1] + s_im * here[0])
            value = csub(load(field_ref, l * rows, short, row, 8), value)
            total = total + squares_of(value)
            store(work_ref, l * rows, short, row, 8, value)
            under, here = here, over
        return total

    total = lax.fori_loop(0, short // 8, residual, jnp.zeros((8, width), jnp.float32))
    sine_rows(work_ref, next_ref, sine_ref, count * rows)

    def sums(row):
        rho, cross_f, cross_b = [load(base_ref.at[n], 0, short, row, 8) for n in range(3)]
        planes = [load(next_ref, l * rows, short, row, 8) for l in range(count)]
        ahead, behind = sums_of(planes, rho, cross_f, cross_b)
        store(next_sums_ref, 0, short, row, 8, ahead)
        store(next_sums_ref, rows, short, row, 8, behind)

    each_strip(short, 8, sums)
    next_sums_ref[pl.ds(2 * rows, TAG), :] = sums_ref[pl.ds(2 * rows, TAG), :]
    next_sums_ref[pl.ds(2 * rows + 1, 1), :] = jnp.sum(total, axis=0, keepdims=True)
    fill_give(z, rows, next_sums_ref, give_refs)


def end_kernel(
    count, levels, flags_ref, numbers_ref, sine_ref, found_ref, modes_ref, base_ref,
    factors_ref, sums_ref, *refs,
):
    came_refs, out_refs, work_ref = refs[:levels], refs[-1 - GROUP : -1], refs[-1]
    before_refs = refs[levels + (levels > 1) : -1 - GROUP]
    z, member = flags_ref[2], flags_ref[3]
    scale = numbers_ref[2]
    short = base_ref.shape[1] // 2
    rows = 2 * short

    def solve(row):
        _, planes, _ = solved(
            count, levels, z, scale, modes_ref, sums_ref, came_refs, base_ref, factors_ref, row
        )
        for l in range(count):
            before = load(found_ref, l * rows, short, row, 8)
            store(work_ref, l * rows, short, row, 8, cadd(before, planes[l]))

    each_strip(short, 8, solve)
    sine_rows(work_ref, work_ref, sine_ref, count * rows)
    part = count // GROUP * rows
    tag_refs = (refs[levels] if levels > 1 else sums_ref, came_refs[-1])
    tag = None
    for ref in tag_refs:
        part_tag = ref[pl.ds(ref.shape[0] - TAG, TAG), :]
        tag = part_tag if tag is None else tag + part_tag
    for d in range(GROUP):
        start, whole = 0, tag
        if d in JOINT:
            held = len(before_refs) // len(JOINT)
            for ref in before_refs[JOINT.index(d) * held : (JOINT.index(d) + 1) * held]:
                out_refs[d][pl.ds(start, part), :] = ref[pl.ds(0, part), :]
                start, whole = start + part, whole + tag_of(ref)
        out_refs[d][pl.ds(start, part), :] = work_ref[rows_at((member ^ d) * part, part), :]
        out_refs[d][pl.ds(start + part, TAG), :] = whole


smem = pl.BlockSpec(memory_space=pltpu.SMEM)
vmem = pl.BlockSpec(memory_space=pltpu.VMEM)
unread = pl.BlockSpec(memory_space=pl.ANY)


def call(kernel, scalars, arrays, outs, scratch=(), flops=0, after=()):
    out_shape = [jax.ShapeDtypeStruct(shape, jnp.float32) for shape in outs]
    head = len(scalars) + len(arrays)

    def run(*refs):
        kernel(*refs[:head], *refs[head + len(after) :])

    moved = sum(a.size * a.dtype.itemsize for a in arrays) + sum(4 * int(np.prod(s)) for s in outs)
    held = moved + sum(4 * int(np.prod(s)) for s in scratch)
    return pl.pallas_call(
        run,
        out_shape=out_shape,
        in_specs=[smem] * len(scalars) + [vmem] * len(arrays) + [unread] * len(after),
        out_specs=[smem if len(shape) == 1 else vmem for shape in outs],
        scratch_shapes=[pltpu.VMEM(shape, jnp.float32) for shape in scratch],
        compiler_params=pltpu.CompilerParams(vmem_limit_bytes=held + 4 * 2**20),
        cost_estimate=pl.CostEstimate(flops=flops, bytes_accessed=moved, transcendentals=0),
    )(*scalars, *arrays, *after)


def pair_up(array, groups, flip):
    return lax.ppermute(array, "gz", [(i, i ^ flip) for i in range(groups)])


def step_by(array, groups, distance):
    return lax.ppermute(
        array, "gz", [(i, i + distance) for i in range(groups) if 0 <= i + distance < groups]
    )


def body(source, layer_ids, conduct_table, shift):
    planes, length_x, length_y = source.shape[1:]
    groups = lax.axis_size("gz")
    blocks = groups // GROUP
    levels = blocks.bit_length() - 1
    count = GROUP * planes
    length_z = planes * groups
    full = length_x // RADIX
    short = full // (HALVES * CHUNKS)
    rows = 2 * short
    if blocks < 2 or groups != GROUP << levels or planes > 2 or short % 8 or length_x != RADIX * full:
        raise ValueError("unsupported layout")
    me = lax.axis_index("gz")
    member = me % GROUP
    flags = jnp.stack([member % RADIX, member // RADIX, me // GROUP, member]).astype(jnp.int32)

    wave = wave_tables(length_x)
    wave_f = jnp.asarray(two_terms(wave))
    wave_b = jnp.asarray(two_terms(np.ascontiguousarray(np.swapaxes(wave, 1, 2)) / length_x))
    sine = jnp.asarray(two_terms(sine_table(length_y)))
    wave_eig = np.broadcast_to(wave_eigen(length_x)[:, :, None], (RADIX, full, length_y))
    wave_eig = jnp.asarray(np.ascontiguousarray(wave_eig).astype(np.float32))
    sine_eig = jnp.asarray(np.tile(sine_eigen(length_y)[None, :], (8, 1)).astype(np.float32))

    chunks = range(CHUNKS)
    row_block = (TAG, length_y)
    block = (count * rows, length_y)
    sums_block = (2 * rows + TAG, length_y)
    single = (rows + TAG, length_y)
    part = (planes * rows + TAG, length_y)
    parts = (CHUNKS * planes * rows + TAG, length_y)
    gives = [single] if levels == 1 else []
    dots = 6 * length_y * length_y

    parted = source.reshape(2, planes, RADIX, full, length_y)
    spectra = {}

    def transform(d, tags, after):
        ways = [(d + RADIX * n, t) for n in range(HALVES) for t in (chunks if d + RADIX * n not in NEAR else (0,))]
        shapes = [parts if way[0] in NEAR else part for way in ways]
        made = call(
            functools.partial(forward_kernel, d, len(tags)), [flags], [parted, wave_f, *tags], shapes,
            scratch=[(planes, 2 * full, length_y)], flops=planes * 2 * full * dots, after=after,
        )
        spectra.update(zip(ways, made))
        return made[:1]

    placed = transform(EARLY[-1], [], [])

    (cells,) = call(conduct_kernel, [conduct_table], [layer_ids], [row_block], after=placed)
    if levels == 1:
        below = above = pair_up(cells, groups, GROUP)
        totals = [cells, below]
    else:
        below = step_by(cells, groups, GROUP)
        above = step_by(cells, groups, -GROUP)
        total = cells
        for level in range(levels):
            (total,) = call(add_kernel, [], [total, pair_up(total, groups, GROUP << level)], [row_block])
        totals = [total]
    tags = [cells, below, above, *totals]
    (own_tag,) = placed = call(functools.partial(tag_kernel, planes), [], tags, [row_block], after=placed)
    for d in (0, 1, 3):
        placed = transform(d, tags, placed)
    tags = {d: pair_up(own_tag, groups, d) for d in EARLY}
    for d in SENDS[:-1]:
        spectra[d, 0] = pair_up(spectra[d, 0], groups, d)
    for t in chunks[1:]:
        for d in NEAR:
            spectra[d, t] = spectra[d, 0]
        for d in LONG:
            spectra[d, t] = pair_up(spectra[d, t], groups, d)
    tags = [tags.get(d, spectra[d, 0]) for d in SENDS]

    state = [{} for _ in chunks]

    def exchange(st, after):
        sums, give = st["sums"][0], st["sums"][-1]
        st["came"], st["tags"] = [], []
        for level in range(levels):
            st["came"].append(pair_up(give, groups, GROUP << level))
            if level + 1 < levels:
                shape = single if level + 2 == levels else sums_block
                (give,) = call(
                    functools.partial(join_kernel, level, levels), [flags], [sums, st["came"][-1], st["base"]],
                    [shape], after=after,
                )
                sums = give
                st["tags"] = [give[-TAG:]]

    def start(t, after):
        st = state[t]
        for d in SHORT[:2] if t else ():
            held, _ = lax.optimization_barrier((spectra[d, t], after[0]))
            spectra[d, t] = pair_up(held, groups, d)
        outs = [block, block, (6, rows, length_y), sums_block, *gives]
        made = call(
            functools.partial(start_kernel, t, planes, blocks, length_y * length_z),
            [flags, state[0]["numbers"] if t else shift],
            [wave_eig, sine_eig, sine] + [spectra[d, t] for d in SENDS] + ([] if t else tags),
            outs if t else [*outs, (6,)], flops=count * rows * dots, after=after,
        )
        if not t:
            *made, st["numbers"] = made
        st["field"], st["modes"], st["base"], *st["sums"] = made
        exchange(st, [])
        return [st["sums"][-1]]

    def faces(t, after):
        state[t]["faces"] = call(
            functools.partial(faces_kernel, planes, blocks), [flags], tags,
            [(6, count, length_y)], scratch=[(count + 16, length_y), row_block, row_block], after=after,
        )[0]
        return [state[t]["faces"]]

    def factors(t, after):
        st = state[t]
        (st["factors"],) = call(
            functools.partial(factors_kernel, t, count, levels), [flags, state[0]["numbers"]],
            [wave_eig, sine_eig, st["base"]], [(4 + count + levels - 1, rows, length_y)], after=after,
        )
        return [st["factors"]]

    def middle(t, after):
        st = state[t]
        st["found"], st["modes"], *st["sums"] = call(
            functools.partial(middle_kernel, t, count, levels), [flags, state[0]["numbers"]],
            [wave_eig, sine, state[0]["faces"], st["field"], st["modes"], st["base"], st["factors"], st["sums"][0], *st["came"]],
            [block, block, sums_block, *gives], scratch=[((count + 2) * rows, length_y)],
            flops=(2 * count + 2) * rows * dots, after=after,
        )
        exchange(st, [])
        return [st["sums"][-1]]

    def end(t, after):
        st = state[t]
        last = t == CHUNKS - 1
        before = [state[u]["made"][d] for d in JOINT for u in range(t)] if last else []
        st["made"] = call(
            functools.partial(end_kernel, count, levels), [flags, state[0]["numbers"]],
            [sine, st["found"], st["modes"], st["base"], st["factors"], st["sums"][0], *st["came"], *st["tags"], *before],
            [parts if last and d in JOINT else part for d in range(GROUP)],
            scratch=[block], flops=count * rows * dots, after=after,
        )
        st["answers"] = {
            d: pair_up(st["made"][d], groups, d) for d in SENDS[:-1] if last or d not in JOINT
        }
        st["answers"][0] = st["made"][0]
        return [st["made"][0]]

    placed = []
    for step, t in (
        (start, 0), (factors, 0), (faces, 0), (middle, 0), (start, 1), (factors, 1), (end, 0), (middle, 1), (end, 1),
    ):
        placed = step(t, placed)
    return call(
        functools.partial(backward_kernel, planes, length_x * length_x * length_y * length_z),
        [flags], [wave_b] + [state[t]["answers"][d] for d, t in answers_of()],
        [(2, planes, length_x, length_y), (2,)],
        scratch=[(planes, RADIX, 2 * full, length_y), (RADIX, planes, 2 * full, length_y)],
        flops=planes * RADIX * 2 * full * dots,
    )


def solution(mesh):
    placed = (P(None, ("node", "gz"), None, None), P(("node", "gz"), None), P(), P("node"))
    return jax.shard_map(
        body,
        mesh=mesh,
        in_specs=placed,
        out_specs=(P(None, ("node", "gz"), None, None), P("node")),
        check_vma=False,
    )
```

```python
import functools

import jax
import jax.numpy as jnp
import ml_dtypes
import numpy as np
from jax import lax
from jax.experimental import pallas as pl
from jax.experimental.pallas import tpu as pltpu
from jax.sharding import PartitionSpec as P

RADIX = 4
HALVES = 2
GROUP = RADIX * HALVES
CHUNKS = 2
CORES = 2
CHIPS = GROUP // CORES
TAG = 8

relax = 0.6


def sine_table(length):
    indices = np.arange(1, length + 1)
    product = indices[:, None] * indices[None, :] % (2 * (length + 1))
    return np.sqrt(2.0 / (length + 1)) * np.sin(np.pi / (length + 1) * product)


def sine_eigen(length):
    indices = np.arange(1, length + 1)
    return 4.0 * np.sin(np.pi / (2 * (length + 1)) * indices) ** 2


def wave_numbers(length):
    return RADIX * np.arange(length // RADIX)[None, :] + np.arange(RADIX)[:, None]


def wave_eigen(length):
    return 4.0 * np.sin(np.pi / length * wave_numbers(length)) ** 2


def wave_tables(length):
    waves = wave_numbers(length)
    short = length // RADIX
    product = waves[:, :, None] * np.arange(short)[None, None, :] % length
    angles = 2.0 * np.pi / length * product
    cos_t, sin_t = np.cos(angles), np.sin(angles)
    pieces = HALVES * CHUNKS
    top = np.concatenate([cos_t, sin_t], axis=2).reshape(RADIX, pieces, short // pieces, 2 * short)
    low = np.concatenate([-sin_t, cos_t], axis=2).reshape(RADIX, pieces, short // pieces, 2 * short)
    return np.concatenate([top, low], axis=2).reshape(RADIX, 2 * short, 2 * short)


def two_terms(table):
    first = table.astype(ml_dtypes.bfloat16)
    return np.stack([first, (table - first.astype(np.float64)).astype(ml_dtypes.bfloat16)])


def split(value):
    first = value.astype(jnp.bfloat16)
    return first, (value - first.astype(jnp.float32)).astype(jnp.bfloat16)


def dot3(a, b):
    def one(x, y):
        return jnp.dot(x, y, preferred_element_type=jnp.float32)

    return one(a[0], b[0]) + (one(a[0], b[1]) + one(a[1], b[0]))


def cmul(a, b):
    return (a[0] * b[0] - a[1] * b[1], a[0] * b[1] + a[1] * b[0])


def csqr(a):
    cross = a[0] * a[1]
    return ((a[0] - a[1]) * (a[0] + a[1]), cross + cross)


def cpow(a, count):
    result = None
    while count:
        if count & 1:
            result = a if result is None else cmul(result, a)
        count >>= 1
        if count:
            a = csqr(a)
    return result


def cadd(a, b):
    return (a[0] + b[0], a[1] + b[1])


def csub(a, b):
    return (a[0] - b[0], a[1] - b[1])


def cscale(a, scale):
    return (a[0] * scale, a[1] * scale)


def cmore(total, factor, term):
    return cadd(total, cmul(factor, term))


def cinv(a):
    scale = 1.0 / (a[0] * a[0] + a[1] * a[1])
    return (a[0] * scale, -a[1] * scale)


def cone(a):
    return (1.0 - a[0], -a[1])


def cpick(cond, a, b):
    return (jnp.where(cond, a[0], b[0]), jnp.where(cond, a[1], b[1]))


def rows_at(start, rows):
    if isinstance(start, int):
        return pl.ds(start, rows)
    return pl.ds(pl.multiple_of(start, 8), rows)


def load(ref, base, short, row, rows):
    return (ref[rows_at(base + row, rows), :], ref[rows_at(base + short + row, rows), :])


def store(ref, base, short, row, rows, value):
    ref[rows_at(base + row, rows), :] = value[0]
    ref[rows_at(base + short + row, rows), :] = value[1]


def each_strip(count, rows, body):
    def step(i, carry):
        body(pl.multiple_of(i * rows, rows))
        return carry

    lax.fori_loop(0, count // rows, step, 0)


def squares_of(a):
    return a[0] * a[0] + a[1] * a[1]


def conduct_of(table_ref, ids_ref, out_ref):
    planes = ids_ref.shape[0]
    ids = ids_ref[...]
    cells = jnp.zeros(ids.shape, jnp.float32)
    for layer in range(table_ref.shape[0]):
        cells = jnp.where(ids == layer, table_ref[layer], cells)
    out_ref[...] = jnp.zeros_like(out_ref)
    out_ref[pl.ds(0, planes), :] = cells
    out_ref[pl.ds(TAG - 1, 1), :] = jnp.sum(cells, axis=0, keepdims=True)


def add_kernel(one_ref, two_ref, out_ref):
    out_ref[...] = one_ref[...] + two_ref[...]


def tag_of(ref):
    return ref[pl.ds(ref.shape[0] - TAG, TAG), :]


def member_tags(part_refs, swapped_ref):
    start = swapped_ref.shape[0] - CHIPS * TAG
    tags = {}
    for e, ref in enumerate(part_refs):
        tags[CORES * e] = tag_of(ref)
        tags[CORES * e + 1] = swapped_ref[pl.ds(start + e * TAG, TAG), :]
    return tags


def find_numbers(cells_total, shift_ref, tags, out_ref):
    total = None
    for tag in tags:
        row = tag[TAG - 1 :]
        total = row if total is None else total + row
    inv = (1.0 / (jnp.sum(total, axis=1, keepdims=True) * (1.0 / cells_total)))[0, 0]
    out_ref[0] = shift_ref[0] * inv
    out_ref[1] = shift_ref[1] * inv
    out_ref[2] = relax * inv
    out_ref[3] = 0.5 * relax * inv
    out_ref[4] = shift_ref[0]
    out_ref[5] = shift_ref[1]


def place_cells(planes, member, tags, cells_ref, start):
    for d, tag in tags.items():
        for p in range(planes):
            cells_ref[pl.ds(start + (member ^ d) * planes + p, 1), :] = tag[p : p + 1]


def summary_kernel(planes, flags_ref, *refs):
    part_refs, swapped_ref, out_ref, cells_ref = refs[:CHIPS], refs[CHIPS], refs[-2], refs[-1]
    place_cells(planes, flags_ref[3], member_tags(part_refs, swapped_ref), cells_ref, 0)
    out_ref[...] = jnp.zeros_like(out_ref)
    out_ref[pl.ds(0, 1), :] = cells_ref[pl.ds(0, 1), :]
    out_ref[pl.ds(1, 1), :] = cells_ref[pl.ds(GROUP * planes - 1, 1), :]
    out_ref[pl.ds(TAG - 1, 1), :] = jnp.sum(cells_ref[...], axis=0, keepdims=True)


def faces_kernel(planes, blocks, flags_ref, *refs):
    part_refs, swapped_ref, extra_refs = refs[:CHIPS], refs[CHIPS], refs[CHIPS + 1 : -3]
    faces_ref, padded_ref, other_ref = refs[-3:]
    z, member = flags_ref[2], flags_ref[3]
    _, count, width = faces_ref.shape
    place_cells(planes, member, member_tags(part_refs, swapped_ref), padded_ref, 8)
    if blocks == 2:
        for core, ref in enumerate(extra_refs):
            tags = {CORES * e + core: ref[pl.ds(e * TAG, TAG), :] for e in range(CHIPS)}
            place_cells(planes, member, tags, other_ref, 0)
        below, above = other_ref[pl.ds(count - 1, 1), :], other_ref[pl.ds(0, 1), :]
    else:
        below, above = extra_refs[1][pl.ds(1, 1), :], extra_refs[2][pl.ds(0, 1), :]
    cells = padded_ref[pl.ds(8, count), :]
    padded_ref[pl.ds(7, 1), :] = jnp.where(z == 0, cells[0:1], below)
    padded_ref[pl.ds(8 + count, 1), :] = jnp.where(z == blocks - 1, cells[count - 1 : count], above)
    lane = lax.broadcasted_iota(jnp.int32, cells.shape, 1)
    last, first = lane == width - 1, lane == 0
    right = 0.5 * (cells + pltpu.roll(cells, width - 1, 1))
    left = 0.5 * (cells + pltpu.roll(cells, 1, 1))
    low = 0.5 * (cells + padded_ref[pl.ds(7, count), :])
    high = 0.5 * (cells + padded_ref[pl.ds(9, count), :])
    faces_ref[0] = jnp.where(last, cells, right) + jnp.where(first, cells, left) + (low + high)
    faces_ref[1] = cells
    faces_ref[2] = jnp.where(last, 0.0, right)
    faces_ref[3] = jnp.where(first, 0.0, left)
    faces_ref[4] = low
    faces_ref[5] = high


def forward_kernel(pair, flags_ref, table_ref, source_ref, wave_ref, ids_ref, *refs):
    out_refs, cells_ref, stage_ref = refs[:-2], refs[-2], refs[-1]
    planes = source_ref.shape[1]
    rows = stage_ref.shape[2] // (HALVES * CHUNKS)
    conduct_of(table_ref, ids_ref, cells_ref)
    for core, distance in enumerate(pair):
        q = flags_ref[0] ^ distance
        sign = (1 - 2 * (q & 1)).astype(jnp.float32)
        turn_re = jnp.where(q == 0, 1.0, jnp.where(q == 2, -1.0, 0.0))
        turn_im = jnp.where(q == 1, 1.0, jnp.where(q == 3, -1.0, 0.0))
        for p in range(planes):
            parts = [[source_ref[c, p, i] for i in range(RADIX)] for c in range(2)]
            even = [parts[c][0] + sign * parts[c][2] for c in range(2)]
            odd = [parts[c][1] + sign * parts[c][3] for c in range(2)]
            mixed = jnp.concatenate(
                [
                    even[0] + (turn_re * odd[0] + turn_im * odd[1]),
                    even[1] + (turn_re * odd[1] - turn_im * odd[0]),
                ],
                axis=0,
            )
            stage_ref[core, p] = dot3((wave_ref[0, q], wave_ref[1, q]), split(mixed))
            for n in range(HALVES):
                h = flags_ref[1] ^ n
                for t in range(CHUNKS):
                    out_refs[n * CHUNKS + t][pl.ds((core * planes + p) * rows, rows), :] = stage_ref[
                        core, p, rows_at((h * CHUNKS + t) * rows, rows), :
                    ]
    for ref in out_refs:
        ref[pl.ds(ref.shape[0] - TAG, TAG), :] = cells_ref[...]


def give_kernel(*refs):
    part_refs, out_ref, tags_ref = refs[:CHIPS], refs[CHIPS], refs[CHIPS + 1]
    part = (part_refs[0].shape[0] - TAG) // CORES
    for e, ref in enumerate(part_refs):
        out_ref[pl.ds(e * part, part), :] = ref[pl.ds(part, part), :]
        tags_ref[pl.ds(e * TAG, TAG), :] = tag_of(ref)
    out_ref[pl.ds(CHIPS * part, CHIPS * TAG), :] = tags_ref[...]


def merge_kernel(keep_ref, swapped_ref, *out_refs):
    part = (keep_ref.shape[0] - TAG) // CHIPS
    for e, ref in enumerate(out_refs):
        ref[pl.ds(0, part), :] = keep_ref[pl.ds(e * part, part), :]
        ref[pl.ds(part, part), :] = swapped_ref[pl.ds(e * part, part), :]
        ref[pl.ds(CORES * part, TAG), :] = tag_of(keep_ref) + tag_of(swapped_ref)


def backward_kernel(planes, cells, flags_ref, wave_ref, *refs):
    arrays, (out_ref, norms_ref, mixed_ref, stage_ref) = refs[:-4], refs[-4:]
    part = (arrays[0].shape[0] - TAG) // CORES
    rows = part // planes
    short = rows * CHUNKS * HALVES // 2
    total = None
    for ref in arrays:
        tag = tag_of(ref)
        total = tag if total is None else total + tag
    for d in range(RADIX):
        q = flags_ref[0] ^ d
        for p in range(planes):
            for n in range(HALVES):
                h = flags_ref[1] ^ n
                for t in range(CHUNKS):
                    ref = arrays[t * CHIPS + (d + RADIX * n) // CORES]
                    stage_ref[d, p, rows_at((h * CHUNKS + t) * rows, rows), :] = ref[
                        pl.ds(d % CORES * part + p * rows, rows), :
                    ]
            mixed_ref[p, q] = dot3((wave_ref[0, q], wave_ref[1, q]), split(stage_ref[d, p]))
    for p in range(planes):

        def strip(row):
            zero, one, two, three = [load(mixed_ref.at[p, q], 0, short, row, 8) for q in range(RADIX)]
            even, odd = cadd(zero, two), cadd(one, three)
            even_d, odd_d = csub(zero, two), csub(one, three)
            parts = (
                cadd(even, odd),
                (even_d[0] - odd_d[1], even_d[1] + odd_d[0]),
                csub(even, odd),
                (even_d[0] + odd_d[1], even_d[1] - odd_d[0]),
            )
            for i in range(RADIX):
                for c in range(2):
                    out_ref[c, p, rows_at(i * short + row, 8), :] = parts[i][c]

        each_strip(short, 8, strip)
    norms = jnp.sqrt(jnp.sum(total, axis=1, keepdims=True) * (1.0 / cells))
    for n in range(norms_ref.shape[0]):
        norms_ref[n] = norms[n, 0]


def decay_root(h):
    sq = (h[0] + 0.25 * (h[0] * h[0] - h[1] * h[1]), h[1] + 0.5 * h[0] * h[1])
    size = jnp.sqrt(squares_of(sq))
    root_re = jnp.sqrt(0.5 * (size + sq[0]))
    root = (root_re, 0.5 * sq[1] / root_re)
    return cinv((1.0 + 0.5 * h[0] + root[0], 0.5 * h[1] + root[1])), root


def two_powers(power, z, stacks):
    low = high = None
    bit = 0
    while (1 << bit) < stacks:
        taken = ((z >> bit) & 1) == 1
        if low is None:
            one = (jnp.ones_like(power[0]), jnp.zeros_like(power[0]))
            low, high = cpick(taken, power, one), cpick(taken, one, power)
        else:
            grown = cmul(cpick(taken, low, high), power)
            low, high = cpick(taken, grown, low), cpick(taken, high, grown)
        power = csqr(power)
        bit += 1
    return low, high


def sums_of(planes, rho, cross_f, cross_b):
    ahead = planes[0]
    for a in planes[1:]:
        ahead = cmore(a, rho, ahead)
    behind = planes[-1]
    for a in planes[-2::-1]:
        behind = cmore(a, rho, behind)
    return csub(ahead, cmul(cross_f, behind)), csub(behind, cmul(cross_b, ahead))


def sine_rows(source_ref, target_ref, sine_ref, count):
    sine = (sine_ref[0], sine_ref[1])
    rows = max(n for n in range(16, 257, 16) if count % n == 0)
    for i in range(0, count, rows):
        target_ref[pl.ds(i, rows), :] = dot3(split(source_ref[pl.ds(i, rows), :]), sine)


def fill_give(z, rows, sums_ref, give_refs):
    for ref in give_refs:
        ref[pl.ds(0, rows), :] = sums_ref[rows_at((z & 1) * rows, rows), :]
        ref[pl.ds(rows, TAG), :] = sums_ref[pl.ds(2 * rows, TAG), :]


def start_kernel(
    chunk, planes, blocks, cells_total, flags_ref, numbers_ref, wave_eig_ref, sine_eig_ref, sine_ref, *refs,
):
    part_refs, swapped_ref, refs = refs[:CHIPS], refs[CHIPS], refs[CHIPS + 1 :]
    if chunk == 0:
        extra_count = 2 if blocks == 2 else 3
        extra_refs, refs = refs[:extra_count], refs[extra_count:]
    (field_ref, modes_ref, base_ref, sums_ref), give_refs = refs[:4], refs[4:]
    if chunk == 0:
        shift_ref, numbers_ref, give_refs = numbers_ref, give_refs[-1], give_refs[:-1]
        if blocks == 2:
            tags = list(member_tags(part_refs, swapped_ref).values())
            tags += [ref[pl.ds(e * TAG, TAG), :] for ref in extra_refs for e in range(CHIPS)]
        else:
            tags = [extra_refs[0][...]]
        find_numbers(cells_total, shift_ref, tags, numbers_ref)
    q, h, z, member = [flags_ref[n] for n in range(4)]
    rows = base_ref.shape[1]
    part = rows * planes
    short = rows // 2
    count = GROUP * planes
    first_row = (h * CHUNKS + chunk) * short
    for e, ref in enumerate(part_refs):
        field_ref[rows_at((member ^ CORES * e) * part, part), :] = ref[pl.ds(0, part), :]
        field_ref[rows_at((member ^ (CORES * e + 1)) * part, part), :] = swapped_ref[pl.ds(e * part, part), :]
    sine_rows(field_ref, modes_ref, sine_ref, count * rows)
    h_re, h_im = numbers_ref[0], numbers_ref[1]
    sine_eig = sine_eig_ref[...]

    def strip(i, total):
        row = pl.multiple_of(i * 8, 8)
        eigen = wave_eig_ref[q, rows_at(first_row + row, 8), :] + sine_eig
        rho, _ = decay_root((eigen + h_re, jnp.full_like(eigen, h_im)))
        block = cpow(rho, count)
        next_one = cmul(block, rho)
        low, high = two_powers(csqr(block), z, blocks)
        cross_f, cross_b = cmul(next_one, low), cmul(next_one, high)
        for n, value in enumerate((rho, cross_f, cross_b, block, low, high)):
            store(base_ref.at[n], 0, short, row, 8, value)
        found = [load(modes_ref, l * rows, short, row, 8) for l in range(count)]
        ahead, behind = sums_of(found, rho, cross_f, cross_b)
        store(sums_ref, 0, short, row, 8, ahead)
        store(sums_ref, rows, short, row, 8, behind)
        for l in range(count):
            total = total + squares_of(load(field_ref, l * rows, short, row, 8))
        return total

    total = lax.fori_loop(0, short // 8, strip, jnp.zeros((8, field_ref.shape[1]), jnp.float32))
    sums_ref[pl.ds(2 * rows, TAG), :] = jnp.zeros((TAG, field_ref.shape[1]), jnp.float32)
    sums_ref[pl.ds(2 * rows, 1), :] = jnp.sum(total, axis=0, keepdims=True)
    fill_give(z, rows, sums_ref, give_refs)


def factors_kernel(
    chunk, count, levels, flags_ref, numbers_ref, wave_eig_ref, sine_eig_ref, base_ref, out_ref,
):
    q, h_part, z = flags_ref[0], flags_ref[1], flags_ref[2]
    short = base_ref.shape[1] // 2
    h_re, h_im, scale = numbers_ref[0], numbers_ref[1], numbers_ref[3]
    sine_eig = sine_eig_ref[...]

    def strip(row):
        eigen = wave_eig_ref[q, rows_at((h_part * CHUNKS + chunk) * short + row, 8), :] + sine_eig
        h = (eigen + h_re, jnp.full_like(eigen, h_im))
        rho, _, _, block, low, high = [load(base_ref.at[n], 0, short, row, 8) for n in range(6)]
        half_gap = csub((1.0 + 0.5 * h[0], 0.5 * h[1]), rho)
        wide = cmul(csqr(block), csqr(rho))
        low_w, high_w = cmul(low, wide), cmul(high, wide)
        whole = cscale(cinv(cmul(half_gap, cone(cmul(low, high_w)))), scale)
        turned = cmul(rho, whole)
        values = [
            cmul(cone(high_w), whole), cmul(cone(low), turned),
            cmul(cone(high), turned), cmul(cone(low_w), whole),
        ]
        pivot = (2.0 + h[0], h[1])
        inverse = cinv(pivot)
        values.append(inverse)
        for _ in range(count - 1):
            inverse = cinv(csub(pivot, inverse))
            values.append(inverse)
        near = far = None
        power = block
        for level in range(1, levels):
            taken = ((z >> (level - 1)) & 1) == 1
            if near is None:
                one = (jnp.ones_like(power[0]), jnp.zeros_like(power[0]))
                near, far = cpick(taken, power, one), cpick(taken, one, power)
            else:
                grown = cmul(cpick(taken, near, far), power)
                near, far = cpick(taken, grown, near), cpick(taken, far, grown)
            power = csqr(power)
            values.append(cpick(((z >> level) & 1) == 1, near, far))
        for n, value in enumerate(values):
            store(out_ref.at[n], 0, short, row, 8, value)

    each_strip(short, 8, strip)


def join_kernel(level, levels, flags_ref, sums_ref, came_ref, base_ref, out_ref):
    z = flags_ref[2]
    short = base_ref.shape[1] // 2
    rows = 2 * short
    above = ((z >> level) & 1) == 1
    last = level + 2 == levels
    upper = ((z >> (level + 1)) & 1) == 1

    def strip(row):
        block = load(base_ref.at[3], 0, short, row, 8)
        for _ in range(level):
            block = csqr(block)
        ahead, behind = load(sums_ref, 0, short, row, 8), load(sums_ref, rows, short, row, 8)
        ahead_c, behind_c = load(came_ref, 0, short, row, 8), load(came_ref, rows, short, row, 8)
        joined = cmore(cpick(above, ahead, ahead_c), block, cpick(above, ahead_c, ahead))
        joined_b = cmore(cpick(above, behind_c, behind), block, cpick(above, behind, behind_c))
        if last:
            store(out_ref, 0, short, row, 8, cpick(upper, joined_b, joined))
        else:
            store(out_ref, 0, short, row, 8, joined)
            store(out_ref, rows, short, row, 8, joined_b)

    each_strip(short, 8, strip)
    out_ref[pl.ds(out_ref.shape[0] - TAG, TAG), :] = (
        sums_ref[pl.ds(2 * rows, TAG), :] + came_ref[pl.ds(2 * rows, TAG), :]
    )


def solved(count, levels, z, scale, modes_ref, sums_ref, came_refs, base_ref, factors_ref, row):
    short = base_ref.shape[1] // 2
    rows = 2 * short

    def factor(n):
        return load(factors_ref.at[n], 0, short, row, 8)

    enter_f = enter_b = None
    for level in range(levels):
        above = ((z >> level) & 1) == 1
        base = 0 if level == levels - 1 else jnp.where(above, 0, rows)
        came = load(came_refs[level], base, short, row, 8)
        if level:
            came = cmul(factor(4 + count + level - 1), came)
        nought = (jnp.zeros_like(came[0]), jnp.zeros_like(came[0]))
        now_f, now_b = cpick(above, came, nought), cpick(above, nought, came)
        enter_f = now_f if enter_f is None else cadd(enter_f, now_f)
        enter_b = now_b if enter_b is None else cadd(enter_b, now_b)
    block = load(base_ref.at[3], 0, short, row, 8)
    all_f = cmore(load(sums_ref, 0, short, row, 8), block, enter_f)
    all_b = cmore(load(sums_ref, rows, short, row, 8), block, enter_b)
    below = cmore(cmul(factor(0), enter_f), factor(1), all_b)
    above = cmore(cmul(factor(3), enter_b), factor(2), all_f)
    planes = [cscale(load(modes_ref, l * rows, short, row, 8), scale) for l in range(count)]
    planes[0] = cadd(planes[0], below)
    planes[-1] = cadd(planes[-1], above)
    for l in range(1, count):
        planes[l] = cmore(planes[l], factor(4 + l - 1), planes[l - 1])
    planes[-1] = cmul(factor(4 + count - 1), planes[-1])
    for l in range(count - 2, -1, -1):
        planes[l] = cmul(factor(4 + l), cadd(planes[l], planes[l + 1]))
    return below, planes, above


def middle_kernel(
    chunk, count, levels, flags_ref, numbers_ref, wave_eig_ref, sine_ref, faces_ref, field_ref,
    modes_ref, base_ref, factors_ref, sums_ref, *refs,
):
    came_refs, (found_ref, next_ref, next_sums_ref) = refs[:levels], refs[levels : levels + 3]
    give_refs, work_ref = refs[levels + 3 : -1], refs[-1]
    q, h, z = flags_ref[0], flags_ref[1], flags_ref[2]
    scale, s_re, s_im = numbers_ref[2], numbers_ref[4], numbers_ref[5]
    short = base_ref.shape[1] // 2
    rows = 2 * short
    width = base_ref.shape[2]

    def solve(row):
        below, planes, above = solved(
            count, levels, z, scale, modes_ref, sums_ref, came_refs, base_ref, factors_ref, row
        )
        store(work_ref, 0, short, row, 8, below)
        store(work_ref, (count + 1) * rows, short, row, 8, above)
        for l in range(count):
            store(work_ref, (l + 1) * rows, short, row, 8, planes[l])
            store(found_ref, l * rows, short, row, 8, planes[l])

    each_strip(short, 8, solve)
    sine_rows(work_ref, work_ref, sine_ref, (count + 2) * rows)

    def residual(i, total):
        row = pl.multiple_of(i * 8, 8)
        eigen = wave_eig_ref[q, rows_at((h * CHUNKS + chunk) * short + row, 8), :]
        under = load(work_ref, 0, short, row, 8)
        here = load(work_ref, rows, short, row, 8)
        for l in range(count):
            over = load(work_ref, (l + 2) * rows, short, row, 8)
            diag, cell, right, left, low, high = [faces_ref[n, pl.ds(l, 1), :] for n in range(6)]
            diag = s_re + (diag + cell * eigen)
            value = []
            for c in range(2):
                v = diag * here[c] - right * pltpu.roll(here[c], width - 1, 1)
                v = v - left * pltpu.roll(here[c], 1, 1)
                value.append(v - (low * under[c] + high * over[c]))
            value = (value[0] - s_im * here[1], value[1] + s_im * here[0])
            value = csub(load(field_ref, l * rows, short, row, 8), value)
            total = total + squares_of(value)
            store(work_ref, l * rows, short, row, 8, value)
            under, here = here, over
        return total

    total = lax.fori_loop(0, short // 8, residual, jnp.zeros((8, width), jnp.float32))
    sine_rows(work_ref, next_ref, sine_ref, count * rows)

    def sums(row):
        rho, cross_f, cross_b = [load(base_ref.at[n], 0, short, row, 8) for n in range(3)]
        planes = [load(next_ref, l * rows, short, row, 8) for l in range(count)]
        ahead, behind = sums_of(planes, rho, cross_f, cross_b)
        store(next_sums_ref, 0, short, row, 8, ahead)
        store(next_sums_ref, rows, short, row, 8, behind)

    each_strip(short, 8, sums)
    next_sums_ref[pl.ds(2 * rows, TAG), :] = sums_ref[pl.ds(2 * rows, TAG), :]
    next_sums_ref[pl.ds(2 * rows + 1, 1), :] = jnp.sum(total, axis=0, keepdims=True)
    fill_give(z, rows, next_sums_ref, give_refs)


def end_kernel(
    count, levels, flags_ref, numbers_ref, sine_ref, found_ref, modes_ref, base_ref,
    factors_ref, sums_ref, *refs,
):
    came_refs, out_refs, work_ref = refs[:levels], refs[-1 - CORES : -1], refs[-1]
    z, member = flags_ref[2], flags_ref[3]
    scale = numbers_ref[2]
    short = base_ref.shape[1] // 2
    rows = 2 * short

    def solve(row):
        _, planes, _ = solved(
            count, levels, z, scale, modes_ref, sums_ref, came_refs, base_ref, factors_ref, row
        )
        for l in range(count):
            before = load(found_ref, l * rows, short, row, 8)
            store(work_ref, l * rows, short, row, 8, cadd(before, planes[l]))

    each_strip(short, 8, solve)
    sine_rows(work_ref, work_ref, sine_ref, count * rows)
    part = count // GROUP * rows
    tag_refs = (refs[levels] if levels > 1 else sums_ref, came_refs[-1])
    tag = None
    for ref in tag_refs:
        part_tag = ref[pl.ds(ref.shape[0] - TAG, TAG), :]
        tag = part_tag if tag is None else tag + part_tag
    for core, ref in enumerate(out_refs):
        for e in range(CHIPS):
            ref[pl.ds(e * part, part), :] = work_ref[rows_at((member ^ (CORES * e + core)) * part, part), :]
        ref[pl.ds(CHIPS * part, TAG), :] = tag


smem = pl.BlockSpec(memory_space=pltpu.SMEM)
vmem = pl.BlockSpec(memory_space=pltpu.VMEM)
unread = pl.BlockSpec(memory_space=pl.ANY)


def call(kernel, scalars, arrays, outs, scratch=(), flops=0, after=()):
    out_shape = [jax.ShapeDtypeStruct(shape, jnp.float32) for shape in outs]
    head = len(scalars) + len(arrays)

    def run(*refs):
        kernel(*refs[:head], *refs[head + len(after) :])

    moved = sum(a.size * a.dtype.itemsize for a in arrays) + sum(4 * int(np.prod(s)) for s in outs)
    held = moved + sum(4 * int(np.prod(s)) for s in scratch)
    return pl.pallas_call(
        run,
        out_shape=out_shape,
        in_specs=[smem] * len(scalars) + [vmem] * len(arrays) + [unread] * len(after),
        out_specs=[smem if len(shape) == 1 else vmem for shape in outs],
        scratch_shapes=[pltpu.VMEM(shape, jnp.float32) for shape in scratch],
        compiler_params=pltpu.CompilerParams(vmem_limit_bytes=held + 4 * 2**20),
        cost_estimate=pl.CostEstimate(flops=flops, bytes_accessed=moved, transcendentals=0),
    )(*scalars, *arrays, *after)


def pair_up(array, groups, flip):
    return lax.ppermute(array, "gz", [(i, i ^ flip) for i in range(groups)])


def step_by(array, groups, distance):
    return lax.ppermute(
        array, "gz", [(i, i + distance) for i in range(groups) if 0 <= i + distance < groups]
    )


def body(source, layer_ids, conduct_table, shift):
    planes, length_x, length_y = source.shape[1:]
    groups = lax.axis_size("gz")
    blocks = groups // GROUP
    levels = blocks.bit_length() - 1
    count = GROUP * planes
    length_z = planes * groups
    full = length_x // RADIX
    short = full // (HALVES * CHUNKS)
    rows = 2 * short
    if blocks < 2 or groups != GROUP << levels or planes > 2 or short % 8 or length_x != RADIX * full:
        raise ValueError("unsupported layout")
    me = lax.axis_index("gz")
    member = me % GROUP
    flags = jnp.stack([member % RADIX, member // RADIX, me // GROUP, member]).astype(jnp.int32)

    wave = wave_tables(length_x)
    wave_f = jnp.asarray(two_terms(wave))
    wave_b = jnp.asarray(two_terms(np.ascontiguousarray(np.swapaxes(wave, 1, 2)) / length_x))
    sine = jnp.asarray(two_terms(sine_table(length_y)))
    wave_eig = np.broadcast_to(wave_eigen(length_x)[:, :, None], (RADIX, full, length_y))
    wave_eig = jnp.asarray(np.ascontiguousarray(wave_eig).astype(np.float32))
    sine_eig = jnp.asarray(np.tile(sine_eigen(length_y)[None, :], (8, 1)).astype(np.float32))

    chunks = range(CHUNKS)
    row_block = (TAG, length_y)
    block = (count * rows, length_y)
    sums_block = (2 * rows + TAG, length_y)
    single = (rows + TAG, length_y)
    chip_part = (CORES * planes * rows + TAG, length_y)
    swap_part = (CHIPS * planes * rows + TAG, length_y)
    give_part = (CHIPS * (planes * rows + TAG), length_y)
    gives = [single] if levels == 1 else []
    dots = 6 * length_y * length_y

    parted = source.reshape(2, planes, RADIX, full, length_y)
    spectra = {}
    placed = []
    for pair in ((2, 3), (0, 1)):
        *made, _ = call(
            functools.partial(forward_kernel, pair), [flags, conduct_table], [parted, wave_f, layer_ids],
            [chip_part] * (HALVES * CHUNKS) + [row_block],
            scratch=[(len(pair), planes, 2 * full, length_y)], flops=2 * planes * 2 * full * dots, after=placed,
        )
        placed = made[:1]
        for n in range(HALVES):
            for t in chunks:
                spectra[pair[0] // CORES + CORES * n, t] = made[n * CHUNKS + t]
    for t in chunks:
        for e in (3, 1, 2):
            spectra[e, t] = pair_up(spectra[e, t], groups, CORES * e)

    state = [{} for _ in chunks]

    def exchange(st, after):
        sums, give = st["sums"][0], st["sums"][-1]
        st["came"], st["tags"] = [], []
        for level in range(levels):
            st["came"].append(pair_up(give, groups, GROUP << level))
            if level + 1 < levels:
                shape = single if level + 2 == levels else sums_block
                (give,) = call(
                    functools.partial(join_kernel, level, levels), [flags], [sums, st["came"][-1], st["base"]],
                    [shape], after=after,
                )
                sums = give
                st["tags"] = [give[-TAG:]]

    def swap(t, after):
        st = state[t]
        st["parts"] = [spectra[e, t] for e in range(CHIPS)]
        give, tags = call(give_kernel, [], st["parts"], [give_part, (CHIPS * TAG, length_y)], after=after)
        st["parts"].append(pair_up(give, groups, 1))
        if t:
            return [give]
        if levels == 1:
            st["extra"] = [pair_up(tags, groups, GROUP + core) for core in range(CORES)]
            return [give]
        (total,) = call(
            functools.partial(summary_kernel, planes), [flags], st["parts"], [row_block],
            scratch=[(count, length_y)],
        )
        st["extra"] = [step_by(total, groups, GROUP), step_by(total, groups, -GROUP)]
        for level in range(levels):
            (total,) = call(add_kernel, [], [total, pair_up(total, groups, GROUP << level)], [row_block])
        st["extra"] = [total, *st["extra"]]
        return [total]

    def start(t, after):
        st = state[t]
        outs = [block, block, (6, rows, length_y), sums_block, *gives]
        made = call(
            functools.partial(start_kernel, t, planes, blocks, length_y * length_z),
            [flags, state[0]["numbers"] if t else shift],
            [wave_eig, sine_eig, sine, *st["parts"], *st.get("extra", [])],
            outs if t else [*outs, (6,)], flops=count * rows * dots, after=after,
        )
        if not t:
            *made, st["numbers"] = made
        st["field"], st["modes"], st["base"], *st["sums"] = made
        exchange(st, [])
        return [st["sums"][-1]]

    def faces(t, after):
        state[t]["faces"] = call(
            functools.partial(faces_kernel, planes, blocks), [flags],
            [*state[t]["parts"], *state[t]["extra"]], [(6, count, length_y)],
            scratch=[(count + 16, length_y), (count, length_y)], after=after,
        )[0]
        return [state[t]["faces"]]

    def factors(t, after):
        st = state[t]
        (st["factors"],) = call(
            functools.partial(factors_kernel, t, count, levels), [flags, state[0]["numbers"]],
            [wave_eig, sine_eig, st["base"]], [(4 + count + levels - 1, rows, length_y)], after=after,
        )
        return [st["factors"]]

    def middle(t, after):
        st = state[t]
        st["found"], st["modes"], *st["sums"] = call(
            functools.partial(middle_kernel, t, count, levels), [flags, state[0]["numbers"]],
            [wave_eig, sine, state[0]["faces"], st["field"], st["modes"], st["base"], st["factors"], st["sums"][0], *st["came"]],
            [block, block, sums_block, *gives], scratch=[((count + 2) * rows, length_y)],
            flops=(2 * count + 2) * rows * dots, after=after,
        )
        exchange(st, [])
        return [st["sums"][-1]]

    def end(t, after):
        st = state[t]
        after = [*after, *(state[t - 1]["answers"][3:] if t else [])]
        st["keep"], give = call(
            functools.partial(end_kernel, count, levels), [flags, state[0]["numbers"]],
            [sine, st["found"], st["modes"], st["base"], st["factors"], st["sums"][0], *st["came"], *st["tags"]],
            [swap_part] * CORES, scratch=[block], flops=count * rows * dots, after=after,
        )
        st["swapped"] = pair_up(give, groups, 1)
        return [st["keep"]]

    def merge(t, after):
        st = state[t]
        after = [*after, *(state[t - 1]["answers"][1:3] if t else state[t + 1]["came"][:1])]
        st["answers"] = call(merge_kernel, [], [st["keep"], st["swapped"]], [chip_part] * CHIPS, after=after)
        placed = st["answers"][:1]
        st["answers"] = [pair_up(a, groups, CORES * e) if e else a for e, a in enumerate(st["answers"])]
        return placed

    for step, t in (
        (swap, 0), (start, 0), (factors, 0), (faces, 0), (middle, 0), (swap, 1), (start, 1), (factors, 1),
        (end, 0), (merge, 0), (middle, 1), (end, 1), (merge, 1),
    ):
        placed = step(t, placed)
    return call(
        functools.partial(backward_kernel, planes, length_x * length_x * length_y * length_z),
        [flags], [wave_b] + [a for st in state for a in st["answers"]],
        [(2, planes, length_x, length_y), (2,)],
        scratch=[(planes, RADIX, 2 * full, length_y), (RADIX, planes, 2 * full, length_y)],
        flops=planes * RADIX * 2 * full * dots,
    )


def solution(mesh):
    placed = (P(None, ("node", "gz"), None, None), P(("node", "gz"), None), P(), P("node"))
    return jax.shard_map(
        body,
        mesh=mesh,
        in_specs=placed,
        out_specs=(P(None, ("node", "gz"), None, None), P("node")),
        check_vma=False,
    )
```

```python
import functools

import jax
import jax.numpy as jnp
import ml_dtypes
import numpy as np
from jax import lax
from jax.experimental import pallas as pl
from jax.experimental.pallas import tpu as pltpu
from jax.sharding import PartitionSpec as P

RADIX = 4
HALVES = 2
GROUP = RADIX * HALVES
CHUNKS = 2
CORES = 2
CHIPS = GROUP // CORES
TAG = 8

relax = 0.6


def sine_table(length):
    indices = np.arange(1, length + 1)
    product = indices[:, None] * indices[None, :] % (2 * (length + 1))
    return np.sqrt(2.0 / (length + 1)) * np.sin(np.pi / (length + 1) * product)


def sine_eigen(length):
    indices = np.arange(1, length + 1)
    return 4.0 * np.sin(np.pi / (2 * (length + 1)) * indices) ** 2


def wave_numbers(length):
    return RADIX * np.arange(length // RADIX)[None, :] + np.arange(RADIX)[:, None]


def wave_eigen(length):
    return 4.0 * np.sin(np.pi / length * wave_numbers(length)) ** 2


def wave_tables(length):
    waves = wave_numbers(length)
    short = length // RADIX
    product = waves[:, :, None] * np.arange(short)[None, None, :] % length
    angles = 2.0 * np.pi / length * product
    cos_t, sin_t = np.cos(angles), np.sin(angles)
    pieces = HALVES * CHUNKS
    top = np.concatenate([cos_t, sin_t], axis=2).reshape(RADIX, pieces, short // pieces, 2 * short)
    low = np.concatenate([-sin_t, cos_t], axis=2).reshape(RADIX, pieces, short // pieces, 2 * short)
    return np.concatenate([top, low], axis=2).reshape(RADIX, 2 * short, 2 * short)


def two_terms(table):
    first = table.astype(ml_dtypes.bfloat16)
    return np.stack([first, (table - first.astype(np.float64)).astype(ml_dtypes.bfloat16)])


def split(value):
    first = value.astype(jnp.bfloat16)
    return first, (value - first.astype(jnp.float32)).astype(jnp.bfloat16)


def dot_right(value, table):
    rows = value.shape[0]
    first, second = split(value)
    wide = jnp.dot(jnp.concatenate([first, second], axis=0), table[0], preferred_element_type=jnp.float32)
    return wide[:rows] + (wide[rows:] + jnp.dot(first, table[1], preferred_element_type=jnp.float32))


def dot_left(table, value):
    rows = table.shape[0] // 2
    first, second = split(value)
    wide = jnp.dot(table, first, preferred_element_type=jnp.float32)
    return wide[:rows] + (wide[rows:] + jnp.dot(table[:rows], second, preferred_element_type=jnp.float32))


def cmul(a, b):
    return (a[0] * b[0] - a[1] * b[1], a[0] * b[1] + a[1] * b[0])


def csqr(a):
    cross = a[0] * a[1]
    return ((a[0] - a[1]) * (a[0] + a[1]), cross + cross)


def cpow(a, count):
    result = None
    while count:
        if count & 1:
            result = a if result is None else cmul(result, a)
        count >>= 1
        if count:
            a = csqr(a)
    return result


def cadd(a, b):
    return (a[0] + b[0], a[1] + b[1])


def csub(a, b):
    return (a[0] - b[0], a[1] - b[1])


def cscale(a, scale):
    return (a[0] * scale, a[1] * scale)


def cmore(total, factor, term):
    return cadd(total, cmul(factor, term))


def cinv(a):
    scale = 1.0 / (a[0] * a[0] + a[1] * a[1])
    return (a[0] * scale, -a[1] * scale)


def cone(a):
    return (1.0 - a[0], -a[1])


def cpick(cond, a, b):
    return (jnp.where(cond, a[0], b[0]), jnp.where(cond, a[1], b[1]))


def rows_at(start, rows):
    if isinstance(start, int):
        return pl.ds(start, rows)
    return pl.ds(pl.multiple_of(start, 8), rows)


def load(ref, base, short, row, rows):
    return (ref[rows_at(base + row, rows), :], ref[rows_at(base + short + row, rows), :])


def store(ref, base, short, row, rows, value):
    ref[rows_at(base + row, rows), :] = value[0]
    ref[rows_at(base + short + row, rows), :] = value[1]


def each_strip(count, rows, body):
    def step(i, carry):
        body(pl.multiple_of(i * rows, rows))
        return carry

    steps = count // rows
    lax.fori_loop(0, steps, step, 0, unroll=min(steps, 4))


def squares_of(a):
    return a[0] * a[0] + a[1] * a[1]


def conduct_of(table_ref, ids_ref, out_ref):
    planes = ids_ref.shape[0]
    ids = ids_ref[...]
    cells = jnp.zeros(ids.shape, jnp.float32)
    for layer in range(table_ref.shape[0]):
        cells = jnp.where(ids == layer, table_ref[layer], cells)
    out_ref[...] = jnp.zeros_like(out_ref)
    out_ref[pl.ds(0, planes), :] = cells
    out_ref[pl.ds(TAG - 1, 1), :] = jnp.sum(cells, axis=0, keepdims=True)


def add_kernel(one_ref, two_ref, out_ref):
    out_ref[...] = one_ref[...] + two_ref[...]


def tag_of(ref):
    return ref[pl.ds(ref.shape[0] - TAG, TAG), :]


def member_tags(part_refs, swapped_ref):
    start = swapped_ref.shape[0] - CHIPS * TAG
    tags = {}
    for e, ref in enumerate(part_refs):
        tags[CORES * e] = tag_of(ref)
        tags[CORES * e + 1] = swapped_ref[pl.ds(start + e * TAG, TAG), :]
    return tags


def find_numbers(cells_total, shift_ref, tags, out_ref):
    total = None
    for tag in tags:
        row = tag[TAG - 1 :]
        total = row if total is None else total + row
    inv = (1.0 / (jnp.sum(total, axis=1, keepdims=True) * (1.0 / cells_total)))[0, 0]
    out_ref[0] = shift_ref[0] * inv
    out_ref[1] = shift_ref[1] * inv
    out_ref[2] = relax * inv
    out_ref[3] = 0.5 * relax * inv
    out_ref[4] = shift_ref[0]
    out_ref[5] = shift_ref[1]


def place_cells(planes, member, tags, cells_ref, start):
    for d, tag in tags.items():
        for p in range(planes):
            cells_ref[pl.ds(start + (member ^ d) * planes + p, 1), :] = tag[p : p + 1]


def summary_kernel(planes, flags_ref, *refs):
    part_refs, swapped_ref, out_ref, cells_ref = refs[:CHIPS], refs[CHIPS], refs[-2], refs[-1]
    place_cells(planes, flags_ref[3], member_tags(part_refs, swapped_ref), cells_ref, 0)
    out_ref[...] = jnp.zeros_like(out_ref)
    out_ref[pl.ds(0, 1), :] = cells_ref[pl.ds(0, 1), :]
    out_ref[pl.ds(1, 1), :] = cells_ref[pl.ds(GROUP * planes - 1, 1), :]
    out_ref[pl.ds(TAG - 1, 1), :] = jnp.sum(cells_ref[...], axis=0, keepdims=True)


def faces_kernel(planes, blocks, flags_ref, *refs):
    part_refs, swapped_ref, extra_refs = refs[:CHIPS], refs[CHIPS], refs[CHIPS + 1 : -3]
    faces_ref, padded_ref, other_ref = refs[-3:]
    z, member = flags_ref[2], flags_ref[3]
    _, count, width = faces_ref.shape
    place_cells(planes, member, member_tags(part_refs, swapped_ref), padded_ref, 8)
    if blocks == 2:
        for core, ref in enumerate(extra_refs):
            tags = {CORES * e + core: ref[pl.ds(e * TAG, TAG), :] for e in range(CHIPS)}
            place_cells(planes, member, tags, other_ref, 0)
        below, above = other_ref[pl.ds(count - 1, 1), :], other_ref[pl.ds(0, 1), :]
    else:
        below, above = extra_refs[1][pl.ds(1, 1), :], extra_refs[2][pl.ds(0, 1), :]
    cells = padded_ref[pl.ds(8, count), :]
    padded_ref[pl.ds(7, 1), :] = jnp.where(z == 0, cells[0:1], below)
    padded_ref[pl.ds(8 + count, 1), :] = jnp.where(z == blocks - 1, cells[count - 1 : count], above)
    lane = lax.broadcasted_iota(jnp.int32, cells.shape, 1)
    last, first = lane == width - 1, lane == 0
    right = 0.5 * (cells + pltpu.roll(cells, width - 1, 1))
    left = 0.5 * (cells + pltpu.roll(cells, 1, 1))
    low = 0.5 * (cells + padded_ref[pl.ds(7, count), :])
    high = 0.5 * (cells + padded_ref[pl.ds(9, count), :])
    faces_ref[0] = jnp.where(last, cells, right) + jnp.where(first, cells, left) + (low + high)
    faces_ref[1] = cells
    faces_ref[2] = jnp.where(last, 0.0, right)
    faces_ref[3] = jnp.where(first, 0.0, left)
    faces_ref[4] = low
    faces_ref[5] = high


def forward_kernel(pair, flags_ref, table_ref, source_ref, wave_ref, ids_ref, *refs):
    out_refs, cells_ref, stage_ref = refs[:-2], refs[-2], refs[-1]
    planes = source_ref.shape[1]
    rows = stage_ref.shape[2] // (HALVES * CHUNKS)
    conduct_of(table_ref, ids_ref, cells_ref)
    for core, distance in enumerate(pair):
        q = flags_ref[0] ^ distance
        sign = (1 - 2 * (q & 1)).astype(jnp.float32)
        turn_re = jnp.where(q == 0, 1.0, jnp.where(q == 2, -1.0, 0.0))
        turn_im = jnp.where(q == 1, 1.0, jnp.where(q == 3, -1.0, 0.0))
        for p in range(planes):
            parts = [[source_ref[c, p, i] for i in range(RADIX)] for c in range(2)]
            even = [parts[c][0] + sign * parts[c][2] for c in range(2)]
            odd = [parts[c][1] + sign * parts[c][3] for c in range(2)]
            mixed = jnp.concatenate(
                [
                    even[0] + (turn_re * odd[0] + turn_im * odd[1]),
                    even[1] + (turn_re * odd[1] - turn_im * odd[0]),
                ],
                axis=0,
            )
            stage_ref[core, p] = dot_left(wave_ref[q], mixed)
            for n in range(HALVES):
                h = flags_ref[1] ^ n
                for t in range(CHUNKS):
                    out_refs[n * CHUNKS + t][pl.ds((core * planes + p) * rows, rows), :] = stage_ref[
                        core, p, rows_at((h * CHUNKS + t) * rows, rows), :
                    ]
    for ref in out_refs:
        ref[pl.ds(ref.shape[0] - TAG, TAG), :] = cells_ref[...]


def give_kernel(*refs):
    part_refs, out_ref, tags_ref = refs[:CHIPS], refs[CHIPS], refs[CHIPS + 1]
    part = (part_refs[0].shape[0] - TAG) // CORES
    for e, ref in enumerate(part_refs):
        out_ref[pl.ds(e * part, part), :] = ref[pl.ds(part, part), :]
        tags_ref[pl.ds(e * TAG, TAG), :] = tag_of(ref)
    out_ref[pl.ds(CHIPS * part, CHIPS * TAG), :] = tags_ref[...]


def merge_kernel(keep_ref, swapped_ref, *out_refs):
    part = (keep_ref.shape[0] - TAG) // CHIPS
    for e, ref in enumerate(out_refs):
        ref[pl.ds(0, part), :] = keep_ref[pl.ds(e * part, part), :]
        ref[pl.ds(part, part), :] = swapped_ref[pl.ds(e * part, part), :]
        ref[pl.ds(CORES * part, TAG), :] = tag_of(keep_ref) + tag_of(swapped_ref)


def backward_kernel(planes, cells, flags_ref, wave_ref, *refs):
    arrays, (out_ref, norms_ref, mixed_ref, stage_ref) = refs[:-4], refs[-4:]
    part = (arrays[0].shape[0] - TAG) // CORES
    rows = part // planes
    short = rows * CHUNKS * HALVES // 2
    total = None
    for ref in arrays:
        tag = tag_of(ref)
        total = tag if total is None else total + tag
    for d in range(RADIX):
        q = flags_ref[0] ^ d
        for p in range(planes):
            for n in range(HALVES):
                h = flags_ref[1] ^ n
                for t in range(CHUNKS):
                    ref = arrays[t * CHIPS + (d + RADIX * n) // CORES]
                    stage_ref[d, p, rows_at((h * CHUNKS + t) * rows, rows), :] = ref[
                        pl.ds(d % CORES * part + p * rows, rows), :
                    ]
            mixed_ref[p, q] = dot_left(wave_ref[q], stage_ref[d, p])
    for p in range(planes):

        def strip(row):
            zero, one, two, three = [load(mixed_ref.at[p, q], 0, short, row, 8) for q in range(RADIX)]
            even, odd = cadd(zero, two), cadd(one, three)
            even_d, odd_d = csub(zero, two), csub(one, three)
            parts = (
                cadd(even, odd),
                (even_d[0] - odd_d[1], even_d[1] + odd_d[0]),
                csub(even, odd),
                (even_d[0] + odd_d[1], even_d[1] - odd_d[0]),
            )
            for i in range(RADIX):
                for c in range(2):
                    out_ref[c, p, rows_at(i * short + row, 8), :] = parts[i][c]

        each_strip(short, 8, strip)
    norms = jnp.sqrt(jnp.sum(total, axis=1, keepdims=True) * (1.0 / cells))
    for n in range(norms_ref.shape[0]):
        norms_ref[n] = norms[n, 0]


def decay_root(h):
    sq = (h[0] + 0.25 * (h[0] * h[0] - h[1] * h[1]), h[1] + 0.5 * h[0] * h[1])
    size = jnp.sqrt(squares_of(sq))
    root_re = jnp.sqrt(0.5 * (size + sq[0]))
    root = (root_re, 0.5 * sq[1] / root_re)
    return cinv((1.0 + 0.5 * h[0] + root[0], 0.5 * h[1] + root[1])), root


def two_powers(power, z, stacks):
    low = high = None
    bit = 0
    while (1 << bit) < stacks:
        taken = ((z >> bit) & 1) == 1
        if low is None:
            one = (jnp.ones_like(power[0]), jnp.zeros_like(power[0]))
            low, high = cpick(taken, power, one), cpick(taken, one, power)
        else:
            grown = cmul(cpick(taken, low, high), power)
            low, high = cpick(taken, grown, low), cpick(taken, high, grown)
        power = csqr(power)
        bit += 1
    return low, high


def sums_of(planes, rho, cross_f, cross_b):
    ahead = planes[0]
    for a in planes[1:]:
        ahead = cmore(a, rho, ahead)
    behind = planes[-1]
    for a in planes[-2::-1]:
        behind = cmore(a, rho, behind)
    return csub(ahead, cmul(cross_f, behind)), csub(behind, cmul(cross_b, ahead))


def sine_rows(source_ref, target_ref, sine_ref, count):
    sine = (sine_ref[0], sine_ref[1])
    rows = max(n for n in range(16, 641, 16) if count % n == 0)
    for i in range(0, count, rows):
        target_ref[pl.ds(i, rows), :] = dot_right(source_ref[pl.ds(i, rows), :], sine)


def fill_give(z, rows, sums_ref, give_refs):
    for ref in give_refs:
        ref[pl.ds(0, rows), :] = sums_ref[rows_at((z & 1) * rows, rows), :]
        ref[pl.ds(rows, TAG), :] = sums_ref[pl.ds(2 * rows, TAG), :]


def start_kernel(
    chunk, planes, blocks, cells_total, flags_ref, numbers_ref, wave_eig_ref, sine_eig_ref, sine_ref, *refs,
):
    part_refs, swapped_ref, refs = refs[:CHIPS], refs[CHIPS], refs[CHIPS + 1 :]
    if chunk == 0:
        extra_count = 2 if blocks == 2 else 3
        extra_refs, refs = refs[:extra_count], refs[extra_count:]
    (field_ref, modes_ref, base_ref, sums_ref), give_refs = refs[:4], refs[4:]
    if chunk == 0:
        shift_ref, numbers_ref, give_refs = numbers_ref, give_refs[-1], give_refs[:-1]
        if blocks == 2:
            tags = list(member_tags(part_refs, swapped_ref).values())
            tags += [ref[pl.ds(e * TAG, TAG), :] for ref in extra_refs for e in range(CHIPS)]
        else:
            tags = [extra_refs[0][...]]
        find_numbers(cells_total, shift_ref, tags, numbers_ref)
    q, h, z, member = [flags_ref[n] for n in range(4)]
    rows = base_ref.shape[1]
    part = rows * planes
    short = rows // 2
    count = GROUP * planes
    first_row = (h * CHUNKS + chunk) * short
    for e, ref in enumerate(part_refs):
        field_ref[rows_at((member ^ CORES * e) * part, part), :] = ref[pl.ds(0, part), :]
        field_ref[rows_at((member ^ (CORES * e + 1)) * part, part), :] = swapped_ref[pl.ds(e * part, part), :]
    sine_rows(field_ref, modes_ref, sine_ref, count * rows)
    h_re, h_im = numbers_ref[0], numbers_ref[1]
    sine_eig = sine_eig_ref[...]

    def strip(i, total):
        row = pl.multiple_of(i * 8, 8)
        eigen = wave_eig_ref[q, rows_at(first_row + row, 8), :] + sine_eig
        rho, _ = decay_root((eigen + h_re, jnp.full_like(eigen, h_im)))
        block = cpow(rho, count)
        next_one = cmul(block, rho)
        low, high = two_powers(csqr(block), z, blocks)
        cross_f, cross_b = cmul(next_one, low), cmul(next_one, high)
        for n, value in enumerate((rho, cross_f, cross_b, block, low, high)):
            store(base_ref.at[n], 0, short, row, 8, value)
        found = [load(modes_ref, l * rows, short, row, 8) for l in range(count)]
        ahead, behind = sums_of(found, rho, cross_f, cross_b)
        store(sums_ref, 0, short, row, 8, ahead)
        store(sums_ref, rows, short, row, 8, behind)
        for l in range(count):
            total = total + squares_of(load(field_ref, l * rows, short, row, 8))
        return total

    total = lax.fori_loop(
        0, short // 8, strip, jnp.zeros((8, field_ref.shape[1]), jnp.float32), unroll=2
    )
    sums_ref[pl.ds(2 * rows, TAG), :] = jnp.zeros((TAG, field_ref.shape[1]), jnp.float32)
    sums_ref[pl.ds(2 * rows, 1), :] = jnp.sum(total, axis=0, keepdims=True)
    fill_give(z, rows, sums_ref, give_refs)


def factors_kernel(
    chunk, count, levels, flags_ref, numbers_ref, wave_eig_ref, sine_eig_ref, base_ref, out_ref,
):
    q, h_part, z = flags_ref[0], flags_ref[1], flags_ref[2]
    short = base_ref.shape[1] // 2
    h_re, h_im, scale = numbers_ref[0], numbers_ref[1], numbers_ref[3]
    sine_eig = sine_eig_ref[...]

    def strip(row):
        eigen = wave_eig_ref[q, rows_at((h_part * CHUNKS + chunk) * short + row, 8), :] + sine_eig
        h = (eigen + h_re, jnp.full_like(eigen, h_im))
        rho, _, _, block, low, high = [load(base_ref.at[n], 0, short, row, 8) for n in range(6)]
        half_gap = csub((1.0 + 0.5 * h[0], 0.5 * h[1]), rho)
        wide = cmul(csqr(block), csqr(rho))
        low_w, high_w = cmul(low, wide), cmul(high, wide)
        whole = cscale(cinv(cmul(half_gap, cone(cmul(low, high_w)))), scale)
        turned = cmul(rho, whole)
        values = [
            cmul(cone(high_w), whole), cmul(cone(low), turned),
            cmul(cone(high), turned), cmul(cone(low_w), whole),
        ]
        pivot = (2.0 + h[0], h[1])
        inverse = cinv(pivot)
        values.append(inverse)
        for _ in range(count - 1):
            inverse = cinv(csub(pivot, inverse))
            values.append(inverse)
        near = far = None
        power = block
        for level in range(1, levels):
            taken = ((z >> (level - 1)) & 1) == 1
            if near is None:
                one = (jnp.ones_like(power[0]), jnp.zeros_like(power[0]))
                near, far = cpick(taken, power, one), cpick(taken, one, power)
            else:
                grown = cmul(cpick(taken, near, far), power)
                near, far = cpick(taken, grown, near), cpick(taken, far, grown)
            power = csqr(power)
            values.append(cpick(((z >> level) & 1) == 1, near, far))
        for n, value in enumerate(values):
            store(out_ref.at[n], 0, short, row, 8, value)

    each_strip(short, 8, strip)


def join_kernel(level, levels, flags_ref, sums_ref, came_ref, base_ref, out_ref):
    z = flags_ref[2]
    short = base_ref.shape[1] // 2
    rows = 2 * short
    above = ((z >> level) & 1) == 1
    last = level + 2 == levels
    upper = ((z >> (level + 1)) & 1) == 1

    def strip(row):
        block = load(base_ref.at[3], 0, short, row, 8)
        for _ in range(level):
            block = csqr(block)
        ahead, behind = load(sums_ref, 0, short, row, 8), load(sums_ref, rows, short, row, 8)
        ahead_c, behind_c = load(came_ref, 0, short, row, 8), load(came_ref, rows, short, row, 8)
        joined = cmore(cpick(above, ahead, ahead_c), block, cpick(above, ahead_c, ahead))
        joined_b = cmore(cpick(above, behind_c, behind), block, cpick(above, behind, behind_c))
        if last:
            store(out_ref, 0, short, row, 8, cpick(upper, joined_b, joined))
        else:
            store(out_ref, 0, short, row, 8, joined)
            store(out_ref, rows, short, row, 8, joined_b)

    each_strip(short, 8, strip)
    out_ref[pl.ds(out_ref.shape[0] - TAG, TAG), :] = (
        sums_ref[pl.ds(2 * rows, TAG), :] + came_ref[pl.ds(2 * rows, TAG), :]
    )


def solved(count, levels, z, scale, modes_ref, sums_ref, came_refs, base_ref, factors_ref, row):
    short = base_ref.shape[1] // 2
    rows = 2 * short

    def factor(n):
        return load(factors_ref.at[n], 0, short, row, 8)

    enter_f = enter_b = None
    for level in range(levels):
        above = ((z >> level) & 1) == 1
        base = 0 if level == levels - 1 else jnp.where(above, 0, rows)
        came = load(came_refs[level], base, short, row, 8)
        if level:
            came = cmul(factor(4 + count + level - 1), came)
        nought = (jnp.zeros_like(came[0]), jnp.zeros_like(came[0]))
        now_f, now_b = cpick(above, came, nought), cpick(above, nought, came)
        enter_f = now_f if enter_f is None else cadd(enter_f, now_f)
        enter_b = now_b if enter_b is None else cadd(enter_b, now_b)
    block = load(base_ref.at[3], 0, short, row, 8)
    all_f = cmore(load(sums_ref, 0, short, row, 8), block, enter_f)
    all_b = cmore(load(sums_ref, rows, short, row, 8), block, enter_b)
    below = cmore(cmul(factor(0), enter_f), factor(1), all_b)
    above = cmore(cmul(factor(3), enter_b), factor(2), all_f)
    planes = [cscale(load(modes_ref, l * rows, short, row, 8), scale) for l in range(count)]
    planes[0] = cadd(planes[0], below)
    planes[-1] = cadd(planes[-1], above)
    for l in range(1, count):
        planes[l] = cmore(planes[l], factor(4 + l - 1), planes[l - 1])
    planes[-1] = cmul(factor(4 + count - 1), planes[-1])
    for l in range(count - 2, -1, -1):
        planes[l] = cmul(factor(4 + l), cadd(planes[l], planes[l + 1]))
    return below, planes, above


def middle_kernel(
    chunk, count, levels, flags_ref, numbers_ref, wave_eig_ref, sine_ref, faces_ref, field_ref,
    modes_ref, base_ref, factors_ref, sums_ref, *refs,
):
    came_refs, (found_ref, next_ref, next_sums_ref) = refs[:levels], refs[levels : levels + 3]
    give_refs, work_ref = refs[levels + 3 : -1], refs[-1]
    q, h, z = flags_ref[0], flags_ref[1], flags_ref[2]
    scale, s_re, s_im = numbers_ref[2], numbers_ref[4], numbers_ref[5]
    short = base_ref.shape[1] // 2
    rows = 2 * short
    width = base_ref.shape[2]

    def solve(row):
        below, planes, above = solved(
            count, levels, z, scale, modes_ref, sums_ref, came_refs, base_ref, factors_ref, row
        )
        store(work_ref, 0, short, row, 8, below)
        store(work_ref, (count + 1) * rows, short, row, 8, above)
        for l in range(count):
            store(work_ref, (l + 1) * rows, short, row, 8, planes[l])
            store(found_ref, l * rows, short, row, 8, planes[l])

    each_strip(short, 8, solve)
    sine_rows(work_ref, work_ref, sine_ref, (count + 2) * rows)

    def residual(i, total):
        row = pl.multiple_of(i * 8, 8)
        eigen = wave_eig_ref[q, rows_at((h * CHUNKS + chunk) * short + row, 8), :]
        under = load(work_ref, 0, short, row, 8)
        here = load(work_ref, rows, short, row, 8)
        for l in range(count):
            over = load(work_ref, (l + 2) * rows, short, row, 8)
            diag, cell, right, left, low, high = [faces_ref[n, pl.ds(l, 1), :] for n in range(6)]
            diag = s_re + (diag + cell * eigen)
            value = []
            for c in range(2):
                v = diag * here[c] - right * pltpu.roll(here[c], width - 1, 1)
                v = v - left * pltpu.roll(here[c], 1, 1)
                value.append(v - (low * under[c] + high * over[c]))
            value = (value[0] - s_im * here[1], value[1] + s_im * here[0])
            value = csub(load(field_ref, l * rows, short, row, 8), value)
            total = total + squares_of(value)
            store(work_ref, l * rows, short, row, 8, value)
            under, here = here, over
        return total

    total = lax.fori_loop(0, short // 8, residual, jnp.zeros((8, width), jnp.float32), unroll=2)
    sine_rows(work_ref, next_ref, sine_ref, count * rows)

    def sums(row):
        rho, cross_f, cross_b = [load(base_ref.at[n], 0, short, row, 8) for n in range(3)]
        planes = [load(next_ref, l * rows, short, row, 8) for l in range(count)]
        ahead, behind = sums_of(planes, rho, cross_f, cross_b)
        store(next_sums_ref, 0, short, row, 8, ahead)
        store(next_sums_ref, rows, short, row, 8, behind)

    each_strip(short, 8, sums)
    next_sums_ref[pl.ds(2 * rows, TAG), :] = sums_ref[pl.ds(2 * rows, TAG), :]
    next_sums_ref[pl.ds(2 * rows + 1, 1), :] = jnp.sum(total, axis=0, keepdims=True)
    fill_give(z, rows, next_sums_ref, give_refs)


def end_kernel(
    count, levels, flags_ref, numbers_ref, sine_ref, found_ref, modes_ref, base_ref,
    factors_ref, sums_ref, *refs,
):
    came_refs, out_refs, work_ref = refs[:levels], refs[-1 - CORES : -1], refs[-1]
    z, member = flags_ref[2], flags_ref[3]
    scale = numbers_ref[2]
    short = base_ref.shape[1] // 2
    rows = 2 * short

    def solve(row):
        _, planes, _ = solved(
            count, levels, z, scale, modes_ref, sums_ref, came_refs, base_ref, factors_ref, row
        )
        for l in range(count):
            before = load(found_ref, l * rows, short, row, 8)
            store(work_ref, l * rows, short, row, 8, cadd(before, planes[l]))

    each_strip(short, 8, solve)
    sine_rows(work_ref, work_ref, sine_ref, count * rows)
    part = count // GROUP * rows
    tag_refs = (refs[levels] if levels > 1 else sums_ref, came_refs[-1])
    tag = None
    for ref in tag_refs:
        part_tag = ref[pl.ds(ref.shape[0] - TAG, TAG), :]
        tag = part_tag if tag is None else tag + part_tag
    for core, ref in enumerate(out_refs):
        for e in range(CHIPS):
            ref[pl.ds(e * part, part), :] = work_ref[rows_at((member ^ (CORES * e + core)) * part, part), :]
        ref[pl.ds(CHIPS * part, TAG), :] = tag


smem = pl.BlockSpec(memory_space=pltpu.SMEM)
vmem = pl.BlockSpec(memory_space=pltpu.VMEM)
unread = pl.BlockSpec(memory_space=pl.ANY)


def call(kernel, scalars, arrays, outs, scratch=(), flops=0, after=()):
    out_shape = [jax.ShapeDtypeStruct(shape, jnp.float32) for shape in outs]
    head = len(scalars) + len(arrays)

    def run(*refs):
        kernel(*refs[:head], *refs[head + len(after) :])

    moved = sum(a.size * a.dtype.itemsize for a in arrays) + sum(4 * int(np.prod(s)) for s in outs)
    held = moved + sum(4 * int(np.prod(s)) for s in scratch)
    return pl.pallas_call(
        run,
        out_shape=out_shape,
        in_specs=[smem] * len(scalars) + [vmem] * len(arrays) + [unread] * len(after),
        out_specs=[smem if len(shape) == 1 else vmem for shape in outs],
        scratch_shapes=[pltpu.VMEM(shape, jnp.float32) for shape in scratch],
        compiler_params=pltpu.CompilerParams(vmem_limit_bytes=held + 4 * 2**20),
        cost_estimate=pl.CostEstimate(flops=flops, bytes_accessed=moved, transcendentals=0),
    )(*scalars, *arrays, *after)


def pair_up(array, groups, flip):
    return lax.ppermute(array, "gz", [(i, i ^ flip) for i in range(groups)])


def step_by(array, groups, distance):
    return lax.ppermute(
        array, "gz", [(i, i + distance) for i in range(groups) if 0 <= i + distance < groups]
    )


def body(source, layer_ids, conduct_table, shift):
    planes, length_x, length_y = source.shape[1:]
    groups = lax.axis_size("gz")
    blocks = groups // GROUP
    levels = blocks.bit_length() - 1
    count = GROUP * planes
    length_z = planes * groups
    full = length_x // RADIX
    short = full // (HALVES * CHUNKS)
    rows = 2 * short
    if blocks < 2 or groups != GROUP << levels or planes > 2 or short % 8 or length_x != RADIX * full:
        raise ValueError("unsupported layout")
    me = lax.axis_index("gz")
    member = me % GROUP
    flags = jnp.stack([member % RADIX, member // RADIX, me // GROUP, member]).astype(jnp.int32)

    wave = wave_tables(length_x)
    wave_f = jnp.asarray(np.concatenate(two_terms(wave), axis=1))
    wave_b = jnp.asarray(np.concatenate(two_terms(np.swapaxes(wave, 1, 2) / length_x), axis=1))
    sine = jnp.asarray(two_terms(sine_table(length_y)))
    wave_eig = np.broadcast_to(wave_eigen(length_x)[:, :, None], (RADIX, full, length_y))
    wave_eig = jnp.asarray(np.ascontiguousarray(wave_eig).astype(np.float32))
    sine_eig = jnp.asarray(np.tile(sine_eigen(length_y)[None, :], (8, 1)).astype(np.float32))

    chunks = range(CHUNKS)
    row_block = (TAG, length_y)
    block = (count * rows, length_y)
    sums_block = (2 * rows + TAG, length_y)
    single = (rows + TAG, length_y)
    chip_part = (CORES * planes * rows + TAG, length_y)
    swap_part = (CHIPS * planes * rows + TAG, length_y)
    give_part = (CHIPS * (planes * rows + TAG), length_y)
    gives = [single] if levels == 1 else []
    dots = 6 * length_y * length_y

    parted = source.reshape(2, planes, RADIX, full, length_y)
    spectra = {}
    placed = []
    for pair in ((2, 3), (0, 1)):
        *made, _ = call(
            functools.partial(forward_kernel, pair), [flags, conduct_table], [parted, wave_f, layer_ids],
            [chip_part] * (HALVES * CHUNKS) + [row_block],
            scratch=[(len(pair), planes, 2 * full, length_y)], flops=2 * planes * 2 * full * dots, after=placed,
        )
        placed = made[:1]
        for n in range(HALVES):
            for t in chunks:
                spectra[pair[0] // CORES + CORES * n, t] = made[n * CHUNKS + t]
    def send(t, after):
        for e in (3, 1, 2):
            held = lax.optimization_barrier((spectra[e, t], *after))[0] if after else spectra[e, t]
            spectra[e, t] = pair_up(held, groups, CORES * e)

    send(0, [])

    state = [{} for _ in chunks]

    def exchange(st, after):
        sums, give = st["sums"][0], st["sums"][-1]
        st["came"], st["tags"] = [], []
        for level in range(levels):
            st["came"].append(pair_up(give, groups, GROUP << level))
            if level + 1 < levels:
                shape = single if level + 2 == levels else sums_block
                (give,) = call(
                    functools.partial(join_kernel, level, levels), [flags], [sums, st["came"][-1], st["base"]],
                    [shape], after=after,
                )
                sums = give
                st["tags"] = [give[-TAG:]]

    def swap(t, after):
        st = state[t]
        if t:
            send(t, state[0]["extra"])
        st["parts"] = [spectra[e, t] for e in range(CHIPS)]
        give, tags = call(give_kernel, [], st["parts"], [give_part, (CHIPS * TAG, length_y)], after=after)
        st["parts"].append(pair_up(give, groups, 1))
        if t:
            return [give]
        if levels == 1:
            st["extra"] = [pair_up(tags, groups, GROUP + core) for core in range(CORES)]
            return [give]
        (total,) = call(
            functools.partial(summary_kernel, planes), [flags], st["parts"], [row_block],
            scratch=[(count, length_y)],
        )
        st["extra"] = [step_by(total, groups, GROUP), step_by(total, groups, -GROUP)]
        for level in range(levels):
            (total,) = call(add_kernel, [], [total, pair_up(total, groups, GROUP << level)], [row_block])
        st["extra"] = [total, *st["extra"]]
        return [total]

    def start(t, after):
        st = state[t]
        outs = [block, block, (6, rows, length_y), sums_block, *gives]
        made = call(
            functools.partial(start_kernel, t, planes, blocks, length_y * length_z),
            [flags, state[0]["numbers"] if t else shift],
            [wave_eig, sine_eig, sine, *st["parts"], *st.get("extra", [])],
            outs if t else [*outs, (6,)], flops=count * rows * dots, after=after,
        )
        if not t:
            *made, st["numbers"] = made
        st["field"], st["modes"], st["base"], *st["sums"] = made
        exchange(st, [])
        return [st["sums"][-1]]

    def faces(t, after):
        state[t]["faces"] = call(
            functools.partial(faces_kernel, planes, blocks), [flags],
            [*state[t]["parts"], *state[t]["extra"]], [(6, count, length_y)],
            scratch=[(count + 16, length_y), (count, length_y)], after=after,
        )[0]
        return [state[t]["faces"]]

    def factors(t, after):
        st = state[t]
        (st["factors"],) = call(
            functools.partial(factors_kernel, t, count, levels), [flags, state[0]["numbers"]],
            [wave_eig, sine_eig, st["base"]], [(4 + count + levels - 1, rows, length_y)], after=after,
        )
        return [st["factors"]]

    def middle(t, after):
        st = state[t]
        st["found"], st["modes"], *st["sums"] = call(
            functools.partial(middle_kernel, t, count, levels), [flags, state[0]["numbers"]],
            [wave_eig, sine, state[0]["faces"], st["field"], st["modes"], st["base"], st["factors"], st["sums"][0], *st["came"]],
            [block, block, sums_block, *gives], scratch=[((count + 2) * rows, length_y)],
            flops=(2 * count + 2) * rows * dots, after=after,
        )
        exchange(st, [])
        return [st["sums"][-1]]

    def end(t, after):
        st = state[t]
        after = [*after, *(state[t - 1]["answers"][1:] if t else [])]
        st["keep"], give = call(
            functools.partial(end_kernel, count, levels), [flags, state[0]["numbers"]],
            [sine, st["found"], st["modes"], st["base"], st["factors"], st["sums"][0], *st["came"], *st["tags"]],
            [swap_part] * CORES, scratch=[block], flops=count * rows * dots, after=after,
        )
        st["swapped"] = pair_up(give, groups, 1)
        return [st["keep"]]

    def merge(t, after):
        st = state[t]
        st["answers"] = call(merge_kernel, [], [st["keep"], st["swapped"]], [chip_part] * CHIPS, after=after)
        placed = st["answers"][:1]
        st["answers"] = [pair_up(a, groups, CORES * e) if e else a for e, a in enumerate(st["answers"])]
        return placed

    for step, t in (
        (swap, 0), (start, 0), (factors, 0), (faces, 0), (middle, 0), (swap, 1), (end, 0), (start, 1),
        (factors, 1), (merge, 0), (middle, 1), (end, 1), (merge, 1),
    ):
        placed = step(t, placed)
    return call(
        functools.partial(backward_kernel, planes, length_x * length_x * length_y * length_z),
        [flags], [wave_b] + [a for st in state for a in st["answers"]],
        [(2, planes, length_x, length_y), (2,)],
        scratch=[(planes, RADIX, 2 * full, length_y), (RADIX, planes, 2 * full, length_y)],
        flops=planes * RADIX * 2 * full * dots,
    )


def solution(mesh):
    placed = (P(None, ("node", "gz"), None, None), P(("node", "gz"), None), P(), P("node"))
    return jax.shard_map(
        body,
        mesh=mesh,
        in_specs=placed,
        out_specs=(P(None, ("node", "gz"), None, None), P("node")),
        check_vma=False,
    )
```

```python
import functools

import jax
import jax.numpy as jnp
import ml_dtypes
import numpy as np
from jax import lax
from jax.experimental import pallas as pl
from jax.experimental.pallas import tpu as pltpu
from jax.sharding import PartitionSpec as P

RADIX = 4
HALVES = 2
GROUP = RADIX * HALVES
CHUNKS = 2
CORES = 2
CHIPS = GROUP // CORES
TAG = 8

relax = 0.6


def sine_table(length):
    indices = np.arange(1, length + 1)
    product = indices[:, None] * indices[None, :] % (2 * (length + 1))
    return np.sqrt(2.0 / (length + 1)) * np.sin(np.pi / (length + 1) * product)


def sine_eigen(length):
    indices = np.arange(1, length + 1)
    return 4.0 * np.sin(np.pi / (2 * (length + 1)) * indices) ** 2


def wave_numbers(length):
    return RADIX * np.arange(length // RADIX)[None, :] + np.arange(RADIX)[:, None]


def wave_eigen(length):
    return 4.0 * np.sin(np.pi / length * wave_numbers(length)) ** 2


def wave_tables(length):
    waves = wave_numbers(length)
    short = length // RADIX
    product = waves[:, :, None] * np.arange(short)[None, None, :] % length
    angles = 2.0 * np.pi / length * product
    cos_t, sin_t = np.cos(angles), np.sin(angles)
    pieces = HALVES * CHUNKS
    top = np.concatenate([cos_t, sin_t], axis=2).reshape(RADIX, pieces, short // pieces, 2 * short)
    low = np.concatenate([-sin_t, cos_t], axis=2).reshape(RADIX, pieces, short // pieces, 2 * short)
    return np.concatenate([top, low], axis=2).reshape(RADIX, 2 * short, 2 * short)


def two_terms(table):
    first = table.astype(ml_dtypes.bfloat16)
    return np.stack([first, (table - first.astype(np.float64)).astype(ml_dtypes.bfloat16)])


def split(value):
    first = value.astype(jnp.bfloat16)
    return first, (value - first.astype(jnp.float32)).astype(jnp.bfloat16)


def dot_right(value, table):
    rows = value.shape[0]
    first, second = split(value)
    wide = jnp.dot(jnp.concatenate([first, second], axis=0), table[0], preferred_element_type=jnp.float32)
    return wide[:rows] + (wide[rows:] + jnp.dot(first, table[1], preferred_element_type=jnp.float32))


def dot_left(table, value):
    rows = table.shape[0] // 2
    first, second = split(value)
    wide = jnp.dot(table, first, preferred_element_type=jnp.float32)
    return wide[:rows] + (wide[rows:] + jnp.dot(table[:rows], second, preferred_element_type=jnp.float32))


def cmul(a, b):
    return (a[0] * b[0] - a[1] * b[1], a[0] * b[1] + a[1] * b[0])


def csqr(a):
    cross = a[0] * a[1]
    return ((a[0] - a[1]) * (a[0] + a[1]), cross + cross)


def cpow(a, count):
    result = None
    while count:
        if count & 1:
            result = a if result is None else cmul(result, a)
        count >>= 1
        if count:
            a = csqr(a)
    return result


def cadd(a, b):
    return (a[0] + b[0], a[1] + b[1])


def csub(a, b):
    return (a[0] - b[0], a[1] - b[1])


def cscale(a, scale):
    return (a[0] * scale, a[1] * scale)


def cmore(total, factor, term):
    return cadd(total, cmul(factor, term))


def cinv(a):
    scale = 1.0 / (a[0] * a[0] + a[1] * a[1])
    return (a[0] * scale, -a[1] * scale)


def cone(a):
    return (1.0 - a[0], -a[1])


def cpick(cond, a, b):
    return (jnp.where(cond, a[0], b[0]), jnp.where(cond, a[1], b[1]))


def rows_at(start, rows):
    if isinstance(start, int):
        return pl.ds(start, rows)
    return pl.ds(pl.multiple_of(start, 8), rows)


def load(ref, base, short, row, rows):
    return (ref[rows_at(base + row, rows), :], ref[rows_at(base + short + row, rows), :])


def store(ref, base, short, row, rows, value):
    ref[rows_at(base + row, rows), :] = value[0]
    ref[rows_at(base + short + row, rows), :] = value[1]


def each_strip(count, rows, body):
    def step(i, carry):
        body(pl.multiple_of(i * rows, rows))
        return carry

    steps = count // rows
    lax.fori_loop(0, steps, step, 0, unroll=min(steps, 4))


def squares_of(a):
    return a[0] * a[0] + a[1] * a[1]


def conduct_of(table_ref, ids_ref, out_ref):
    planes = ids_ref.shape[0]
    ids = ids_ref[...]
    cells = jnp.zeros(ids.shape, jnp.float32)
    for layer in range(table_ref.shape[0]):
        cells = jnp.where(ids == layer, table_ref[layer], cells)
    out_ref[...] = jnp.zeros_like(out_ref)
    out_ref[pl.ds(0, planes), :] = cells
    out_ref[pl.ds(TAG - 1, 1), :] = jnp.sum(cells, axis=0, keepdims=True)


def add_kernel(one_ref, two_ref, out_ref):
    out_ref[...] = one_ref[...] + two_ref[...]


def tag_of(ref):
    return ref[pl.ds(ref.shape[0] - TAG, TAG), :]


def member_tags(part_refs, swapped_ref):
    start = (part_refs[0].shape[0] - TAG) // CORES * CHIPS
    tags = {}
    for e, ref in enumerate(part_refs):
        tags[CORES * e] = tag_of(ref)
        tags[CORES * e + 1] = swapped_ref[pl.ds(start + e * TAG, TAG), :]
    return tags


def far_tags(part_refs, swapped_ref, far_refs):
    start = (part_refs[0].shape[0] - TAG) // CORES * CHIPS + CHIPS * TAG
    tags = {}
    for e, ref in enumerate(far_refs):
        tags[CORES * e] = ref[...]
        tags[CORES * e + 1] = swapped_ref[pl.ds(start + e * TAG, TAG), :]
    return tags


def find_numbers(cells_total, shift_ref, tags, out_ref):
    total = None
    for tag in tags:
        row = tag[TAG - 1 :]
        total = row if total is None else total + row
    inv = (1.0 / (jnp.sum(total, axis=1, keepdims=True) * (1.0 / cells_total)))[0, 0]
    out_ref[0] = shift_ref[0] * inv
    out_ref[1] = shift_ref[1] * inv
    out_ref[2] = relax * inv
    out_ref[3] = 0.5 * relax * inv
    out_ref[4] = shift_ref[0]
    out_ref[5] = shift_ref[1]


def place_cells(planes, member, tags, cells_ref, start):
    for d, tag in tags.items():
        for p in range(planes):
            cells_ref[pl.ds(start + (member ^ d) * planes + p, 1), :] = tag[p : p + 1]


def summary_kernel(planes, flags_ref, *refs):
    part_refs, swapped_ref, out_ref, cells_ref = refs[:CHIPS], refs[CHIPS], refs[-2], refs[-1]
    place_cells(planes, flags_ref[3], member_tags(part_refs, swapped_ref), cells_ref, 0)
    out_ref[...] = jnp.zeros_like(out_ref)
    out_ref[pl.ds(0, 1), :] = cells_ref[pl.ds(0, 1), :]
    out_ref[pl.ds(1, 1), :] = cells_ref[pl.ds(GROUP * planes - 1, 1), :]
    out_ref[pl.ds(TAG - 1, 1), :] = jnp.sum(cells_ref[...], axis=0, keepdims=True)


def faces_kernel(planes, blocks, flags_ref, *refs):
    part_refs, swapped_ref, extra_refs = refs[:CHIPS], refs[CHIPS], refs[CHIPS + 1 : -3]
    faces_ref, padded_ref, other_ref = refs[-3:]
    z, member = flags_ref[2], flags_ref[3]
    _, count, width = faces_ref.shape
    place_cells(planes, member, member_tags(part_refs, swapped_ref), padded_ref, 8)
    if blocks == 2:
        place_cells(planes, member, far_tags(part_refs, swapped_ref, extra_refs), other_ref, 0)
        below, above = other_ref[pl.ds(count - 1, 1), :], other_ref[pl.ds(0, 1), :]
    else:
        below, above = extra_refs[1][pl.ds(1, 1), :], extra_refs[2][pl.ds(0, 1), :]
    cells = padded_ref[pl.ds(8, count), :]
    padded_ref[pl.ds(7, 1), :] = jnp.where(z == 0, cells[0:1], below)
    padded_ref[pl.ds(8 + count, 1), :] = jnp.where(z == blocks - 1, cells[count - 1 : count], above)
    lane = lax.broadcasted_iota(jnp.int32, cells.shape, 1)
    last, first = lane == width - 1, lane == 0
    right = 0.5 * (cells + pltpu.roll(cells, width - 1, 1))
    left = 0.5 * (cells + pltpu.roll(cells, 1, 1))
    low = 0.5 * (cells + padded_ref[pl.ds(7, count), :])
    high = 0.5 * (cells + padded_ref[pl.ds(9, count), :])
    faces_ref[0] = jnp.where(last, cells, right) + jnp.where(first, cells, left) + (low + high)
    faces_ref[1] = cells
    faces_ref[2] = jnp.where(last, 0.0, right)
    faces_ref[3] = jnp.where(first, 0.0, left)
    faces_ref[4] = low
    faces_ref[5] = high


def forward_kernel(pair, flags_ref, table_ref, source_ref, wave_ref, ids_ref, *refs):
    out_refs, cells_ref, stage_ref = refs[:-2], refs[-2], refs[-1]
    planes = source_ref.shape[1]
    rows = stage_ref.shape[2] // (HALVES * CHUNKS)
    conduct_of(table_ref, ids_ref, cells_ref)
    for core, distance in enumerate(pair):
        q = flags_ref[0] ^ distance
        sign = (1 - 2 * (q & 1)).astype(jnp.float32)
        turn_re = jnp.where(q == 0, 1.0, jnp.where(q == 2, -1.0, 0.0))
        turn_im = jnp.where(q == 1, 1.0, jnp.where(q == 3, -1.0, 0.0))
        for p in range(planes):
            parts = [[source_ref[c, p, i] for i in range(RADIX)] for c in range(2)]
            even = [parts[c][0] + sign * parts[c][2] for c in range(2)]
            odd = [parts[c][1] + sign * parts[c][3] for c in range(2)]
            mixed = jnp.concatenate(
                [
                    even[0] + (turn_re * odd[0] + turn_im * odd[1]),
                    even[1] + (turn_re * odd[1] - turn_im * odd[0]),
                ],
                axis=0,
            )
            stage_ref[core, p] = dot_left(wave_ref[q], mixed)
            for n in range(HALVES):
                h = flags_ref[1] ^ n
                for t in range(CHUNKS):
                    out_refs[n * CHUNKS + t][pl.ds((core * planes + p) * rows, rows), :] = stage_ref[
                        core, p, rows_at((h * CHUNKS + t) * rows, rows), :
                    ]
    for ref in out_refs:
        ref[pl.ds(ref.shape[0] - TAG, TAG), :] = cells_ref[...]


def give_kernel(*refs):
    part_refs, tag_refs, out_ref = refs[:CHIPS], refs[CHIPS:-1], refs[-1]
    part = (part_refs[0].shape[0] - TAG) // CORES
    for e, ref in enumerate(part_refs):
        out_ref[pl.ds(e * part, part), :] = ref[pl.ds(part, part), :]
    for e, ref in enumerate((*part_refs, *tag_refs)):
        if (CHIPS * part + e * TAG) < out_ref.shape[0]:
            out_ref[pl.ds(CHIPS * part + e * TAG, TAG), :] = tag_of(ref)


def merge_kernel(keep_ref, swapped_ref, *out_refs):
    part = (keep_ref.shape[0] - TAG) // CHIPS
    for e, ref in enumerate(out_refs):
        ref[pl.ds(0, part), :] = keep_ref[pl.ds(e * part, part), :]
        ref[pl.ds(part, part), :] = swapped_ref[pl.ds(e * part, part), :]
        ref[pl.ds(CORES * part, TAG), :] = tag_of(keep_ref) + tag_of(swapped_ref)


def backward_kernel(planes, cells, flags_ref, wave_ref, *refs):
    arrays, (out_ref, norms_ref, mixed_ref, stage_ref) = refs[:-4], refs[-4:]
    part = (arrays[0].shape[0] - TAG) // CORES
    rows = part // planes
    short = rows * CHUNKS * HALVES // 2
    total = None
    for ref in arrays:
        tag = tag_of(ref)
        total = tag if total is None else total + tag
    for d in range(RADIX):
        q = flags_ref[0] ^ d
        for p in range(planes):
            for n in range(HALVES):
                h = flags_ref[1] ^ n
                for t in range(CHUNKS):
                    ref = arrays[t * CHIPS + (d + RADIX * n) // CORES]
                    stage_ref[d, p, rows_at((h * CHUNKS + t) * rows, rows), :] = ref[
                        pl.ds(d % CORES * part + p * rows, rows), :
                    ]
            mixed_ref[p, q] = dot_left(wave_ref[q], stage_ref[d, p])
    for p in range(planes):

        def strip(row):
            zero, one, two, three = [load(mixed_ref.at[p, q], 0, short, row, 8) for q in range(RADIX)]
            even, odd = cadd(zero, two), cadd(one, three)
            even_d, odd_d = csub(zero, two), csub(one, three)
            parts = (
                cadd(even, odd),
                (even_d[0] - odd_d[1], even_d[1] + odd_d[0]),
                csub(even, odd),
                (even_d[0] + odd_d[1], even_d[1] - odd_d[0]),
            )
            for i in range(RADIX):
                for c in range(2):
                    out_ref[c, p, rows_at(i * short + row, 8), :] = parts[i][c]

        each_strip(short, 8, strip)
    norms = jnp.sqrt(jnp.sum(total, axis=1, keepdims=True) * (1.0 / cells))
    for n in range(norms_ref.shape[0]):
        norms_ref[n] = norms[n, 0]


def decay_root(h):
    sq = (h[0] + 0.25 * (h[0] * h[0] - h[1] * h[1]), h[1] + 0.5 * h[0] * h[1])
    size = jnp.sqrt(squares_of(sq))
    root_re = jnp.sqrt(0.5 * (size + sq[0]))
    root = (root_re, 0.5 * sq[1] / root_re)
    return cinv((1.0 + 0.5 * h[0] + root[0], 0.5 * h[1] + root[1])), root


def two_powers(power, z, stacks):
    low = high = None
    bit = 0
    while (1 << bit) < stacks:
        taken = ((z >> bit) & 1) == 1
        if low is None:
            one = (jnp.ones_like(power[0]), jnp.zeros_like(power[0]))
            low, high = cpick(taken, power, one), cpick(taken, one, power)
        else:
            grown = cmul(cpick(taken, low, high), power)
            low, high = cpick(taken, grown, low), cpick(taken, high, grown)
        power = csqr(power)
        bit += 1
    return low, high


def sums_of(planes, rho, cross_f, cross_b):
    ahead = planes[0]
    for a in planes[1:]:
        ahead = cmore(a, rho, ahead)
    behind = planes[-1]
    for a in planes[-2::-1]:
        behind = cmore(a, rho, behind)
    return csub(ahead, cmul(cross_f, behind)), csub(behind, cmul(cross_b, ahead))


def sine_rows(source_ref, target_ref, sine_ref, count):
    sine = (sine_ref[0], sine_ref[1])
    rows = max(n for n in range(16, 641, 16) if count % n == 0)
    for i in range(0, count, rows):
        target_ref[pl.ds(i, rows), :] = dot_right(source_ref[pl.ds(i, rows), :], sine)


def fill_give(z, rows, sums_ref, give_refs):
    for ref in give_refs:
        ref[pl.ds(0, rows), :] = sums_ref[rows_at((z & 1) * rows, rows), :]
        ref[pl.ds(rows, TAG), :] = sums_ref[pl.ds(2 * rows, TAG), :]


def start_kernel(
    chunk, planes, blocks, cells_total, flags_ref, numbers_ref, wave_eig_ref, sine_eig_ref, sine_ref, *refs,
):
    part_refs, swapped_ref, refs = refs[:CHIPS], refs[CHIPS], refs[CHIPS + 1 :]
    if chunk == 0:
        extra_count = CHIPS if blocks == 2 else 3
        extra_refs, refs = refs[:extra_count], refs[extra_count:]
    (field_ref, modes_ref, base_ref, sums_ref), give_refs = refs[:4], refs[4:]
    if chunk == 0:
        shift_ref, numbers_ref, give_refs = numbers_ref, give_refs[-1], give_refs[:-1]
        if blocks == 2:
            tags = list(member_tags(part_refs, swapped_ref).values())
            tags += list(far_tags(part_refs, swapped_ref, extra_refs).values())
        else:
            tags = [extra_refs[0][...]]
        find_numbers(cells_total, shift_ref, tags, numbers_ref)
    q, h, z, member = [flags_ref[n] for n in range(4)]
    rows = base_ref.shape[1]
    part = rows * planes
    short = rows // 2
    count = GROUP * planes
    first_row = (h * CHUNKS + chunk) * short
    for e, ref in enumerate(part_refs):
        field_ref[rows_at((member ^ CORES * e) * part, part), :] = ref[pl.ds(0, part), :]
        field_ref[rows_at((member ^ (CORES * e + 1)) * part, part), :] = swapped_ref[pl.ds(e * part, part), :]
    sine_rows(field_ref, modes_ref, sine_ref, count * rows)
    h_re, h_im = numbers_ref[0], numbers_ref[1]
    sine_eig = sine_eig_ref[...]

    def strip(i, total):
        row = pl.multiple_of(i * 8, 8)
        eigen = wave_eig_ref[q, rows_at(first_row + row, 8), :] + sine_eig
        rho, _ = decay_root((eigen + h_re, jnp.full_like(eigen, h_im)))
        block = cpow(rho, count)
        next_one = cmul(block, rho)
        low, high = two_powers(csqr(block), z, blocks)
        cross_f, cross_b = cmul(next_one, low), cmul(next_one, high)
        for n, value in enumerate((rho, cross_f, cross_b, block, low, high)):
            store(base_ref.at[n], 0, short, row, 8, value)
        found = [load(modes_ref, l * rows, short, row, 8) for l in range(count)]
        ahead, behind = sums_of(found, rho, cross_f, cross_b)
        store(sums_ref, 0, short, row, 8, ahead)
        store(sums_ref, rows, short, row, 8, behind)
        for l in range(count):
            total = total + squares_of(load(field_ref, l * rows, short, row, 8))
        return total

    total = lax.fori_loop(
        0, short // 8, strip, jnp.zeros((8, field_ref.shape[1]), jnp.float32), unroll=2
    )
    sums_ref[pl.ds(2 * rows, TAG), :] = jnp.zeros((TAG, field_ref.shape[1]), jnp.float32)
    sums_ref[pl.ds(2 * rows, 1), :] = jnp.sum(total, axis=0, keepdims=True)
    fill_give(z, rows, sums_ref, give_refs)


def factors_kernel(
    chunk, count, levels, flags_ref, numbers_ref, wave_eig_ref, sine_eig_ref, base_ref, out_ref,
):
    q, h_part, z = flags_ref[0], flags_ref[1], flags_ref[2]
    short = base_ref.shape[1] // 2
    h_re, h_im, scale = numbers_ref[0], numbers_ref[1], numbers_ref[3]
    sine_eig = sine_eig_ref[...]

    def strip(row):
        eigen = wave_eig_ref[q, rows_at((h_part * CHUNKS + chunk) * short + row, 8), :] + sine_eig
        h = (eigen + h_re, jnp.full_like(eigen, h_im))
        rho, _, _, block, low, high = [load(base_ref.at[n], 0, short, row, 8) for n in range(6)]
        half_gap = csub((1.0 + 0.5 * h[0], 0.5 * h[1]), rho)
        wide = cmul(csqr(block), csqr(rho))
        low_w, high_w = cmul(low, wide), cmul(high, wide)
        whole = cscale(cinv(cmul(half_gap, cone(cmul(low, high_w)))), scale)
        turned = cmul(rho, whole)
        values = [
            cmul(cone(high_w), whole), cmul(cone(low), turned),
            cmul(cone(high), turned), cmul(cone(low_w), whole),
        ]
        pivot = (2.0 + h[0], h[1])
        inverse = cinv(pivot)
        values.append(inverse)
        for _ in range(count - 1):
            inverse = cinv(csub(pivot, inverse))
            values.append(inverse)
        near = far = None
        power = block
        for level in range(1, levels):
            taken = ((z >> (level - 1)) & 1) == 1
            if near is None:
                one = (jnp.ones_like(power[0]), jnp.zeros_like(power[0]))
                near, far = cpick(taken, power, one), cpick(taken, one, power)
            else:
                grown = cmul(cpick(taken, near, far), power)
                near, far = cpick(taken, grown, near), cpick(taken, far, grown)
            power = csqr(power)
            values.append(cpick(((z >> level) & 1) == 1, near, far))
        for n, value in enumerate(values):
            store(out_ref.at[n], 0, short, row, 8, value)

    each_strip(short, 8, strip)


def join_kernel(level, levels, flags_ref, sums_ref, came_ref, base_ref, out_ref):
    z = flags_ref[2]
    short = base_ref.shape[1] // 2
    rows = 2 * short
    above = ((z >> level) & 1) == 1
    last = level + 2 == levels
    upper = ((z >> (level + 1)) & 1) == 1

    def strip(row):
        block = load(base_ref.at[3], 0, short, row, 8)
        for _ in range(level):
            block = csqr(block)
        ahead, behind = load(sums_ref, 0, short, row, 8), load(sums_ref, rows, short, row, 8)
        ahead_c, behind_c = load(came_ref, 0, short, row, 8), load(came_ref, rows, short, row, 8)
        joined = cmore(cpick(above, ahead, ahead_c), block, cpick(above, ahead_c, ahead))
        joined_b = cmore(cpick(above, behind_c, behind), block, cpick(above, behind, behind_c))
        if last:
            store(out_ref, 0, short, row, 8, cpick(upper, joined_b, joined))
        else:
            store(out_ref, 0, short, row, 8, joined)
            store(out_ref, rows, short, row, 8, joined_b)

    each_strip(short, 8, strip)
    out_ref[pl.ds(out_ref.shape[0] - TAG, TAG), :] = (
        sums_ref[pl.ds(2 * rows, TAG), :] + came_ref[pl.ds(2 * rows, TAG), :]
    )


def solved(count, levels, z, scale, modes_ref, sums_ref, came_refs, base_ref, factors_ref, row):
    short = base_ref.shape[1] // 2
    rows = 2 * short

    def factor(n):
        return load(factors_ref.at[n], 0, short, row, 8)

    enter_f = enter_b = None
    for level in range(levels):
        above = ((z >> level) & 1) == 1
        base = 0 if level == levels - 1 else jnp.where(above, 0, rows)
        came = load(came_refs[level], base, short, row, 8)
        if level:
            came = cmul(factor(4 + count + level - 1), came)
        nought = (jnp.zeros_like(came[0]), jnp.zeros_like(came[0]))
        now_f, now_b = cpick(above, came, nought), cpick(above, nought, came)
        enter_f = now_f if enter_f is None else cadd(enter_f, now_f)
        enter_b = now_b if enter_b is None else cadd(enter_b, now_b)
    block = load(base_ref.at[3], 0, short, row, 8)
    all_f = cmore(load(sums_ref, 0, short, row, 8), block, enter_f)
    all_b = cmore(load(sums_ref, rows, short, row, 8), block, enter_b)
    below = cmore(cmul(factor(0), enter_f), factor(1), all_b)
    above = cmore(cmul(factor(3), enter_b), factor(2), all_f)
    planes = [cscale(load(modes_ref, l * rows, short, row, 8), scale) for l in range(count)]
    planes[0] = cadd(planes[0], below)
    planes[-1] = cadd(planes[-1], above)
    for l in range(1, count):
        planes[l] = cmore(planes[l], factor(4 + l - 1), planes[l - 1])
    planes[-1] = cmul(factor(4 + count - 1), planes[-1])
    for l in range(count - 2, -1, -1):
        planes[l] = cmul(factor(4 + l), cadd(planes[l], planes[l + 1]))
    return below, planes, above


def middle_kernel(
    chunk, count, levels, flags_ref, numbers_ref, wave_eig_ref, sine_ref, faces_ref, field_ref,
    modes_ref, base_ref, factors_ref, sums_ref, *refs,
):
    came_refs, (found_ref, next_ref, next_sums_ref) = refs[:levels], refs[levels : levels + 3]
    give_refs, work_ref = refs[levels + 3 : -1], refs[-1]
    q, h, z = flags_ref[0], flags_ref[1], flags_ref[2]
    scale, s_re, s_im = numbers_ref[2], numbers_ref[4], numbers_ref[5]
    short = base_ref.shape[1] // 2
    rows = 2 * short
    width = base_ref.shape[2]

    def solve(row):
        below, planes, above = solved(
            count, levels, z, scale, modes_ref, sums_ref, came_refs, base_ref, factors_ref, row
        )
        store(work_ref, 0, short, row, 8, below)
        store(work_ref, (count + 1) * rows, short, row, 8, above)
        for l in range(count):
            store(work_ref, (l + 1) * rows, short, row, 8, planes[l])
            store(found_ref, l * rows, short, row, 8, planes[l])

    each_strip(short, 8, solve)
    sine_rows(work_ref, work_ref, sine_ref, (count + 2) * rows)

    def residual(i, total):
        row = pl.multiple_of(i * 8, 8)
        eigen = wave_eig_ref[q, rows_at((h * CHUNKS + chunk) * short + row, 8), :]
        under = load(work_ref, 0, short, row, 8)
        here = load(work_ref, rows, short, row, 8)
        for l in range(count):
            over = load(work_ref, (l + 2) * rows, short, row, 8)
            diag, cell, right, left, low, high = [faces_ref[n, pl.ds(l, 1), :] for n in range(6)]
            diag = s_re + (diag + cell * eigen)
            value = []
            for c in range(2):
                v = diag * here[c] - right * pltpu.roll(here[c], width - 1, 1)
                v = v - left * pltpu.roll(here[c], 1, 1)
                value.append(v - (low * under[c] + high * over[c]))
            value = (value[0] - s_im * here[1], value[1] + s_im * here[0])
            value = csub(load(field_ref, l * rows, short, row, 8), value)
            total = total + squares_of(value)
            store(work_ref, l * rows, short, row, 8, value)
            under, here = here, over
        return total

    total = lax.fori_loop(0, short // 8, residual, jnp.zeros((8, width), jnp.float32), unroll=2)
    sine_rows(work_ref, next_ref, sine_ref, count * rows)

    def sums(row):
        rho, cross_f, cross_b = [load(base_ref.at[n], 0, short, row, 8) for n in range(3)]
        planes = [load(next_ref, l * rows, short, row, 8) for l in range(count)]
        ahead, behind = sums_of(planes, rho, cross_f, cross_b)
        store(next_sums_ref, 0, short, row, 8, ahead)
        store(next_sums_ref, rows, short, row, 8, behind)

    each_strip(short, 8, sums)
    next_sums_ref[pl.ds(2 * rows, TAG), :] = sums_ref[pl.ds(2 * rows, TAG), :]
    next_sums_ref[pl.ds(2 * rows + 1, 1), :] = jnp.sum(total, axis=0, keepdims=True)
    fill_give(z, rows, next_sums_ref, give_refs)


def end_kernel(
    count, levels, flags_ref, numbers_ref, sine_ref, found_ref, modes_ref, base_ref,
    factors_ref, sums_ref, *refs,
):
    came_refs, out_refs, work_ref = refs[:levels], refs[-1 - CORES : -1], refs[-1]
    z, member = flags_ref[2], flags_ref[3]
    scale = numbers_ref[2]
    short = base_ref.shape[1] // 2
    rows = 2 * short

    def solve(row):
        _, planes, _ = solved(
            count, levels, z, scale, modes_ref, sums_ref, came_refs, base_ref, factors_ref, row
        )
        for l in range(count):
            before = load(found_ref, l * rows, short, row, 8)
            store(work_ref, l * rows, short, row, 8, cadd(before, planes[l]))

    each_strip(short, 8, solve)
    sine_rows(work_ref, work_ref, sine_ref, count * rows)
    part = count // GROUP * rows
    tag_refs = (refs[levels] if levels > 1 else sums_ref, came_refs[-1])
    tag = None
    for ref in tag_refs:
        part_tag = ref[pl.ds(ref.shape[0] - TAG, TAG), :]
        tag = part_tag if tag is None else tag + part_tag
    for core, ref in enumerate(out_refs):
        for e in range(CHIPS):
            ref[pl.ds(e * part, part), :] = work_ref[rows_at((member ^ (CORES * e + core)) * part, part), :]
        ref[pl.ds(CHIPS * part, TAG), :] = tag


smem = pl.BlockSpec(memory_space=pltpu.SMEM)
vmem = pl.BlockSpec(memory_space=pltpu.VMEM)
unread = pl.BlockSpec(memory_space=pl.ANY)


def call(kernel, scalars, arrays, outs, scratch=(), flops=0, after=()):
    out_shape = [jax.ShapeDtypeStruct(shape, jnp.float32) for shape in outs]
    head = len(scalars) + len(arrays)

    def run(*refs):
        kernel(*refs[:head], *refs[head + len(after) :])

    moved = sum(a.size * a.dtype.itemsize for a in arrays) + sum(4 * int(np.prod(s)) for s in outs)
    held = moved + sum(4 * int(np.prod(s)) for s in scratch)
    return pl.pallas_call(
        run,
        out_shape=out_shape,
        in_specs=[smem] * len(scalars) + [vmem] * len(arrays) + [unread] * len(after),
        out_specs=[smem if len(shape) == 1 else vmem for shape in outs],
        scratch_shapes=[pltpu.VMEM(shape, jnp.float32) for shape in scratch],
        compiler_params=pltpu.CompilerParams(vmem_limit_bytes=held + 4 * 2**20),
        cost_estimate=pl.CostEstimate(flops=flops, bytes_accessed=moved, transcendentals=0),
    )(*scalars, *arrays, *after)


def pair_up(array, groups, flip):
    return lax.ppermute(array, "gz", [(i, i ^ flip) for i in range(groups)])


def step_by(array, groups, distance):
    return lax.ppermute(
        array, "gz", [(i, i + distance) for i in range(groups) if 0 <= i + distance < groups]
    )


def body(source, layer_ids, conduct_table, shift):
    planes, length_x, length_y = source.shape[1:]
    groups = lax.axis_size("gz")
    blocks = groups // GROUP
    levels = blocks.bit_length() - 1
    count = GROUP * planes
    length_z = planes * groups
    full = length_x // RADIX
    short = full // (HALVES * CHUNKS)
    rows = 2 * short
    if blocks < 2 or groups != GROUP << levels or planes > 2 or short % 8 or length_x != RADIX * full:
        raise ValueError("unsupported layout")
    me = lax.axis_index("gz")
    member = me % GROUP
    flags = jnp.stack([member % RADIX, member // RADIX, me // GROUP, member]).astype(jnp.int32)

    wave = wave_tables(length_x)
    wave_f = jnp.asarray(np.concatenate(two_terms(wave), axis=1))
    wave_b = jnp.asarray(np.concatenate(two_terms(np.swapaxes(wave, 1, 2) / length_x), axis=1))
    sine = jnp.asarray(two_terms(sine_table(length_y)))
    wave_eig = np.broadcast_to(wave_eigen(length_x)[:, :, None], (RADIX, full, length_y))
    wave_eig = jnp.asarray(np.ascontiguousarray(wave_eig).astype(np.float32))
    sine_eig = jnp.asarray(np.tile(sine_eigen(length_y)[None, :], (8, 1)).astype(np.float32))

    chunks = range(CHUNKS)
    row_block = (TAG, length_y)
    block = (count * rows, length_y)
    sums_block = (2 * rows + TAG, length_y)
    single = (rows + TAG, length_y)
    chip_part = (CORES * planes * rows + TAG, length_y)
    swap_part = (CHIPS * planes * rows + TAG, length_y)
    give_parts = [(CHIPS * planes * rows + TAG * CHIPS * (2 if levels == 1 else 1), length_y)]
    give_parts += [(CHIPS * planes * rows, length_y)] * (CHUNKS - 1)
    gives = [single] if levels == 1 else []
    dots = 6 * length_y * length_y

    parted = source.reshape(2, planes, RADIX, full, length_y)
    spectra = {}
    placed = []
    for pair in ((2, 3), (0, 1)):
        *made, cells = call(
            functools.partial(forward_kernel, pair), [flags, conduct_table], [parted, wave_f, layer_ids],
            [chip_part] * (HALVES * CHUNKS) + [row_block],
            scratch=[(len(pair), planes, 2 * full, length_y)], flops=2 * planes * 2 * full * dots, after=placed,
        )
        placed = made[:1]
        for n in range(HALVES):
            for t in chunks:
                spectra[pair[0] // CORES + CORES * n, t] = made[n * CHUNKS + t]
    def send(array, e, after):
        if after:
            array = lax.optimization_barrier((array, *after))[0]
        return pair_up(array, groups, CORES * e) if e else array

    for e in (3, 1, 2):
        spectra[e, 0] = send(spectra[e, 0], e, [])
    if levels == 1:
        cells = pair_up(cells, groups, GROUP)
        cells = [send(cells, e, []) for e in range(CHIPS)]

    state = [{} for _ in chunks]

    def exchange(st, after):
        sums, give = st["sums"][0], st["sums"][-1]
        st["came"], st["tags"] = [], []
        for level in range(levels):
            st["came"].append(pair_up(give, groups, GROUP << level))
            if level + 1 < levels:
                shape = single if level + 2 == levels else sums_block
                (give,) = call(
                    functools.partial(join_kernel, level, levels), [flags], [sums, st["came"][-1], st["base"]],
                    [shape], after=after,
                )
                sums = give
                st["tags"] = [give[-TAG:]]

    def swap(t, after):
        st = state[t]
        st["parts"] = [spectra[e, t] for e in range(CHIPS)]
        tags = cells if t == 0 and levels == 1 else []
        (give,) = call(give_kernel, [], [*st["parts"], *tags], [give_parts[t]], after=after)
        st["parts"].append(pair_up(give, groups, 1))
        if t == 0:
            st["extra"] = tags
        if t or levels == 1:
            return [give]
        (total,) = call(
            functools.partial(summary_kernel, planes), [flags], st["parts"], [row_block],
            scratch=[(count, length_y)],
        )
        st["extra"] = [step_by(total, groups, GROUP), step_by(total, groups, -GROUP)]
        for level in range(levels):
            (total,) = call(add_kernel, [], [total, pair_up(total, groups, GROUP << level)], [row_block])
        st["extra"] = [total, *st["extra"]]
        return [total]

    def start(t, after):
        st = state[t]
        outs = [block, block, (6, rows, length_y), sums_block, *gives]
        made = call(
            functools.partial(start_kernel, t, planes, blocks, length_y * length_z),
            [flags, state[0]["numbers"] if t else shift],
            [wave_eig, sine_eig, sine, *st["parts"], *st.get("extra", [])],
            outs if t else [*outs, (6,)], flops=count * rows * dots, after=after,
        )
        if not t:
            *made, st["numbers"] = made
        st["field"], st["modes"], st["base"], *st["sums"] = made
        exchange(st, [])
        return [st["sums"][-1]]

    def faces(t, after):
        state[t]["faces"] = call(
            functools.partial(faces_kernel, planes, blocks), [flags],
            [*state[t]["parts"], *state[t]["extra"]], [(6, count, length_y)],
            scratch=[(count + 16, length_y), (count, length_y)], after=after,
        )[0]
        return [state[t]["faces"]]

    def factors(t, after):
        st = state[t]
        (st["factors"],) = call(
            functools.partial(factors_kernel, t, count, levels), [flags, state[0]["numbers"]],
            [wave_eig, sine_eig, st["base"]], [(4 + count + levels - 1, rows, length_y)], after=after,
        )
        return [st["factors"]]

    def middle(t, after):
        st = state[t]
        st["found"], st["modes"], *st["sums"] = call(
            functools.partial(middle_kernel, t, count, levels), [flags, state[0]["numbers"]],
            [wave_eig, sine, state[0]["faces"], st["field"], st["modes"], st["base"], st["factors"], st["sums"][0], *st["came"]],
            [block, block, sums_block, *gives], scratch=[((count + 2) * rows, length_y)],
            flops=(2 * count + 2) * rows * dots, after=after,
        )
        exchange(st, [])
        return [st["sums"][-1]]

    def end(t, after):
        st = state[t]
        if t:
            before = state[t - 1]["answers"]
            after = [*after, before[1], before[3]]
        st["keep"], give = call(
            functools.partial(end_kernel, count, levels), [flags, state[0]["numbers"]],
            [sine, st["found"], st["modes"], st["base"], st["factors"], st["sums"][0], *st["came"], *st["tags"]],
            [swap_part] * CORES, scratch=[block], flops=count * rows * dots, after=after,
        )
        st["swapped"] = pair_up(give, groups, 1)
        return [st["keep"]]

    def merge(t, after):
        st = state[t]
        st["answers"] = call(merge_kernel, [], [st["keep"], st["swapped"]], [chip_part] * CHIPS, after=after)
        placed = st["answers"][:1]
        st["answers"] = list(st["answers"])
        return placed

    def answer(t, e, after):
        st = state[t]
        st["answers"][e] = send(st["answers"][e], e, after)

    placed = swap(0, [])
    for e in (1, 3):
        spectra[e, 1] = send(spectra[e, 1], e, [])
    for step in (start, factors, faces):
        placed = step(0, placed)
    spectra[2, 1] = send(spectra[2, 1], 2, [*placed, *state[0]["came"][:1]])
    placed = middle(0, [*placed, spectra[1, 1]])
    for step, t in ((swap, 1), (end, 0), (start, 1), (factors, 1), (merge, 0)):
        placed = step(t, placed)
    answer(0, 1, [])
    answer(0, 3, state[1]["came"][:1])
    placed = middle(1, placed)
    answer(0, 2, state[1]["came"][:1])
    placed = end(1, placed)
    merge(1, placed)
    for e in (3, 1, 2):
        answer(1, e, [])
    return call(
        functools.partial(backward_kernel, planes, length_x * length_x * length_y * length_z),
        [flags], [wave_b] + [a for st in state for a in st["answers"]],
        [(2, planes, length_x, length_y), (2,)],
        scratch=[(planes, RADIX, 2 * full, length_y), (RADIX, planes, 2 * full, length_y)],
        flops=planes * RADIX * 2 * full * dots,
    )


def solution(mesh):
    placed = (P(None, ("node", "gz"), None, None), P(("node", "gz"), None), P(), P("node"))
    return jax.shard_map(
        body,
        mesh=mesh,
        in_specs=placed,
        out_specs=(P(None, ("node", "gz"), None, None), P("node")),
        check_vma=False,
    )
```

```python
import functools

import jax
import jax.numpy as jnp
import ml_dtypes
import numpy as np
from jax import lax
from jax.experimental import pallas as pl
from jax.experimental.pallas import tpu as pltpu
from jax.sharding import PartitionSpec as P

RADIX = 4
HALVES = 2
GROUP = RADIX * HALVES
CHUNKS = 2
SENDS = ((6, 7, 2, 4, 3, 5, 1, 0), (2, 6, 7, 3, 4, 5, 1, 0))
TAG = 8

relax = 0.6


def sine_table(length):
    indices = np.arange(1, length + 1)
    product = indices[:, None] * indices[None, :] % (2 * (length + 1))
    return np.sqrt(2.0 / (length + 1)) * np.sin(np.pi / (length + 1) * product)


def sine_eigen(length):
    indices = np.arange(1, length + 1)
    return 4.0 * np.sin(np.pi / (2 * (length + 1)) * indices) ** 2


def wave_numbers(length):
    return RADIX * np.arange(length // RADIX)[None, :] + np.arange(RADIX)[:, None]


def wave_eigen(length):
    return 4.0 * np.sin(np.pi / length * wave_numbers(length)) ** 2


def wave_tables(length):
    waves = wave_numbers(length)
    short = length // RADIX
    product = waves[:, :, None] * np.arange(short)[None, None, :] % length
    angles = 2.0 * np.pi / length * product
    cos_t, sin_t = np.cos(angles), np.sin(angles)
    pieces = HALVES * CHUNKS
    top = np.concatenate([cos_t, sin_t], axis=2).reshape(RADIX, pieces, short // pieces, 2 * short)
    low = np.concatenate([-sin_t, cos_t], axis=2).reshape(RADIX, pieces, short // pieces, 2 * short)
    return np.concatenate([top, low], axis=2).reshape(RADIX, 2 * short, 2 * short)


def two_terms(table):
    first = table.astype(ml_dtypes.bfloat16)
    return np.stack([first, (table - first.astype(np.float64)).astype(ml_dtypes.bfloat16)])


def split(value):
    first = value.astype(jnp.bfloat16)
    return first, (value - first.astype(jnp.float32)).astype(jnp.bfloat16)


def dot_right(value, table):
    rows = value.shape[0]
    first, second = split(value)
    wide = jnp.dot(jnp.concatenate([first, second], axis=0), table[0], preferred_element_type=jnp.float32)
    return wide[:rows] + (wide[rows:] + jnp.dot(first, table[1], preferred_element_type=jnp.float32))


def dot_left(table, value):
    rows = table.shape[0] // 2
    first, second = split(value)
    wide = jnp.dot(table, first, preferred_element_type=jnp.float32)
    return wide[:rows] + (wide[rows:] + jnp.dot(table[:rows], second, preferred_element_type=jnp.float32))


def cmul(a, b):
    return (a[0] * b[0] - a[1] * b[1], a[0] * b[1] + a[1] * b[0])


def csqr(a):
    cross = a[0] * a[1]
    return ((a[0] - a[1]) * (a[0] + a[1]), cross + cross)


def cpow(a, count):
    result = None
    while count:
        if count & 1:
            result = a if result is None else cmul(result, a)
        count >>= 1
        if count:
            a = csqr(a)
    return result


def cadd(a, b):
    return (a[0] + b[0], a[1] + b[1])


def csub(a, b):
    return (a[0] - b[0], a[1] - b[1])


def cscale(a, scale):
    return (a[0] * scale, a[1] * scale)


def cmore(total, factor, term):
    return cadd(total, cmul(factor, term))


def cinv(a):
    scale = 1.0 / (a[0] * a[0] + a[1] * a[1])
    return (a[0] * scale, -a[1] * scale)


def cone(a):
    return (1.0 - a[0], -a[1])


def cpick(cond, a, b):
    return (jnp.where(cond, a[0], b[0]), jnp.where(cond, a[1], b[1]))


def rows_at(start, rows):
    if isinstance(start, int):
        return pl.ds(start, rows)
    return pl.ds(pl.multiple_of(start, 8), rows)


def load(ref, base, short, row, rows):
    return (ref[rows_at(base + row, rows), :], ref[rows_at(base + short + row, rows), :])


def store(ref, base, short, row, rows, value):
    ref[rows_at(base + row, rows), :] = value[0]
    ref[rows_at(base + short + row, rows), :] = value[1]


def each_strip(count, rows, body):
    def step(i, carry):
        body(pl.multiple_of(i * rows, rows))
        return carry

    steps = count // rows
    lax.fori_loop(0, steps, step, 0, unroll=min(steps, 4))


def squares_of(a):
    return a[0] * a[0] + a[1] * a[1]


def conduct_kernel(table_ref, ids_ref, out_ref):
    planes = ids_ref.shape[0]
    ids = ids_ref[...]
    cells = jnp.zeros(ids.shape, jnp.float32)
    for layer in range(table_ref.shape[0]):
        cells = jnp.where(ids == layer, table_ref[layer], cells)
    out_ref[...] = jnp.zeros_like(out_ref)
    out_ref[pl.ds(0, planes), :] = cells
    out_ref[pl.ds(TAG - 1, 1), :] = jnp.sum(cells, axis=0, keepdims=True)


def add_kernel(one_ref, two_ref, out_ref):
    out_ref[...] = one_ref[...] + two_ref[...]


def fill_tag(out_ref, planes, own_ref, below_ref, above_ref, part_refs):
    start = out_ref.shape[0] - TAG
    for n, ref in enumerate((own_ref, below_ref, above_ref)):
        out_ref[pl.ds(start + n * planes, planes), :] = ref[pl.ds(0, planes), :]
    total = part_refs[0][pl.ds(TAG - 1, 1), :]
    for ref in part_refs[1:]:
        total = total + ref[pl.ds(TAG - 1, 1), :]
    out_ref[pl.ds(start + TAG - 1, 1), :] = total


def tag_of(ref):
    return ref[pl.ds(ref.shape[0] - TAG, TAG), :]


def find_numbers(cells_total, shift_ref, part_refs, numbers_ref):
    total = None
    for ref in part_refs:
        row = ref[pl.ds(ref.shape[0] - 1, 1), :]
        total = row if total is None else total + row
    inv = (1.0 / (jnp.sum(total, axis=1, keepdims=True) * (1.0 / cells_total)))[0, 0]
    numbers_ref[0] = shift_ref[0] * inv
    numbers_ref[1] = shift_ref[1] * inv
    numbers_ref[2] = relax * inv
    numbers_ref[3] = 0.5 * relax * inv
    numbers_ref[4] = shift_ref[0]
    numbers_ref[5] = shift_ref[1]


def faces_kernel(planes, blocks, flags_ref, *refs):
    part_refs, (faces_ref, padded_ref, below_ref, above_ref) = refs[:GROUP], refs[GROUP:]
    z, member = flags_ref[2], flags_ref[3]
    _, count, width = faces_ref.shape
    for d, ref in enumerate(part_refs):
        tag = tag_of(ref)
        place = member ^ d
        for p in range(planes):
            padded_ref[pl.ds(8 + place * planes + p, 1), :] = tag[p : p + 1]
        below_ref[pl.ds(place, 1), :] = tag[2 * planes - 1 : 2 * planes]
        above_ref[pl.ds(place, 1), :] = tag[2 * planes : 2 * planes + 1]
    cells = padded_ref[pl.ds(8, count), :]
    padded_ref[pl.ds(7, 1), :] = jnp.where(z == 0, cells[0:1], below_ref[pl.ds(GROUP - 1, 1), :])
    padded_ref[pl.ds(8 + count, 1), :] = jnp.where(
        z == blocks - 1, cells[count - 1 : count], above_ref[pl.ds(0, 1), :]
    )
    lane = lax.broadcasted_iota(jnp.int32, cells.shape, 1)
    last, first = lane == width - 1, lane == 0
    right = 0.5 * (cells + pltpu.roll(cells, width - 1, 1))
    left = 0.5 * (cells + pltpu.roll(cells, 1, 1))
    low = 0.5 * (cells + padded_ref[pl.ds(7, count), :])
    high = 0.5 * (cells + padded_ref[pl.ds(9, count), :])
    faces_ref[0] = jnp.where(last, cells, right) + jnp.where(first, cells, left) + (low + high)
    faces_ref[1] = cells
    faces_ref[2] = jnp.where(last, 0.0, right)
    faces_ref[3] = jnp.where(first, 0.0, left)
    faces_ref[4] = low
    faces_ref[5] = high


def forward_kernel(distance, parts_count, flags_ref, source_ref, wave_ref, own_ref, below_ref, above_ref, *refs):
    part_refs, out_refs, stage_ref = refs[:parts_count], refs[parts_count:-1], refs[-1]
    planes = source_ref.shape[1]
    q = flags_ref[0] ^ distance
    sign = (1 - 2 * (q & 1)).astype(jnp.float32)
    turn_re = jnp.where(q == 0, 1.0, jnp.where(q == 2, -1.0, 0.0))
    turn_im = jnp.where(q == 1, 1.0, jnp.where(q == 3, -1.0, 0.0))
    rows = stage_ref.shape[1] // (HALVES * CHUNKS)
    for p in range(planes):
        parts = [[source_ref[c, p, i] for i in range(RADIX)] for c in range(2)]
        even = [parts[c][0] + sign * parts[c][2] for c in range(2)]
        odd = [parts[c][1] + sign * parts[c][3] for c in range(2)]
        mixed = jnp.concatenate(
            [
                even[0] + (turn_re * odd[0] + turn_im * odd[1]),
                even[1] + (turn_re * odd[1] - turn_im * odd[0]),
            ],
            axis=0,
        )
        stage_ref[p] = dot_left(wave_ref[q], mixed)
        for n in range(HALVES):
            h = flags_ref[1] ^ n
            for t in range(CHUNKS):
                out_refs[n * CHUNKS + t][pl.ds(p * rows, rows), :] = stage_ref[
                    p, rows_at((h * CHUNKS + t) * rows, rows), :
                ]
    for ref in out_refs:
        fill_tag(ref, planes, own_ref, below_ref, above_ref, part_refs)


def backward_kernel(planes, cells, flags_ref, wave_ref, *refs):
    arrays, (out_ref, norms_ref, mixed_ref, stage_ref) = refs[:-4], refs[-4:]
    came = {(d, t): arrays[t * GROUP + n] for t in range(CHUNKS) for n, d in enumerate(SENDS[t])}
    rows = (arrays[0].shape[0] - TAG) // planes
    short = rows * CHUNKS * HALVES // 2
    total = None
    for ref in arrays:
        tag = ref[pl.ds(planes * rows, TAG), :]
        total = tag if total is None else total + tag
    for d in range(RADIX):
        q = flags_ref[0] ^ d
        for p in range(planes):
            for n in range(HALVES):
                h = flags_ref[1] ^ n
                for t in range(CHUNKS):
                    stage_ref[d, p, rows_at((h * CHUNKS + t) * rows, rows), :] = came[d + RADIX * n, t][
                        pl.ds(p * rows, rows), :
                    ]
            mixed_ref[p, q] = dot_left(wave_ref[q], stage_ref[d, p])
    for p in range(planes):

        def strip(row):
            zero, one, two, three = [load(mixed_ref.at[p, q], 0, short, row, 8) for q in range(RADIX)]
            even, odd = cadd(zero, two), cadd(one, three)
            even_d, odd_d = csub(zero, two), csub(one, three)
            parts = (
                cadd(even, odd),
                (even_d[0] - odd_d[1], even_d[1] + odd_d[0]),
                csub(even, odd),
                (even_d[0] + odd_d[1], even_d[1] - odd_d[0]),
            )
            for i in range(RADIX):
                for c in range(2):
                    out_ref[c, p, rows_at(i * short + row, 8), :] = parts[i][c]

        each_strip(short, 8, strip)
    norms = jnp.sqrt(jnp.sum(total, axis=1, keepdims=True) * (1.0 / cells))
    for n in range(norms_ref.shape[0]):
        norms_ref[n] = norms[n, 0]


def decay_root(h):
    sq = (h[0] + 0.25 * (h[0] * h[0] - h[1] * h[1]), h[1] + 0.5 * h[0] * h[1])
    size = jnp.sqrt(squares_of(sq))
    root_re = jnp.sqrt(0.5 * (size + sq[0]))
    root = (root_re, 0.5 * sq[1] / root_re)
    return cinv((1.0 + 0.5 * h[0] + root[0], 0.5 * h[1] + root[1])), root


def two_powers(power, z, stacks):
    low = high = None
    bit = 0
    while (1 << bit) < stacks:
        taken = ((z >> bit) & 1) == 1
        if low is None:
            one = (jnp.ones_like(power[0]), jnp.zeros_like(power[0]))
            low, high = cpick(taken, power, one), cpick(taken, one, power)
        else:
            grown = cmul(cpick(taken, low, high), power)
            low, high = cpick(taken, grown, low), cpick(taken, high, grown)
        power = csqr(power)
        bit += 1
    return low, high


def sums_of(planes, rho, cross_f, cross_b):
    ahead = planes[0]
    for a in planes[1:]:
        ahead = cmore(a, rho, ahead)
    behind = planes[-1]
    for a in planes[-2::-1]:
        behind = cmore(a, rho, behind)
    return csub(ahead, cmul(cross_f, behind)), csub(behind, cmul(cross_b, ahead))


def sine_rows(source_ref, target_ref, sine_ref, count):
    sine = (sine_ref[0], sine_ref[1])
    rows = max(n for n in range(16, 641, 16) if count % n == 0)
    for i in range(0, count, rows):
        target_ref[pl.ds(i, rows), :] = dot_right(source_ref[pl.ds(i, rows), :], sine)


def fill_give(z, rows, sums_ref, give_refs):
    for ref in give_refs:
        ref[pl.ds(0, rows), :] = sums_ref[rows_at((z & 1) * rows, rows), :]
        ref[pl.ds(rows, TAG), :] = sums_ref[pl.ds(2 * rows, TAG), :]


def start_kernel(
    chunk, planes, blocks, cells_total, flags_ref, numbers_ref, wave_eig_ref, sine_eig_ref, sine_ref, *refs,
):
    part_refs, (field_ref, modes_ref, base_ref, sums_ref), give_refs = refs[:GROUP], refs[GROUP : GROUP + 4], refs[GROUP + 4 :]
    if chunk == 0:
        shift_ref, numbers_ref, give_refs = numbers_ref, give_refs[-1], give_refs[:-1]
        find_numbers(cells_total, shift_ref, part_refs, numbers_ref)
    q, h, z, member = [flags_ref[n] for n in range(4)]
    rows = base_ref.shape[1]
    part = rows * planes
    short = rows // 2
    count = GROUP * planes
    first_row = (h * CHUNKS + chunk) * short
    for d, ref in enumerate(part_refs):
        field_ref[rows_at((member ^ d) * part, part), :] = ref[pl.ds(0, part), :]
    sine_rows(field_ref, modes_ref, sine_ref, count * rows)
    h_re, h_im = numbers_ref[0], numbers_ref[1]
    sine_eig = sine_eig_ref[...]

    def strip(i, total):
        row = pl.multiple_of(i * 8, 8)
        eigen = wave_eig_ref[q, rows_at(first_row + row, 8), :] + sine_eig
        rho, _ = decay_root((eigen + h_re, jnp.full_like(eigen, h_im)))
        block = cpow(rho, count)
        next_one = cmul(block, rho)
        low, high = two_powers(csqr(block), z, blocks)
        cross_f, cross_b = cmul(next_one, low), cmul(next_one, high)
        for n, value in enumerate((rho, cross_f, cross_b, block, low, high)):
            store(base_ref.at[n], 0, short, row, 8, value)
        found = [load(modes_ref, l * rows, short, row, 8) for l in range(count)]
        ahead, behind = sums_of(found, rho, cross_f, cross_b)
        store(sums_ref, 0, short, row, 8, ahead)
        store(sums_ref, rows, short, row, 8, behind)
        for l in range(count):
            total = total + squares_of(load(field_ref, l * rows, short, row, 8))
        return total

    total = lax.fori_loop(
        0, short // 8, strip, jnp.zeros((8, field_ref.shape[1]), jnp.float32), unroll=2
    )
    sums_ref[pl.ds(2 * rows, TAG), :] = jnp.zeros((TAG, field_ref.shape[1]), jnp.float32)
    sums_ref[pl.ds(2 * rows, 1), :] = jnp.sum(total, axis=0, keepdims=True)
    fill_give(z, rows, sums_ref, give_refs)


def factors_kernel(
    chunk, count, levels, flags_ref, numbers_ref, wave_eig_ref, sine_eig_ref, base_ref, out_ref,
):
    q, h_part, z = flags_ref[0], flags_ref[1], flags_ref[2]
    short = base_ref.shape[1] // 2
    h_re, h_im, scale = numbers_ref[0], numbers_ref[1], numbers_ref[3]
    sine_eig = sine_eig_ref[...]

    def strip(row):
        eigen = wave_eig_ref[q, rows_at((h_part * CHUNKS + chunk) * short + row, 8), :] + sine_eig
        h = (eigen + h_re, jnp.full_like(eigen, h_im))
        rho, _, _, block, low, high = [load(base_ref.at[n], 0, short, row, 8) for n in range(6)]
        half_gap = csub((1.0 + 0.5 * h[0], 0.5 * h[1]), rho)
        wide = cmul(csqr(block), csqr(rho))
        low_w, high_w = cmul(low, wide), cmul(high, wide)
        whole = cscale(cinv(cmul(half_gap, cone(cmul(low, high_w)))), scale)
        turned = cmul(rho, whole)
        values = [
            cmul(cone(high_w), whole), cmul(cone(low), turned),
            cmul(cone(high), turned), cmul(cone(low_w), whole),
        ]
        pivot = (2.0 + h[0], h[1])
        inverse = cinv(pivot)
        values.append(inverse)
        for _ in range(count - 1):
            inverse = cinv(csub(pivot, inverse))
            values.append(inverse)
        near = far = None
        power = block
        for level in range(1, levels):
            taken = ((z >> (level - 1)) & 1) == 1
            if near is None:
                one = (jnp.ones_like(power[0]), jnp.zeros_like(power[0]))
                near, far = cpick(taken, power, one), cpick(taken, one, power)
            else:
                grown = cmul(cpick(taken, near, far), power)
                near, far = cpick(taken, grown, near), cpick(taken, far, grown)
            power = csqr(power)
            values.append(cpick(((z >> level) & 1) == 1, near, far))
        for n, value in enumerate(values):
            store(out_ref.at[n], 0, short, row, 8, value)

    each_strip(short, 8, strip)


def join_kernel(level, levels, flags_ref, sums_ref, came_ref, base_ref, out_ref):
    z = flags_ref[2]
    short = base_ref.shape[1] // 2
    rows = 2 * short
    above = ((z >> level) & 1) == 1
    last = level + 2 == levels
    upper = ((z >> (level + 1)) & 1) == 1

    def strip(row):
        block = load(base_ref.at[3], 0, short, row, 8)
        for _ in range(level):
            block = csqr(block)
        ahead, behind = load(sums_ref, 0, short, row, 8), load(sums_ref, rows, short, row, 8)
        ahead_c, behind_c = load(came_ref, 0, short, row, 8), load(came_ref, rows, short, row, 8)
        joined = cmore(cpick(above, ahead, ahead_c), block, cpick(above, ahead_c, ahead))
        joined_b = cmore(cpick(above, behind_c, behind), block, cpick(above, behind, behind_c))
        if last:
            store(out_ref, 0, short, row, 8, cpick(upper, joined_b, joined))
        else:
            store(out_ref, 0, short, row, 8, joined)
            store(out_ref, rows, short, row, 8, joined_b)

    each_strip(short, 8, strip)
    out_ref[pl.ds(out_ref.shape[0] - TAG, TAG), :] = (
        sums_ref[pl.ds(2 * rows, TAG), :] + came_ref[pl.ds(2 * rows, TAG), :]
    )


def solved(count, levels, z, scale, modes_ref, sums_ref, came_refs, base_ref, factors_ref, row):
    short = base_ref.shape[1] // 2
    rows = 2 * short

    def factor(n):
        return load(factors_ref.at[n], 0, short, row, 8)

    enter_f = enter_b = None
    for level in range(levels):
        above = ((z >> level) & 1) == 1
        base = 0 if level == levels - 1 else jnp.where(above, 0, rows)
        came = load(came_refs[level], base, short, row, 8)
        if level:
            came = cmul(factor(4 + count + level - 1), came)
        nought = (jnp.zeros_like(came[0]), jnp.zeros_like(came[0]))
        now_f, now_b = cpick(above, came, nought), cpick(above, nought, came)
        enter_f = now_f if enter_f is None else cadd(enter_f, now_f)
        enter_b = now_b if enter_b is None else cadd(enter_b, now_b)
    block = load(base_ref.at[3], 0, short, row, 8)
    all_f = cmore(load(sums_ref, 0, short, row, 8), block, enter_f)
    all_b = cmore(load(sums_ref, rows, short, row, 8), block, enter_b)
    below = cmore(cmul(factor(0), enter_f), factor(1), all_b)
    above = cmore(cmul(factor(3), enter_b), factor(2), all_f)
    planes = [cscale(load(modes_ref, l * rows, short, row, 8), scale) for l in range(count)]
    planes[0] = cadd(planes[0], below)
    planes[-1] = cadd(planes[-1], above)
    for l in range(1, count):
        planes[l] = cmore(planes[l], factor(4 + l - 1), planes[l - 1])
    planes[-1] = cmul(factor(4 + count - 1), planes[-1])
    for l in range(count - 2, -1, -1):
        planes[l] = cmul(factor(4 + l), cadd(planes[l], planes[l + 1]))
    return below, planes, above


def middle_kernel(
    chunk, count, levels, flags_ref, numbers_ref, wave_eig_ref, sine_ref, faces_ref, field_ref,
    modes_ref, base_ref, factors_ref, sums_ref, *refs,
):
    came_refs, (found_ref, next_ref, next_sums_ref) = refs[:levels], refs[levels : levels + 3]
    give_refs, work_ref = refs[levels + 3 : -1], refs[-1]
    q, h, z = flags_ref[0], flags_ref[1], flags_ref[2]
    scale, s_re, s_im = numbers_ref[2], numbers_ref[4], numbers_ref[5]
    short = base_ref.shape[1] // 2
    rows = 2 * short
    width = base_ref.shape[2]

    def solve(row):
        below, planes, above = solved(
            count, levels, z, scale, modes_ref, sums_ref, came_refs, base_ref, factors_ref, row
        )
        store(work_ref, 0, short, row, 8, below)
        store(work_ref, (count + 1) * rows, short, row, 8, above)
        for l in range(count):
            store(work_ref, (l + 1) * rows, short, row, 8, planes[l])
            store(found_ref, l * rows, short, row, 8, planes[l])

    each_strip(short, 8, solve)
    sine_rows(work_ref, work_ref, sine_ref, (count + 2) * rows)

    def residual(i, total):
        row = pl.multiple_of(i * 8, 8)
        eigen = wave_eig_ref[q, rows_at((h * CHUNKS + chunk) * short + row, 8), :]
        under = load(work_ref, 0, short, row, 8)
        here = load(work_ref, rows, short, row, 8)
        for l in range(count):
            over = load(work_ref, (l + 2) * rows, short, row, 8)
            diag, cell, right, left, low, high = [faces_ref[n, pl.ds(l, 1), :] for n in range(6)]
            diag = s_re + (diag + cell * eigen)
            value = []
            for c in range(2):
                v = diag * here[c] - right * pltpu.roll(here[c], width - 1, 1)
                v = v - left * pltpu.roll(here[c], 1, 1)
                value.append(v - (low * under[c] + high * over[c]))
            value = (value[0] - s_im * here[1], value[1] + s_im * here[0])
            value = csub(load(field_ref, l * rows, short, row, 8), value)
            total = total + squares_of(value)
            store(work_ref, l * rows, short, row, 8, value)
            under, here = here, over
        return total

    total = lax.fori_loop(0, short // 8, residual, jnp.zeros((8, width), jnp.float32), unroll=2)
    sine_rows(work_ref, next_ref, sine_ref, count * rows)

    def sums(row):
        rho, cross_f, cross_b = [load(base_ref.at[n], 0, short, row, 8) for n in range(3)]
        planes = [load(next_ref, l * rows, short, row, 8) for l in range(count)]
        ahead, behind = sums_of(planes, rho, cross_f, cross_b)
        store(next_sums_ref, 0, short, row, 8, ahead)
        store(next_sums_ref, rows, short, row, 8, behind)

    each_strip(short, 8, sums)
    next_sums_ref[pl.ds(2 * rows, TAG), :] = sums_ref[pl.ds(2 * rows, TAG), :]
    next_sums_ref[pl.ds(2 * rows + 1, 1), :] = jnp.sum(total, axis=0, keepdims=True)
    fill_give(z, rows, next_sums_ref, give_refs)


def end_kernel(
    count, levels, flags_ref, numbers_ref, sine_ref, found_ref, modes_ref, base_ref,
    factors_ref, sums_ref, *refs,
):
    came_refs, out_refs, work_ref = refs[:levels], refs[-1 - GROUP : -1], refs[-1]
    z, member = flags_ref[2], flags_ref[3]
    scale = numbers_ref[2]
    short = base_ref.shape[1] // 2
    rows = 2 * short

    def solve(row):
        _, planes, _ = solved(
            count, levels, z, scale, modes_ref, sums_ref, came_refs, base_ref, factors_ref, row
        )
        for l in range(count):
            before = load(found_ref, l * rows, short, row, 8)
            store(work_ref, l * rows, short, row, 8, cadd(before, planes[l]))

    each_strip(short, 8, solve)
    sine_rows(work_ref, work_ref, sine_ref, count * rows)
    part = count // GROUP * rows
    tag_refs = (refs[levels] if levels > 1 else sums_ref, came_refs[-1])
    tag = None
    for ref in tag_refs:
        part_tag = ref[pl.ds(ref.shape[0] - TAG, TAG), :]
        tag = part_tag if tag is None else tag + part_tag
    for d in range(GROUP):
        out_refs[d][pl.ds(0, part), :] = work_ref[rows_at((member ^ d) * part, part), :]
        out_refs[d][pl.ds(part, TAG), :] = tag


smem = pl.BlockSpec(memory_space=pltpu.SMEM)
vmem = pl.BlockSpec(memory_space=pltpu.VMEM)
unread = pl.BlockSpec(memory_space=pl.ANY)


def call(kernel, scalars, arrays, outs, scratch=(), flops=0, after=()):
    out_shape = [jax.ShapeDtypeStruct(shape, jnp.float32) for shape in outs]
    head = len(scalars) + len(arrays)

    def run(*refs):
        kernel(*refs[:head], *refs[head + len(after) :])

    moved = sum(a.size * a.dtype.itemsize for a in arrays) + sum(4 * int(np.prod(s)) for s in outs)
    held = moved + sum(4 * int(np.prod(s)) for s in scratch)
    return pl.pallas_call(
        run,
        out_shape=out_shape,
        in_specs=[smem] * len(scalars) + [vmem] * len(arrays) + [unread] * len(after),
        out_specs=[smem if len(shape) == 1 else vmem for shape in outs],
        scratch_shapes=[pltpu.VMEM(shape, jnp.float32) for shape in scratch],
        compiler_params=pltpu.CompilerParams(vmem_limit_bytes=held + 4 * 2**20),
        cost_estimate=pl.CostEstimate(flops=flops, bytes_accessed=moved, transcendentals=0),
    )(*scalars, *arrays, *after)


def pair_up(array, groups, flip):
    return lax.ppermute(array, "gz", [(i, i ^ flip) for i in range(groups)])


def step_by(array, groups, distance):
    return lax.ppermute(
        array, "gz", [(i, i + distance) for i in range(groups) if 0 <= i + distance < groups]
    )


def body(source, layer_ids, conduct_table, shift):
    planes, length_x, length_y = source.shape[1:]
    groups = lax.axis_size("gz")
    blocks = groups // GROUP
    levels = blocks.bit_length() - 1
    count = GROUP * planes
    length_z = planes * groups
    full = length_x // RADIX
    short = full // (HALVES * CHUNKS)
    rows = 2 * short
    if blocks < 2 or groups != GROUP << levels or planes > 2 or short % 8 or length_x != RADIX * full:
        raise ValueError("unsupported layout")
    me = lax.axis_index("gz")
    member = me % GROUP
    flags = jnp.stack([member % RADIX, member // RADIX, me // GROUP, member]).astype(jnp.int32)

    wave = wave_tables(length_x)
    wave_f = jnp.asarray(np.concatenate(two_terms(wave), axis=1))
    wave_b = jnp.asarray(np.concatenate(two_terms(np.swapaxes(wave, 1, 2) / length_x), axis=1))
    sine = jnp.asarray(two_terms(sine_table(length_y)))
    wave_eig = np.broadcast_to(wave_eigen(length_x)[:, :, None], (RADIX, full, length_y))
    wave_eig = jnp.asarray(np.ascontiguousarray(wave_eig).astype(np.float32))
    sine_eig = jnp.asarray(np.tile(sine_eigen(length_y)[None, :], (8, 1)).astype(np.float32))

    chunks = range(CHUNKS)
    row_block = (TAG, length_y)
    block = (count * rows, length_y)
    sums_block = (2 * rows + TAG, length_y)
    single = (rows + TAG, length_y)
    part = (planes * rows + TAG, length_y)
    gives = [single] if levels == 1 else []
    dots = 6 * length_y * length_y

    (cells,) = call(conduct_kernel, [conduct_table], [layer_ids], [row_block])
    if levels == 1:
        below = above = pair_up(cells, groups, GROUP)
        totals = [cells, below]
    else:
        below = step_by(cells, groups, GROUP)
        above = step_by(cells, groups, -GROUP)
        total = cells
        for level in range(levels):
            (total,) = call(add_kernel, [], [total, pair_up(total, groups, GROUP << level)], [row_block])
        totals = [total]

    parted = source.reshape(2, planes, RADIX, full, length_y)
    spectra = {}
    placed = []
    for d in (2, 0, 3, 1):
        made = call(
            functools.partial(forward_kernel, d, len(totals)), [flags],
            [parted, wave_f, cells, below, above, *totals], [part] * (HALVES * CHUNKS),
            scratch=[(planes, 2 * full, length_y)], flops=planes * 2 * full * dots, after=placed,
        )
        placed = made[:1]
        for n in range(HALVES):
            for t in chunks:
                spectra[d + RADIX * n, t] = made[n * CHUNKS + t]
    for t in chunks:
        for d in (6, 2, 4, 7, 3, 5, 1):
            spectra[d, t] = pair_up(spectra[d, t], groups, d)

    state = [{} for _ in chunks]

    def exchange(st, after):
        sums, give = st["sums"][0], st["sums"][-1]
        st["came"], st["tags"] = [], []
        for level in range(levels):
            st["came"].append(pair_up(give, groups, GROUP << level))
            if level + 1 < levels:
                shape = single if level + 2 == levels else sums_block
                (give,) = call(
                    functools.partial(join_kernel, level, levels), [flags], [sums, st["came"][-1], st["base"]],
                    [shape], after=after,
                )
                sums = give
                st["tags"] = [give[-TAG:]]

    def start(t, after):
        st = state[t]
        outs = [block, block, (6, rows, length_y), sums_block, *gives]
        made = call(
            functools.partial(start_kernel, t, planes, blocks, length_y * length_z),
            [flags, state[0]["numbers"] if t else shift],
            [wave_eig, sine_eig, sine] + [spectra[d, t] for d in range(GROUP)],
            outs if t else [*outs, (6,)], flops=count * rows * dots, after=after,
        )
        if not t:
            *made, st["numbers"] = made
        st["field"], st["modes"], st["base"], *st["sums"] = made
        exchange(st, [])
        return [st["sums"][-1]]

    def faces(t, after):
        state[t]["faces"] = call(
            functools.partial(faces_kernel, planes, blocks), [flags], [spectra[d, 0] for d in range(GROUP)],
            [(6, count, length_y)], scratch=[(count + 16, length_y), row_block, row_block], after=after,
        )[0]
        return [state[t]["faces"]]

    def factors(t, after):
        st = state[t]
        (st["factors"],) = call(
            functools.partial(factors_kernel, t, count, levels), [flags, state[0]["numbers"]],
            [wave_eig, sine_eig, st["base"]], [(4 + count + levels - 1, rows, length_y)], after=after,
        )
        return [st["factors"]]

    def middle(t, after):
        st = state[t]
        st["found"], st["modes"], *st["sums"] = call(
            functools.partial(middle_kernel, t, count, levels), [flags, state[0]["numbers"]],
            [wave_eig, sine, state[0]["faces"], st["field"], st["modes"], st["base"], st["factors"], st["sums"][0], *st["came"]],
            [block, block, sums_block, *gives], scratch=[((count + 2) * rows, length_y)],
            flops=(2 * count + 2) * rows * dots, after=after,
        )
        exchange(st, [])
        return [st["sums"][-1]]

    def end(t, after):
        st = state[t]
        made = call(
            functools.partial(end_kernel, count, levels), [flags, state[0]["numbers"]],
            [sine, st["found"], st["modes"], st["base"], st["factors"], st["sums"][0], *st["came"], *st["tags"]],
            [part] * GROUP, scratch=[block], flops=count * rows * dots, after=after,
        )
        st["answers"] = list(made)
        for d in SENDS[t][:-1]:
            st["answers"][d] = pair_up(made[d], groups, d)
        return made[:1]

    placed = []
    for step, t in (
        (start, 0), (faces, 0), (factors, 0), (middle, 0), (start, 1), (factors, 1), (end, 0), (middle, 1), (end, 1),
    ):
        placed = step(t, placed)
    return call(
        functools.partial(backward_kernel, planes, length_x * length_x * length_y * length_z),
        [flags], [wave_b] + [state[t]["answers"][d] for t in chunks for d in SENDS[t]],
        [(2, planes, length_x, length_y), (2,)],
        scratch=[(planes, RADIX, 2 * full, length_y), (RADIX, planes, 2 * full, length_y)],
        flops=planes * RADIX * 2 * full * dots,
    )


def solution(mesh):
    placed = (P(None, ("node", "gz"), None, None), P(("node", "gz"), None), P(), P("node"))
    return jax.shard_map(
        body,
        mesh=mesh,
        in_specs=placed,
        out_specs=(P(None, ("node", "gz"), None, None), P("node")),
        check_vma=False,
    )
```

```python
import functools

import jax
import jax.numpy as jnp
import ml_dtypes
import numpy as np
from jax import lax
from jax.experimental import pallas as pl
from jax.experimental.pallas import tpu as pltpu
from jax.sharding import PartitionSpec as P

RADIX = 4
HALVES = 2
GROUP = RADIX * HALVES
CHUNKS = 2
SENDS = ((6, 7, 2, 3, 4, 0), (2, 6, 7, 3, 4, 5, 1, 0))
JOINT = (5, 1)
TAG = 8

relax = 0.6


def sine_table(length):
    indices = np.arange(1, length + 1)
    product = indices[:, None] * indices[None, :] % (2 * (length + 1))
    return np.sqrt(2.0 / (length + 1)) * np.sin(np.pi / (length + 1) * product)


def sine_eigen(length):
    indices = np.arange(1, length + 1)
    return 4.0 * np.sin(np.pi / (2 * (length + 1)) * indices) ** 2


def wave_numbers(length):
    return RADIX * np.arange(length // RADIX)[None, :] + np.arange(RADIX)[:, None]


def wave_eigen(length):
    return 4.0 * np.sin(np.pi / length * wave_numbers(length)) ** 2


def wave_tables(length):
    waves = wave_numbers(length)
    short = length // RADIX
    product = waves[:, :, None] * np.arange(short)[None, None, :] % length
    angles = 2.0 * np.pi / length * product
    cos_t, sin_t = np.cos(angles), np.sin(angles)
    pieces = HALVES * CHUNKS
    top = np.concatenate([cos_t, sin_t], axis=2).reshape(RADIX, pieces, short // pieces, 2 * short)
    low = np.concatenate([-sin_t, cos_t], axis=2).reshape(RADIX, pieces, short // pieces, 2 * short)
    return np.concatenate([top, low], axis=2).reshape(RADIX, 2 * short, 2 * short)


def two_terms(table):
    first = table.astype(ml_dtypes.bfloat16)
    return np.stack([first, (table - first.astype(np.float64)).astype(ml_dtypes.bfloat16)])


def split(value):
    first = value.astype(jnp.bfloat16)
    return first, (value - first.astype(jnp.float32)).astype(jnp.bfloat16)


def dot_right(value, table):
    rows = value.shape[0]
    first, second = split(value)
    wide = jnp.dot(jnp.concatenate([first, second], axis=0), table[0], preferred_element_type=jnp.float32)
    return wide[:rows] + (wide[rows:] + jnp.dot(first, table[1], preferred_element_type=jnp.float32))


def dot_left(table, value):
    rows = table.shape[0] // 2
    first, second = split(value)
    wide = jnp.dot(table, first, preferred_element_type=jnp.float32)
    return wide[:rows] + (wide[rows:] + jnp.dot(table[:rows], second, preferred_element_type=jnp.float32))


def cmul(a, b):
    return (a[0] * b[0] - a[1] * b[1], a[0] * b[1] + a[1] * b[0])


def csqr(a):
    cross = a[0] * a[1]
    return ((a[0] - a[1]) * (a[0] + a[1]), cross + cross)


def cpow(a, count):
    result = None
    while count:
        if count & 1:
            result = a if result is None else cmul(result, a)
        count >>= 1
        if count:
            a = csqr(a)
    return result


def cadd(a, b):
    return (a[0] + b[0], a[1] + b[1])


def csub(a, b):
    return (a[0] - b[0], a[1] - b[1])


def cscale(a, scale):
    return (a[0] * scale, a[1] * scale)


def cmore(total, factor, term):
    return cadd(total, cmul(factor, term))


def cinv(a):
    scale = 1.0 / (a[0] * a[0] + a[1] * a[1])
    return (a[0] * scale, -a[1] * scale)


def cone(a):
    return (1.0 - a[0], -a[1])


def cpick(cond, a, b):
    return (jnp.where(cond, a[0], b[0]), jnp.where(cond, a[1], b[1]))


def rows_at(start, rows):
    if isinstance(start, int):
        return pl.ds(start, rows)
    return pl.ds(pl.multiple_of(start, 8), rows)


def load(ref, base, short, row, rows):
    return (ref[rows_at(base + row, rows), :], ref[rows_at(base + short + row, rows), :])


def store(ref, base, short, row, rows, value):
    ref[rows_at(base + row, rows), :] = value[0]
    ref[rows_at(base + short + row, rows), :] = value[1]


def each_strip(count, rows, body):
    def step(i, carry):
        body(pl.multiple_of(i * rows, rows))
        return carry

    steps = count // rows
    lax.fori_loop(0, steps, step, 0, unroll=min(steps, 4))


def squares_of(a):
    return a[0] * a[0] + a[1] * a[1]


def conduct_kernel(table_ref, ids_ref, out_ref):
    planes = ids_ref.shape[0]
    ids = ids_ref[...]
    cells = jnp.zeros(ids.shape, jnp.float32)
    for layer in range(table_ref.shape[0]):
        cells = jnp.where(ids == layer, table_ref[layer], cells)
    out_ref[...] = jnp.zeros_like(out_ref)
    out_ref[pl.ds(0, planes), :] = cells
    out_ref[pl.ds(TAG - 1, 1), :] = jnp.sum(cells, axis=0, keepdims=True)


def ready_kernel(source_ref, wave_ref, out_ref):
    out_ref[...] = source_ref[0, 0, 0, pl.ds(0, TAG), :]


def add_kernel(one_ref, two_ref, out_ref):
    out_ref[...] = one_ref[...] + two_ref[...]


def fill_tag(out_ref, planes, own_ref, below_ref, above_ref, part_refs):
    start = out_ref.shape[0] - TAG
    for n, ref in enumerate((own_ref, below_ref, above_ref)):
        out_ref[pl.ds(start + n * planes, planes), :] = ref[pl.ds(0, planes), :]
    total = part_refs[0][pl.ds(TAG - 1, 1), :]
    for ref in part_refs[1:]:
        total = total + ref[pl.ds(TAG - 1, 1), :]
    out_ref[pl.ds(start + TAG - 1, 1), :] = total


def tag_of(ref):
    return ref[pl.ds(ref.shape[0] - TAG, TAG), :]


def find_numbers(cells_total, shift_ref, part_refs, numbers_ref):
    total = None
    for ref in part_refs:
        row = ref[pl.ds(ref.shape[0] - 1, 1), :]
        total = row if total is None else total + row
    inv = (1.0 / (jnp.sum(total, axis=1, keepdims=True) * (1.0 / cells_total)))[0, 0]
    numbers_ref[0] = shift_ref[0] * inv
    numbers_ref[1] = shift_ref[1] * inv
    numbers_ref[2] = relax * inv
    numbers_ref[3] = 0.5 * relax * inv
    numbers_ref[4] = shift_ref[0]
    numbers_ref[5] = shift_ref[1]


def faces_kernel(planes, blocks, flags_ref, *refs):
    part_refs, (faces_ref, padded_ref, below_ref, above_ref) = refs[:GROUP], refs[GROUP:]
    z, member = flags_ref[2], flags_ref[3]
    _, count, width = faces_ref.shape
    for d, ref in enumerate(part_refs):
        tag = tag_of(ref)
        place = member ^ d
        for p in range(planes):
            padded_ref[pl.ds(8 + place * planes + p, 1), :] = tag[p : p + 1]
        below_ref[pl.ds(place, 1), :] = tag[2 * planes - 1 : 2 * planes]
        above_ref[pl.ds(place, 1), :] = tag[2 * planes : 2 * planes + 1]
    cells = padded_ref[pl.ds(8, count), :]
    padded_ref[pl.ds(7, 1), :] = jnp.where(z == 0, cells[0:1], below_ref[pl.ds(GROUP - 1, 1), :])
    padded_ref[pl.ds(8 + count, 1), :] = jnp.where(
        z == blocks - 1, cells[count - 1 : count], above_ref[pl.ds(0, 1), :]
    )
    lane = lax.broadcasted_iota(jnp.int32, cells.shape, 1)
    last, first = lane == width - 1, lane == 0
    right = 0.5 * (cells + pltpu.roll(cells, width - 1, 1))
    left = 0.5 * (cells + pltpu.roll(cells, 1, 1))
    low = 0.5 * (cells + padded_ref[pl.ds(7, count), :])
    high = 0.5 * (cells + padded_ref[pl.ds(9, count), :])
    faces_ref[0] = jnp.where(last, cells, right) + jnp.where(first, cells, left) + (low + high)
    faces_ref[1] = cells
    faces_ref[2] = jnp.where(last, 0.0, right)
    faces_ref[3] = jnp.where(first, 0.0, left)
    faces_ref[4] = low
    faces_ref[5] = high


def forward_kernel(distance, parts_count, flags_ref, source_ref, wave_ref, own_ref, below_ref, above_ref, *refs):
    part_refs, out_refs, stage_ref = refs[:parts_count], refs[parts_count:-1], refs[-1]
    planes = source_ref.shape[1]
    q = flags_ref[0] ^ distance
    sign = (1 - 2 * (q & 1)).astype(jnp.float32)
    turn_re = jnp.where(q == 0, 1.0, jnp.where(q == 2, -1.0, 0.0))
    turn_im = jnp.where(q == 1, 1.0, jnp.where(q == 3, -1.0, 0.0))
    rows = stage_ref.shape[1] // (HALVES * CHUNKS)
    for p in range(planes):
        parts = [[source_ref[c, p, i] for i in range(RADIX)] for c in range(2)]
        even = [parts[c][0] + sign * parts[c][2] for c in range(2)]
        odd = [parts[c][1] + sign * parts[c][3] for c in range(2)]
        mixed = jnp.concatenate(
            [
                even[0] + (turn_re * odd[0] + turn_im * odd[1]),
                even[1] + (turn_re * odd[1] - turn_im * odd[0]),
            ],
            axis=0,
        )
        stage_ref[p] = dot_left(wave_ref[q], mixed)
        for n in range(HALVES):
            h = flags_ref[1] ^ n
            for t in range(CHUNKS):
                out_refs[n * CHUNKS + t][pl.ds(p * rows, rows), :] = stage_ref[
                    p, rows_at((h * CHUNKS + t) * rows, rows), :
                ]
    for ref in out_refs:
        fill_tag(ref, planes, own_ref, below_ref, above_ref, part_refs)


def backward_kernel(planes, cells, flags_ref, wave_ref, *refs):
    arrays, (out_ref, norms_ref, mixed_ref, stage_ref) = refs[:-4], refs[-4:]
    rows = (arrays[0].shape[0] - TAG) // planes
    came = {}
    for (t, d), ref in zip([(t, d) for t in range(CHUNKS) for d in SENDS[t]], arrays):
        for n in range(CHUNKS if d in JOINT else 1):
            came[d, n if d in JOINT else t] = ref.at[pl.ds(n * planes * rows, planes * rows)]
    short = rows * CHUNKS * HALVES // 2
    total = None
    for ref in arrays:
        tag = tag_of(ref)
        total = tag if total is None else total + tag
    for d in range(RADIX):
        q = flags_ref[0] ^ d
        for p in range(planes):
            for n in range(HALVES):
                h = flags_ref[1] ^ n
                for t in range(CHUNKS):
                    stage_ref[d, p, rows_at((h * CHUNKS + t) * rows, rows), :] = came[d + RADIX * n, t][
                        pl.ds(p * rows, rows), :
                    ]
            mixed_ref[p, q] = dot_left(wave_ref[q], stage_ref[d, p])
    for p in range(planes):

        def strip(row):
            zero, one, two, three = [load(mixed_ref.at[p, q], 0, short, row, 8) for q in range(RADIX)]
            even, odd = cadd(zero, two), cadd(one, three)
            even_d, odd_d = csub(zero, two), csub(one, three)
            parts = (
                cadd(even, odd),
                (even_d[0] - odd_d[1], even_d[1] + odd_d[0]),
                csub(even, odd),
                (even_d[0] + odd_d[1], even_d[1] - odd_d[0]),
            )
            for i in range(RADIX):
                for c in range(2):
                    out_ref[c, p, rows_at(i * short + row, 8), :] = parts[i][c]

        each_strip(short, 8, strip)
    norms = jnp.sqrt(jnp.sum(total, axis=1, keepdims=True) * (1.0 / cells))
    for n in range(norms_ref.shape[0]):
        norms_ref[n] = norms[n, 0]


def decay_root(h):
    sq = (h[0] + 0.25 * (h[0] * h[0] - h[1] * h[1]), h[1] + 0.5 * h[0] * h[1])
    size = jnp.sqrt(squares_of(sq))
    root_re = jnp.sqrt(0.5 * (size + sq[0]))
    root = (root_re, 0.5 * sq[1] / root_re)
    return cinv((1.0 + 0.5 * h[0] + root[0], 0.5 * h[1] + root[1])), root


def two_powers(power, z, stacks):
    low = high = None
    bit = 0
    while (1 << bit) < stacks:
        taken = ((z >> bit) & 1) == 1
        if low is None:
            one = (jnp.ones_like(power[0]), jnp.zeros_like(power[0]))
            low, high = cpick(taken, power, one), cpick(taken, one, power)
        else:
            grown = cmul(cpick(taken, low, high), power)
            low, high = cpick(taken, grown, low), cpick(taken, high, grown)
        power = csqr(power)
        bit += 1
    return low, high


def sums_of(planes, rho, cross_f, cross_b):
    ahead = planes[0]
    for a in planes[1:]:
        ahead = cmore(a, rho, ahead)
    behind = planes[-1]
    for a in planes[-2::-1]:
        behind = cmore(a, rho, behind)
    return csub(ahead, cmul(cross_f, behind)), csub(behind, cmul(cross_b, ahead))


def sine_rows(source_ref, target_ref, sine_ref, count):
    sine = (sine_ref[0], sine_ref[1])
    rows = max(n for n in range(16, 641, 16) if count % n == 0)
    for i in range(0, count, rows):
        target_ref[pl.ds(i, rows), :] = dot_right(source_ref[pl.ds(i, rows), :], sine)


def fill_give(z, rows, sums_ref, give_refs):
    for ref in give_refs:
        ref[pl.ds(0, rows), :] = sums_ref[rows_at((z & 1) * rows, rows), :]
        ref[pl.ds(rows, TAG), :] = sums_ref[pl.ds(2 * rows, TAG), :]


def start_kernel(
    chunk, planes, blocks, cells_total, flags_ref, numbers_ref, wave_eig_ref, sine_eig_ref, sine_ref, *refs,
):
    part_refs, (field_ref, modes_ref, base_ref, sums_ref), give_refs = refs[:GROUP], refs[GROUP : GROUP + 4], refs[GROUP + 4 :]
    if chunk == 0:
        shift_ref, numbers_ref, give_refs = numbers_ref, give_refs[-1], give_refs[:-1]
        find_numbers(cells_total, shift_ref, part_refs, numbers_ref)
    q, h, z, member = [flags_ref[n] for n in range(4)]
    rows = base_ref.shape[1]
    part = rows * planes
    short = rows // 2
    count = GROUP * planes
    first_row = (h * CHUNKS + chunk) * short
    for d, ref in enumerate(part_refs):
        field_ref[rows_at((member ^ d) * part, part), :] = ref[pl.ds(0, part), :]
    sine_rows(field_ref, modes_ref, sine_ref, count * rows)
    h_re, h_im = numbers_ref[0], numbers_ref[1]
    sine_eig = sine_eig_ref[...]

    def strip(i, total):
        row = pl.multiple_of(i * 8, 8)
        eigen = wave_eig_ref[q, rows_at(first_row + row, 8), :] + sine_eig
        rho, _ = decay_root((eigen + h_re, jnp.full_like(eigen, h_im)))
        block = cpow(rho, count)
        next_one = cmul(block, rho)
        low, high = two_powers(csqr(block), z, blocks)
        cross_f, cross_b = cmul(next_one, low), cmul(next_one, high)
        for n, value in enumerate((rho, cross_f, cross_b, block, low, high)):
            store(base_ref.at[n], 0, short, row, 8, value)
        found = [load(modes_ref, l * rows, short, row, 8) for l in range(count)]
        ahead, behind = sums_of(found, rho, cross_f, cross_b)
        store(sums_ref, 0, short, row, 8, ahead)
        store(sums_ref, rows, short, row, 8, behind)
        for l in range(count):
            total = total + squares_of(load(field_ref, l * rows, short, row, 8))
        return total

    total = lax.fori_loop(
        0, short // 8, strip, jnp.zeros((8, field_ref.shape[1]), jnp.float32), unroll=2
    )
    sums_ref[pl.ds(2 * rows, TAG), :] = jnp.zeros((TAG, field_ref.shape[1]), jnp.float32)
    sums_ref[pl.ds(2 * rows, 1), :] = jnp.sum(total, axis=0, keepdims=True)
    fill_give(z, rows, sums_ref, give_refs)


def factors_kernel(
    chunk, count, levels, flags_ref, numbers_ref, wave_eig_ref, sine_eig_ref, base_ref, out_ref,
):
    q, h_part, z = flags_ref[0], flags_ref[1], flags_ref[2]
    short = base_ref.shape[1] // 2
    h_re, h_im, scale = numbers_ref[0], numbers_ref[1], numbers_ref[3]
    sine_eig = sine_eig_ref[...]

    def strip(row):
        eigen = wave_eig_ref[q, rows_at((h_part * CHUNKS + chunk) * short + row, 8), :] + sine_eig
        h = (eigen + h_re, jnp.full_like(eigen, h_im))
        rho, _, _, block, low, high = [load(base_ref.at[n], 0, short, row, 8) for n in range(6)]
        half_gap = csub((1.0 + 0.5 * h[0], 0.5 * h[1]), rho)
        wide = cmul(csqr(block), csqr(rho))
        low_w, high_w = cmul(low, wide), cmul(high, wide)
        whole = cscale(cinv(cmul(half_gap, cone(cmul(low, high_w)))), scale)
        turned = cmul(rho, whole)
        values = [
            cmul(cone(high_w), whole), cmul(cone(low), turned),
            cmul(cone(high), turned), cmul(cone(low_w), whole),
        ]
        pivot = (2.0 + h[0], h[1])
        inverse = cinv(pivot)
        values.append(inverse)
        for _ in range(count - 1):
            inverse = cinv(csub(pivot, inverse))
            values.append(inverse)
        near = far = None
        power = block
        for level in range(1, levels):
            taken = ((z >> (level - 1)) & 1) == 1
            if near is None:
                one = (jnp.ones_like(power[0]), jnp.zeros_like(power[0]))
                near, far = cpick(taken, power, one), cpick(taken, one, power)
            else:
                grown = cmul(cpick(taken, near, far), power)
                near, far = cpick(taken, grown, near), cpick(taken, far, grown)
            power = csqr(power)
            values.append(cpick(((z >> level) & 1) == 1, near, far))
        for n, value in enumerate(values):
            store(out_ref.at[n], 0, short, row, 8, value)

    each_strip(short, 8, strip)


def join_kernel(level, levels, flags_ref, sums_ref, came_ref, base_ref, out_ref):
    z = flags_ref[2]
    short = base_ref.shape[1] // 2
    rows = 2 * short
    above = ((z >> level) & 1) == 1
    last = level + 2 == levels
    upper = ((z >> (level + 1)) & 1) == 1

    def strip(row):
        block = load(base_ref.at[3], 0, short, row, 8)
        for _ in range(level):
            block = csqr(block)
        ahead, behind = load(sums_ref, 0, short, row, 8), load(sums_ref, rows, short, row, 8)
        ahead_c, behind_c = load(came_ref, 0, short, row, 8), load(came_ref, rows, short, row, 8)
        joined = cmore(cpick(above, ahead, ahead_c), block, cpick(above, ahead_c, ahead))
        joined_b = cmore(cpick(above, behind_c, behind), block, cpick(above, behind, behind_c))
        if last:
            store(out_ref, 0, short, row, 8, cpick(upper, joined_b, joined))
        else:
            store(out_ref, 0, short, row, 8, joined)
            store(out_ref, rows, short, row, 8, joined_b)

    each_strip(short, 8, strip)
    out_ref[pl.ds(out_ref.shape[0] - TAG, TAG), :] = (
        sums_ref[pl.ds(2 * rows, TAG), :] + came_ref[pl.ds(2 * rows, TAG), :]
    )


def solved(count, levels, z, scale, modes_ref, sums_ref, came_refs, base_ref, factors_ref, row):
    short = base_ref.shape[1] // 2
    rows = 2 * short

    def factor(n):
        return load(factors_ref.at[n], 0, short, row, 8)

    enter_f = enter_b = None
    for level in range(levels):
        above = ((z >> level) & 1) == 1
        base = 0 if level == levels - 1 else jnp.where(above, 0, rows)
        came = load(came_refs[level], base, short, row, 8)
        if level:
            came = cmul(factor(4 + count + level - 1), came)
        nought = (jnp.zeros_like(came[0]), jnp.zeros_like(came[0]))
        now_f, now_b = cpick(above, came, nought), cpick(above, nought, came)
        enter_f = now_f if enter_f is None else cadd(enter_f, now_f)
        enter_b = now_b if enter_b is None else cadd(enter_b, now_b)
    block = load(base_ref.at[3], 0, short, row, 8)
    all_f = cmore(load(sums_ref, 0, short, row, 8), block, enter_f)
    all_b = cmore(load(sums_ref, rows, short, row, 8), block, enter_b)
    below = cmore(cmul(factor(0), enter_f), factor(1), all_b)
    above = cmore(cmul(factor(3), enter_b), factor(2), all_f)
    planes = [cscale(load(modes_ref, l * rows, short, row, 8), scale) for l in range(count)]
    planes[0] = cadd(planes[0], below)
    planes[-1] = cadd(planes[-1], above)
    for l in range(1, count):
        planes[l] = cmore(planes[l], factor(4 + l - 1), planes[l - 1])
    planes[-1] = cmul(factor(4 + count - 1), planes[-1])
    for l in range(count - 2, -1, -1):
        planes[l] = cmul(factor(4 + l), cadd(planes[l], planes[l + 1]))
    return below, planes, above


def middle_kernel(
    chunk, count, levels, flags_ref, numbers_ref, wave_eig_ref, sine_ref, faces_ref, field_ref,
    modes_ref, base_ref, factors_ref, sums_ref, *refs,
):
    came_refs, (found_ref, next_ref, next_sums_ref) = refs[:levels], refs[levels : levels + 3]
    give_refs, work_ref = refs[levels + 3 : -1], refs[-1]
    q, h, z = flags_ref[0], flags_ref[1], flags_ref[2]
    scale, s_re, s_im = numbers_ref[2], numbers_ref[4], numbers_ref[5]
    short = base_ref.shape[1] // 2
    rows = 2 * short
    width = base_ref.shape[2]

    def solve(row):
        below, planes, above = solved(
            count, levels, z, scale, modes_ref, sums_ref, came_refs, base_ref, factors_ref, row
        )
        store(work_ref, 0, short, row, 8, below)
        store(work_ref, (count + 1) * rows, short, row, 8, above)
        for l in range(count):
            store(work_ref, (l + 1) * rows, short, row, 8, planes[l])
            store(found_ref, l * rows, short, row, 8, planes[l])

    each_strip(short, 8, solve)
    sine_rows(work_ref, work_ref, sine_ref, (count + 2) * rows)

    def residual(i, total):
        row = pl.multiple_of(i * 8, 8)
        eigen = wave_eig_ref[q, rows_at((h * CHUNKS + chunk) * short + row, 8), :]
        under = load(work_ref, 0, short, row, 8)
        here = load(work_ref, rows, short, row, 8)
        for l in range(count):
            over = load(work_ref, (l + 2) * rows, short, row, 8)
            diag, cell, right, left, low, high = [faces_ref[n, pl.ds(l, 1), :] for n in range(6)]
            diag = s_re + (diag + cell * eigen)
            value = []
            for c in range(2):
                v = diag * here[c] - right * pltpu.roll(here[c], width - 1, 1)
                v = v - left * pltpu.roll(here[c], 1, 1)
                value.append(v - (low * under[c] + high * over[c]))
            value = (value[0] - s_im * here[1], value[1] + s_im * here[0])
            value = csub(load(field_ref, l * rows, short, row, 8), value)
            total = total + squares_of(value)
            store(work_ref, l * rows, short, row, 8, value)
            under, here = here, over
        return total

    total = lax.fori_loop(0, short // 8, residual, jnp.zeros((8, width), jnp.float32), unroll=2)
    sine_rows(work_ref, next_ref, sine_ref, count * rows)

    def sums(row):
        rho, cross_f, cross_b = [load(base_ref.at[n], 0, short, row, 8) for n in range(3)]
        planes = [load(next_ref, l * rows, short, row, 8) for l in range(count)]
        ahead, behind = sums_of(planes, rho, cross_f, cross_b)
        store(next_sums_ref, 0, short, row, 8, ahead)
        store(next_sums_ref, rows, short, row, 8, behind)

    each_strip(short, 8, sums)
    next_sums_ref[pl.ds(2 * rows, TAG), :] = sums_ref[pl.ds(2 * rows, TAG), :]
    next_sums_ref[pl.ds(2 * rows + 1, 1), :] = jnp.sum(total, axis=0, keepdims=True)
    fill_give(z, rows, next_sums_ref, give_refs)


def end_kernel(
    count, levels, flags_ref, numbers_ref, sine_ref, found_ref, modes_ref, base_ref,
    factors_ref, sums_ref, *refs,
):
    came_refs, out_refs, work_ref = refs[:levels], refs[-1 - GROUP : -1], refs[-1]
    before_refs = refs[levels + (levels > 1) : -1 - GROUP]
    z, member = flags_ref[2], flags_ref[3]
    scale = numbers_ref[2]
    short = base_ref.shape[1] // 2
    rows = 2 * short

    def solve(row):
        _, planes, _ = solved(
            count, levels, z, scale, modes_ref, sums_ref, came_refs, base_ref, factors_ref, row
        )
        for l in range(count):
            before = load(found_ref, l * rows, short, row, 8)
            store(work_ref, l * rows, short, row, 8, cadd(before, planes[l]))

    each_strip(short, 8, solve)
    sine_rows(work_ref, work_ref, sine_ref, count * rows)
    part = count // GROUP * rows
    tag_refs = (refs[levels] if levels > 1 else sums_ref, came_refs[-1])
    tag = None
    for ref in tag_refs:
        part_tag = ref[pl.ds(ref.shape[0] - TAG, TAG), :]
        tag = part_tag if tag is None else tag + part_tag
    for d in range(GROUP):
        start, whole = 0, tag
        if d in JOINT:
            held = len(before_refs) // len(JOINT)
            for ref in before_refs[JOINT.index(d) * held : (JOINT.index(d) + 1) * held]:
                out_refs[d][pl.ds(start, part), :] = ref[pl.ds(0, part), :]
                start, whole = start + part, whole + tag_of(ref)
        out_refs[d][pl.ds(start, part), :] = work_ref[rows_at((member ^ d) * part, part), :]
        out_refs[d][pl.ds(start + part, TAG), :] = whole


smem = pl.BlockSpec(memory_space=pltpu.SMEM)
vmem = pl.BlockSpec(memory_space=pltpu.VMEM)
unread = pl.BlockSpec(memory_space=pl.ANY)


def call(kernel, scalars, arrays, outs, scratch=(), flops=0, after=()):
    out_shape = [jax.ShapeDtypeStruct(shape, jnp.float32) for shape in outs]
    head = len(scalars) + len(arrays)

    def run(*refs):
        kernel(*refs[:head], *refs[head + len(after) :])

    moved = sum(a.size * a.dtype.itemsize for a in arrays) + sum(4 * int(np.prod(s)) for s in outs)
    held = moved + sum(4 * int(np.prod(s)) for s in scratch)
    return pl.pallas_call(
        run,
        out_shape=out_shape,
        in_specs=[smem] * len(scalars) + [vmem] * len(arrays) + [unread] * len(after),
        out_specs=[smem if len(shape) == 1 else vmem for shape in outs],
        scratch_shapes=[pltpu.VMEM(shape, jnp.float32) for shape in scratch],
        compiler_params=pltpu.CompilerParams(vmem_limit_bytes=held + 4 * 2**20),
        cost_estimate=pl.CostEstimate(flops=flops, bytes_accessed=moved, transcendentals=0),
    )(*scalars, *arrays, *after)


def pair_up(array, groups, flip):
    return lax.ppermute(array, "gz", [(i, i ^ flip) for i in range(groups)])


def step_by(array, groups, distance):
    return lax.ppermute(
        array, "gz", [(i, i + distance) for i in range(groups) if 0 <= i + distance < groups]
    )


def body(source, layer_ids, conduct_table, shift):
    planes, length_x, length_y = source.shape[1:]
    groups = lax.axis_size("gz")
    blocks = groups // GROUP
    levels = blocks.bit_length() - 1
    count = GROUP * planes
    length_z = planes * groups
    full = length_x // RADIX
    short = full // (HALVES * CHUNKS)
    rows = 2 * short
    if blocks < 2 or groups != GROUP << levels or planes > 2 or short % 8 or length_x != RADIX * full:
        raise ValueError("unsupported layout")
    me = lax.axis_index("gz")
    member = me % GROUP
    flags = jnp.stack([member % RADIX, member // RADIX, me // GROUP, member]).astype(jnp.int32)

    wave = wave_tables(length_x)
    wave_f = jnp.asarray(np.concatenate(two_terms(wave), axis=1))
    wave_b = jnp.asarray(np.concatenate(two_terms(np.swapaxes(wave, 1, 2) / length_x), axis=1))
    sine = jnp.asarray(two_terms(sine_table(length_y)))
    wave_eig = np.broadcast_to(wave_eigen(length_x)[:, :, None], (RADIX, full, length_y))
    wave_eig = jnp.asarray(np.ascontiguousarray(wave_eig).astype(np.float32))
    sine_eig = jnp.asarray(np.tile(sine_eigen(length_y)[None, :], (8, 1)).astype(np.float32))

    chunks = range(CHUNKS)
    row_block = (TAG, length_y)
    block = (count * rows, length_y)
    sums_block = (2 * rows + TAG, length_y)
    single = (rows + TAG, length_y)
    part = (planes * rows + TAG, length_y)
    parts = (CHUNKS * planes * rows + TAG, length_y)
    gives = [single] if levels == 1 else []
    dots = 6 * length_y * length_y

    (cells,) = call(conduct_kernel, [conduct_table], [layer_ids], [row_block])
    if levels == 1:
        below = above = pair_up(cells, groups, GROUP)
        totals = [cells, below]
    else:
        below = step_by(cells, groups, GROUP)
        above = step_by(cells, groups, -GROUP)
        total = cells
        for level in range(levels):
            (total,) = call(add_kernel, [], [total, pair_up(total, groups, GROUP << level)], [row_block])
        totals = [total]

    (ready,) = call(ready_kernel, [], [source.reshape(2, planes, RADIX, full, length_y), wave_f], [row_block], after=[cells])

    parted = source.reshape(2, planes, RADIX, full, length_y)
    spectra = {}
    placed = [ready]
    for d in (2, 0, 3, 1):
        made = call(
            functools.partial(forward_kernel, d, len(totals)), [flags],
            [parted, wave_f, cells, below, above, *totals], [part] * (HALVES * CHUNKS),
            scratch=[(planes, 2 * full, length_y)], flops=planes * 2 * full * dots, after=placed,
        )
        placed = made[:1]
        for n in range(HALVES):
            for t in chunks:
                spectra[d + RADIX * n, t] = made[n * CHUNKS + t]
    for t in chunks:
        for d in (6, 2, 4, 7, 3, 5, 1):
            spectra[d, t] = pair_up(spectra[d, t], groups, d)

    state = [{} for _ in chunks]

    def exchange(st, after):
        sums, give = st["sums"][0], st["sums"][-1]
        st["came"], st["tags"] = [], []
        for level in range(levels):
            st["came"].append(pair_up(give, groups, GROUP << level))
            if level + 1 < levels:
                shape = single if level + 2 == levels else sums_block
                (give,) = call(
                    functools.partial(join_kernel, level, levels), [flags], [sums, st["came"][-1], st["base"]],
                    [shape], after=after,
                )
                sums = give
                st["tags"] = [give[-TAG:]]

    def start(t, after):
        st = state[t]
        outs = [block, block, (6, rows, length_y), sums_block, *gives]
        made = call(
            functools.partial(start_kernel, t, planes, blocks, length_y * length_z),
            [flags, state[0]["numbers"] if t else shift],
            [wave_eig, sine_eig, sine] + [spectra[d, t] for d in range(GROUP)],
            outs if t else [*outs, (6,)], flops=count * rows * dots, after=after,
        )
        if not t:
            *made, st["numbers"] = made
        st["field"], st["modes"], st["base"], *st["sums"] = made
        exchange(st, [])
        return [st["sums"][-1]]

    def faces(t, after):
        state[t]["faces"] = call(
            functools.partial(faces_kernel, planes, blocks), [flags], [spectra[d, 0] for d in range(GROUP)],
            [(6, count, length_y)], scratch=[(count + 16, length_y), row_block, row_block], after=after,
        )[0]
        return [state[t]["faces"]]

    def factors(t, after):
        st = state[t]
        (st["factors"],) = call(
            functools.partial(factors_kernel, t, count, levels), [flags, state[0]["numbers"]],
            [wave_eig, sine_eig, st["base"]], [(4 + count + levels - 1, rows, length_y)], after=after,
        )
        return [st["factors"]]

    def middle(t, after):
        st = state[t]
        st["found"], st["modes"], *st["sums"] = call(
            functools.partial(middle_kernel, t, count, levels), [flags, state[0]["numbers"]],
            [wave_eig, sine, state[0]["faces"], st["field"], st["modes"], st["base"], st["factors"], st["sums"][0], *st["came"]],
            [block, block, sums_block, *gives], scratch=[((count + 2) * rows, length_y)],
            flops=(2 * count + 2) * rows * dots, after=after,
        )
        exchange(st, [])
        return [st["sums"][-1]]

    def end(t, after):
        st = state[t]
        last = t == CHUNKS - 1
        before = [state[u]["made"][d] for d in JOINT for u in range(t)] if last else []
        st["made"] = call(
            functools.partial(end_kernel, count, levels), [flags, state[0]["numbers"]],
            [sine, st["found"], st["modes"], st["base"], st["factors"], st["sums"][0], *st["came"], *st["tags"], *before],
            [parts if last and d in JOINT else part for d in range(GROUP)],
            scratch=[block], flops=count * rows * dots, after=after,
        )
        st["answers"] = {d: st["made"][d] for d in SENDS[t]}
        return [st["made"][0]]

    def answer(t):
        answers = state[t]["answers"]
        for d in SENDS[t][:-1]:
            answers[d] = pair_up(answers[d], groups, d)

    placed = []
    for step, t in (
        (start, 0), (faces, 0), (factors, 0), (middle, 0), (start, 1), (factors, 1), (end, 0),
    ):
        placed = step(t, placed)
    answer(0)
    placed = middle(1, placed)
    end(1, [*placed, *[state[0]["answers"][d] for d in SENDS[0][:2]]])
    answer(1)
    return call(
        functools.partial(backward_kernel, planes, length_x * length_x * length_y * length_z),
        [flags], [wave_b] + [state[t]["answers"][d] for t in chunks for d in SENDS[t]],
        [(2, planes, length_x, length_y), (2,)],
        scratch=[(planes, RADIX, 2 * full, length_y), (RADIX, planes, 2 * full, length_y)],
        flops=planes * RADIX * 2 * full * dots,
    )


def solution(mesh):
    placed = (P(None, ("node", "gz"), None, None), P(("node", "gz"), None), P(), P("node"))
    return jax.shard_map(
        body,
        mesh=mesh,
        in_specs=placed,
        out_specs=(P(None, ("node", "gz"), None, None), P("node")),
        check_vma=False,
    )
```

```python
import functools

import jax
import jax.numpy as jnp
import ml_dtypes
import numpy as np
from jax import lax
from jax.experimental import pallas as pl
from jax.experimental.pallas import tpu as pltpu
from jax.sharding import PartitionSpec as P

RADIX = 4
HALVES = 2
GROUP = RADIX * HALVES
CHUNKS = 2
SENDS = ((6, 7, 4, 2, 3, 0), (2, 6, 7, 3, 4, 5, 1, 0))
LATER = (3,)
BEFORE = (6, 7, 4)
JOINT = (5, 1)
TAG = 8

relax = 0.6


def sine_table(length):
    indices = np.arange(1, length + 1)
    product = indices[:, None] * indices[None, :] % (2 * (length + 1))
    return np.sqrt(2.0 / (length + 1)) * np.sin(np.pi / (length + 1) * product)


def sine_eigen(length):
    indices = np.arange(1, length + 1)
    return 4.0 * np.sin(np.pi / (2 * (length + 1)) * indices) ** 2


def wave_numbers(length):
    return RADIX * np.arange(length // RADIX)[None, :] + np.arange(RADIX)[:, None]


def wave_eigen(length):
    return 4.0 * np.sin(np.pi / length * wave_numbers(length)) ** 2


def wave_tables(length):
    waves = wave_numbers(length)
    short = length // RADIX
    product = waves[:, :, None] * np.arange(short)[None, None, :] % length
    angles = 2.0 * np.pi / length * product
    cos_t, sin_t = np.cos(angles), np.sin(angles)
    pieces = HALVES * CHUNKS
    top = np.concatenate([cos_t, sin_t], axis=2).reshape(RADIX, pieces, short // pieces, 2 * short)
    low = np.concatenate([-sin_t, cos_t], axis=2).reshape(RADIX, pieces, short // pieces, 2 * short)
    return np.concatenate([top, low], axis=2).reshape(RADIX, 2 * short, 2 * short)


def two_terms(table):
    first = table.astype(ml_dtypes.bfloat16)
    return np.stack([first, (table - first.astype(np.float64)).astype(ml_dtypes.bfloat16)])


def split(value):
    first = value.astype(jnp.bfloat16)
    return first, (value - first.astype(jnp.float32)).astype(jnp.bfloat16)


def dot_right(value, table):
    rows = value.shape[0]
    first, second = split(value)
    wide = jnp.dot(jnp.concatenate([first, second], axis=0), table[0], preferred_element_type=jnp.float32)
    return wide[:rows] + (wide[rows:] + jnp.dot(first, table[1], preferred_element_type=jnp.float32))


def dot_left(table, value):
    rows = table.shape[0] // 2
    first, second = split(value)
    wide = jnp.dot(table, first, preferred_element_type=jnp.float32)
    return wide[:rows] + (wide[rows:] + jnp.dot(table[:rows], second, preferred_element_type=jnp.float32))


def cmul(a, b):
    return (a[0] * b[0] - a[1] * b[1], a[0] * b[1] + a[1] * b[0])


def csqr(a):
    cross = a[0] * a[1]
    return ((a[0] - a[1]) * (a[0] + a[1]), cross + cross)


def cpow(a, count):
    result = None
    while count:
        if count & 1:
            result = a if result is None else cmul(result, a)
        count >>= 1
        if count:
            a = csqr(a)
    return result


def cadd(a, b):
    return (a[0] + b[0], a[1] + b[1])


def csub(a, b):
    return (a[0] - b[0], a[1] - b[1])


def cscale(a, scale):
    return (a[0] * scale, a[1] * scale)


def cmore(total, factor, term):
    return cadd(total, cmul(factor, term))


def cinv(a):
    scale = 1.0 / (a[0] * a[0] + a[1] * a[1])
    return (a[0] * scale, -a[1] * scale)


def cone(a):
    return (1.0 - a[0], -a[1])


def cpick(cond, a, b):
    return (jnp.where(cond, a[0], b[0]), jnp.where(cond, a[1], b[1]))


def rows_at(start, rows):
    if isinstance(start, int):
        return pl.ds(start, rows)
    return pl.ds(pl.multiple_of(start, 8), rows)


def load(ref, base, short, row, rows):
    return (ref[rows_at(base + row, rows), :], ref[rows_at(base + short + row, rows), :])


def store(ref, base, short, row, rows, value):
    ref[rows_at(base + row, rows), :] = value[0]
    ref[rows_at(base + short + row, rows), :] = value[1]


def each_strip(count, rows, body):
    def step(i, carry):
        body(pl.multiple_of(i * rows, rows))
        return carry

    steps = count // rows
    lax.fori_loop(0, steps, step, 0, unroll=min(steps, 4))


def squares_of(a):
    return a[0] * a[0] + a[1] * a[1]


def conduct_kernel(table_ref, ids_ref, out_ref):
    planes = ids_ref.shape[0]
    ids = ids_ref[...]
    cells = jnp.zeros(ids.shape, jnp.float32)
    for layer in range(table_ref.shape[0]):
        cells = jnp.where(ids == layer, table_ref[layer], cells)
    out_ref[...] = jnp.zeros_like(out_ref)
    out_ref[pl.ds(0, planes), :] = cells
    out_ref[pl.ds(TAG - 1, 1), :] = jnp.sum(cells, axis=0, keepdims=True)


def ready_kernel(wave_ref, out_ref):
    out_ref[...] = wave_ref[0, pl.ds(0, 2 * TAG), :][:TAG].astype(jnp.float32)


def add_kernel(one_ref, two_ref, out_ref):
    out_ref[...] = one_ref[...] + two_ref[...]


def fill_tag(out_ref, planes, own_ref, below_ref, above_ref, part_refs):
    start = out_ref.shape[0] - TAG
    for n, ref in enumerate((own_ref, below_ref, above_ref)):
        out_ref[pl.ds(start + n * planes, planes), :] = ref[pl.ds(0, planes), :]
    total = part_refs[0][pl.ds(TAG - 1, 1), :]
    for ref in part_refs[1:]:
        total = total + ref[pl.ds(TAG - 1, 1), :]
    out_ref[pl.ds(start + TAG - 1, 1), :] = total


def tag_of(ref):
    return ref[pl.ds(ref.shape[0] - TAG, TAG), :]


def find_numbers(cells_total, shift_ref, part_refs, numbers_ref):
    total = None
    for ref in part_refs:
        row = ref[pl.ds(ref.shape[0] - 1, 1), :]
        total = row if total is None else total + row
    inv = (1.0 / (jnp.sum(total, axis=1, keepdims=True) * (1.0 / cells_total)))[0, 0]
    numbers_ref[0] = shift_ref[0] * inv
    numbers_ref[1] = shift_ref[1] * inv
    numbers_ref[2] = relax * inv
    numbers_ref[3] = 0.5 * relax * inv
    numbers_ref[4] = shift_ref[0]
    numbers_ref[5] = shift_ref[1]


def faces_kernel(planes, blocks, flags_ref, *refs):
    part_refs, (faces_ref, padded_ref, below_ref, above_ref) = refs[:GROUP], refs[GROUP:]
    z, member = flags_ref[2], flags_ref[3]
    _, count, width = faces_ref.shape
    for d, ref in enumerate(part_refs):
        tag = tag_of(ref)
        place = member ^ d
        for p in range(planes):
            padded_ref[pl.ds(8 + place * planes + p, 1), :] = tag[p : p + 1]
        below_ref[pl.ds(place, 1), :] = tag[2 * planes - 1 : 2 * planes]
        above_ref[pl.ds(place, 1), :] = tag[2 * planes : 2 * planes + 1]
    cells = padded_ref[pl.ds(8, count), :]
    padded_ref[pl.ds(7, 1), :] = jnp.where(z == 0, cells[0:1], below_ref[pl.ds(GROUP - 1, 1), :])
    padded_ref[pl.ds(8 + count, 1), :] = jnp.where(
        z == blocks - 1, cells[count - 1 : count], above_ref[pl.ds(0, 1), :]
    )
    lane = lax.broadcasted_iota(jnp.int32, cells.shape, 1)
    last, first = lane == width - 1, lane == 0
    right = 0.5 * (cells + pltpu.roll(cells, width - 1, 1))
    left = 0.5 * (cells + pltpu.roll(cells, 1, 1))
    low = 0.5 * (cells + padded_ref[pl.ds(7, count), :])
    high = 0.5 * (cells + padded_ref[pl.ds(9, count), :])
    faces_ref[0] = jnp.where(last, cells, right) + jnp.where(first, cells, left) + (low + high)
    faces_ref[1] = cells
    faces_ref[2] = jnp.where(last, 0.0, right)
    faces_ref[3] = jnp.where(first, 0.0, left)
    faces_ref[4] = low
    faces_ref[5] = high


def forward_kernel(distance, parts_count, flags_ref, source_ref, wave_ref, own_ref, below_ref, above_ref, *refs):
    part_refs, out_refs, stage_ref = refs[:parts_count], refs[parts_count:-1], refs[-1]
    planes = source_ref.shape[1]
    q = flags_ref[0] ^ distance
    sign = (1 - 2 * (q & 1)).astype(jnp.float32)
    turn_re = jnp.where(q == 0, 1.0, jnp.where(q == 2, -1.0, 0.0))
    turn_im = jnp.where(q == 1, 1.0, jnp.where(q == 3, -1.0, 0.0))
    rows = stage_ref.shape[1] // (HALVES * CHUNKS)
    for p in range(planes):
        parts = [[source_ref[c, p, i] for i in range(RADIX)] for c in range(2)]
        even = [parts[c][0] + sign * parts[c][2] for c in range(2)]
        odd = [parts[c][1] + sign * parts[c][3] for c in range(2)]
        mixed = jnp.concatenate(
            [
                even[0] + (turn_re * odd[0] + turn_im * odd[1]),
                even[1] + (turn_re * odd[1] - turn_im * odd[0]),
            ],
            axis=0,
        )
        stage_ref[p] = dot_left(wave_ref[q], mixed)
        for n in range(HALVES):
            h = flags_ref[1] ^ n
            for t in range(CHUNKS):
                out_refs[n * CHUNKS + t][pl.ds(p * rows, rows), :] = stage_ref[
                    p, rows_at((h * CHUNKS + t) * rows, rows), :
                ]
    for ref in out_refs:
        fill_tag(ref, planes, own_ref, below_ref, above_ref, part_refs)


def backward_kernel(planes, cells, flags_ref, wave_ref, *refs):
    arrays, (out_ref, norms_ref, mixed_ref, stage_ref) = refs[:-4], refs[-4:]
    rows = (arrays[0].shape[0] - TAG) // planes
    came = {}
    for (t, d), ref in zip([(t, d) for t in range(CHUNKS) for d in SENDS[t]], arrays):
        for n in range(CHUNKS if d in JOINT else 1):
            came[d, n if d in JOINT else t] = ref.at[pl.ds(n * planes * rows, planes * rows)]
    short = rows * CHUNKS * HALVES // 2
    total = None
    for ref in arrays:
        tag = tag_of(ref)
        total = tag if total is None else total + tag
    for d in range(RADIX):
        q = flags_ref[0] ^ d
        for p in range(planes):
            for n in range(HALVES):
                h = flags_ref[1] ^ n
                for t in range(CHUNKS):
                    stage_ref[d, p, rows_at((h * CHUNKS + t) * rows, rows), :] = came[d + RADIX * n, t][
                        pl.ds(p * rows, rows), :
                    ]
            mixed_ref[p, q] = dot_left(wave_ref[q], stage_ref[d, p])
    for p in range(planes):

        def strip(row):
            zero, one, two, three = [load(mixed_ref.at[p, q], 0, short, row, 8) for q in range(RADIX)]
            even, odd = cadd(zero, two), cadd(one, three)
            even_d, odd_d = csub(zero, two), csub(one, three)
            parts = (
                cadd(even, odd),
                (even_d[0] - odd_d[1], even_d[1] + odd_d[0]),
                csub(even, odd),
                (even_d[0] + odd_d[1], even_d[1] - odd_d[0]),
            )
            for i in range(RADIX):
                for c in range(2):
                    out_ref[c, p, rows_at(i * short + row, 8), :] = parts[i][c]

        each_strip(short, 8, strip)
    norms = jnp.sqrt(jnp.sum(total, axis=1, keepdims=True) * (1.0 / cells))
    for n in range(norms_ref.shape[0]):
        norms_ref[n] = norms[n, 0]


def decay_root(h):
    sq = (h[0] + 0.25 * (h[0] * h[0] - h[1] * h[1]), h[1] + 0.5 * h[0] * h[1])
    size = jnp.sqrt(squares_of(sq))
    root_re = jnp.sqrt(0.5 * (size + sq[0]))
    root = (root_re, 0.5 * sq[1] / root_re)
    return cinv((1.0 + 0.5 * h[0] + root[0], 0.5 * h[1] + root[1])), root


def two_powers(power, z, stacks):
    low = high = None
    bit = 0
    while (1 << bit) < stacks:
        taken = ((z >> bit) & 1) == 1
        if low is None:
            one = (jnp.ones_like(power[0]), jnp.zeros_like(power[0]))
            low, high = cpick(taken, power, one), cpick(taken, one, power)
        else:
            grown = cmul(cpick(taken, low, high), power)
            low, high = cpick(taken, grown, low), cpick(taken, high, grown)
        power = csqr(power)
        bit += 1
    return low, high


def sums_of(planes, rho, cross_f, cross_b):
    ahead = planes[0]
    for a in planes[1:]:
        ahead = cmore(a, rho, ahead)
    behind = planes[-1]
    for a in planes[-2::-1]:
        behind = cmore(a, rho, behind)
    return csub(ahead, cmul(cross_f, behind)), csub(behind, cmul(cross_b, ahead))


def sine_rows(source_ref, target_ref, sine_ref, count):
    sine = (sine_ref[0], sine_ref[1])
    rows = max(n for n in range(16, 641, 16) if count % n == 0)
    for i in range(0, count, rows):
        target_ref[pl.ds(i, rows), :] = dot_right(source_ref[pl.ds(i, rows), :], sine)


def fill_give(z, rows, sums_ref, give_refs):
    for ref in give_refs:
        ref[pl.ds(0, rows), :] = sums_ref[rows_at((z & 1) * rows, rows), :]
        ref[pl.ds(rows, TAG), :] = sums_ref[pl.ds(2 * rows, TAG), :]


def start_kernel(
    chunk, planes, blocks, cells_total, flags_ref, numbers_ref, wave_eig_ref, sine_eig_ref, sine_ref, *refs,
):
    part_refs, (field_ref, modes_ref, base_ref, sums_ref), give_refs = refs[:GROUP], refs[GROUP : GROUP + 4], refs[GROUP + 4 :]
    if chunk == 0:
        shift_ref, numbers_ref, give_refs = numbers_ref, give_refs[-1], give_refs[:-1]
        find_numbers(cells_total, shift_ref, part_refs, numbers_ref)
    q, h, z, member = [flags_ref[n] for n in range(4)]
    rows = base_ref.shape[1]
    part = rows * planes
    short = rows // 2
    count = GROUP * planes
    first_row = (h * CHUNKS + chunk) * short
    for d, ref in enumerate(part_refs):
        field_ref[rows_at((member ^ d) * part, part), :] = ref[pl.ds(0, part), :]
    sine_rows(field_ref, modes_ref, sine_ref, count * rows)
    h_re, h_im = numbers_ref[0], numbers_ref[1]
    sine_eig = sine_eig_ref[...]

    def strip(i, total):
        row = pl.multiple_of(i * 8, 8)
        eigen = wave_eig_ref[q, rows_at(first_row + row, 8), :] + sine_eig
        rho, _ = decay_root((eigen + h_re, jnp.full_like(eigen, h_im)))
        block = cpow(rho, count)
        next_one = cmul(block, rho)
        low, high = two_powers(csqr(block), z, blocks)
        cross_f, cross_b = cmul(next_one, low), cmul(next_one, high)
        for n, value in enumerate((rho, cross_f, cross_b, block, low, high)):
            store(base_ref.at[n], 0, short, row, 8, value)
        found = [load(modes_ref, l * rows, short, row, 8) for l in range(count)]
        ahead, behind = sums_of(found, rho, cross_f, cross_b)
        store(sums_ref, 0, short, row, 8, ahead)
        store(sums_ref, rows, short, row, 8, behind)
        for l in range(count):
            total = total + squares_of(load(field_ref, l * rows, short, row, 8))
        return total

    total = lax.fori_loop(
        0, short // 8, strip, jnp.zeros((8, field_ref.shape[1]), jnp.float32), unroll=2
    )
    sums_ref[pl.ds(2 * rows, TAG), :] = jnp.zeros((TAG, field_ref.shape[1]), jnp.float32)
    sums_ref[pl.ds(2 * rows, 1), :] = jnp.sum(total, axis=0, keepdims=True)
    fill_give(z, rows, sums_ref, give_refs)


def factors_kernel(
    chunk, count, levels, flags_ref, numbers_ref, wave_eig_ref, sine_eig_ref, base_ref, out_ref,
):
    q, h_part, z = flags_ref[0], flags_ref[1], flags_ref[2]
    short = base_ref.shape[1] // 2
    h_re, h_im, scale = numbers_ref[0], numbers_ref[1], numbers_ref[3]
    sine_eig = sine_eig_ref[...]

    def strip(row):
        eigen = wave_eig_ref[q, rows_at((h_part * CHUNKS + chunk) * short + row, 8), :] + sine_eig
        h = (eigen + h_re, jnp.full_like(eigen, h_im))
        rho, _, _, block, low, high = [load(base_ref.at[n], 0, short, row, 8) for n in range(6)]
        half_gap = csub((1.0 + 0.5 * h[0], 0.5 * h[1]), rho)
        wide = cmul(csqr(block), csqr(rho))
        low_w, high_w = cmul(low, wide), cmul(high, wide)
        whole = cscale(cinv(cmul(half_gap, cone(cmul(low, high_w)))), scale)
        turned = cmul(rho, whole)
        values = [
            cmul(cone(high_w), whole), cmul(cone(low), turned),
            cmul(cone(high), turned), cmul(cone(low_w), whole),
        ]
        pivot = (2.0 + h[0], h[1])
        inverse = cinv(pivot)
        values.append(inverse)
        for _ in range(count - 1):
            inverse = cinv(csub(pivot, inverse))
            values.append(inverse)
        near = far = None
        power = block
        for level in range(1, levels):
            taken = ((z >> (level - 1)) & 1) == 1
            if near is None:
                one = (jnp.ones_like(power[0]), jnp.zeros_like(power[0]))
                near, far = cpick(taken, power, one), cpick(taken, one, power)
            else:
                grown = cmul(cpick(taken, near, far), power)
                near, far = cpick(taken, grown, near), cpick(taken, far, grown)
            power = csqr(power)
            values.append(cpick(((z >> level) & 1) == 1, near, far))
        for n, value in enumerate(values):
            store(out_ref.at[n], 0, short, row, 8, value)

    each_strip(short, 8, strip)


def join_kernel(level, levels, flags_ref, sums_ref, came_ref, base_ref, out_ref):
    z = flags_ref[2]
    short = base_ref.shape[1] // 2
    rows = 2 * short
    above = ((z >> level) & 1) == 1
    last = level + 2 == levels
    upper = ((z >> (level + 1)) & 1) == 1

    def strip(row):
        block = load(base_ref.at[3], 0, short, row, 8)
        for _ in range(level):
            block = csqr(block)
        ahead, behind = load(sums_ref, 0, short, row, 8), load(sums_ref, rows, short, row, 8)
        ahead_c, behind_c = load(came_ref, 0, short, row, 8), load(came_ref, rows, short, row, 8)
        joined = cmore(cpick(above, ahead, ahead_c), block, cpick(above, ahead_c, ahead))
        joined_b = cmore(cpick(above, behind_c, behind), block, cpick(above, behind, behind_c))
        if last:
            store(out_ref, 0, short, row, 8, cpick(upper, joined_b, joined))
        else:
            store(out_ref, 0, short, row, 8, joined)
            store(out_ref, rows, short, row, 8, joined_b)

    each_strip(short, 8, strip)
    out_ref[pl.ds(out_ref.shape[0] - TAG, TAG), :] = (
        sums_ref[pl.ds(2 * rows, TAG), :] + came_ref[pl.ds(2 * rows, TAG), :]
    )


def solved(count, levels, z, scale, modes_ref, sums_ref, came_refs, base_ref, factors_ref, row):
    short = base_ref.shape[1] // 2
    rows = 2 * short

    def factor(n):
        return load(factors_ref.at[n], 0, short, row, 8)

    enter_f = enter_b = None
    for level in range(levels):
        above = ((z >> level) & 1) == 1
        base = 0 if level == levels - 1 else jnp.where(above, 0, rows)
        came = load(came_refs[level], base, short, row, 8)
        if level:
            came = cmul(factor(4 + count + level - 1), came)
        nought = (jnp.zeros_like(came[0]), jnp.zeros_like(came[0]))
        now_f, now_b = cpick(above, came, nought), cpick(above, nought, came)
        enter_f = now_f if enter_f is None else cadd(enter_f, now_f)
        enter_b = now_b if enter_b is None else cadd(enter_b, now_b)
    block = load(base_ref.at[3], 0, short, row, 8)
    all_f = cmore(load(sums_ref, 0, short, row, 8), block, enter_f)
    all_b = cmore(load(sums_ref, rows, short, row, 8), block, enter_b)
    below = cmore(cmul(factor(0), enter_f), factor(1), all_b)
    above = cmore(cmul(factor(3), enter_b), factor(2), all_f)
    planes = [cscale(load(modes_ref, l * rows, short, row, 8), scale) for l in range(count)]
    planes[0] = cadd(planes[0], below)
    planes[-1] = cadd(planes[-1], above)
    for l in range(1, count):
        planes[l] = cmore(planes[l], factor(4 + l - 1), planes[l - 1])
    planes[-1] = cmul(factor(4 + count - 1), planes[-1])
    for l in range(count - 2, -1, -1):
        planes[l] = cmul(factor(4 + l), cadd(planes[l], planes[l + 1]))
    return below, planes, above


def middle_kernel(
    chunk, count, levels, flags_ref, numbers_ref, wave_eig_ref, sine_ref, faces_ref, field_ref,
    modes_ref, base_ref, factors_ref, sums_ref, *refs,
):
    came_refs, (found_ref, next_ref, next_sums_ref) = refs[:levels], refs[levels : levels + 3]
    give_refs, work_ref = refs[levels + 3 : -1], refs[-1]
    q, h, z = flags_ref[0], flags_ref[1], flags_ref[2]
    scale, s_re, s_im = numbers_ref[2], numbers_ref[4], numbers_ref[5]
    short = base_ref.shape[1] // 2
    rows = 2 * short
    width = base_ref.shape[2]

    def solve(row):
        below, planes, above = solved(
            count, levels, z, scale, modes_ref, sums_ref, came_refs, base_ref, factors_ref, row
        )
        store(work_ref, 0, short, row, 8, below)
        store(work_ref, (count + 1) * rows, short, row, 8, above)
        for l in range(count):
            store(work_ref, (l + 1) * rows, short, row, 8, planes[l])
            store(found_ref, l * rows, short, row, 8, planes[l])

    each_strip(short, 8, solve)
    sine_rows(work_ref, work_ref, sine_ref, (count + 2) * rows)

    def residual(i, total):
        row = pl.multiple_of(i * 8, 8)
        eigen = wave_eig_ref[q, rows_at((h * CHUNKS + chunk) * short + row, 8), :]
        under = load(work_ref, 0, short, row, 8)
        here = load(work_ref, rows, short, row, 8)
        for l in range(count):
            over = load(work_ref, (l + 2) * rows, short, row, 8)
            diag, cell, right, left, low, high = [faces_ref[n, pl.ds(l, 1), :] for n in range(6)]
            diag = s_re + (diag + cell * eigen)
            value = []
            for c in range(2):
                v = diag * here[c] - right * pltpu.roll(here[c], width - 1, 1)
                v = v - left * pltpu.roll(here[c], 1, 1)
                value.append(v - (low * under[c] + high * over[c]))
            value = (value[0] - s_im * here[1], value[1] + s_im * here[0])
            value = csub(load(field_ref, l * rows, short, row, 8), value)
            total = total + squares_of(value)
            store(work_ref, l * rows, short, row, 8, value)
            under, here = here, over
        return total

    total = lax.fori_loop(0, short // 8, residual, jnp.zeros((8, width), jnp.float32), unroll=2)
    sine_rows(work_ref, next_ref, sine_ref, count * rows)

    def sums(row):
        rho, cross_f, cross_b = [load(base_ref.at[n], 0, short, row, 8) for n in range(3)]
        planes = [load(next_ref, l * rows, short, row, 8) for l in range(count)]
        ahead, behind = sums_of(planes, rho, cross_f, cross_b)
        store(next_sums_ref, 0, short, row, 8, ahead)
        store(next_sums_ref, rows, short, row, 8, behind)

    each_strip(short, 8, sums)
    next_sums_ref[pl.ds(2 * rows, TAG), :] = sums_ref[pl.ds(2 * rows, TAG), :]
    next_sums_ref[pl.ds(2 * rows + 1, 1), :] = jnp.sum(total, axis=0, keepdims=True)
    fill_give(z, rows, next_sums_ref, give_refs)


def end_kernel(
    count, levels, flags_ref, numbers_ref, sine_ref, found_ref, modes_ref, base_ref,
    factors_ref, sums_ref, *refs,
):
    came_refs, out_refs, work_ref = refs[:levels], refs[-1 - GROUP : -1], refs[-1]
    before_refs = refs[levels + (levels > 1) : -1 - GROUP]
    z, member = flags_ref[2], flags_ref[3]
    scale = numbers_ref[2]
    short = base_ref.shape[1] // 2
    rows = 2 * short

    def solve(row):
        _, planes, _ = solved(
            count, levels, z, scale, modes_ref, sums_ref, came_refs, base_ref, factors_ref, row
        )
        for l in range(count):
            before = load(found_ref, l * rows, short, row, 8)
            store(work_ref, l * rows, short, row, 8, cadd(before, planes[l]))

    each_strip(short, 8, solve)
    sine_rows(work_ref, work_ref, sine_ref, count * rows)
    part = count // GROUP * rows
    tag_refs = (refs[levels] if levels > 1 else sums_ref, came_refs[-1])
    tag = None
    for ref in tag_refs:
        part_tag = ref[pl.ds(ref.shape[0] - TAG, TAG), :]
        tag = part_tag if tag is None else tag + part_tag
    for d in range(GROUP):
        start, whole = 0, tag
        if d in JOINT:
            held = len(before_refs) // len(JOINT)
            for ref in before_refs[JOINT.index(d) * held : (JOINT.index(d) + 1) * held]:
                out_refs[d][pl.ds(start, part), :] = ref[pl.ds(0, part), :]
                start, whole = start + part, whole + tag_of(ref)
        out_refs[d][pl.ds(start, part), :] = work_ref[rows_at((member ^ d) * part, part), :]
        out_refs[d][pl.ds(start + part, TAG), :] = whole


smem = pl.BlockSpec(memory_space=pltpu.SMEM)
vmem = pl.BlockSpec(memory_space=pltpu.VMEM)
unread = pl.BlockSpec(memory_space=pl.ANY)


def call(kernel, scalars, arrays, outs, scratch=(), flops=0, after=()):
    out_shape = [jax.ShapeDtypeStruct(shape, jnp.float32) for shape in outs]
    head = len(scalars) + len(arrays)

    def run(*refs):
        kernel(*refs[:head], *refs[head + len(after) :])

    moved = sum(a.size * a.dtype.itemsize for a in arrays) + sum(4 * int(np.prod(s)) for s in outs)
    held = moved + sum(4 * int(np.prod(s)) for s in scratch)
    return pl.pallas_call(
        run,
        out_shape=out_shape,
        in_specs=[smem] * len(scalars) + [vmem] * len(arrays) + [unread] * len(after),
        out_specs=[smem if len(shape) == 1 else vmem for shape in outs],
        scratch_shapes=[pltpu.VMEM(shape, jnp.float32) for shape in scratch],
        compiler_params=pltpu.CompilerParams(vmem_limit_bytes=held + 4 * 2**20),
        cost_estimate=pl.CostEstimate(flops=flops, bytes_accessed=moved, transcendentals=0),
    )(*scalars, *arrays, *after)


def pair_up(array, groups, flip):
    return lax.ppermute(array, "gz", [(i, i ^ flip) for i in range(groups)])


def step_by(array, groups, distance):
    return lax.ppermute(
        array, "gz", [(i, i + distance) for i in range(groups) if 0 <= i + distance < groups]
    )


def body(source, layer_ids, conduct_table, shift):
    planes, length_x, length_y = source.shape[1:]
    groups = lax.axis_size("gz")
    blocks = groups // GROUP
    levels = blocks.bit_length() - 1
    count = GROUP * planes
    length_z = planes * groups
    full = length_x // RADIX
    short = full // (HALVES * CHUNKS)
    rows = 2 * short
    if blocks < 2 or groups != GROUP << levels or planes > 2 or short % 8 or length_x != RADIX * full:
        raise ValueError("unsupported layout")
    me = lax.axis_index("gz")
    member = me % GROUP
    flags = jnp.stack([member % RADIX, member // RADIX, me // GROUP, member]).astype(jnp.int32)

    wave = wave_tables(length_x)
    wave_f = jnp.asarray(np.concatenate(two_terms(wave), axis=1))
    wave_b = jnp.asarray(np.concatenate(two_terms(np.swapaxes(wave, 1, 2) / length_x), axis=1))
    sine = jnp.asarray(two_terms(sine_table(length_y)))
    wave_eig = np.broadcast_to(wave_eigen(length_x)[:, :, None], (RADIX, full, length_y))
    wave_eig = jnp.asarray(np.ascontiguousarray(wave_eig).astype(np.float32))
    sine_eig = jnp.asarray(np.tile(sine_eigen(length_y)[None, :], (8, 1)).astype(np.float32))

    chunks = range(CHUNKS)
    row_block = (TAG, length_y)
    block = (count * rows, length_y)
    sums_block = (2 * rows + TAG, length_y)
    single = (rows + TAG, length_y)
    part = (planes * rows + TAG, length_y)
    parts = (CHUNKS * planes * rows + TAG, length_y)
    gives = [single] if levels == 1 else []
    dots = 6 * length_y * length_y

    (cells,) = call(conduct_kernel, [conduct_table], [layer_ids], [row_block])
    if levels == 1:
        below = above = pair_up(cells, groups, GROUP)
        totals = [cells, below]
    else:
        below = step_by(cells, groups, GROUP)
        above = step_by(cells, groups, -GROUP)
        total = cells
        for level in range(levels):
            (total,) = call(add_kernel, [], [total, pair_up(total, groups, GROUP << level)], [row_block])
        totals = [total]

    (ready,) = call(ready_kernel, [], [wave_f], [row_block], after=[cells])

    parted = source.reshape(2, planes, RADIX, full, length_y)
    spectra = {}
    placed = [ready]
    for d in (2, 0, 3, 1):
        made = call(
            functools.partial(forward_kernel, d, len(totals)), [flags],
            [parted, wave_f, cells, below, above, *totals], [part] * (HALVES * CHUNKS),
            scratch=[(planes, 2 * full, length_y)], flops=planes * 2 * full * dots, after=placed,
        )
        placed = made[:1]
        for n in range(HALVES):
            for t in chunks:
                spectra[d + RADIX * n, t] = made[n * CHUNKS + t]
    for t in chunks:
        for d in (6, 2, 4, 7, 3, 5, 1):
            spectra[d, t] = pair_up(spectra[d, t], groups, d)

    state = [{} for _ in chunks]

    def exchange(st, after):
        sums, give = st["sums"][0], st["sums"][-1]
        st["came"], st["tags"] = [], []
        for level in range(levels):
            st["came"].append(pair_up(give, groups, GROUP << level))
            if level + 1 < levels:
                shape = single if level + 2 == levels else sums_block
                (give,) = call(
                    functools.partial(join_kernel, level, levels), [flags], [sums, st["came"][-1], st["base"]],
                    [shape], after=after,
                )
                sums = give
                st["tags"] = [give[-TAG:]]

    def start(t, after):
        st = state[t]
        outs = [block, block, (6, rows, length_y), sums_block, *gives]
        made = call(
            functools.partial(start_kernel, t, planes, blocks, length_y * length_z),
            [flags, state[0]["numbers"] if t else shift],
            [wave_eig, sine_eig, sine] + [spectra[d, t] for d in range(GROUP)],
            outs if t else [*outs, (6,)], flops=count * rows * dots, after=after,
        )
        if not t:
            *made, st["numbers"] = made
        st["field"], st["modes"], st["base"], *st["sums"] = made
        exchange(st, [])
        return [st["sums"][-1]]

    def faces(t, after):
        state[t]["faces"] = call(
            functools.partial(faces_kernel, planes, blocks), [flags], [spectra[d, 0] for d in range(GROUP)],
            [(6, count, length_y)], scratch=[(count + 16, length_y), row_block, row_block], after=after,
        )[0]
        return [state[t]["faces"]]

    def factors(t, after):
        st = state[t]
        (st["factors"],) = call(
            functools.partial(factors_kernel, t, count, levels), [flags, state[0]["numbers"]],
            [wave_eig, sine_eig, st["base"]], [(4 + count + levels - 1, rows, length_y)], after=after,
        )
        return [st["factors"]]

    def middle(t, after):
        st = state[t]
        st["found"], st["modes"], *st["sums"] = call(
            functools.partial(middle_kernel, t, count, levels), [flags, state[0]["numbers"]],
            [wave_eig, sine, state[0]["faces"], st["field"], st["modes"], st["base"], st["factors"], st["sums"][0], *st["came"]],
            [block, block, sums_block, *gives], scratch=[((count + 2) * rows, length_y)],
            flops=(2 * count + 2) * rows * dots, after=after,
        )
        exchange(st, [])
        return [st["sums"][-1]]

    def end(t, after):
        st = state[t]
        last = t == CHUNKS - 1
        before = [state[u]["made"][d] for d in JOINT for u in range(t)] if last else []
        st["made"] = call(
            functools.partial(end_kernel, count, levels), [flags, state[0]["numbers"]],
            [sine, st["found"], st["modes"], st["base"], st["factors"], st["sums"][0], *st["came"], *st["tags"], *before],
            [parts if last and d in JOINT else part for d in range(GROUP)],
            scratch=[block], flops=count * rows * dots, after=after,
        )
        st["answers"] = {d: st["made"][d] for d in SENDS[t]}
        return [st["made"][0]]

    def answer(t, distances, after):
        answers = state[t]["answers"]
        for d in distances:
            array = answers[d]
            if after:
                array = lax.optimization_barrier((array, *after))[0]
            answers[d] = pair_up(array, groups, d)

    placed = []
    for step, t in (
        (start, 0), (faces, 0), (factors, 0), (middle, 0), (start, 1), (factors, 1), (end, 0),
    ):
        placed = step(t, placed)
    answer(0, [d for d in SENDS[0][:-1] if d not in LATER], [])
    placed = middle(1, placed)
    answer(0, LATER, placed)
    end(1, [*placed, *[state[0]["answers"][d] for d in BEFORE]])
    answer(1, SENDS[1][:-1], [])
    return call(
        functools.partial(backward_kernel, planes, length_x * length_x * length_y * length_z),
        [flags], [wave_b] + [state[t]["answers"][d] for t in chunks for d in SENDS[t]],
        [(2, planes, length_x, length_y), (2,)],
        scratch=[(planes, RADIX, 2 * full, length_y), (RADIX, planes, 2 * full, length_y)],
        flops=planes * RADIX * 2 * full * dots,
    )


def solution(mesh):
    placed = (P(None, ("node", "gz"), None, None), P(("node", "gz"), None), P(), P("node"))
    return jax.shard_map(
        body,
        mesh=mesh,
        in_specs=placed,
        out_specs=(P(None, ("node", "gz"), None, None), P("node")),
        check_vma=False,
    )
```

```python
import functools

import jax
import jax.numpy as jnp
import ml_dtypes
import numpy as np
from jax import lax
from jax.experimental import pallas as pl
from jax.experimental.pallas import tpu as pltpu
from jax.sharding import PartitionSpec as P

RADIX = 4
HALVES = 2
GROUP = RADIX * HALVES
CHUNKS = 2
SENDS = ((6, 7, 2, 3, 4, 0), (2, 6, 7, 3, 4, 5, 1, 0))
JOINT = (5, 1)
TAG = 8

relax = 0.6


def sine_table(length):
    indices = np.arange(1, length + 1)
    product = indices[:, None] * indices[None, :] % (2 * (length + 1))
    return np.sqrt(2.0 / (length + 1)) * np.sin(np.pi / (length + 1) * product)


def sine_eigen(length):
    indices = np.arange(1, length + 1)
    return 4.0 * np.sin(np.pi / (2 * (length + 1)) * indices) ** 2


def wave_numbers(length):
    return RADIX * np.arange(length // RADIX)[None, :] + np.arange(RADIX)[:, None]


def wave_eigen(length):
    return 4.0 * np.sin(np.pi / length * wave_numbers(length)) ** 2


def wave_tables(length):
    waves = wave_numbers(length)
    short = length // RADIX
    product = waves[:, :, None] * np.arange(short)[None, None, :] % length
    angles = 2.0 * np.pi / length * product
    cos_t, sin_t = np.cos(angles), np.sin(angles)
    pieces = HALVES * CHUNKS
    top = np.concatenate([cos_t, sin_t], axis=2).reshape(RADIX, pieces, short // pieces, 2 * short)
    low = np.concatenate([-sin_t, cos_t], axis=2).reshape(RADIX, pieces, short // pieces, 2 * short)
    return np.concatenate([top, low], axis=2).reshape(RADIX, 2 * short, 2 * short)


def two_terms(table):
    first = table.astype(ml_dtypes.bfloat16)
    return np.stack([first, (table - first.astype(np.float64)).astype(ml_dtypes.bfloat16)])


def split(value):
    first = value.astype(jnp.bfloat16)
    return first, (value - first.astype(jnp.float32)).astype(jnp.bfloat16)


def dot_right(value, table):
    rows = value.shape[0]
    first, second = split(value)
    wide = jnp.dot(jnp.concatenate([first, second], axis=0), table[0], preferred_element_type=jnp.float32)
    return wide[:rows] + (wide[rows:] + jnp.dot(first, table[1], preferred_element_type=jnp.float32))


def dot_left(table, value):
    rows = table.shape[0] // 2
    first, second = split(value)
    wide = jnp.dot(table, first, preferred_element_type=jnp.float32)
    return wide[:rows] + (wide[rows:] + jnp.dot(table[:rows], second, preferred_element_type=jnp.float32))


def cmul(a, b):
    return (a[0] * b[0] - a[1] * b[1], a[0] * b[1] + a[1] * b[0])


def csqr(a):
    cross = a[0] * a[1]
    return ((a[0] - a[1]) * (a[0] + a[1]), cross + cross)


def cpow(a, count):
    result = None
    while count:
        if count & 1:
            result = a if result is None else cmul(result, a)
        count >>= 1
        if count:
            a = csqr(a)
    return result


def cadd(a, b):
    return (a[0] + b[0], a[1] + b[1])


def csub(a, b):
    return (a[0] - b[0], a[1] - b[1])


def cscale(a, scale):
    return (a[0] * scale, a[1] * scale)


def cmore(total, factor, term):
    return cadd(total, cmul(factor, term))


def cinv(a):
    scale = 1.0 / (a[0] * a[0] + a[1] * a[1])
    return (a[0] * scale, -a[1] * scale)


def cone(a):
    return (1.0 - a[0], -a[1])


def cpick(cond, a, b):
    return (jnp.where(cond, a[0], b[0]), jnp.where(cond, a[1], b[1]))


def rows_at(start, rows):
    if isinstance(start, int):
        return pl.ds(start, rows)
    return pl.ds(pl.multiple_of(start, 8), rows)


def load(ref, base, short, row, rows):
    return (ref[rows_at(base + row, rows), :], ref[rows_at(base + short + row, rows), :])


def store(ref, base, short, row, rows, value):
    ref[rows_at(base + row, rows), :] = value[0]
    ref[rows_at(base + short + row, rows), :] = value[1]


def each_strip(count, rows, body):
    def step(i, carry):
        body(pl.multiple_of(i * rows, rows))
        return carry

    steps = count // rows
    lax.fori_loop(0, steps, step, 0, unroll=min(steps, 4))


def squares_of(a):
    return a[0] * a[0] + a[1] * a[1]


def conduct_kernel(table_ref, ids_ref, out_ref):
    planes = ids_ref.shape[0]
    ids = ids_ref[...]
    cells = jnp.zeros(ids.shape, jnp.float32)
    for layer in range(table_ref.shape[0]):
        cells = jnp.where(ids == layer, table_ref[layer], cells)
    out_ref[...] = jnp.zeros_like(out_ref)
    out_ref[pl.ds(0, planes), :] = cells
    out_ref[pl.ds(TAG - 1, 1), :] = jnp.sum(cells, axis=0, keepdims=True)


def ready_kernel(source_ref, wave_ref, out_ref):
    out_ref[...] = source_ref[0, 0, 0, pl.ds(0, TAG), :]


def add_kernel(one_ref, two_ref, out_ref):
    out_ref[...] = one_ref[...] + two_ref[...]


def fill_tag(out_ref, planes, own_ref, below_ref, above_ref, part_refs):
    start = out_ref.shape[0] - TAG
    for n, ref in enumerate((own_ref, below_ref, above_ref)):
        out_ref[pl.ds(start + n * planes, planes), :] = ref[pl.ds(0, planes), :]
    total = part_refs[0][pl.ds(TAG - 1, 1), :]
    for ref in part_refs[1:]:
        total = total + ref[pl.ds(TAG - 1, 1), :]
    out_ref[pl.ds(start + TAG - 1, 1), :] = total


def tag_of(ref):
    return ref[pl.ds(ref.shape[0] - TAG, TAG), :]


def find_numbers(cells_total, shift_ref, part_refs, numbers_ref):
    total = None
    for ref in part_refs:
        row = ref[pl.ds(ref.shape[0] - 1, 1), :]
        total = row if total is None else total + row
    inv = (1.0 / (jnp.sum(total, axis=1, keepdims=True) * (1.0 / cells_total)))[0, 0]
    numbers_ref[0] = shift_ref[0] * inv
    numbers_ref[1] = shift_ref[1] * inv
    numbers_ref[2] = relax * inv
    numbers_ref[3] = 0.5 * relax * inv
    numbers_ref[4] = shift_ref[0]
    numbers_ref[5] = shift_ref[1]


def faces_kernel(planes, blocks, flags_ref, *refs):
    part_refs, (faces_ref, padded_ref, below_ref, above_ref) = refs[:GROUP], refs[GROUP:]
    z, member = flags_ref[2], flags_ref[3]
    _, count, width = faces_ref.shape
    for d, ref in enumerate(part_refs):
        tag = tag_of(ref)
        place = member ^ d
        for p in range(planes):
            padded_ref[pl.ds(8 + place * planes + p, 1), :] = tag[p : p + 1]
        below_ref[pl.ds(place, 1), :] = tag[2 * planes - 1 : 2 * planes]
        above_ref[pl.ds(place, 1), :] = tag[2 * planes : 2 * planes + 1]
    cells = padded_ref[pl.ds(8, count), :]
    padded_ref[pl.ds(7, 1), :] = jnp.where(z == 0, cells[0:1], below_ref[pl.ds(GROUP - 1, 1), :])
    padded_ref[pl.ds(8 + count, 1), :] = jnp.where(
        z == blocks - 1, cells[count - 1 : count], above_ref[pl.ds(0, 1), :]
    )
    lane = lax.broadcasted_iota(jnp.int32, cells.shape, 1)
    last, first = lane == width - 1, lane == 0
    right = 0.5 * (cells + pltpu.roll(cells, width - 1, 1))
    left = 0.5 * (cells + pltpu.roll(cells, 1, 1))
    low = 0.5 * (cells + padded_ref[pl.ds(7, count), :])
    high = 0.5 * (cells + padded_ref[pl.ds(9, count), :])
    faces_ref[0] = jnp.where(last, cells, right) + jnp.where(first, cells, left) + (low + high)
    faces_ref[1] = cells
    faces_ref[2] = jnp.where(last, 0.0, right)
    faces_ref[3] = jnp.where(first, 0.0, left)
    faces_ref[4] = low
    faces_ref[5] = high


def forward_kernel(distance, parts_count, flags_ref, source_ref, wave_ref, own_ref, below_ref, above_ref, *refs):
    part_refs, out_refs, stage_ref = refs[:parts_count], refs[parts_count:-1], refs[-1]
    planes = source_ref.shape[1]
    q = flags_ref[0] ^ distance
    sign = (1 - 2 * (q & 1)).astype(jnp.float32)
    turn_re = jnp.where(q == 0, 1.0, jnp.where(q == 2, -1.0, 0.0))
    turn_im = jnp.where(q == 1, 1.0, jnp.where(q == 3, -1.0, 0.0))
    rows = stage_ref.shape[1] // (HALVES * CHUNKS)
    for p in range(planes):
        parts = [[source_ref[c, p, i] for i in range(RADIX)] for c in range(2)]
        even = [parts[c][0] + sign * parts[c][2] for c in range(2)]
        odd = [parts[c][1] + sign * parts[c][3] for c in range(2)]
        mixed = jnp.concatenate(
            [
                even[0] + (turn_re * odd[0] + turn_im * odd[1]),
                even[1] + (turn_re * odd[1] - turn_im * odd[0]),
            ],
            axis=0,
        )
        stage_ref[p] = dot_left(wave_ref[q], mixed)
        for n in range(HALVES):
            h = flags_ref[1] ^ n
            for t in range(CHUNKS):
                out_refs[n * CHUNKS + t][pl.ds(p * rows, rows), :] = stage_ref[
                    p, rows_at((h * CHUNKS + t) * rows, rows), :
                ]
    for ref in out_refs:
        fill_tag(ref, planes, own_ref, below_ref, above_ref, part_refs)


def backward_kernel(planes, cells, flags_ref, wave_ref, *refs):
    arrays, (out_ref, norms_ref, mixed_ref, stage_ref) = refs[:-4], refs[-4:]
    rows = (arrays[0].shape[0] - TAG) // planes
    came = {}
    for (t, d), ref in zip([(t, d) for t in range(CHUNKS) for d in SENDS[t]], arrays):
        for n in range(CHUNKS if d in JOINT else 1):
            came[d, n if d in JOINT else t] = ref.at[pl.ds(n * planes * rows, planes * rows)]
    short = rows * CHUNKS * HALVES // 2
    total = None
    for ref in arrays:
        tag = tag_of(ref)
        total = tag if total is None else total + tag
    for d in range(RADIX):
        q = flags_ref[0] ^ d
        for p in range(planes):
            for n in range(HALVES):
                h = flags_ref[1] ^ n
                for t in range(CHUNKS):
                    stage_ref[d, p, rows_at((h * CHUNKS + t) * rows, rows), :] = came[d + RADIX * n, t][
                        pl.ds(p * rows, rows), :
                    ]
            mixed_ref[p, q] = dot_left(wave_ref[q], stage_ref[d, p])
    for p in range(planes):

        def strip(row):
            zero, one, two, three = [load(mixed_ref.at[p, q], 0, short, row, 8) for q in range(RADIX)]
            even, odd = cadd(zero, two), cadd(one, three)
            even_d, odd_d = csub(zero, two), csub(one, three)
            parts = (
                cadd(even, odd),
                (even_d[0] - odd_d[1], even_d[1] + odd_d[0]),
                csub(even, odd),
                (even_d[0] + odd_d[1], even_d[1] - odd_d[0]),
            )
            for i in range(RADIX):
                for c in range(2):
                    out_ref[c, p, rows_at(i * short + row, 8), :] = parts[i][c]

        each_strip(short, 8, strip)
    norms = jnp.sqrt(jnp.sum(total, axis=1, keepdims=True) * (1.0 / cells))
    for n in range(norms_ref.shape[0]):
        norms_ref[n] = norms[n, 0]


def decay_root(h):
    sq = (h[0] + 0.25 * (h[0] * h[0] - h[1] * h[1]), h[1] + 0.5 * h[0] * h[1])
    size = jnp.sqrt(squares_of(sq))
    root_re = jnp.sqrt(0.5 * (size + sq[0]))
    root = (root_re, 0.5 * sq[1] / root_re)
    return cinv((1.0 + 0.5 * h[0] + root[0], 0.5 * h[1] + root[1])), root


def two_powers(power, z, stacks):
    low = high = None
    bit = 0
    while (1 << bit) < stacks:
        taken = ((z >> bit) & 1) == 1
        if low is None:
            one = (jnp.ones_like(power[0]), jnp.zeros_like(power[0]))
            low, high = cpick(taken, power, one), cpick(taken, one, power)
        else:
            grown = cmul(cpick(taken, low, high), power)
            low, high = cpick(taken, grown, low), cpick(taken, high, grown)
        power = csqr(power)
        bit += 1
    return low, high


def sums_of(planes, rho, cross_f, cross_b):
    ahead = planes[0]
    for a in planes[1:]:
        ahead = cmore(a, rho, ahead)
    behind = planes[-1]
    for a in planes[-2::-1]:
        behind = cmore(a, rho, behind)
    return csub(ahead, cmul(cross_f, behind)), csub(behind, cmul(cross_b, ahead))


def sine_rows(source_ref, target_ref, sine_ref, count):
    sine = (sine_ref[0], sine_ref[1])
    rows = max(n for n in range(16, 641, 16) if count % n == 0)
    for i in range(0, count, rows):
        target_ref[pl.ds(i, rows), :] = dot_right(source_ref[pl.ds(i, rows), :], sine)


def fill_give(z, rows, sums_ref, give_refs):
    for ref in give_refs:
        ref[pl.ds(0, rows), :] = sums_ref[rows_at((z & 1) * rows, rows), :]
        ref[pl.ds(rows, TAG), :] = sums_ref[pl.ds(2 * rows, TAG), :]


def start_kernel(
    chunk, planes, blocks, cells_total, flags_ref, numbers_ref, wave_eig_ref, sine_eig_ref, sine_ref, *refs,
):
    part_refs, (field_ref, modes_ref, base_ref, sums_ref), give_refs = refs[:GROUP], refs[GROUP : GROUP + 4], refs[GROUP + 4 :]
    if chunk == 0:
        shift_ref, numbers_ref, give_refs = numbers_ref, give_refs[-1], give_refs[:-1]
        find_numbers(cells_total, shift_ref, part_refs, numbers_ref)
    q, h, z, member = [flags_ref[n] for n in range(4)]
    rows = base_ref.shape[1]
    part = rows * planes
    short = rows // 2
    count = GROUP * planes
    first_row = (h * CHUNKS + chunk) * short
    for d, ref in enumerate(part_refs):
        field_ref[rows_at((member ^ d) * part, part), :] = ref[pl.ds(0, part), :]
    sine_rows(field_ref, modes_ref, sine_ref, count * rows)
    h_re, h_im = numbers_ref[0], numbers_ref[1]
    sine_eig = sine_eig_ref[...]

    def strip(i, total):
        row = pl.multiple_of(i * 8, 8)
        eigen = wave_eig_ref[q, rows_at(first_row + row, 8), :] + sine_eig
        rho, _ = decay_root((eigen + h_re, jnp.full_like(eigen, h_im)))
        block = cpow(rho, count)
        next_one = cmul(block, rho)
        low, high = two_powers(csqr(block), z, blocks)
        cross_f, cross_b = cmul(next_one, low), cmul(next_one, high)
        for n, value in enumerate((rho, cross_f, cross_b, block, low, high)):
            store(base_ref.at[n], 0, short, row, 8, value)
        found = [load(modes_ref, l * rows, short, row, 8) for l in range(count)]
        ahead, behind = sums_of(found, rho, cross_f, cross_b)
        store(sums_ref, 0, short, row, 8, ahead)
        store(sums_ref, rows, short, row, 8, behind)
        for l in range(count):
            total = total + squares_of(load(field_ref, l * rows, short, row, 8))
        return total

    total = lax.fori_loop(
        0, short // 8, strip, jnp.zeros((8, field_ref.shape[1]), jnp.float32), unroll=2
    )
    sums_ref[pl.ds(2 * rows, TAG), :] = jnp.zeros((TAG, field_ref.shape[1]), jnp.float32)
    sums_ref[pl.ds(2 * rows, 1), :] = jnp.sum(total, axis=0, keepdims=True)
    fill_give(z, rows, sums_ref, give_refs)


def factors_kernel(
    chunk, count, levels, flags_ref, numbers_ref, wave_eig_ref, sine_eig_ref, base_ref, out_ref,
):
    q, h_part, z = flags_ref[0], flags_ref[1], flags_ref[2]
    short = base_ref.shape[1] // 2
    h_re, h_im, scale = numbers_ref[0], numbers_ref[1], numbers_ref[3]
    sine_eig = sine_eig_ref[...]

    def strip(row):
        eigen = wave_eig_ref[q, rows_at((h_part * CHUNKS + chunk) * short + row, 8), :] + sine_eig
        h = (eigen + h_re, jnp.full_like(eigen, h_im))
        rho, _, _, block, low, high = [load(base_ref.at[n], 0, short, row, 8) for n in range(6)]
        half_gap = csub((1.0 + 0.5 * h[0], 0.5 * h[1]), rho)
        wide = cmul(csqr(block), csqr(rho))
        low_w, high_w = cmul(low, wide), cmul(high, wide)
        whole = cscale(cinv(cmul(half_gap, cone(cmul(low, high_w)))), scale)
        turned = cmul(rho, whole)
        values = [
            cmul(cone(high_w), whole), cmul(cone(low), turned),
            cmul(cone(high), turned), cmul(cone(low_w), whole),
        ]
        pivot = (2.0 + h[0], h[1])
        inverse = cinv(pivot)
        values.append(inverse)
        for _ in range(count - 1):
            inverse = cinv(csub(pivot, inverse))
            values.append(inverse)
        near = far = None
        power = block
        for level in range(1, levels):
            taken = ((z >> (level - 1)) & 1) == 1
            if near is None:
                one = (jnp.ones_like(power[0]), jnp.zeros_like(power[0]))
                near, far = cpick(taken, power, one), cpick(taken, one, power)
            else:
                grown = cmul(cpick(taken, near, far), power)
                near, far = cpick(taken, grown, near), cpick(taken, far, grown)
            power = csqr(power)
            values.append(cpick(((z >> level) & 1) == 1, near, far))
        for n, value in enumerate(values):
            store(out_ref.at[n], 0, short, row, 8, value)

    each_strip(short, 8, strip)


def join_kernel(level, levels, flags_ref, sums_ref, came_ref, base_ref, out_ref):
    z = flags_ref[2]
    short = base_ref.shape[1] // 2
    rows = 2 * short
    above = ((z >> level) & 1) == 1
    last = level + 2 == levels
    upper = ((z >> (level + 1)) & 1) == 1

    def strip(row):
        block = load(base_ref.at[3], 0, short, row, 8)
        for _ in range(level):
            block = csqr(block)
        ahead, behind = load(sums_ref, 0, short, row, 8), load(sums_ref, rows, short, row, 8)
        ahead_c, behind_c = load(came_ref, 0, short, row, 8), load(came_ref, rows, short, row, 8)
        joined = cmore(cpick(above, ahead, ahead_c), block, cpick(above, ahead_c, ahead))
        joined_b = cmore(cpick(above, behind_c, behind), block, cpick(above, behind, behind_c))
        if last:
            store(out_ref, 0, short, row, 8, cpick(upper, joined_b, joined))
        else:
            store(out_ref, 0, short, row, 8, joined)
            store(out_ref, rows, short, row, 8, joined_b)

    each_strip(short, 8, strip)
    out_ref[pl.ds(out_ref.shape[0] - TAG, TAG), :] = (
        sums_ref[pl.ds(2 * rows, TAG), :] + came_ref[pl.ds(2 * rows, TAG), :]
    )


def solved(count, levels, z, scale, modes_ref, sums_ref, came_refs, base_ref, factors_ref, row):
    short = base_ref.shape[1] // 2
    rows = 2 * short

    def factor(n):
        return load(factors_ref.at[n], 0, short, row, 8)

    enter_f = enter_b = None
    for level in range(levels):
        above = ((z >> level) & 1) == 1
        base = 0 if level == levels - 1 else jnp.where(above, 0, rows)
        came = load(came_refs[level], base, short, row, 8)
        if level:
            came = cmul(factor(4 + count + level - 1), came)
        nought = (jnp.zeros_like(came[0]), jnp.zeros_like(came[0]))
        now_f, now_b = cpick(above, came, nought), cpick(above, nought, came)
        enter_f = now_f if enter_f is None else cadd(enter_f, now_f)
        enter_b = now_b if enter_b is None else cadd(enter_b, now_b)
    block = load(base_ref.at[3], 0, short, row, 8)
    all_f = cmore(load(sums_ref, 0, short, row, 8), block, enter_f)
    all_b = cmore(load(sums_ref, rows, short, row, 8), block, enter_b)
    below = cmore(cmul(factor(0), enter_f), factor(1), all_b)
    above = cmore(cmul(factor(3), enter_b), factor(2), all_f)
    planes = [cscale(load(modes_ref, l * rows, short, row, 8), scale) for l in range(count)]
    planes[0] = cadd(planes[0], below)
    planes[-1] = cadd(planes[-1], above)
    for l in range(1, count):
        planes[l] = cmore(planes[l], factor(4 + l - 1), planes[l - 1])
    planes[-1] = cmul(factor(4 + count - 1), planes[-1])
    for l in range(count - 2, -1, -1):
        planes[l] = cmul(factor(4 + l), cadd(planes[l], planes[l + 1]))
    return below, planes, above


def middle_kernel(
    chunk, count, levels, flags_ref, numbers_ref, wave_eig_ref, sine_ref, faces_ref, field_ref,
    modes_ref, base_ref, factors_ref, sums_ref, *refs,
):
    came_refs, (found_ref, next_ref, next_sums_ref) = refs[:levels], refs[levels : levels + 3]
    give_refs, work_ref = refs[levels + 3 : -1], refs[-1]
    q, h, z = flags_ref[0], flags_ref[1], flags_ref[2]
    scale, s_re, s_im = numbers_ref[2], numbers_ref[4], numbers_ref[5]
    short = base_ref.shape[1] // 2
    rows = 2 * short
    width = base_ref.shape[2]

    def solve(row):
        below, planes, above = solved(
            count, levels, z, scale, modes_ref, sums_ref, came_refs, base_ref, factors_ref, row
        )
        store(work_ref, 0, short, row, 8, below)
        store(work_ref, (count + 1) * rows, short, row, 8, above)
        for l in range(count):
            store(work_ref, (l + 1) * rows, short, row, 8, planes[l])
            store(found_ref, l * rows, short, row, 8, planes[l])

    each_strip(short, 8, solve)
    sine_rows(work_ref, work_ref, sine_ref, (count + 2) * rows)

    def residual(i, total):
        row = pl.multiple_of(i * 8, 8)
        eigen = wave_eig_ref[q, rows_at((h * CHUNKS + chunk) * short + row, 8), :]
        under = load(work_ref, 0, short, row, 8)
        here = load(work_ref, rows, short, row, 8)
        for l in range(count):
            over = load(work_ref, (l + 2) * rows, short, row, 8)
            diag, cell, right, left, low, high = [faces_ref[n, pl.ds(l, 1), :] for n in range(6)]
            diag = s_re + (diag + cell * eigen)
            value = []
            for c in range(2):
                v = diag * here[c] - right * pltpu.roll(here[c], width - 1, 1)
                v = v - left * pltpu.roll(here[c], 1, 1)
                value.append(v - (low * under[c] + high * over[c]))
            value = (value[0] - s_im * here[1], value[1] + s_im * here[0])
            value = csub(load(field_ref, l * rows, short, row, 8), value)
            total = total + squares_of(value)
            store(work_ref, l * rows, short, row, 8, value)
            under, here = here, over
        return total

    total = lax.fori_loop(0, short // 8, residual, jnp.zeros((8, width), jnp.float32), unroll=2)
    sine_rows(work_ref, next_ref, sine_ref, count * rows)

    def sums(row):
        rho, cross_f, cross_b = [load(base_ref.at[n], 0, short, row, 8) for n in range(3)]
        planes = [load(next_ref, l * rows, short, row, 8) for l in range(count)]
        ahead, behind = sums_of(planes, rho, cross_f, cross_b)
        store(next_sums_ref, 0, short, row, 8, ahead)
        store(next_sums_ref, rows, short, row, 8, behind)

    each_strip(short, 8, sums)
    next_sums_ref[pl.ds(2 * rows, TAG), :] = sums_ref[pl.ds(2 * rows, TAG), :]
    next_sums_ref[pl.ds(2 * rows + 1, 1), :] = jnp.sum(total, axis=0, keepdims=True)
    fill_give(z, rows, next_sums_ref, give_refs)


def end_kernel(
    count, levels, flags_ref, numbers_ref, sine_ref, found_ref, modes_ref, base_ref,
    factors_ref, sums_ref, *refs,
):
    came_refs, out_refs, work_ref = refs[:levels], refs[-1 - GROUP : -1], refs[-1]
    before_refs = refs[levels + (levels > 1) : -1 - GROUP]
    z, member = flags_ref[2], flags_ref[3]
    scale = numbers_ref[2]
    short = base_ref.shape[1] // 2
    rows = 2 * short

    def solve(row):
        _, planes, _ = solved(
            count, levels, z, scale, modes_ref, sums_ref, came_refs, base_ref, factors_ref, row
        )
        for l in range(count):
            before = load(found_ref, l * rows, short, row, 8)
            store(work_ref, l * rows, short, row, 8, cadd(before, planes[l]))

    each_strip(short, 8, solve)
    sine_rows(work_ref, work_ref, sine_ref, count * rows)
    part = count // GROUP * rows
    tag_refs = (refs[levels] if levels > 1 else sums_ref, came_refs[-1])
    tag = None
    for ref in tag_refs:
        part_tag = ref[pl.ds(ref.shape[0] - TAG, TAG), :]
        tag = part_tag if tag is None else tag + part_tag
    for d in range(GROUP):
        start, whole = 0, tag
        if d in JOINT:
            held = len(before_refs) // len(JOINT)
            for ref in before_refs[JOINT.index(d) * held : (JOINT.index(d) + 1) * held]:
                out_refs[d][pl.ds(start, part), :] = ref[pl.ds(0, part), :]
                start, whole = start + part, whole + tag_of(ref)
        out_refs[d][pl.ds(start, part), :] = work_ref[rows_at((member ^ d) * part, part), :]
        out_refs[d][pl.ds(start + part, TAG), :] = whole


smem = pl.BlockSpec(memory_space=pltpu.SMEM)
vmem = pl.BlockSpec(memory_space=pltpu.VMEM)
unread = pl.BlockSpec(memory_space=pl.ANY)


def call(kernel, scalars, arrays, outs, scratch=(), flops=0, after=()):
    out_shape = [jax.ShapeDtypeStruct(shape, jnp.float32) for shape in outs]
    head = len(scalars) + len(arrays)

    def run(*refs):
        kernel(*refs[:head], *refs[head + len(after) :])

    moved = sum(a.size * a.dtype.itemsize for a in arrays) + sum(4 * int(np.prod(s)) for s in outs)
    held = moved + sum(4 * int(np.prod(s)) for s in scratch)
    return pl.pallas_call(
        run,
        out_shape=out_shape,
        in_specs=[smem] * len(scalars) + [vmem] * len(arrays) + [unread] * len(after),
        out_specs=[smem if len(shape) == 1 else vmem for shape in outs],
        scratch_shapes=[pltpu.VMEM(shape, jnp.float32) for shape in scratch],
        compiler_params=pltpu.CompilerParams(vmem_limit_bytes=held + 4 * 2**20),
        cost_estimate=pl.CostEstimate(flops=flops, bytes_accessed=moved, transcendentals=0),
    )(*scalars, *arrays, *after)


def pair_up(array, groups, flip):
    return lax.ppermute(array, "gz", [(i, i ^ flip) for i in range(groups)])


def step_by(array, groups, distance):
    return lax.ppermute(
        array, "gz", [(i, i + distance) for i in range(groups) if 0 <= i + distance < groups]
    )


def body(source, layer_ids, conduct_table, shift):
    planes, length_x, length_y = source.shape[1:]
    groups = lax.axis_size("gz")
    blocks = groups // GROUP
    levels = blocks.bit_length() - 1
    count = GROUP * planes
    length_z = planes * groups
    full = length_x // RADIX
    short = full // (HALVES * CHUNKS)
    rows = 2 * short
    if blocks < 2 or groups != GROUP << levels or planes > 2 or short % 8 or length_x != RADIX * full:
        raise ValueError("unsupported layout")
    me = lax.axis_index("gz")
    member = me % GROUP
    flags = jnp.stack([member % RADIX, member // RADIX, me // GROUP, member]).astype(jnp.int32)

    wave = wave_tables(length_x)
    wave_f = jnp.asarray(np.concatenate(two_terms(wave), axis=1))
    wave_b = jnp.asarray(np.concatenate(two_terms(np.swapaxes(wave, 1, 2) / length_x), axis=1))
    sine = jnp.asarray(two_terms(sine_table(length_y)))
    wave_eig = np.broadcast_to(wave_eigen(length_x)[:, :, None], (RADIX, full, length_y))
    wave_eig = jnp.asarray(np.ascontiguousarray(wave_eig).astype(np.float32))
    sine_eig = jnp.asarray(np.tile(sine_eigen(length_y)[None, :], (8, 1)).astype(np.float32))

    chunks = range(CHUNKS)
    row_block = (TAG, length_y)
    block = (count * rows, length_y)
    sums_block = (2 * rows + TAG, length_y)
    single = (rows + TAG, length_y)
    part = (planes * rows + TAG, length_y)
    parts = (CHUNKS * planes * rows + TAG, length_y)
    gives = [single] if levels == 1 else []
    dots = 6 * length_y * length_y

    (cells,) = call(conduct_kernel, [conduct_table], [layer_ids], [row_block])
    if levels == 1:
        below = above = pair_up(cells, groups, GROUP)
        totals = [cells, below]
    else:
        below = step_by(cells, groups, GROUP)
        above = step_by(cells, groups, -GROUP)
        total = cells
        for level in range(levels):
            (total,) = call(add_kernel, [], [total, pair_up(total, groups, GROUP << level)], [row_block])
        totals = [total]

    (ready,) = call(ready_kernel, [], [source.reshape(2, planes, RADIX, full, length_y), wave_f], [row_block], after=[cells])

    parted = source.reshape(2, planes, RADIX, full, length_y)
    spectra = {}
    placed = [ready]
    for d in (2, 0, 3, 1):
        made = call(
            functools.partial(forward_kernel, d, len(totals)), [flags],
            [parted, wave_f, cells, below, above, *totals], [part] * (HALVES * CHUNKS),
            scratch=[(planes, 2 * full, length_y)], flops=planes * 2 * full * dots, after=placed,
        )
        placed = made[:1]
        for n in range(HALVES):
            for t in chunks:
                spectra[d + RADIX * n, t] = made[n * CHUNKS + t]
    for t in chunks:
        for d in (6, 2, 4, 7, 3, 5, 1):
            spectra[d, t] = pair_up(spectra[d, t], groups, d)

    state = [{} for _ in chunks]

    def exchange(st, after):
        sums, give = st["sums"][0], st["sums"][-1]
        st["came"], st["tags"] = [], []
        for level in range(levels):
            st["came"].append(pair_up(give, groups, GROUP << level))
            if level + 1 < levels:
                shape = single if level + 2 == levels else sums_block
                (give,) = call(
                    functools.partial(join_kernel, level, levels), [flags], [sums, st["came"][-1], st["base"]],
                    [shape], after=after,
                )
                sums = give
                st["tags"] = [give[-TAG:]]

    def start(t, after):
        st = state[t]
        outs = [block, block, (6, rows, length_y), sums_block, *gives]
        made = call(
            functools.partial(start_kernel, t, planes, blocks, length_y * length_z),
            [flags, state[0]["numbers"] if t else shift],
            [wave_eig, sine_eig, sine] + [spectra[d, t] for d in range(GROUP)],
            outs if t else [*outs, (6,)], flops=count * rows * dots, after=after,
        )
        if not t:
            *made, st["numbers"] = made
        st["field"], st["modes"], st["base"], *st["sums"] = made
        exchange(st, [])
        return [st["sums"][-1]]

    def faces(t, after):
        state[t]["faces"] = call(
            functools.partial(faces_kernel, planes, blocks), [flags], [spectra[d, 0] for d in range(GROUP)],
            [(6, count, length_y)], scratch=[(count + 16, length_y), row_block, row_block], after=after,
        )[0]
        return [state[t]["faces"]]

    def factors(t, after):
        st = state[t]
        (st["factors"],) = call(
            functools.partial(factors_kernel, t, count, levels), [flags, state[0]["numbers"]],
            [wave_eig, sine_eig, st["base"]], [(4 + count + levels - 1, rows, length_y)], after=after,
        )
        return [st["factors"]]

    def middle(t, after):
        st = state[t]
        st["found"], st["modes"], *st["sums"] = call(
            functools.partial(middle_kernel, t, count, levels), [flags, state[0]["numbers"]],
            [wave_eig, sine, state[0]["faces"], st["field"], st["modes"], st["base"], st["factors"], st["sums"][0], *st["came"]],
            [block, block, sums_block, *gives], scratch=[((count + 2) * rows, length_y)],
            flops=(2 * count + 2) * rows * dots, after=after,
        )
        exchange(st, [])
        return [st["sums"][-1]]

    def end(t, after):
        st = state[t]
        last = t == CHUNKS - 1
        before = [state[u]["made"][d] for d in JOINT for u in range(t)] if last else []
        st["made"] = call(
            functools.partial(end_kernel, count, levels), [flags, state[0]["numbers"]],
            [sine, st["found"], st["modes"], st["base"], st["factors"], st["sums"][0], *st["came"], *st["tags"], *before],
            [parts if last and d in JOINT else part for d in range(GROUP)],
            scratch=[block], flops=count * rows * dots, after=after,
        )
        st["answers"] = {d: st["made"][d] for d in SENDS[t]}
        return [st["made"][0]]

    def answer(t):
        answers = state[t]["answers"]
        for d in SENDS[t][:-1]:
            array = answers[d]
            if d in JOINT:
                array, _ = lax.optimization_barrier((array, answers[SENDS[t][0]]))
            answers[d] = pair_up(array, groups, d)

    placed = []
    for step, t in (
        (start, 0), (faces, 0), (factors, 0), (middle, 0), (start, 1), (factors, 1), (end, 0),
    ):
        placed = step(t, placed)
    answer(0)
    placed = middle(1, placed)
    end(1, [*placed, *[state[0]["answers"][d] for d in SENDS[0][:2]]])
    answer(1)
    return call(
        functools.partial(backward_kernel, planes, length_x * length_x * length_y * length_z),
        [flags], [wave_b] + [state[t]["answers"][d] for t in chunks for d in SENDS[t]],
        [(2, planes, length_x, length_y), (2,)],
        scratch=[(planes, RADIX, 2 * full, length_y), (RADIX, planes, 2 * full, length_y)],
        flops=planes * RADIX * 2 * full * dots,
    )


def solution(mesh):
    placed = (P(None, ("node", "gz"), None, None), P(("node", "gz"), None), P(), P("node"))
    return jax.shard_map(
        body,
        mesh=mesh,
        in_specs=placed,
        out_specs=(P(None, ("node", "gz"), None, None), P("node")),
        check_vma=False,
    )
```

```python
import functools

import jax
import jax.numpy as jnp
import ml_dtypes
import numpy as np
from jax import lax
from jax.experimental import pallas as pl
from jax.experimental.pallas import tpu as pltpu
from jax.sharding import PartitionSpec as P

RADIX = 4
HALVES = 2
GROUP = RADIX * HALVES
CHUNKS = 2
SENDS = ((6, 7, 2, 3, 4, 0), (2, 6, 7, 3, 4, 5, 1, 0))
ANSWERS = (
    *((0, d) for d in (6, 7, 2, 3, 0)),
    *((1, d) for d in (2, 6)),
    (0, 4),
    *((1, d) for d in (7, 3, 4, 5, 1, 0)),
)
JOINT = (5, 1)
TAG = 8

relax = 0.6


def sine_table(length):
    indices = np.arange(1, length + 1)
    product = indices[:, None] * indices[None, :] % (2 * (length + 1))
    return np.sqrt(2.0 / (length + 1)) * np.sin(np.pi / (length + 1) * product)


def sine_eigen(length):
    indices = np.arange(1, length + 1)
    return 4.0 * np.sin(np.pi / (2 * (length + 1)) * indices) ** 2


def wave_numbers(length):
    return RADIX * np.arange(length // RADIX)[None, :] + np.arange(RADIX)[:, None]


def wave_eigen(length):
    return 4.0 * np.sin(np.pi / length * wave_numbers(length)) ** 2


def wave_tables(length):
    waves = wave_numbers(length)
    short = length // RADIX
    product = waves[:, :, None] * np.arange(short)[None, None, :] % length
    angles = 2.0 * np.pi / length * product
    cos_t, sin_t = np.cos(angles), np.sin(angles)
    pieces = HALVES * CHUNKS
    top = np.concatenate([cos_t, sin_t], axis=2).reshape(RADIX, pieces, short // pieces, 2 * short)
    low = np.concatenate([-sin_t, cos_t], axis=2).reshape(RADIX, pieces, short // pieces, 2 * short)
    return np.concatenate([top, low], axis=2).reshape(RADIX, 2 * short, 2 * short)


def two_terms(table):
    first = table.astype(ml_dtypes.bfloat16)
    return np.stack([first, (table - first.astype(np.float64)).astype(ml_dtypes.bfloat16)])


def split(value):
    first = value.astype(jnp.bfloat16)
    return first, (value - first.astype(jnp.float32)).astype(jnp.bfloat16)


def dot_right(value, table):
    rows = value.shape[0]
    first, second = split(value)
    wide = jnp.dot(jnp.concatenate([first, second], axis=0), table[0], preferred_element_type=jnp.float32)
    return wide[:rows] + (wide[rows:] + jnp.dot(first, table[1], preferred_element_type=jnp.float32))


def dot_left(table, value):
    rows = table.shape[0] // 2
    first, second = split(value)
    wide = jnp.dot(table, first, preferred_element_type=jnp.float32)
    return wide[:rows] + (wide[rows:] + jnp.dot(table[:rows], second, preferred_element_type=jnp.float32))


def cmul(a, b):
    return (a[0] * b[0] - a[1] * b[1], a[0] * b[1] + a[1] * b[0])


def csqr(a):
    cross = a[0] * a[1]
    return ((a[0] - a[1]) * (a[0] + a[1]), cross + cross)


def cpow(a, count):
    result = None
    while count:
        if count & 1:
            result = a if result is None else cmul(result, a)
        count >>= 1
        if count:
            a = csqr(a)
    return result


def cadd(a, b):
    return (a[0] + b[0], a[1] + b[1])


def csub(a, b):
    return (a[0] - b[0], a[1] - b[1])


def cscale(a, scale):
    return (a[0] * scale, a[1] * scale)


def cmore(total, factor, term):
    return cadd(total, cmul(factor, term))


def cinv(a):
    scale = 1.0 / (a[0] * a[0] + a[1] * a[1])
    return (a[0] * scale, -a[1] * scale)


def cone(a):
    return (1.0 - a[0], -a[1])


def cpick(cond, a, b):
    return (jnp.where(cond, a[0], b[0]), jnp.where(cond, a[1], b[1]))


def rows_at(start, rows):
    if isinstance(start, int):
        return pl.ds(start, rows)
    return pl.ds(pl.multiple_of(start, 8), rows)


def load(ref, base, short, row, rows):
    return (ref[rows_at(base + row, rows), :], ref[rows_at(base + short + row, rows), :])


def store(ref, base, short, row, rows, value):
    ref[rows_at(base + row, rows), :] = value[0]
    ref[rows_at(base + short + row, rows), :] = value[1]


def each_strip(count, rows, body):
    def step(i, carry):
        body(pl.multiple_of(i * rows, rows))
        return carry

    steps = count // rows
    lax.fori_loop(0, steps, step, 0, unroll=min(steps, 4))


def squares_of(a):
    return a[0] * a[0] + a[1] * a[1]


def conduct_kernel(table_ref, ids_ref, out_ref):
    planes = ids_ref.shape[0]
    ids = ids_ref[...]
    cells = jnp.zeros(ids.shape, jnp.float32)
    for layer in range(table_ref.shape[0]):
        cells = jnp.where(ids == layer, table_ref[layer], cells)
    out_ref[...] = jnp.zeros_like(out_ref)
    out_ref[pl.ds(0, planes), :] = cells
    out_ref[pl.ds(TAG - 1, 1), :] = jnp.sum(cells, axis=0, keepdims=True)


def ready_kernel(source_ref, wave_ref, out_ref):
    out_ref[...] = source_ref[0, 0, 0, pl.ds(0, TAG), :]


def add_kernel(one_ref, two_ref, out_ref):
    out_ref[...] = one_ref[...] + two_ref[...]


def fill_tag(out_ref, planes, own_ref, below_ref, above_ref, part_refs):
    start = out_ref.shape[0] - TAG
    for n, ref in enumerate((own_ref, below_ref, above_ref)):
        out_ref[pl.ds(start + n * planes, planes), :] = ref[pl.ds(0, planes), :]
    total = part_refs[0][pl.ds(TAG - 1, 1), :]
    for ref in part_refs[1:]:
        total = total + ref[pl.ds(TAG - 1, 1), :]
    out_ref[pl.ds(start + TAG - 1, 1), :] = total


def tag_of(ref):
    return ref[pl.ds(ref.shape[0] - TAG, TAG), :]


def find_numbers(cells_total, shift_ref, part_refs, numbers_ref):
    total = None
    for ref in part_refs:
        row = ref[pl.ds(ref.shape[0] - 1, 1), :]
        total = row if total is None else total + row
    inv = (1.0 / (jnp.sum(total, axis=1, keepdims=True) * (1.0 / cells_total)))[0, 0]
    numbers_ref[0] = shift_ref[0] * inv
    numbers_ref[1] = shift_ref[1] * inv
    numbers_ref[2] = relax * inv
    numbers_ref[3] = 0.5 * relax * inv
    numbers_ref[4] = shift_ref[0]
    numbers_ref[5] = shift_ref[1]


def faces_kernel(planes, blocks, flags_ref, *refs):
    part_refs, (faces_ref, padded_ref, below_ref, above_ref) = refs[:GROUP], refs[GROUP:]
    z, member = flags_ref[2], flags_ref[3]
    _, count, width = faces_ref.shape
    for d, ref in enumerate(part_refs):
        tag = tag_of(ref)
        place = member ^ d
        for p in range(planes):
            padded_ref[pl.ds(8 + place * planes + p, 1), :] = tag[p : p + 1]
        below_ref[pl.ds(place, 1), :] = tag[2 * planes - 1 : 2 * planes]
        above_ref[pl.ds(place, 1), :] = tag[2 * planes : 2 * planes + 1]
    cells = padded_ref[pl.ds(8, count), :]
    padded_ref[pl.ds(7, 1), :] = jnp.where(z == 0, cells[0:1], below_ref[pl.ds(GROUP - 1, 1), :])
    padded_ref[pl.ds(8 + count, 1), :] = jnp.where(
        z == blocks - 1, cells[count - 1 : count], above_ref[pl.ds(0, 1), :]
    )
    lane = lax.broadcasted_iota(jnp.int32, cells.shape, 1)
    last, first = lane == width - 1, lane == 0
    right = 0.5 * (cells + pltpu.roll(cells, width - 1, 1))
    left = 0.5 * (cells + pltpu.roll(cells, 1, 1))
    low = 0.5 * (cells + padded_ref[pl.ds(7, count), :])
    high = 0.5 * (cells + padded_ref[pl.ds(9, count), :])
    faces_ref[0] = jnp.where(last, cells, right) + jnp.where(first, cells, left) + (low + high)
    faces_ref[1] = cells
    faces_ref[2] = jnp.where(last, 0.0, right)
    faces_ref[3] = jnp.where(first, 0.0, left)
    faces_ref[4] = low
    faces_ref[5] = high


def forward_kernel(distance, parts_count, flags_ref, source_ref, wave_ref, own_ref, below_ref, above_ref, *refs):
    part_refs, out_refs, stage_ref = refs[:parts_count], refs[parts_count:-1], refs[-1]
    planes = source_ref.shape[1]
    q = flags_ref[0] ^ distance
    sign = (1 - 2 * (q & 1)).astype(jnp.float32)
    turn_re = jnp.where(q == 0, 1.0, jnp.where(q == 2, -1.0, 0.0))
    turn_im = jnp.where(q == 1, 1.0, jnp.where(q == 3, -1.0, 0.0))
    rows = stage_ref.shape[1] // (HALVES * CHUNKS)
    for p in range(planes):
        parts = [[source_ref[c, p, i] for i in range(RADIX)] for c in range(2)]
        even = [parts[c][0] + sign * parts[c][2] for c in range(2)]
        odd = [parts[c][1] + sign * parts[c][3] for c in range(2)]
        mixed = jnp.concatenate(
            [
                even[0] + (turn_re * odd[0] + turn_im * odd[1]),
                even[1] + (turn_re * odd[1] - turn_im * odd[0]),
            ],
            axis=0,
        )
        stage_ref[p] = dot_left(wave_ref[q], mixed)
        for n in range(HALVES):
            h = flags_ref[1] ^ n
            for t in range(CHUNKS):
                out_refs[n * CHUNKS + t][pl.ds(p * rows, rows), :] = stage_ref[
                    p, rows_at((h * CHUNKS + t) * rows, rows), :
                ]
    for ref in out_refs:
        fill_tag(ref, planes, own_ref, below_ref, above_ref, part_refs)


def backward_kernel(planes, cells, flags_ref, wave_ref, *refs):
    arrays, (out_ref, norms_ref, mixed_ref, stage_ref) = refs[:-4], refs[-4:]
    rows = (arrays[0].shape[0] - TAG) // planes
    came = {}
    for (t, d), ref in zip(ANSWERS, arrays):
        for n in range(CHUNKS if d in JOINT else 1):
            came[d, n if d in JOINT else t] = ref.at[pl.ds(n * planes * rows, planes * rows)]
    short = rows * CHUNKS * HALVES // 2
    total = None
    for ref in arrays:
        tag = tag_of(ref)
        total = tag if total is None else total + tag
    for d in range(RADIX):
        q = flags_ref[0] ^ d
        for p in range(planes):
            for n in range(HALVES):
                h = flags_ref[1] ^ n
                for t in range(CHUNKS):
                    stage_ref[d, p, rows_at((h * CHUNKS + t) * rows, rows), :] = came[d + RADIX * n, t][
                        pl.ds(p * rows, rows), :
                    ]
            mixed_ref[p, q] = dot_left(wave_ref[q], stage_ref[d, p])
    for p in range(planes):

        def strip(row):
            zero, one, two, three = [load(mixed_ref.at[p, q], 0, short, row, 8) for q in range(RADIX)]
            even, odd = cadd(zero, two), cadd(one, three)
            even_d, odd_d = csub(zero, two), csub(one, three)
            parts = (
                cadd(even, odd),
                (even_d[0] - odd_d[1], even_d[1] + odd_d[0]),
                csub(even, odd),
                (even_d[0] + odd_d[1], even_d[1] - odd_d[0]),
            )
            for i in range(RADIX):
                for c in range(2):
                    out_ref[c, p, rows_at(i * short + row, 8), :] = parts[i][c]

        each_strip(short, 8, strip)
    norms = jnp.sqrt(jnp.sum(total, axis=1, keepdims=True) * (1.0 / cells))
    for n in range(norms_ref.shape[0]):
        norms_ref[n] = norms[n, 0]


def decay_root(h):
    sq = (h[0] + 0.25 * (h[0] * h[0] - h[1] * h[1]), h[1] + 0.5 * h[0] * h[1])
    size = jnp.sqrt(squares_of(sq))
    root_re = jnp.sqrt(0.5 * (size + sq[0]))
    root = (root_re, 0.5 * sq[1] / root_re)
    return cinv((1.0 + 0.5 * h[0] + root[0], 0.5 * h[1] + root[1])), root


def two_powers(power, z, stacks):
    low = high = None
    bit = 0
    while (1 << bit) < stacks:
        taken = ((z >> bit) & 1) == 1
        if low is None:
            one = (jnp.ones_like(power[0]), jnp.zeros_like(power[0]))
            low, high = cpick(taken, power, one), cpick(taken, one, power)
        else:
            grown = cmul(cpick(taken, low, high), power)
            low, high = cpick(taken, grown, low), cpick(taken, high, grown)
        power = csqr(power)
        bit += 1
    return low, high


def sums_of(planes, rho, cross_f, cross_b):
    ahead = planes[0]
    for a in planes[1:]:
        ahead = cmore(a, rho, ahead)
    behind = planes[-1]
    for a in planes[-2::-1]:
        behind = cmore(a, rho, behind)
    return csub(ahead, cmul(cross_f, behind)), csub(behind, cmul(cross_b, ahead))


def sine_rows(source_ref, target_ref, sine_ref, count):
    sine = (sine_ref[0], sine_ref[1])
    rows = max(n for n in range(16, 641, 16) if count % n == 0)
    for i in range(0, count, rows):
        target_ref[pl.ds(i, rows), :] = dot_right(source_ref[pl.ds(i, rows), :], sine)


def fill_give(z, rows, sums_ref, give_refs):
    for ref in give_refs:
        ref[pl.ds(0, rows), :] = sums_ref[rows_at((z & 1) * rows, rows), :]
        ref[pl.ds(rows, TAG), :] = sums_ref[pl.ds(2 * rows, TAG), :]


def start_kernel(
    chunk, planes, blocks, cells_total, flags_ref, numbers_ref, wave_eig_ref, sine_eig_ref, sine_ref, *refs,
):
    part_refs, (field_ref, modes_ref, base_ref, sums_ref), give_refs = refs[:GROUP], refs[GROUP : GROUP + 4], refs[GROUP + 4 :]
    if chunk == 0:
        shift_ref, numbers_ref, give_refs = numbers_ref, give_refs[-1], give_refs[:-1]
        find_numbers(cells_total, shift_ref, part_refs, numbers_ref)
    q, h, z, member = [flags_ref[n] for n in range(4)]
    rows = base_ref.shape[1]
    part = rows * planes
    short = rows // 2
    count = GROUP * planes
    first_row = (h * CHUNKS + chunk) * short
    for d, ref in enumerate(part_refs):
        field_ref[rows_at((member ^ d) * part, part), :] = ref[pl.ds(0, part), :]
    sine_rows(field_ref, modes_ref, sine_ref, count * rows)
    h_re, h_im = numbers_ref[0], numbers_ref[1]
    sine_eig = sine_eig_ref[...]

    def strip(i, total):
        row = pl.multiple_of(i * 8, 8)
        eigen = wave_eig_ref[q, rows_at(first_row + row, 8), :] + sine_eig
        rho, _ = decay_root((eigen + h_re, jnp.full_like(eigen, h_im)))
        block = cpow(rho, count)
        next_one = cmul(block, rho)
        low, high = two_powers(csqr(block), z, blocks)
        cross_f, cross_b = cmul(next_one, low), cmul(next_one, high)
        for n, value in enumerate((rho, cross_f, cross_b, block, low, high)):
            store(base_ref.at[n], 0, short, row, 8, value)
        found = [load(modes_ref, l * rows, short, row, 8) for l in range(count)]
        ahead, behind = sums_of(found, rho, cross_f, cross_b)
        store(sums_ref, 0, short, row, 8, ahead)
        store(sums_ref, rows, short, row, 8, behind)
        for l in range(count):
            total = total + squares_of(load(field_ref, l * rows, short, row, 8))
        return total

    total = lax.fori_loop(
        0, short // 8, strip, jnp.zeros((8, field_ref.shape[1]), jnp.float32), unroll=2
    )
    sums_ref[pl.ds(2 * rows, TAG), :] = jnp.zeros((TAG, field_ref.shape[1]), jnp.float32)
    sums_ref[pl.ds(2 * rows, 1), :] = jnp.sum(total, axis=0, keepdims=True)
    fill_give(z, rows, sums_ref, give_refs)


def factors_kernel(
    chunk, count, levels, flags_ref, numbers_ref, wave_eig_ref, sine_eig_ref, base_ref, out_ref,
):
    q, h_part, z = flags_ref[0], flags_ref[1], flags_ref[2]
    short = base_ref.shape[1] // 2
    h_re, h_im, scale = numbers_ref[0], numbers_ref[1], numbers_ref[3]
    sine_eig = sine_eig_ref[...]

    def strip(row):
        eigen = wave_eig_ref[q, rows_at((h_part * CHUNKS + chunk) * short + row, 8), :] + sine_eig
        h = (eigen + h_re, jnp.full_like(eigen, h_im))
        rho, _, _, block, low, high = [load(base_ref.at[n], 0, short, row, 8) for n in range(6)]
        half_gap = csub((1.0 + 0.5 * h[0], 0.5 * h[1]), rho)
        wide = cmul(csqr(block), csqr(rho))
        low_w, high_w = cmul(low, wide), cmul(high, wide)
        whole = cscale(cinv(cmul(half_gap, cone(cmul(low, high_w)))), scale)
        turned = cmul(rho, whole)
        values = [
            cmul(cone(high_w), whole), cmul(cone(low), turned),
            cmul(cone(high), turned), cmul(cone(low_w), whole),
        ]
        pivot = (2.0 + h[0], h[1])
        inverse = cinv(pivot)
        values.append(inverse)
        for _ in range(count - 1):
            inverse = cinv(csub(pivot, inverse))
            values.append(inverse)
        near = far = None
        power = block
        for level in range(1, levels):
            taken = ((z >> (level - 1)) & 1) == 1
            if near is None:
                one = (jnp.ones_like(power[0]), jnp.zeros_like(power[0]))
                near, far = cpick(taken, power, one), cpick(taken, one, power)
            else:
                grown = cmul(cpick(taken, near, far), power)
                near, far = cpick(taken, grown, near), cpick(taken, far, grown)
            power = csqr(power)
            values.append(cpick(((z >> level) & 1) == 1, near, far))
        for n, value in enumerate(values):
            store(out_ref.at[n], 0, short, row, 8, value)

    each_strip(short, 8, strip)


def join_kernel(level, levels, flags_ref, sums_ref, came_ref, base_ref, out_ref):
    z = flags_ref[2]
    short = base_ref.shape[1] // 2
    rows = 2 * short
    above = ((z >> level) & 1) == 1
    last = level + 2 == levels
    upper = ((z >> (level + 1)) & 1) == 1

    def strip(row):
        block = load(base_ref.at[3], 0, short, row, 8)
        for _ in range(level):
            block = csqr(block)
        ahead, behind = load(sums_ref, 0, short, row, 8), load(sums_ref, rows, short, row, 8)
        ahead_c, behind_c = load(came_ref, 0, short, row, 8), load(came_ref, rows, short, row, 8)
        joined = cmore(cpick(above, ahead, ahead_c), block, cpick(above, ahead_c, ahead))
        joined_b = cmore(cpick(above, behind_c, behind), block, cpick(above, behind, behind_c))
        if last:
            store(out_ref, 0, short, row, 8, cpick(upper, joined_b, joined))
        else:
            store(out_ref, 0, short, row, 8, joined)
            store(out_ref, rows, short, row, 8, joined_b)

    each_strip(short, 8, strip)
    out_ref[pl.ds(out_ref.shape[0] - TAG, TAG), :] = (
        sums_ref[pl.ds(2 * rows, TAG), :] + came_ref[pl.ds(2 * rows, TAG), :]
    )


def solved(count, levels, z, scale, modes_ref, sums_ref, came_refs, base_ref, factors_ref, row):
    short = base_ref.shape[1] // 2
    rows = 2 * short

    def factor(n):
        return load(factors_ref.at[n], 0, short, row, 8)

    enter_f = enter_b = None
    for level in range(levels):
        above = ((z >> level) & 1) == 1
        base = 0 if level == levels - 1 else jnp.where(above, 0, rows)
        came = load(came_refs[level], base, short, row, 8)
        if level:
            came = cmul(factor(4 + count + level - 1), came)
        nought = (jnp.zeros_like(came[0]), jnp.zeros_like(came[0]))
        now_f, now_b = cpick(above, came, nought), cpick(above, nought, came)
        enter_f = now_f if enter_f is None else cadd(enter_f, now_f)
        enter_b = now_b if enter_b is None else cadd(enter_b, now_b)
    block = load(base_ref.at[3], 0, short, row, 8)
    all_f = cmore(load(sums_ref, 0, short, row, 8), block, enter_f)
    all_b = cmore(load(sums_ref, rows, short, row, 8), block, enter_b)
    below = cmore(cmul(factor(0), enter_f), factor(1), all_b)
    above = cmore(cmul(factor(3), enter_b), factor(2), all_f)
    planes = [cscale(load(modes_ref, l * rows, short, row, 8), scale) for l in range(count)]
    planes[0] = cadd(planes[0], below)
    planes[-1] = cadd(planes[-1], above)
    for l in range(1, count):
        planes[l] = cmore(planes[l], factor(4 + l - 1), planes[l - 1])
    planes[-1] = cmul(factor(4 + count - 1), planes[-1])
    for l in range(count - 2, -1, -1):
        planes[l] = cmul(factor(4 + l), cadd(planes[l], planes[l + 1]))
    return below, planes, above


def middle_kernel(
    chunk, count, levels, flags_ref, numbers_ref, wave_eig_ref, sine_ref, faces_ref, field_ref,
    modes_ref, base_ref, factors_ref, sums_ref, *refs,
):
    came_refs, (found_ref, next_ref, next_sums_ref) = refs[:levels], refs[levels : levels + 3]
    give_refs, work_ref = refs[levels + 3 : -1], refs[-1]
    q, h, z = flags_ref[0], flags_ref[1], flags_ref[2]
    scale, s_re, s_im = numbers_ref[2], numbers_ref[4], numbers_ref[5]
    short = base_ref.shape[1] // 2
    rows = 2 * short
    width = base_ref.shape[2]

    def solve(row):
        below, planes, above = solved(
            count, levels, z, scale, modes_ref, sums_ref, came_refs, base_ref, factors_ref, row
        )
        store(work_ref, 0, short, row, 8, below)
        store(work_ref, (count + 1) * rows, short, row, 8, above)
        for l in range(count):
            store(work_ref, (l + 1) * rows, short, row, 8, planes[l])
            store(found_ref, l * rows, short, row, 8, planes[l])

    each_strip(short, 8, solve)
    sine_rows(work_ref, work_ref, sine_ref, (count + 2) * rows)

    def residual(i, total):
        row = pl.multiple_of(i * 8, 8)
        eigen = wave_eig_ref[q, rows_at((h * CHUNKS + chunk) * short + row, 8), :]
        under = load(work_ref, 0, short, row, 8)
        here = load(work_ref, rows, short, row, 8)
        for l in range(count):
            over = load(work_ref, (l + 2) * rows, short, row, 8)
            diag, cell, right, left, low, high = [faces_ref[n, pl.ds(l, 1), :] for n in range(6)]
            diag = s_re + (diag + cell * eigen)
            value = []
            for c in range(2):
                v = diag * here[c] - right * pltpu.roll(here[c], width - 1, 1)
                v = v - left * pltpu.roll(here[c], 1, 1)
                value.append(v - (low * under[c] + high * over[c]))
            value = (value[0] - s_im * here[1], value[1] + s_im * here[0])
            value = csub(load(field_ref, l * rows, short, row, 8), value)
            total = total + squares_of(value)
            store(work_ref, l * rows, short, row, 8, value)
            under, here = here, over
        return total

    total = lax.fori_loop(0, short // 8, residual, jnp.zeros((8, width), jnp.float32), unroll=2)
    sine_rows(work_ref, next_ref, sine_ref, count * rows)

    def sums(row):
        rho, cross_f, cross_b = [load(base_ref.at[n], 0, short, row, 8) for n in range(3)]
        planes = [load(next_ref, l * rows, short, row, 8) for l in range(count)]
        ahead, behind = sums_of(planes, rho, cross_f, cross_b)
        store(next_sums_ref, 0, short, row, 8, ahead)
        store(next_sums_ref, rows, short, row, 8, behind)

    each_strip(short, 8, sums)
    next_sums_ref[pl.ds(2 * rows, TAG), :] = sums_ref[pl.ds(2 * rows, TAG), :]
    next_sums_ref[pl.ds(2 * rows + 1, 1), :] = jnp.sum(total, axis=0, keepdims=True)
    fill_give(z, rows, next_sums_ref, give_refs)


def end_kernel(
    count, levels, flags_ref, numbers_ref, sine_ref, found_ref, modes_ref, base_ref,
    factors_ref, sums_ref, *refs,
):
    came_refs, out_refs, work_ref = refs[:levels], refs[-1 - GROUP : -1], refs[-1]
    before_refs = refs[levels + (levels > 1) : -1 - GROUP]
    z, member = flags_ref[2], flags_ref[3]
    scale = numbers_ref[2]
    short = base_ref.shape[1] // 2
    rows = 2 * short

    def solve(row):
        _, planes, _ = solved(
            count, levels, z, scale, modes_ref, sums_ref, came_refs, base_ref, factors_ref, row
        )
        for l in range(count):
            before = load(found_ref, l * rows, short, row, 8)
            store(work_ref, l * rows, short, row, 8, cadd(before, planes[l]))

    each_strip(short, 8, solve)
    sine_rows(work_ref, work_ref, sine_ref, count * rows)
    part = count // GROUP * rows
    tag_refs = (refs[levels] if levels > 1 else sums_ref, came_refs[-1])
    tag = None
    for ref in tag_refs:
        part_tag = ref[pl.ds(ref.shape[0] - TAG, TAG), :]
        tag = part_tag if tag is None else tag + part_tag
    for d in range(GROUP):
        start, whole = 0, tag
        if d in JOINT:
            held = len(before_refs) // len(JOINT)
            for ref in before_refs[JOINT.index(d) * held : (JOINT.index(d) + 1) * held]:
                out_refs[d][pl.ds(start, part), :] = ref[pl.ds(0, part), :]
                start, whole = start + part, whole + tag_of(ref)
        out_refs[d][pl.ds(start, part), :] = work_ref[rows_at((member ^ d) * part, part), :]
        out_refs[d][pl.ds(start + part, TAG), :] = whole


smem = pl.BlockSpec(memory_space=pltpu.SMEM)
vmem = pl.BlockSpec(memory_space=pltpu.VMEM)
unread = pl.BlockSpec(memory_space=pl.ANY)


def call(kernel, scalars, arrays, outs, scratch=(), flops=0, after=()):
    out_shape = [jax.ShapeDtypeStruct(shape, jnp.float32) for shape in outs]
    head = len(scalars) + len(arrays)

    def run(*refs):
        kernel(*refs[:head], *refs[head + len(after) :])

    moved = sum(a.size * a.dtype.itemsize for a in arrays) + sum(4 * int(np.prod(s)) for s in outs)
    held = moved + sum(4 * int(np.prod(s)) for s in scratch)
    return pl.pallas_call(
        run,
        out_shape=out_shape,
        in_specs=[smem] * len(scalars) + [vmem] * len(arrays) + [unread] * len(after),
        out_specs=[smem if len(shape) == 1 else vmem for shape in outs],
        scratch_shapes=[pltpu.VMEM(shape, jnp.float32) for shape in scratch],
        compiler_params=pltpu.CompilerParams(vmem_limit_bytes=held + 4 * 2**20),
        cost_estimate=pl.CostEstimate(flops=flops, bytes_accessed=moved, transcendentals=0),
    )(*scalars, *arrays, *after)


def pair_up(array, groups, flip):
    return lax.ppermute(array, "gz", [(i, i ^ flip) for i in range(groups)])


def step_by(array, groups, distance):
    return lax.ppermute(
        array, "gz", [(i, i + distance) for i in range(groups) if 0 <= i + distance < groups]
    )


def body(source, layer_ids, conduct_table, shift):
    planes, length_x, length_y = source.shape[1:]
    groups = lax.axis_size("gz")
    blocks = groups // GROUP
    levels = blocks.bit_length() - 1
    count = GROUP * planes
    length_z = planes * groups
    full = length_x // RADIX
    short = full // (HALVES * CHUNKS)
    rows = 2 * short
    if blocks < 2 or groups != GROUP << levels or planes > 2 or short % 8 or length_x != RADIX * full:
        raise ValueError("unsupported layout")
    me = lax.axis_index("gz")
    member = me % GROUP
    flags = jnp.stack([member % RADIX, member // RADIX, me // GROUP, member]).astype(jnp.int32)

    wave = wave_tables(length_x)
    wave_f = jnp.asarray(np.concatenate(two_terms(wave), axis=1))
    wave_b = jnp.asarray(np.concatenate(two_terms(np.swapaxes(wave, 1, 2) / length_x), axis=1))
    sine = jnp.asarray(two_terms(sine_table(length_y)))
    wave_eig = np.broadcast_to(wave_eigen(length_x)[:, :, None], (RADIX, full, length_y))
    wave_eig = jnp.asarray(np.ascontiguousarray(wave_eig).astype(np.float32))
    sine_eig = jnp.asarray(np.tile(sine_eigen(length_y)[None, :], (8, 1)).astype(np.float32))

    chunks = range(CHUNKS)
    row_block = (TAG, length_y)
    block = (count * rows, length_y)
    sums_block = (2 * rows + TAG, length_y)
    single = (rows + TAG, length_y)
    part = (planes * rows + TAG, length_y)
    parts = (CHUNKS * planes * rows + TAG, length_y)
    gives = [single] if levels == 1 else []
    dots = 6 * length_y * length_y

    (cells,) = call(conduct_kernel, [conduct_table], [layer_ids], [row_block])
    if levels == 1:
        below = above = pair_up(cells, groups, GROUP)
        totals = [cells, below]
    else:
        below = step_by(cells, groups, GROUP)
        above = step_by(cells, groups, -GROUP)
        total = cells
        for level in range(levels):
            (total,) = call(add_kernel, [], [total, pair_up(total, groups, GROUP << level)], [row_block])
        totals = [total]

    (ready,) = call(ready_kernel, [], [source.reshape(2, planes, RADIX, full, length_y), wave_f], [row_block], after=[cells])

    parted = source.reshape(2, planes, RADIX, full, length_y)
    spectra = {}
    placed = [ready]
    for d in (2, 0, 3, 1):
        made = call(
            functools.partial(forward_kernel, d, len(totals)), [flags],
            [parted, wave_f, cells, below, above, *totals], [part] * (HALVES * CHUNKS),
            scratch=[(planes, 2 * full, length_y)], flops=planes * 2 * full * dots, after=placed,
        )
        placed = made[:1]
        for n in range(HALVES):
            for t in chunks:
                spectra[d + RADIX * n, t] = made[n * CHUNKS + t]
    for t in chunks:
        for d in (6, 2, 4, 7, 3, 5, 1):
            if t == 0 or d not in JOINT:
                spectra[d, t] = pair_up(spectra[d, t], groups, d)

    state = [{} for _ in chunks]

    def exchange(st, after):
        sums, give = st["sums"][0], st["sums"][-1]
        st["came"], st["tags"] = [], []
        for level in range(levels):
            st["came"].append(pair_up(give, groups, GROUP << level))
            if level + 1 < levels:
                shape = single if level + 2 == levels else sums_block
                (give,) = call(
                    functools.partial(join_kernel, level, levels), [flags], [sums, st["came"][-1], st["base"]],
                    [shape], after=after,
                )
                sums = give
                st["tags"] = [give[-TAG:]]

    def start(t, after):
        st = state[t]
        outs = [block, block, (6, rows, length_y), sums_block, *gives]
        made = call(
            functools.partial(start_kernel, t, planes, blocks, length_y * length_z),
            [flags, state[0]["numbers"] if t else shift],
            [wave_eig, sine_eig, sine] + [spectra[d, t] for d in range(GROUP)],
            outs if t else [*outs, (6,)], flops=count * rows * dots, after=after,
        )
        if not t:
            *made, st["numbers"] = made
        st["field"], st["modes"], st["base"], *st["sums"] = made
        exchange(st, [])
        return [st["sums"][-1]]

    def faces(t, after):
        state[t]["faces"] = call(
            functools.partial(faces_kernel, planes, blocks), [flags], [spectra[d, 0] for d in range(GROUP)],
            [(6, count, length_y)], scratch=[(count + 16, length_y), row_block, row_block], after=after,
        )[0]
        return [state[t]["faces"]]

    def factors(t, after):
        st = state[t]
        (st["factors"],) = call(
            functools.partial(factors_kernel, t, count, levels), [flags, state[0]["numbers"]],
            [wave_eig, sine_eig, st["base"]], [(4 + count + levels - 1, rows, length_y)], after=after,
        )
        return [st["factors"]]

    def middle(t, after):
        st = state[t]
        st["found"], st["modes"], *st["sums"] = call(
            functools.partial(middle_kernel, t, count, levels), [flags, state[0]["numbers"]],
            [wave_eig, sine, state[0]["faces"], st["field"], st["modes"], st["base"], st["factors"], st["sums"][0], *st["came"]],
            [block, block, sums_block, *gives], scratch=[((count + 2) * rows, length_y)],
            flops=(2 * count + 2) * rows * dots, after=after,
        )
        exchange(st, [])
        return [st["sums"][-1]]

    def end(t, after):
        st = state[t]
        last = t == CHUNKS - 1
        before = [state[u]["made"][d] for d in JOINT for u in range(t)] if last else []
        st["made"] = call(
            functools.partial(end_kernel, count, levels), [flags, state[0]["numbers"]],
            [sine, st["found"], st["modes"], st["base"], st["factors"], st["sums"][0], *st["came"], *st["tags"], *before],
            [parts if last and d in JOINT else part for d in range(GROUP)],
            scratch=[block], flops=count * rows * dots, after=after,
        )
        st["answers"] = {d: st["made"][d] for d in SENDS[t]}
        return [st["made"][0]]

    def held(array, after):
        return lax.optimization_barrier((array, *after))[0]

    def answer(t, distances):
        answers = state[t]["answers"]
        for d in distances:
            answers[d] = pair_up(answers[d], groups, d)

    placed = []
    for step in (start, faces, factors):
        placed = step(0, placed)
    for d in JOINT:
        spectra[d, 1] = pair_up(held(spectra[d, 1], placed), groups, d)
    for step, t in ((middle, 0), (start, 1), (factors, 1), (end, 0)):
        placed = step(t, placed)
    answer(0, SENDS[0][:4])
    placed = middle(1, placed)
    placed = end(1, [*placed, *[state[0]["answers"][d] for d in SENDS[0][:2]]])
    state[0]["answers"][SENDS[0][4]] = held(state[0]["answers"][SENDS[0][4]], placed)
    answer(0, SENDS[0][4:5])
    answer(1, SENDS[1][:-1])
    return call(
        functools.partial(backward_kernel, planes, length_x * length_x * length_y * length_z),
        [flags], [wave_b] + [state[t]["answers"][d] for t, d in ANSWERS],
        [(2, planes, length_x, length_y), (2,)],
        scratch=[(planes, RADIX, 2 * full, length_y), (RADIX, planes, 2 * full, length_y)],
        flops=planes * RADIX * 2 * full * dots,
    )


def solution(mesh):
    placed = (P(None, ("node", "gz"), None, None), P(("node", "gz"), None), P(), P("node"))
    return jax.shard_map(
        body,
        mesh=mesh,
        in_specs=placed,
        out_specs=(P(None, ("node", "gz"), None, None), P("node")),
        check_vma=False,
    )
```

```python
import functools

import jax
import jax.numpy as jnp
import ml_dtypes
import numpy as np
from jax import lax
from jax.experimental import pallas as pl
from jax.experimental.pallas import tpu as pltpu
from jax.sharding import PartitionSpec as P

RADIX = 4
HALVES = 2
GROUP = RADIX * HALVES
CHUNKS = 2
SENDS = ((6, 7, 2, 3, 4, 0), (2, 6, 7, 3, 4, 5, 1, 0))
ANSWERS = tuple((t, d) for t in range(CHUNKS) for d in SENDS[t])
JOINT = (5, 1)
TAG = 8

relax = 0.6


def sine_table(length):
    indices = np.arange(1, length + 1)
    product = indices[:, None] * indices[None, :] % (2 * (length + 1))
    return np.sqrt(2.0 / (length + 1)) * np.sin(np.pi / (length + 1) * product)


def sine_eigen(length):
    indices = np.arange(1, length + 1)
    return 4.0 * np.sin(np.pi / (2 * (length + 1)) * indices) ** 2


def wave_numbers(length):
    return RADIX * np.arange(length // RADIX)[None, :] + np.arange(RADIX)[:, None]


def wave_eigen(length):
    return 4.0 * np.sin(np.pi / length * wave_numbers(length)) ** 2


def wave_tables(length):
    waves = wave_numbers(length)
    short = length // RADIX
    product = waves[:, :, None] * np.arange(short)[None, None, :] % length
    angles = 2.0 * np.pi / length * product
    cos_t, sin_t = np.cos(angles), np.sin(angles)
    pieces = HALVES * CHUNKS
    top = np.concatenate([cos_t, sin_t], axis=2).reshape(RADIX, pieces, short // pieces, 2 * short)
    low = np.concatenate([-sin_t, cos_t], axis=2).reshape(RADIX, pieces, short // pieces, 2 * short)
    return np.concatenate([top, low], axis=2).reshape(RADIX, 2 * short, 2 * short)


def two_terms(table):
    first = table.astype(ml_dtypes.bfloat16)
    return np.stack([first, (table - first.astype(np.float64)).astype(ml_dtypes.bfloat16)])


def split(value):
    first = value.astype(jnp.bfloat16)
    return first, (value - first.astype(jnp.float32)).astype(jnp.bfloat16)


def dot_right(value, table):
    rows = value.shape[0]
    first, second = split(value)
    wide = jnp.dot(jnp.concatenate([first, second], axis=0), table[0], preferred_element_type=jnp.float32)
    return wide[:rows] + (wide[rows:] + jnp.dot(first, table[1], preferred_element_type=jnp.float32))


def dot_left(table, value):
    rows = table.shape[0] // 2
    first, second = split(value)
    wide = jnp.dot(table, first, preferred_element_type=jnp.float32)
    return wide[:rows] + (wide[rows:] + jnp.dot(table[:rows], second, preferred_element_type=jnp.float32))


def cmul(a, b):
    return (a[0] * b[0] - a[1] * b[1], a[0] * b[1] + a[1] * b[0])


def csqr(a):
    cross = a[0] * a[1]
    return ((a[0] - a[1]) * (a[0] + a[1]), cross + cross)


def cpow(a, count):
    result = None
    while count:
        if count & 1:
            result = a if result is None else cmul(result, a)
        count >>= 1
        if count:
            a = csqr(a)
    return result


def cadd(a, b):
    return (a[0] + b[0], a[1] + b[1])


def csub(a, b):
    return (a[0] - b[0], a[1] - b[1])


def cscale(a, scale):
    return (a[0] * scale, a[1] * scale)


def cmore(total, factor, term):
    return cadd(total, cmul(factor, term))


def cinv(a):
    scale = 1.0 / (a[0] * a[0] + a[1] * a[1])
    return (a[0] * scale, -a[1] * scale)


def cone(a):
    return (1.0 - a[0], -a[1])


def cpick(cond, a, b):
    return (jnp.where(cond, a[0], b[0]), jnp.where(cond, a[1], b[1]))


def rows_at(start, rows):
    if isinstance(start, int):
        return pl.ds(start, rows)
    return pl.ds(pl.multiple_of(start, 8), rows)


def load(ref, base, short, row, rows):
    return (ref[rows_at(base + row, rows), :], ref[rows_at(base + short + row, rows), :])


def store(ref, base, short, row, rows, value):
    ref[rows_at(base + row, rows), :] = value[0]
    ref[rows_at(base + short + row, rows), :] = value[1]


def each_strip(count, rows, body):
    def step(i, carry):
        body(pl.multiple_of(i * rows, rows))
        return carry

    steps = count // rows
    lax.fori_loop(0, steps, step, 0, unroll=min(steps, 4))


def squares_of(a):
    return a[0] * a[0] + a[1] * a[1]


def conduct_kernel(table_ref, ids_ref, out_ref):
    planes = ids_ref.shape[0]
    ids = ids_ref[...]
    cells = jnp.zeros(ids.shape, jnp.float32)
    for layer in range(table_ref.shape[0]):
        cells = jnp.where(ids == layer, table_ref[layer], cells)
    out_ref[...] = jnp.zeros_like(out_ref)
    out_ref[pl.ds(0, planes), :] = cells
    out_ref[pl.ds(TAG - 1, 1), :] = jnp.sum(cells, axis=0, keepdims=True)


def ready_kernel(source_ref, wave_ref, out_ref):
    out_ref[...] = source_ref[0, 0, 0, pl.ds(0, TAG), :]


def add_kernel(one_ref, two_ref, out_ref):
    out_ref[...] = one_ref[...] + two_ref[...]


def fill_tag(out_ref, planes, own_ref, below_ref, above_ref, part_refs):
    start = out_ref.shape[0] - TAG
    for n, ref in enumerate((own_ref, below_ref, above_ref)):
        out_ref[pl.ds(start + n * planes, planes), :] = ref[pl.ds(0, planes), :]
    total = part_refs[0][pl.ds(TAG - 1, 1), :]
    for ref in part_refs[1:]:
        total = total + ref[pl.ds(TAG - 1, 1), :]
    out_ref[pl.ds(start + TAG - 1, 1), :] = total


def tag_of(ref):
    return ref[pl.ds(ref.shape[0] - TAG, TAG), :]


def find_numbers(cells_total, shift_ref, part_refs, numbers_ref):
    total = None
    for ref in part_refs:
        row = ref[pl.ds(ref.shape[0] - 1, 1), :]
        total = row if total is None else total + row
    inv = (1.0 / (jnp.sum(total, axis=1, keepdims=True) * (1.0 / cells_total)))[0, 0]
    numbers_ref[0] = shift_ref[0] * inv
    numbers_ref[1] = shift_ref[1] * inv
    numbers_ref[2] = relax * inv
    numbers_ref[3] = 0.5 * relax * inv
    numbers_ref[4] = shift_ref[0]
    numbers_ref[5] = shift_ref[1]


def faces_kernel(planes, blocks, flags_ref, *refs):
    part_refs, (faces_ref, padded_ref, below_ref, above_ref) = refs[:GROUP], refs[GROUP:]
    z, member = flags_ref[2], flags_ref[3]
    _, count, width = faces_ref.shape
    for d, ref in enumerate(part_refs):
        tag = tag_of(ref)
        place = member ^ d
        for p in range(planes):
            padded_ref[pl.ds(8 + place * planes + p, 1), :] = tag[p : p + 1]
        below_ref[pl.ds(place, 1), :] = tag[2 * planes - 1 : 2 * planes]
        above_ref[pl.ds(place, 1), :] = tag[2 * planes : 2 * planes + 1]
    cells = padded_ref[pl.ds(8, count), :]
    padded_ref[pl.ds(7, 1), :] = jnp.where(z == 0, cells[0:1], below_ref[pl.ds(GROUP - 1, 1), :])
    padded_ref[pl.ds(8 + count, 1), :] = jnp.where(
        z == blocks - 1, cells[count - 1 : count], above_ref[pl.ds(0, 1), :]
    )
    lane = lax.broadcasted_iota(jnp.int32, cells.shape, 1)
    last, first = lane == width - 1, lane == 0
    right = 0.5 * (cells + pltpu.roll(cells, width - 1, 1))
    left = 0.5 * (cells + pltpu.roll(cells, 1, 1))
    low = 0.5 * (cells + padded_ref[pl.ds(7, count), :])
    high = 0.5 * (cells + padded_ref[pl.ds(9, count), :])
    faces_ref[0] = jnp.where(last, cells, right) + jnp.where(first, cells, left) + (low + high)
    faces_ref[1] = cells
    faces_ref[2] = jnp.where(last, 0.0, right)
    faces_ref[3] = jnp.where(first, 0.0, left)
    faces_ref[4] = low
    faces_ref[5] = high


def forward_kernel(distance, parts_count, flags_ref, source_ref, wave_ref, own_ref, below_ref, above_ref, *refs):
    part_refs, out_refs, stage_ref = refs[:parts_count], refs[parts_count:-1], refs[-1]
    planes = source_ref.shape[1]
    q = flags_ref[0] ^ distance
    sign = (1 - 2 * (q & 1)).astype(jnp.float32)
    turn_re = jnp.where(q == 0, 1.0, jnp.where(q == 2, -1.0, 0.0))
    turn_im = jnp.where(q == 1, 1.0, jnp.where(q == 3, -1.0, 0.0))
    rows = stage_ref.shape[1] // (HALVES * CHUNKS)
    for p in range(planes):
        parts = [[source_ref[c, p, i] for i in range(RADIX)] for c in range(2)]
        even = [parts[c][0] + sign * parts[c][2] for c in range(2)]
        odd = [parts[c][1] + sign * parts[c][3] for c in range(2)]
        mixed = jnp.concatenate(
            [
                even[0] + (turn_re * odd[0] + turn_im * odd[1]),
                even[1] + (turn_re * odd[1] - turn_im * odd[0]),
            ],
            axis=0,
        )
        stage_ref[p] = dot_left(wave_ref[q], mixed)
        for n in range(HALVES):
            h = flags_ref[1] ^ n
            for t in range(CHUNKS):
                out_refs[n * CHUNKS + t][pl.ds(p * rows, rows), :] = stage_ref[
                    p, rows_at((h * CHUNKS + t) * rows, rows), :
                ]
    for ref in out_refs:
        fill_tag(ref, planes, own_ref, below_ref, above_ref, part_refs)


def backward_kernel(planes, cells, flags_ref, wave_ref, *refs):
    arrays, (out_ref, norms_ref, mixed_ref, stage_ref) = refs[:-4], refs[-4:]
    rows = (arrays[0].shape[0] - TAG) // planes
    came = {}
    for (t, d), ref in zip(ANSWERS, arrays):
        for n in range(CHUNKS if d in JOINT else 1):
            came[d, n if d in JOINT else t] = ref.at[pl.ds(n * planes * rows, planes * rows)]
    short = rows * CHUNKS * HALVES // 2
    total = None
    for ref in arrays:
        tag = tag_of(ref)
        total = tag if total is None else total + tag
    for d in range(RADIX):
        q = flags_ref[0] ^ d
        for p in range(planes):
            for n in range(HALVES):
                h = flags_ref[1] ^ n
                for t in range(CHUNKS):
                    stage_ref[d, p, rows_at((h * CHUNKS + t) * rows, rows), :] = came[d + RADIX * n, t][
                        pl.ds(p * rows, rows), :
                    ]
            mixed_ref[p, q] = dot_left(wave_ref[q], stage_ref[d, p])
    for p in range(planes):

        def strip(row):
            zero, one, two, three = [load(mixed_ref.at[p, q], 0, short, row, 8) for q in range(RADIX)]
            even, odd = cadd(zero, two), cadd(one, three)
            even_d, odd_d = csub(zero, two), csub(one, three)
            parts = (
                cadd(even, odd),
                (even_d[0] - odd_d[1], even_d[1] + odd_d[0]),
                csub(even, odd),
                (even_d[0] + odd_d[1], even_d[1] - odd_d[0]),
            )
            for i in range(RADIX):
                for c in range(2):
                    out_ref[c, p, rows_at(i * short + row, 8), :] = parts[i][c]

        each_strip(short, 8, strip)
    norms = jnp.sqrt(jnp.sum(total, axis=1, keepdims=True) * (1.0 / cells))
    for n in range(norms_ref.shape[0]):
        norms_ref[n] = norms[n, 0]


def decay_root(h):
    sq = (h[0] + 0.25 * (h[0] * h[0] - h[1] * h[1]), h[1] + 0.5 * h[0] * h[1])
    size = jnp.sqrt(squares_of(sq))
    root_re = jnp.sqrt(0.5 * (size + sq[0]))
    root = (root_re, 0.5 * sq[1] / root_re)
    return cinv((1.0 + 0.5 * h[0] + root[0], 0.5 * h[1] + root[1])), root


def two_powers(power, z, stacks):
    low = high = None
    bit = 0
    while (1 << bit) < stacks:
        taken = ((z >> bit) & 1) == 1
        if low is None:
            one = (jnp.ones_like(power[0]), jnp.zeros_like(power[0]))
            low, high = cpick(taken, power, one), cpick(taken, one, power)
        else:
            grown = cmul(cpick(taken, low, high), power)
            low, high = cpick(taken, grown, low), cpick(taken, high, grown)
        power = csqr(power)
        bit += 1
    return low, high


def sums_of(planes, rho, cross_f, cross_b):
    ahead = planes[0]
    for a in planes[1:]:
        ahead = cmore(a, rho, ahead)
    behind = planes[-1]
    for a in planes[-2::-1]:
        behind = cmore(a, rho, behind)
    return csub(ahead, cmul(cross_f, behind)), csub(behind, cmul(cross_b, ahead))


def sine_rows(source_ref, target_ref, sine_ref, count):
    sine = (sine_ref[0], sine_ref[1])
    rows = max(n for n in range(16, 641, 16) if count % n == 0)
    for i in range(0, count, rows):
        target_ref[pl.ds(i, rows), :] = dot_right(source_ref[pl.ds(i, rows), :], sine)


def fill_give(z, rows, sums_ref, give_refs):
    for ref in give_refs:
        ref[pl.ds(0, rows), :] = sums_ref[rows_at((z & 1) * rows, rows), :]
        ref[pl.ds(rows, TAG), :] = sums_ref[pl.ds(2 * rows, TAG), :]


def start_kernel(
    chunk, planes, blocks, cells_total, flags_ref, numbers_ref, wave_eig_ref, sine_eig_ref, sine_ref, *refs,
):
    part_refs, (field_ref, modes_ref, base_ref, sums_ref), give_refs = refs[:GROUP], refs[GROUP : GROUP + 4], refs[GROUP + 4 :]
    if chunk == 0:
        shift_ref, numbers_ref, give_refs = numbers_ref, give_refs[-1], give_refs[:-1]
        find_numbers(cells_total, shift_ref, part_refs, numbers_ref)
    q, h, z, member = [flags_ref[n] for n in range(4)]
    rows = base_ref.shape[1]
    part = rows * planes
    short = rows // 2
    count = GROUP * planes
    first_row = (h * CHUNKS + chunk) * short
    for d, ref in enumerate(part_refs):
        field_ref[rows_at((member ^ d) * part, part), :] = ref[pl.ds(0, part), :]
    sine_rows(field_ref, modes_ref, sine_ref, count * rows)
    h_re, h_im = numbers_ref[0], numbers_ref[1]
    sine_eig = sine_eig_ref[...]

    def strip(i, total):
        row = pl.multiple_of(i * 8, 8)
        eigen = wave_eig_ref[q, rows_at(first_row + row, 8), :] + sine_eig
        rho, _ = decay_root((eigen + h_re, jnp.full_like(eigen, h_im)))
        block = cpow(rho, count)
        next_one = cmul(block, rho)
        low, high = two_powers(csqr(block), z, blocks)
        cross_f, cross_b = cmul(next_one, low), cmul(next_one, high)
        for n, value in enumerate((rho, cross_f, cross_b, block, low, high)):
            store(base_ref.at[n], 0, short, row, 8, value)
        found = [load(modes_ref, l * rows, short, row, 8) for l in range(count)]
        ahead, behind = sums_of(found, rho, cross_f, cross_b)
        store(sums_ref, 0, short, row, 8, ahead)
        store(sums_ref, rows, short, row, 8, behind)
        for l in range(count):
            total = total + squares_of(load(field_ref, l * rows, short, row, 8))
        return total

    total = lax.fori_loop(
        0, short // 8, strip, jnp.zeros((8, field_ref.shape[1]), jnp.float32), unroll=2
    )
    sums_ref[pl.ds(2 * rows, TAG), :] = jnp.zeros((TAG, field_ref.shape[1]), jnp.float32)
    sums_ref[pl.ds(2 * rows, 1), :] = jnp.sum(total, axis=0, keepdims=True)
    fill_give(z, rows, sums_ref, give_refs)


def factors_kernel(
    chunk, count, levels, flags_ref, numbers_ref, wave_eig_ref, sine_eig_ref, base_ref, out_ref,
):
    q, h_part, z = flags_ref[0], flags_ref[1], flags_ref[2]
    short = base_ref.shape[1] // 2
    h_re, h_im, scale = numbers_ref[0], numbers_ref[1], numbers_ref[3]
    sine_eig = sine_eig_ref[...]

    def strip(row):
        eigen = wave_eig_ref[q, rows_at((h_part * CHUNKS + chunk) * short + row, 8), :] + sine_eig
        h = (eigen + h_re, jnp.full_like(eigen, h_im))
        rho, _, _, block, low, high = [load(base_ref.at[n], 0, short, row, 8) for n in range(6)]
        half_gap = csub((1.0 + 0.5 * h[0], 0.5 * h[1]), rho)
        wide = cmul(csqr(block), csqr(rho))
        low_w, high_w = cmul(low, wide), cmul(high, wide)
        whole = cscale(cinv(cmul(half_gap, cone(cmul(low, high_w)))), scale)
        turned = cmul(rho, whole)
        values = [
            cmul(cone(high_w), whole), cmul(cone(low), turned),
            cmul(cone(high), turned), cmul(cone(low_w), whole),
        ]
        pivot = (2.0 + h[0], h[1])
        inverse = cinv(pivot)
        values.append(inverse)
        for _ in range(count - 1):
            inverse = cinv(csub(pivot, inverse))
            values.append(inverse)
        near = far = None
        power = block
        for level in range(1, levels):
            taken = ((z >> (level - 1)) & 1) == 1
            if near is None:
                one = (jnp.ones_like(power[0]), jnp.zeros_like(power[0]))
                near, far = cpick(taken, power, one), cpick(taken, one, power)
            else:
                grown = cmul(cpick(taken, near, far), power)
                near, far = cpick(taken, grown, near), cpick(taken, far, grown)
            power = csqr(power)
            values.append(cpick(((z >> level) & 1) == 1, near, far))
        for n, value in enumerate(values):
            store(out_ref.at[n], 0, short, row, 8, value)

    each_strip(short, 8, strip)


def join_kernel(level, levels, flags_ref, sums_ref, came_ref, base_ref, out_ref):
    z = flags_ref[2]
    short = base_ref.shape[1] // 2
    rows = 2 * short
    above = ((z >> level) & 1) == 1
    last = level + 2 == levels
    upper = ((z >> (level + 1)) & 1) == 1

    def strip(row):
        block = load(base_ref.at[3], 0, short, row, 8)
        for _ in range(level):
            block = csqr(block)
        ahead, behind = load(sums_ref, 0, short, row, 8), load(sums_ref, rows, short, row, 8)
        ahead_c, behind_c = load(came_ref, 0, short, row, 8), load(came_ref, rows, short, row, 8)
        joined = cmore(cpick(above, ahead, ahead_c), block, cpick(above, ahead_c, ahead))
        joined_b = cmore(cpick(above, behind_c, behind), block, cpick(above, behind, behind_c))
        if last:
            store(out_ref, 0, short, row, 8, cpick(upper, joined_b, joined))
        else:
            store(out_ref, 0, short, row, 8, joined)
            store(out_ref, rows, short, row, 8, joined_b)

    each_strip(short, 8, strip)
    out_ref[pl.ds(out_ref.shape[0] - TAG, TAG), :] = (
        sums_ref[pl.ds(2 * rows, TAG), :] + came_ref[pl.ds(2 * rows, TAG), :]
    )


def solved(count, levels, z, scale, modes_ref, sums_ref, came_refs, base_ref, factors_ref, row):
    short = base_ref.shape[1] // 2
    rows = 2 * short

    def factor(n):
        return load(factors_ref.at[n], 0, short, row, 8)

    enter_f = enter_b = None
    for level in range(levels):
        above = ((z >> level) & 1) == 1
        base = 0 if level == levels - 1 else jnp.where(above, 0, rows)
        came = load(came_refs[level], base, short, row, 8)
        if level:
            came = cmul(factor(4 + count + level - 1), came)
        nought = (jnp.zeros_like(came[0]), jnp.zeros_like(came[0]))
        now_f, now_b = cpick(above, came, nought), cpick(above, nought, came)
        enter_f = now_f if enter_f is None else cadd(enter_f, now_f)
        enter_b = now_b if enter_b is None else cadd(enter_b, now_b)
    block = load(base_ref.at[3], 0, short, row, 8)
    all_f = cmore(load(sums_ref, 0, short, row, 8), block, enter_f)
    all_b = cmore(load(sums_ref, rows, short, row, 8), block, enter_b)
    below = cmore(cmul(factor(0), enter_f), factor(1), all_b)
    above = cmore(cmul(factor(3), enter_b), factor(2), all_f)
    planes = [cscale(load(modes_ref, l * rows, short, row, 8), scale) for l in range(count)]
    planes[0] = cadd(planes[0], below)
    planes[-1] = cadd(planes[-1], above)
    for l in range(1, count):
        planes[l] = cmore(planes[l], factor(4 + l - 1), planes[l - 1])
    planes[-1] = cmul(factor(4 + count - 1), planes[-1])
    for l in range(count - 2, -1, -1):
        planes[l] = cmul(factor(4 + l), cadd(planes[l], planes[l + 1]))
    return below, planes, above


def middle_kernel(
    chunk, count, levels, flags_ref, numbers_ref, wave_eig_ref, sine_ref, faces_ref, field_ref,
    modes_ref, base_ref, factors_ref, sums_ref, *refs,
):
    came_refs, (found_ref, next_ref, next_sums_ref) = refs[:levels], refs[levels : levels + 3]
    give_refs, work_ref = refs[levels + 3 : -1], refs[-1]
    q, h, z = flags_ref[0], flags_ref[1], flags_ref[2]
    scale, s_re, s_im = numbers_ref[2], numbers_ref[4], numbers_ref[5]
    short = base_ref.shape[1] // 2
    rows = 2 * short
    width = base_ref.shape[2]

    def solve(row):
        below, planes, above = solved(
            count, levels, z, scale, modes_ref, sums_ref, came_refs, base_ref, factors_ref, row
        )
        store(work_ref, 0, short, row, 8, below)
        store(work_ref, (count + 1) * rows, short, row, 8, above)
        for l in range(count):
            store(work_ref, (l + 1) * rows, short, row, 8, planes[l])
            store(found_ref, l * rows, short, row, 8, planes[l])

    each_strip(short, 8, solve)
    sine_rows(work_ref, work_ref, sine_ref, (count + 2) * rows)

    def residual(i, total):
        row = pl.multiple_of(i * 8, 8)
        eigen = wave_eig_ref[q, rows_at((h * CHUNKS + chunk) * short + row, 8), :]
        under = load(work_ref, 0, short, row, 8)
        here = load(work_ref, rows, short, row, 8)
        for l in range(count):
            over = load(work_ref, (l + 2) * rows, short, row, 8)
            diag, cell, right, left, low, high = [faces_ref[n, pl.ds(l, 1), :] for n in range(6)]
            diag = s_re + (diag + cell * eigen)
            value = []
            for c in range(2):
                v = diag * here[c] - right * pltpu.roll(here[c], width - 1, 1)
                v = v - left * pltpu.roll(here[c], 1, 1)
                value.append(v - (low * under[c] + high * over[c]))
            value = (value[0] - s_im * here[1], value[1] + s_im * here[0])
            value = csub(load(field_ref, l * rows, short, row, 8), value)
            total = total + squares_of(value)
            store(work_ref, l * rows, short, row, 8, value)
            under, here = here, over
        return total

    total = lax.fori_loop(0, short // 8, residual, jnp.zeros((8, width), jnp.float32), unroll=2)
    sine_rows(work_ref, next_ref, sine_ref, count * rows)

    def sums(row):
        rho, cross_f, cross_b = [load(base_ref.at[n], 0, short, row, 8) for n in range(3)]
        planes = [load(next_ref, l * rows, short, row, 8) for l in range(count)]
        ahead, behind = sums_of(planes, rho, cross_f, cross_b)
        store(next_sums_ref, 0, short, row, 8, ahead)
        store(next_sums_ref, rows, short, row, 8, behind)

    each_strip(short, 8, sums)
    next_sums_ref[pl.ds(2 * rows, TAG), :] = sums_ref[pl.ds(2 * rows, TAG), :]
    next_sums_ref[pl.ds(2 * rows + 1, 1), :] = jnp.sum(total, axis=0, keepdims=True)
    fill_give(z, rows, next_sums_ref, give_refs)


def end_kernel(
    count, levels, flags_ref, numbers_ref, sine_ref, found_ref, modes_ref, base_ref,
    factors_ref, sums_ref, *refs,
):
    came_refs, out_refs, work_ref = refs[:levels], refs[-1 - GROUP : -1], refs[-1]
    before_refs = refs[levels + (levels > 1) : -1 - GROUP]
    z, member = flags_ref[2], flags_ref[3]
    scale = numbers_ref[2]
    short = base_ref.shape[1] // 2
    rows = 2 * short

    def solve(row):
        _, planes, _ = solved(
            count, levels, z, scale, modes_ref, sums_ref, came_refs, base_ref, factors_ref, row
        )
        for l in range(count):
            before = load(found_ref, l * rows, short, row, 8)
            store(work_ref, l * rows, short, row, 8, cadd(before, planes[l]))

    each_strip(short, 8, solve)
    sine_rows(work_ref, work_ref, sine_ref, count * rows)
    part = count // GROUP * rows
    tag_refs = (refs[levels] if levels > 1 else sums_ref, came_refs[-1])
    tag = None
    for ref in tag_refs:
        part_tag = ref[pl.ds(ref.shape[0] - TAG, TAG), :]
        tag = part_tag if tag is None else tag + part_tag
    for d in range(GROUP):
        start, whole = 0, tag
        if d in JOINT:
            held = len(before_refs) // len(JOINT)
            for ref in before_refs[JOINT.index(d) * held : (JOINT.index(d) + 1) * held]:
                out_refs[d][pl.ds(start, part), :] = ref[pl.ds(0, part), :]
                start, whole = start + part, whole + tag_of(ref)
        out_refs[d][pl.ds(start, part), :] = work_ref[rows_at((member ^ d) * part, part), :]
        out_refs[d][pl.ds(start + part, TAG), :] = whole


smem = pl.BlockSpec(memory_space=pltpu.SMEM)
vmem = pl.BlockSpec(memory_space=pltpu.VMEM)
unread = pl.BlockSpec(memory_space=pl.ANY)


def call(kernel, scalars, arrays, outs, scratch=(), flops=0, after=()):
    out_shape = [jax.ShapeDtypeStruct(shape, jnp.float32) for shape in outs]
    head = len(scalars) + len(arrays)

    def run(*refs):
        kernel(*refs[:head], *refs[head + len(after) :])

    moved = sum(a.size * a.dtype.itemsize for a in arrays) + sum(4 * int(np.prod(s)) for s in outs)
    held = moved + sum(4 * int(np.prod(s)) for s in scratch)
    return pl.pallas_call(
        run,
        out_shape=out_shape,
        in_specs=[smem] * len(scalars) + [vmem] * len(arrays) + [unread] * len(after),
        out_specs=[smem if len(shape) == 1 else vmem for shape in outs],
        scratch_shapes=[pltpu.VMEM(shape, jnp.float32) for shape in scratch],
        compiler_params=pltpu.CompilerParams(vmem_limit_bytes=held + 4 * 2**20),
        cost_estimate=pl.CostEstimate(flops=flops, bytes_accessed=moved, transcendentals=0),
    )(*scalars, *arrays, *after)


def pair_up(array, groups, flip):
    return lax.ppermute(array, "gz", [(i, i ^ flip) for i in range(groups)])


def step_by(array, groups, distance):
    return lax.ppermute(
        array, "gz", [(i, i + distance) for i in range(groups) if 0 <= i + distance < groups]
    )


def body(source, layer_ids, conduct_table, shift):
    planes, length_x, length_y = source.shape[1:]
    groups = lax.axis_size("gz")
    blocks = groups // GROUP
    levels = blocks.bit_length() - 1
    count = GROUP * planes
    length_z = planes * groups
    full = length_x // RADIX
    short = full // (HALVES * CHUNKS)
    rows = 2 * short
    if blocks < 2 or groups != GROUP << levels or planes > 2 or short % 8 or length_x != RADIX * full:
        raise ValueError("unsupported layout")
    me = lax.axis_index("gz")
    member = me % GROUP
    flags = jnp.stack([member % RADIX, member // RADIX, me // GROUP, member]).astype(jnp.int32)

    wave = wave_tables(length_x)
    wave_f = jnp.asarray(np.concatenate(two_terms(wave), axis=1))
    wave_b = jnp.asarray(np.concatenate(two_terms(np.swapaxes(wave, 1, 2) / length_x), axis=1))
    sine = jnp.asarray(two_terms(sine_table(length_y)))
    wave_eig = np.broadcast_to(wave_eigen(length_x)[:, :, None], (RADIX, full, length_y))
    wave_eig = jnp.asarray(np.ascontiguousarray(wave_eig).astype(np.float32))
    sine_eig = jnp.asarray(np.tile(sine_eigen(length_y)[None, :], (8, 1)).astype(np.float32))

    chunks = range(CHUNKS)
    row_block = (TAG, length_y)
    block = (count * rows, length_y)
    sums_block = (2 * rows + TAG, length_y)
    single = (rows + TAG, length_y)
    part = (planes * rows + TAG, length_y)
    parts = (CHUNKS * planes * rows + TAG, length_y)
    gives = [single] if levels == 1 else []
    dots = 6 * length_y * length_y

    (cells,) = call(conduct_kernel, [conduct_table], [layer_ids], [row_block])
    if levels == 1:
        below = above = pair_up(cells, groups, GROUP)
        totals = [cells, below]
    else:
        below = step_by(cells, groups, GROUP)
        above = step_by(cells, groups, -GROUP)
        total = cells
        for level in range(levels):
            (total,) = call(add_kernel, [], [total, pair_up(total, groups, GROUP << level)], [row_block])
        totals = [total]

    (ready,) = call(ready_kernel, [], [source.reshape(2, planes, RADIX, full, length_y), wave_f], [row_block], after=[cells])

    parted = source.reshape(2, planes, RADIX, full, length_y)
    spectra = {}
    placed = [ready]
    for d in (2, 0, 3, 1):
        made = call(
            functools.partial(forward_kernel, d, len(totals)), [flags],
            [parted, wave_f, cells, below, above, *totals], [part] * (HALVES * CHUNKS),
            scratch=[(planes, 2 * full, length_y)], flops=planes * 2 * full * dots, after=placed,
        )
        placed = made[:1]
        for n in range(HALVES):
            for t in chunks:
                spectra[d + RADIX * n, t] = made[n * CHUNKS + t]
    for t in chunks:
        for d in (6, 2, 4, 7, 3, 5, 1):
            if t == 0 or d not in JOINT:
                spectra[d, t] = pair_up(spectra[d, t], groups, d)

    state = [{} for _ in chunks]

    def exchange(st, after):
        sums, give = st["sums"][0], st["sums"][-1]
        st["came"], st["tags"] = [], []
        for level in range(levels):
            st["came"].append(pair_up(give, groups, GROUP << level))
            if level + 1 < levels:
                shape = single if level + 2 == levels else sums_block
                (give,) = call(
                    functools.partial(join_kernel, level, levels), [flags], [sums, st["came"][-1], st["base"]],
                    [shape], after=after,
                )
                sums = give
                st["tags"] = [give[-TAG:]]

    def start(t, after):
        st = state[t]
        outs = [block, block, (6, rows, length_y), sums_block, *gives]
        made = call(
            functools.partial(start_kernel, t, planes, blocks, length_y * length_z),
            [flags, state[0]["numbers"] if t else shift],
            [wave_eig, sine_eig, sine] + [spectra[d, t] for d in range(GROUP)],
            outs if t else [*outs, (6,)], flops=count * rows * dots, after=after,
        )
        if not t:
            *made, st["numbers"] = made
        st["field"], st["modes"], st["base"], *st["sums"] = made
        exchange(st, [])
        return [st["sums"][-1]]

    def faces(t, after):
        state[t]["faces"] = call(
            functools.partial(faces_kernel, planes, blocks), [flags], [spectra[d, 0] for d in range(GROUP)],
            [(6, count, length_y)], scratch=[(count + 16, length_y), row_block, row_block], after=after,
        )[0]
        return [state[t]["faces"]]

    def factors(t, after):
        st = state[t]
        (st["factors"],) = call(
            functools.partial(factors_kernel, t, count, levels), [flags, state[0]["numbers"]],
            [wave_eig, sine_eig, st["base"]], [(4 + count + levels - 1, rows, length_y)], after=after,
        )
        return [st["factors"]]

    def middle(t, after):
        st = state[t]
        st["found"], st["modes"], *st["sums"] = call(
            functools.partial(middle_kernel, t, count, levels), [flags, state[0]["numbers"]],
            [wave_eig, sine, state[0]["faces"], st["field"], st["modes"], st["base"], st["factors"], st["sums"][0], *st["came"]],
            [block, block, sums_block, *gives], scratch=[((count + 2) * rows, length_y)],
            flops=(2 * count + 2) * rows * dots, after=after,
        )
        exchange(st, [])
        return [st["sums"][-1]]

    def end(t, after):
        st = state[t]
        last = t == CHUNKS - 1
        before = [state[u]["made"][d] for d in JOINT for u in range(t)] if last else []
        st["made"] = call(
            functools.partial(end_kernel, count, levels), [flags, state[0]["numbers"]],
            [sine, st["found"], st["modes"], st["base"], st["factors"], st["sums"][0], *st["came"], *st["tags"], *before],
            [parts if last and d in JOINT else part for d in range(GROUP)],
            scratch=[block], flops=count * rows * dots, after=after,
        )
        st["answers"] = {d: st["made"][d] for d in SENDS[t]}
        return [st["made"][0]]

    def held(array, after):
        return lax.optimization_barrier((array, *after))[0]

    def answer(t, distances):
        answers = state[t]["answers"]
        for d in distances:
            answers[d] = pair_up(answers[d], groups, d)

    placed = []
    for step in (start, faces, factors):
        placed = step(0, placed)
    for d in JOINT:
        spectra[d, 1] = pair_up(held(spectra[d, 1], placed), groups, d)
    for step, t in ((middle, 0), (start, 1), (factors, 1), (end, 0)):
        placed = step(t, placed)
    answer(0, SENDS[0][:-1])
    placed = middle(1, placed)
    end(1, [*placed, *[state[0]["answers"][d] for d in SENDS[0][:2]]])
    answer(1, SENDS[1][:-1])
    return call(
        functools.partial(backward_kernel, planes, length_x * length_x * length_y * length_z),
        [flags], [wave_b] + [state[t]["answers"][d] for t, d in ANSWERS],
        [(2, planes, length_x, length_y), (2,)],
        scratch=[(planes, RADIX, 2 * full, length_y), (RADIX, planes, 2 * full, length_y)],
        flops=planes * RADIX * 2 * full * dots,
    )


def solution(mesh):
    placed = (P(None, ("node", "gz"), None, None), P(("node", "gz"), None), P(), P("node"))
    return jax.shard_map(
        body,
        mesh=mesh,
        in_specs=placed,
        out_specs=(P(None, ("node", "gz"), None, None), P("node")),
        check_vma=False,
    )
```

```python
import functools

import jax
import jax.numpy as jnp
import ml_dtypes
import numpy as np
from jax import lax
from jax.experimental import pallas as pl
from jax.experimental.pallas import tpu as pltpu
from jax.sharding import PartitionSpec as P

RADIX = 4
HALVES = 2
GROUP = RADIX * HALVES
CHUNKS = 2
SENDS = ((6, 7, 2, 3, 4, 0), (2, 6, 7, 3, 4, 5, 1, 0))
ANSWERS = tuple((t, d) for t in range(CHUNKS) for d in SENDS[t])
JOINT = (5, 1)
TAG = 8

relax = 0.6


def sine_table(length):
    indices = np.arange(1, length + 1)
    product = indices[:, None] * indices[None, :] % (2 * (length + 1))
    return np.sqrt(2.0 / (length + 1)) * np.sin(np.pi / (length + 1) * product)


def sine_eigen(length):
    indices = np.arange(1, length + 1)
    return 4.0 * np.sin(np.pi / (2 * (length + 1)) * indices) ** 2


def wave_numbers(length):
    return RADIX * np.arange(length // RADIX)[None, :] + np.arange(RADIX)[:, None]


def wave_eigen(length):
    return 4.0 * np.sin(np.pi / length * wave_numbers(length)) ** 2


def wave_tables(length):
    waves = wave_numbers(length)
    short = length // RADIX
    product = waves[:, :, None] * np.arange(short)[None, None, :] % length
    angles = 2.0 * np.pi / length * product
    cos_t, sin_t = np.cos(angles), np.sin(angles)
    pieces = HALVES * CHUNKS
    top = np.concatenate([cos_t, sin_t], axis=2).reshape(RADIX, pieces, short // pieces, 2 * short)
    low = np.concatenate([-sin_t, cos_t], axis=2).reshape(RADIX, pieces, short // pieces, 2 * short)
    return np.concatenate([top, low], axis=2).reshape(RADIX, 2 * short, 2 * short)


def two_terms(table):
    first = table.astype(ml_dtypes.bfloat16)
    return np.stack([first, (table - first.astype(np.float64)).astype(ml_dtypes.bfloat16)])


def split(value):
    first = value.astype(jnp.bfloat16)
    return first, (value - first.astype(jnp.float32)).astype(jnp.bfloat16)


def dot_right(value, table):
    rows = value.shape[0]
    first, second = split(value)
    wide = jnp.dot(jnp.concatenate([first, second], axis=0), table[0], preferred_element_type=jnp.float32)
    return wide[:rows] + (wide[rows:] + jnp.dot(first, table[1], preferred_element_type=jnp.float32))


def dot_left(table, value):
    rows = table.shape[0] // 2
    first, second = split(value)
    wide = jnp.dot(table, first, preferred_element_type=jnp.float32)
    return wide[:rows] + (wide[rows:] + jnp.dot(table[:rows], second, preferred_element_type=jnp.float32))


def cmul(a, b):
    return (a[0] * b[0] - a[1] * b[1], a[0] * b[1] + a[1] * b[0])


def csqr(a):
    cross = a[0] * a[1]
    return ((a[0] - a[1]) * (a[0] + a[1]), cross + cross)


def cpow(a, count):
    result = None
    while count:
        if count & 1:
            result = a if result is None else cmul(result, a)
        count >>= 1
        if count:
            a = csqr(a)
    return result


def cadd(a, b):
    return (a[0] + b[0], a[1] + b[1])


def csub(a, b):
    return (a[0] - b[0], a[1] - b[1])


def cscale(a, scale):
    return (a[0] * scale, a[1] * scale)


def cmore(total, factor, term):
    return cadd(total, cmul(factor, term))


def cinv(a):
    scale = 1.0 / (a[0] * a[0] + a[1] * a[1])
    return (a[0] * scale, -a[1] * scale)


def cone(a):
    return (1.0 - a[0], -a[1])


def cpick(cond, a, b):
    return (jnp.where(cond, a[0], b[0]), jnp.where(cond, a[1], b[1]))


def rows_at(start, rows):
    if isinstance(start, int):
        return pl.ds(start, rows)
    return pl.ds(pl.multiple_of(start, 8), rows)


def load(ref, base, short, row, rows):
    return (ref[rows_at(base + row, rows), :], ref[rows_at(base + short + row, rows), :])


def store(ref, base, short, row, rows, value):
    ref[rows_at(base + row, rows), :] = value[0]
    ref[rows_at(base + short + row, rows), :] = value[1]


def each_strip(count, rows, body):
    def step(i, carry):
        body(pl.multiple_of(i * rows, rows))
        return carry

    steps = count // rows
    lax.fori_loop(0, steps, step, 0, unroll=min(steps, 4))


def squares_of(a):
    return a[0] * a[0] + a[1] * a[1]


def conduct_kernel(table_ref, ids_ref, out_ref):
    planes = ids_ref.shape[0]
    ids = ids_ref[...]
    cells = jnp.zeros(ids.shape, jnp.float32)
    for layer in range(table_ref.shape[0]):
        cells = jnp.where(ids == layer, table_ref[layer], cells)
    out_ref[...] = jnp.zeros_like(out_ref)
    out_ref[pl.ds(0, planes), :] = cells
    out_ref[pl.ds(TAG - 1, 1), :] = jnp.sum(cells, axis=0, keepdims=True)


def add_kernel(one_ref, two_ref, out_ref):
    out_ref[...] = one_ref[...] + two_ref[...]


def fill_tag(out_ref, planes, own_ref, below_ref, above_ref, *part_refs):
    start = out_ref.shape[0] - TAG
    for n, ref in enumerate((own_ref, below_ref, above_ref)):
        out_ref[pl.ds(start + n * planes, planes), :] = ref[pl.ds(0, planes), :]
    total = part_refs[0][pl.ds(TAG - 1, 1), :]
    for ref in part_refs[1:]:
        total = total + ref[pl.ds(TAG - 1, 1), :]
    out_ref[pl.ds(start + TAG - 1, 1), :] = total


def tag_of(ref):
    return ref[pl.ds(ref.shape[0] - TAG, TAG), :]


def find_numbers(cells_total, shift_ref, part_refs, numbers_ref):
    total = None
    for ref in part_refs:
        row = ref[pl.ds(ref.shape[0] - 1, 1), :]
        total = row if total is None else total + row
    inv = (1.0 / (jnp.sum(total, axis=1, keepdims=True) * (1.0 / cells_total)))[0, 0]
    numbers_ref[0] = shift_ref[0] * inv
    numbers_ref[1] = shift_ref[1] * inv
    numbers_ref[2] = relax * inv
    numbers_ref[3] = 0.5 * relax * inv
    numbers_ref[4] = shift_ref[0]
    numbers_ref[5] = shift_ref[1]


def faces_kernel(planes, blocks, flags_ref, *refs):
    part_refs, (faces_ref, padded_ref, below_ref, above_ref) = refs[:GROUP], refs[GROUP:]
    z, member = flags_ref[2], flags_ref[3]
    _, count, width = faces_ref.shape
    for d, ref in enumerate(part_refs):
        tag = tag_of(ref)
        place = member ^ d
        for p in range(planes):
            padded_ref[pl.ds(8 + place * planes + p, 1), :] = tag[p : p + 1]
        below_ref[pl.ds(place, 1), :] = tag[2 * planes - 1 : 2 * planes]
        above_ref[pl.ds(place, 1), :] = tag[2 * planes : 2 * planes + 1]
    cells = padded_ref[pl.ds(8, count), :]
    padded_ref[pl.ds(7, 1), :] = jnp.where(z == 0, cells[0:1], below_ref[pl.ds(GROUP - 1, 1), :])
    padded_ref[pl.ds(8 + count, 1), :] = jnp.where(
        z == blocks - 1, cells[count - 1 : count], above_ref[pl.ds(0, 1), :]
    )
    lane = lax.broadcasted_iota(jnp.int32, cells.shape, 1)
    last, first = lane == width - 1, lane == 0
    right = 0.5 * (cells + pltpu.roll(cells, width - 1, 1))
    left = 0.5 * (cells + pltpu.roll(cells, 1, 1))
    low = 0.5 * (cells + padded_ref[pl.ds(7, count), :])
    high = 0.5 * (cells + padded_ref[pl.ds(9, count), :])
    faces_ref[0] = jnp.where(last, cells, right) + jnp.where(first, cells, left) + (low + high)
    faces_ref[1] = cells
    faces_ref[2] = jnp.where(last, 0.0, right)
    faces_ref[3] = jnp.where(first, 0.0, left)
    faces_ref[4] = low
    faces_ref[5] = high


def forward_kernel(distance, tags_count, flags_ref, source_ref, wave_ref, *refs):
    tag_refs, out_refs, stage_ref = refs[:tags_count], refs[tags_count:-1], refs[-1]
    planes = source_ref.shape[1]
    q = flags_ref[0] ^ distance
    sign = (1 - 2 * (q & 1)).astype(jnp.float32)
    turn_re = jnp.where(q == 0, 1.0, jnp.where(q == 2, -1.0, 0.0))
    turn_im = jnp.where(q == 1, 1.0, jnp.where(q == 3, -1.0, 0.0))
    rows = stage_ref.shape[1] // (HALVES * CHUNKS)
    for p in range(planes):
        parts = [[source_ref[c, p, i] for i in range(RADIX)] for c in range(2)]
        even = [parts[c][0] + sign * parts[c][2] for c in range(2)]
        odd = [parts[c][1] + sign * parts[c][3] for c in range(2)]
        mixed = jnp.concatenate(
            [
                even[0] + (turn_re * odd[0] + turn_im * odd[1]),
                even[1] + (turn_re * odd[1] - turn_im * odd[0]),
            ],
            axis=0,
        )
        stage_ref[p] = dot_left(wave_ref[q], mixed)
        for n in range(HALVES):
            h = flags_ref[1] ^ n
            for t in range(CHUNKS):
                out_refs[n * CHUNKS + t][pl.ds(p * rows, rows), :] = stage_ref[
                    p, rows_at((h * CHUNKS + t) * rows, rows), :
                ]
    for ref in out_refs if tags_count else ():
        fill_tag(ref, planes, *tag_refs)


def tagged_kernel(planes, count, *refs):
    for ref, out_ref in zip(refs[:count], refs[-count:]):
        rows = ref.shape[0] - TAG
        out_ref[pl.ds(0, rows), :] = ref[pl.ds(0, rows), :]
        fill_tag(out_ref, planes, *refs[count:-count])


def backward_kernel(planes, cells, flags_ref, wave_ref, *refs):
    arrays, (out_ref, norms_ref, mixed_ref, stage_ref) = refs[:-4], refs[-4:]
    rows = (arrays[0].shape[0] - TAG) // planes
    came = {}
    for (t, d), ref in zip(ANSWERS, arrays):
        for n in range(CHUNKS if d in JOINT else 1):
            came[d, n if d in JOINT else t] = ref.at[pl.ds(n * planes * rows, planes * rows)]
    short = rows * CHUNKS * HALVES // 2
    total = None
    for ref in arrays:
        tag = tag_of(ref)
        total = tag if total is None else total + tag
    for d in range(RADIX):
        q = flags_ref[0] ^ d
        for p in range(planes):
            for n in range(HALVES):
                h = flags_ref[1] ^ n
                for t in range(CHUNKS):
                    stage_ref[d, p, rows_at((h * CHUNKS + t) * rows, rows), :] = came[d + RADIX * n, t][
                        pl.ds(p * rows, rows), :
                    ]
            mixed_ref[p, q] = dot_left(wave_ref[q], stage_ref[d, p])
    for p in range(planes):

        def strip(row):
            zero, one, two, three = [load(mixed_ref.at[p, q], 0, short, row, 8) for q in range(RADIX)]
            even, odd = cadd(zero, two), cadd(one, three)
            even_d, odd_d = csub(zero, two), csub(one, three)
            parts = (
                cadd(even, odd),
                (even_d[0] - odd_d[1], even_d[1] + odd_d[0]),
                csub(even, odd),
                (even_d[0] + odd_d[1], even_d[1] - odd_d[0]),
            )
            for i in range(RADIX):
                for c in range(2):
                    out_ref[c, p, rows_at(i * short + row, 8), :] = parts[i][c]

        each_strip(short, 8, strip)
    norms = jnp.sqrt(jnp.sum(total, axis=1, keepdims=True) * (1.0 / cells))
    for n in range(norms_ref.shape[0]):
        norms_ref[n] = norms[n, 0]


def decay_root(h):
    sq = (h[0] + 0.25 * (h[0] * h[0] - h[1] * h[1]), h[1] + 0.5 * h[0] * h[1])
    size = jnp.sqrt(squares_of(sq))
    root_re = jnp.sqrt(0.5 * (size + sq[0]))
    root = (root_re, 0.5 * sq[1] / root_re)
    return cinv((1.0 + 0.5 * h[0] + root[0], 0.5 * h[1] + root[1])), root


def two_powers(power, z, stacks):
    low = high = None
    bit = 0
    while (1 << bit) < stacks:
        taken = ((z >> bit) & 1) == 1
        if low is None:
            one = (jnp.ones_like(power[0]), jnp.zeros_like(power[0]))
            low, high = cpick(taken, power, one), cpick(taken, one, power)
        else:
            grown = cmul(cpick(taken, low, high), power)
            low, high = cpick(taken, grown, low), cpick(taken, high, grown)
        power = csqr(power)
        bit += 1
    return low, high


def sums_of(planes, rho, cross_f, cross_b):
    ahead = planes[0]
    for a in planes[1:]:
        ahead = cmore(a, rho, ahead)
    behind = planes[-1]
    for a in planes[-2::-1]:
        behind = cmore(a, rho, behind)
    return csub(ahead, cmul(cross_f, behind)), csub(behind, cmul(cross_b, ahead))


def sine_rows(source_ref, target_ref, sine_ref, count):
    sine = (sine_ref[0], sine_ref[1])
    rows = max(n for n in range(16, 641, 16) if count % n == 0)
    for i in range(0, count, rows):
        target_ref[pl.ds(i, rows), :] = dot_right(source_ref[pl.ds(i, rows), :], sine)


def fill_give(z, rows, sums_ref, give_refs):
    for ref in give_refs:
        ref[pl.ds(0, rows), :] = sums_ref[rows_at((z & 1) * rows, rows), :]
        ref[pl.ds(rows, TAG), :] = sums_ref[pl.ds(2 * rows, TAG), :]


def start_kernel(
    chunk, planes, blocks, cells_total, flags_ref, numbers_ref, wave_eig_ref, sine_eig_ref, sine_ref, *refs,
):
    part_refs, (field_ref, modes_ref, base_ref, sums_ref), give_refs = refs[:GROUP], refs[GROUP : GROUP + 4], refs[GROUP + 4 :]
    if chunk == 0:
        shift_ref, numbers_ref, give_refs = numbers_ref, give_refs[-1], give_refs[:-1]
        find_numbers(cells_total, shift_ref, part_refs, numbers_ref)
    q, h, z, member = [flags_ref[n] for n in range(4)]
    rows = base_ref.shape[1]
    part = rows * planes
    short = rows // 2
    count = GROUP * planes
    first_row = (h * CHUNKS + chunk) * short
    for d, ref in enumerate(part_refs):
        field_ref[rows_at((member ^ d) * part, part), :] = ref[pl.ds(0, part), :]
    sine_rows(field_ref, modes_ref, sine_ref, count * rows)
    h_re, h_im = numbers_ref[0], numbers_ref[1]
    sine_eig = sine_eig_ref[...]

    def strip(i, total):
        row = pl.multiple_of(i * 8, 8)
        eigen = wave_eig_ref[q, rows_at(first_row + row, 8), :] + sine_eig
        rho, _ = decay_root((eigen + h_re, jnp.full_like(eigen, h_im)))
        block = cpow(rho, count)
        next_one = cmul(block, rho)
        low, high = two_powers(csqr(block), z, blocks)
        cross_f, cross_b = cmul(next_one, low), cmul(next_one, high)
        for n, value in enumerate((rho, cross_f, cross_b, block, low, high)):
            store(base_ref.at[n], 0, short, row, 8, value)
        found = [load(modes_ref, l * rows, short, row, 8) for l in range(count)]
        ahead, behind = sums_of(found, rho, cross_f, cross_b)
        store(sums_ref, 0, short, row, 8, ahead)
        store(sums_ref, rows, short, row, 8, behind)
        for l in range(count):
            total = total + squares_of(load(field_ref, l * rows, short, row, 8))
        return total

    total = lax.fori_loop(
        0, short // 8, strip, jnp.zeros((8, field_ref.shape[1]), jnp.float32), unroll=2
    )
    sums_ref[pl.ds(2 * rows, TAG), :] = jnp.zeros((TAG, field_ref.shape[1]), jnp.float32)
    sums_ref[pl.ds(2 * rows, 1), :] = jnp.sum(total, axis=0, keepdims=True)
    fill_give(z, rows, sums_ref, give_refs)


def factors_kernel(
    chunk, count, levels, flags_ref, numbers_ref, wave_eig_ref, sine_eig_ref, base_ref, out_ref,
):
    q, h_part, z = flags_ref[0], flags_ref[1], flags_ref[2]
    short = base_ref.shape[1] // 2
    h_re, h_im, scale = numbers_ref[0], numbers_ref[1], numbers_ref[3]
    sine_eig = sine_eig_ref[...]

    def strip(row):
        eigen = wave_eig_ref[q, rows_at((h_part * CHUNKS + chunk) * short + row, 8), :] + sine_eig
        h = (eigen + h_re, jnp.full_like(eigen, h_im))
        rho, _, _, block, low, high = [load(base_ref.at[n], 0, short, row, 8) for n in range(6)]
        half_gap = csub((1.0 + 0.5 * h[0], 0.5 * h[1]), rho)
        wide = cmul(csqr(block), csqr(rho))
        low_w, high_w = cmul(low, wide), cmul(high, wide)
        whole = cscale(cinv(cmul(half_gap, cone(cmul(low, high_w)))), scale)
        turned = cmul(rho, whole)
        values = [
            cmul(cone(high_w), whole), cmul(cone(low), turned),
            cmul(cone(high), turned), cmul(cone(low_w), whole),
        ]
        pivot = (2.0 + h[0], h[1])
        inverse = cinv(pivot)
        values.append(inverse)
        for _ in range(count - 1):
            inverse = cinv(csub(pivot, inverse))
            values.append(inverse)
        near = far = None
        power = block
        for level in range(1, levels):
            taken = ((z >> (level - 1)) & 1) == 1
            if near is None:
                one = (jnp.ones_like(power[0]), jnp.zeros_like(power[0]))
                near, far = cpick(taken, power, one), cpick(taken, one, power)
            else:
                grown = cmul(cpick(taken, near, far), power)
                near, far = cpick(taken, grown, near), cpick(taken, far, grown)
            power = csqr(power)
            values.append(cpick(((z >> level) & 1) == 1, near, far))
        for n, value in enumerate(values):
            store(out_ref.at[n], 0, short, row, 8, value)

    each_strip(short, 8, strip)


def join_kernel(level, levels, flags_ref, sums_ref, came_ref, base_ref, out_ref):
    z = flags_ref[2]
    short = base_ref.shape[1] // 2
    rows = 2 * short
    above = ((z >> level) & 1) == 1
    last = level + 2 == levels
    upper = ((z >> (level + 1)) & 1) == 1

    def strip(row):
        block = load(base_ref.at[3], 0, short, row, 8)
        for _ in range(level):
            block = csqr(block)
        ahead, behind = load(sums_ref, 0, short, row, 8), load(sums_ref, rows, short, row, 8)
        ahead_c, behind_c = load(came_ref, 0, short, row, 8), load(came_ref, rows, short, row, 8)
        joined = cmore(cpick(above, ahead, ahead_c), block, cpick(above, ahead_c, ahead))
        joined_b = cmore(cpick(above, behind_c, behind), block, cpick(above, behind, behind_c))
        if last:
            store(out_ref, 0, short, row, 8, cpick(upper, joined_b, joined))
        else:
            store(out_ref, 0, short, row, 8, joined)
            store(out_ref, rows, short, row, 8, joined_b)

    each_strip(short, 8, strip)
    out_ref[pl.ds(out_ref.shape[0] - TAG, TAG), :] = (
        sums_ref[pl.ds(2 * rows, TAG), :] + came_ref[pl.ds(2 * rows, TAG), :]
    )


def solved(count, levels, z, scale, modes_ref, sums_ref, came_refs, base_ref, factors_ref, row):
    short = base_ref.shape[1] // 2
    rows = 2 * short

    def factor(n):
        return load(factors_ref.at[n], 0, short, row, 8)

    enter_f = enter_b = None
    for level in range(levels):
        above = ((z >> level) & 1) == 1
        base = 0 if level == levels - 1 else jnp.where(above, 0, rows)
        came = load(came_refs[level], base, short, row, 8)
        if level:
            came = cmul(factor(4 + count + level - 1), came)
        nought = (jnp.zeros_like(came[0]), jnp.zeros_like(came[0]))
        now_f, now_b = cpick(above, came, nought), cpick(above, nought, came)
        enter_f = now_f if enter_f is None else cadd(enter_f, now_f)
        enter_b = now_b if enter_b is None else cadd(enter_b, now_b)
    block = load(base_ref.at[3], 0, short, row, 8)
    all_f = cmore(load(sums_ref, 0, short, row, 8), block, enter_f)
    all_b = cmore(load(sums_ref, rows, short, row, 8), block, enter_b)
    below = cmore(cmul(factor(0), enter_f), factor(1), all_b)
    above = cmore(cmul(factor(3), enter_b), factor(2), all_f)
    planes = [cscale(load(modes_ref, l * rows, short, row, 8), scale) for l in range(count)]
    planes[0] = cadd(planes[0], below)
    planes[-1] = cadd(planes[-1], above)
    for l in range(1, count):
        planes[l] = cmore(planes[l], factor(4 + l - 1), planes[l - 1])
    planes[-1] = cmul(factor(4 + count - 1), planes[-1])
    for l in range(count - 2, -1, -1):
        planes[l] = cmul(factor(4 + l), cadd(planes[l], planes[l + 1]))
    return below, planes, above


def middle_kernel(
    chunk, count, levels, flags_ref, numbers_ref, wave_eig_ref, sine_ref, faces_ref, field_ref,
    modes_ref, base_ref, factors_ref, sums_ref, *refs,
):
    came_refs, (found_ref, next_ref, next_sums_ref) = refs[:levels], refs[levels : levels + 3]
    give_refs, work_ref = refs[levels + 3 : -1], refs[-1]
    q, h, z = flags_ref[0], flags_ref[1], flags_ref[2]
    scale, s_re, s_im = numbers_ref[2], numbers_ref[4], numbers_ref[5]
    short = base_ref.shape[1] // 2
    rows = 2 * short
    width = base_ref.shape[2]

    def solve(row):
        below, planes, above = solved(
            count, levels, z, scale, modes_ref, sums_ref, came_refs, base_ref, factors_ref, row
        )
        store(work_ref, 0, short, row, 8, below)
        store(work_ref, (count + 1) * rows, short, row, 8, above)
        for l in range(count):
            store(work_ref, (l + 1) * rows, short, row, 8, planes[l])
            store(found_ref, l * rows, short, row, 8, planes[l])

    each_strip(short, 8, solve)
    sine_rows(work_ref, work_ref, sine_ref, (count + 2) * rows)

    def residual(i, total):
        row = pl.multiple_of(i * 8, 8)
        eigen = wave_eig_ref[q, rows_at((h * CHUNKS + chunk) * short + row, 8), :]
        under = load(work_ref, 0, short, row, 8)
        here = load(work_ref, rows, short, row, 8)
        for l in range(count):
            over = load(work_ref, (l + 2) * rows, short, row, 8)
            diag, cell, right, left, low, high = [faces_ref[n, pl.ds(l, 1), :] for n in range(6)]
            diag = s_re + (diag + cell * eigen)
            value = []
            for c in range(2):
                v = diag * here[c] - right * pltpu.roll(here[c], width - 1, 1)
                v = v - left * pltpu.roll(here[c], 1, 1)
                value.append(v - (low * under[c] + high * over[c]))
            value = (value[0] - s_im * here[1], value[1] + s_im * here[0])
            value = csub(load(field_ref, l * rows, short, row, 8), value)
            total = total + squares_of(value)
            store(work_ref, l * rows, short, row, 8, value)
            under, here = here, over
        return total

    total = lax.fori_loop(0, short // 8, residual, jnp.zeros((8, width), jnp.float32), unroll=2)
    sine_rows(work_ref, next_ref, sine_ref, count * rows)

    def sums(row):
        rho, cross_f, cross_b = [load(base_ref.at[n], 0, short, row, 8) for n in range(3)]
        planes = [load(next_ref, l * rows, short, row, 8) for l in range(count)]
        ahead, behind = sums_of(planes, rho, cross_f, cross_b)
        store(next_sums_ref, 0, short, row, 8, ahead)
        store(next_sums_ref, rows, short, row, 8, behind)

    each_strip(short, 8, sums)
    next_sums_ref[pl.ds(2 * rows, TAG), :] = sums_ref[pl.ds(2 * rows, TAG), :]
    next_sums_ref[pl.ds(2 * rows + 1, 1), :] = jnp.sum(total, axis=0, keepdims=True)
    fill_give(z, rows, next_sums_ref, give_refs)


def end_kernel(
    count, levels, flags_ref, numbers_ref, sine_ref, found_ref, modes_ref, base_ref,
    factors_ref, sums_ref, *refs,
):
    came_refs, out_refs, work_ref = refs[:levels], refs[-1 - GROUP : -1], refs[-1]
    before_refs = refs[levels + (levels > 1) : -1 - GROUP]
    z, member = flags_ref[2], flags_ref[3]
    scale = numbers_ref[2]
    short = base_ref.shape[1] // 2
    rows = 2 * short

    def solve(row):
        _, planes, _ = solved(
            count, levels, z, scale, modes_ref, sums_ref, came_refs, base_ref, factors_ref, row
        )
        for l in range(count):
            before = load(found_ref, l * rows, short, row, 8)
            store(work_ref, l * rows, short, row, 8, cadd(before, planes[l]))

    each_strip(short, 8, solve)
    sine_rows(work_ref, work_ref, sine_ref, count * rows)
    part = count // GROUP * rows
    tag_refs = (refs[levels] if levels > 1 else sums_ref, came_refs[-1])
    tag = None
    for ref in tag_refs:
        part_tag = ref[pl.ds(ref.shape[0] - TAG, TAG), :]
        tag = part_tag if tag is None else tag + part_tag
    for d in range(GROUP):
        start, whole = 0, tag
        if d in JOINT:
            held = len(before_refs) // len(JOINT)
            for ref in before_refs[JOINT.index(d) * held : (JOINT.index(d) + 1) * held]:
                out_refs[d][pl.ds(start, part), :] = ref[pl.ds(0, part), :]
                start, whole = start + part, whole + tag_of(ref)
        out_refs[d][pl.ds(start, part), :] = work_ref[rows_at((member ^ d) * part, part), :]
        out_refs[d][pl.ds(start + part, TAG), :] = whole


smem = pl.BlockSpec(memory_space=pltpu.SMEM)
vmem = pl.BlockSpec(memory_space=pltpu.VMEM)
unread = pl.BlockSpec(memory_space=pl.ANY)


def call(kernel, scalars, arrays, outs, scratch=(), flops=0, after=()):
    out_shape = [jax.ShapeDtypeStruct(shape, jnp.float32) for shape in outs]
    head = len(scalars) + len(arrays)

    def run(*refs):
        kernel(*refs[:head], *refs[head + len(after) :])

    moved = sum(a.size * a.dtype.itemsize for a in arrays) + sum(4 * int(np.prod(s)) for s in outs)
    held = moved + sum(4 * int(np.prod(s)) for s in scratch)
    return pl.pallas_call(
        run,
        out_shape=out_shape,
        in_specs=[smem] * len(scalars) + [vmem] * len(arrays) + [unread] * len(after),
        out_specs=[smem if len(shape) == 1 else vmem for shape in outs],
        scratch_shapes=[pltpu.VMEM(shape, jnp.float32) for shape in scratch],
        compiler_params=pltpu.CompilerParams(vmem_limit_bytes=held + 4 * 2**20),
        cost_estimate=pl.CostEstimate(flops=flops, bytes_accessed=moved, transcendentals=0),
    )(*scalars, *arrays, *after)


def pair_up(array, groups, flip):
    return lax.ppermute(array, "gz", [(i, i ^ flip) for i in range(groups)])


def step_by(array, groups, distance):
    return lax.ppermute(
        array, "gz", [(i, i + distance) for i in range(groups) if 0 <= i + distance < groups]
    )


def body(source, layer_ids, conduct_table, shift):
    planes, length_x, length_y = source.shape[1:]
    groups = lax.axis_size("gz")
    blocks = groups // GROUP
    levels = blocks.bit_length() - 1
    count = GROUP * planes
    length_z = planes * groups
    full = length_x // RADIX
    short = full // (HALVES * CHUNKS)
    rows = 2 * short
    if blocks < 2 or groups != GROUP << levels or planes > 2 or short % 8 or length_x != RADIX * full:
        raise ValueError("unsupported layout")
    me = lax.axis_index("gz")
    member = me % GROUP
    flags = jnp.stack([member % RADIX, member // RADIX, me // GROUP, member]).astype(jnp.int32)

    wave = wave_tables(length_x)
    wave_f = jnp.asarray(np.concatenate(two_terms(wave), axis=1))
    wave_b = jnp.asarray(np.concatenate(two_terms(np.swapaxes(wave, 1, 2) / length_x), axis=1))
    sine = jnp.asarray(two_terms(sine_table(length_y)))
    wave_eig = np.broadcast_to(wave_eigen(length_x)[:, :, None], (RADIX, full, length_y))
    wave_eig = jnp.asarray(np.ascontiguousarray(wave_eig).astype(np.float32))
    sine_eig = jnp.asarray(np.tile(sine_eigen(length_y)[None, :], (8, 1)).astype(np.float32))

    chunks = range(CHUNKS)
    row_block = (TAG, length_y)
    block = (count * rows, length_y)
    sums_block = (2 * rows + TAG, length_y)
    single = (rows + TAG, length_y)
    part = (planes * rows + TAG, length_y)
    parts = (CHUNKS * planes * rows + TAG, length_y)
    gives = [single] if levels == 1 else []
    dots = 6 * length_y * length_y

    (cells,) = call(conduct_kernel, [conduct_table], [layer_ids], [row_block])
    if levels == 1:
        below = above = pair_up(cells, groups, GROUP)
        totals = [cells, below]
    else:
        below = step_by(cells, groups, GROUP)
        above = step_by(cells, groups, -GROUP)
        total = cells
        for level in range(levels):
            (total,) = call(add_kernel, [], [total, pair_up(total, groups, GROUP << level)], [row_block])
        totals = [total]

    parted = source.reshape(2, planes, RADIX, full, length_y)
    spectra = {}
    placed = [cells]
    tags = [cells, below, above, *totals]
    for d in (2, 0, 3, 1):
        early = d == 2
        made = call(
            functools.partial(forward_kernel, d, 0 if early else len(tags)), [flags],
            [parted, wave_f, *([] if early else tags)], [part] * (HALVES * CHUNKS),
            scratch=[(planes, 2 * full, length_y)], flops=planes * 2 * full * dots, after=placed,
        )
        if early:
            made = call(
                functools.partial(tagged_kernel, planes, len(made)), [], [*made, *tags], [part] * len(made),
            )
        placed = made[:1]
        for n in range(HALVES):
            for t in chunks:
                spectra[d + RADIX * n, t] = made[n * CHUNKS + t]
    for t in chunks:
        for d in (6, 2, 4, 7, 3, 5, 1):
            if t == 0 or d not in JOINT:
                spectra[d, t] = pair_up(spectra[d, t], groups, d)

    state = [{} for _ in chunks]

    def exchange(st, after):
        sums, give = st["sums"][0], st["sums"][-1]
        st["came"], st["tags"] = [], []
        for level in range(levels):
            st["came"].append(pair_up(give, groups, GROUP << level))
            if level + 1 < levels:
                shape = single if level + 2 == levels else sums_block
                (give,) = call(
                    functools.partial(join_kernel, level, levels), [flags], [sums, st["came"][-1], st["base"]],
                    [shape], after=after,
                )
                sums = give
                st["tags"] = [give[-TAG:]]

    def start(t, after):
        st = state[t]
        outs = [block, block, (6, rows, length_y), sums_block, *gives]
        made = call(
            functools.partial(start_kernel, t, planes, blocks, length_y * length_z),
            [flags, state[0]["numbers"] if t else shift],
            [wave_eig, sine_eig, sine] + [spectra[d, t] for d in range(GROUP)],
            outs if t else [*outs, (6,)], flops=count * rows * dots, after=after,
        )
        if not t:
            *made, st["numbers"] = made
        st["field"], st["modes"], st["base"], *st["sums"] = made
        exchange(st, [])
        return [st["sums"][-1]]

    def faces(t, after):
        state[t]["faces"] = call(
            functools.partial(faces_kernel, planes, blocks), [flags], [spectra[d, 0] for d in range(GROUP)],
            [(6, count, length_y)], scratch=[(count + 16, length_y), row_block, row_block], after=after,
        )[0]
        return [state[t]["faces"]]

    def factors(t, after):
        st = state[t]
        (st["factors"],) = call(
            functools.partial(factors_kernel, t, count, levels), [flags, state[0]["numbers"]],
            [wave_eig, sine_eig, st["base"]], [(4 + count + levels - 1, rows, length_y)], after=after,
        )
        return [st["factors"]]

    def middle(t, after):
        st = state[t]
        st["found"], st["modes"], *st["sums"] = call(
            functools.partial(middle_kernel, t, count, levels), [flags, state[0]["numbers"]],
            [wave_eig, sine, state[0]["faces"], st["field"], st["modes"], st["base"], st["factors"], st["sums"][0], *st["came"]],
            [block, block, sums_block, *gives], scratch=[((count + 2) * rows, length_y)],
            flops=(2 * count + 2) * rows * dots, after=after,
        )
        exchange(st, [])
        return [st["sums"][-1]]

    def end(t, after):
        st = state[t]
        last = t == CHUNKS - 1
        before = [state[u]["made"][d] for d in JOINT for u in range(t)] if last else []
        st["made"] = call(
            functools.partial(end_kernel, count, levels), [flags, state[0]["numbers"]],
            [sine, st["found"], st["modes"], st["base"], st["factors"], st["sums"][0], *st["came"], *st["tags"], *before],
            [parts if last and d in JOINT else part for d in range(GROUP)],
            scratch=[block], flops=count * rows * dots, after=after,
        )
        st["answers"] = {d: st["made"][d] for d in SENDS[t]}
        return [st["made"][0]]

    def held(array, after):
        return lax.optimization_barrier((array, *after))[0]

    def answer(t, distances):
        answers = state[t]["answers"]
        for d in distances:
            answers[d] = pair_up(answers[d], groups, d)

    placed = []
    for step in (start, faces, factors):
        placed = step(0, placed)
    for d in JOINT:
        spectra[d, 1] = pair_up(held(spectra[d, 1], placed), groups, d)
    for step, t in ((middle, 0), (start, 1), (factors, 1), (end, 0)):
        placed = step(t, placed)
    answer(0, SENDS[0][:-1])
    placed = middle(1, placed)
    end(1, [*placed, *[state[0]["answers"][d] for d in SENDS[0][:2]]])
    answer(1, SENDS[1][:-1])
    return call(
        functools.partial(backward_kernel, planes, length_x * length_x * length_y * length_z),
        [flags], [wave_b] + [state[t]["answers"][d] for t, d in ANSWERS],
        [(2, planes, length_x, length_y), (2,)],
        scratch=[(planes, RADIX, 2 * full, length_y), (RADIX, planes, 2 * full, length_y)],
        flops=planes * RADIX * 2 * full * dots,
    )


def solution(mesh):
    placed = (P(None, ("node", "gz"), None, None), P(("node", "gz"), None), P(), P("node"))
    return jax.shard_map(
        body,
        mesh=mesh,
        in_specs=placed,
        out_specs=(P(None, ("node", "gz"), None, None), P("node")),
        check_vma=False,
    )
```

```python
import functools

import jax
import jax.numpy as jnp
import ml_dtypes
import numpy as np
from jax import lax
from jax.experimental import pallas as pl
from jax.experimental.pallas import tpu as pltpu
from jax.sharding import PartitionSpec as P

RADIX = 4
HALVES = 2
GROUP = RADIX * HALVES
CHUNKS = 2
SENDS = ((6, 7, 2, 3, 4, 0), (2, 6, 7, 3, 4, 5, 1, 0))
ANSWERS = tuple((t, d) for t in range(CHUNKS) for d in SENDS[t])
JOINT = (5, 1)
TAG = 8

relax = 0.6


def sine_table(length):
    indices = np.arange(1, length + 1)
    product = indices[:, None] * indices[None, :] % (2 * (length + 1))
    return np.sqrt(2.0 / (length + 1)) * np.sin(np.pi / (length + 1) * product)


def sine_eigen(length):
    indices = np.arange(1, length + 1)
    return 4.0 * np.sin(np.pi / (2 * (length + 1)) * indices) ** 2


def wave_numbers(length):
    return RADIX * np.arange(length // RADIX)[None, :] + np.arange(RADIX)[:, None]


def wave_eigen(length):
    return 4.0 * np.sin(np.pi / length * wave_numbers(length)) ** 2


def wave_tables(length):
    waves = wave_numbers(length)
    short = length // RADIX
    product = waves[:, :, None] * np.arange(short)[None, None, :] % length
    angles = 2.0 * np.pi / length * product
    cos_t, sin_t = np.cos(angles), np.sin(angles)
    pieces = HALVES * CHUNKS
    top = np.concatenate([cos_t, sin_t], axis=2).reshape(RADIX, pieces, short // pieces, 2 * short)
    low = np.concatenate([-sin_t, cos_t], axis=2).reshape(RADIX, pieces, short // pieces, 2 * short)
    return np.concatenate([top, low], axis=2).reshape(RADIX, 2 * short, 2 * short)


def two_terms(table):
    first = table.astype(ml_dtypes.bfloat16)
    return np.stack([first, (table - first.astype(np.float64)).astype(ml_dtypes.bfloat16)])


def split(value):
    first = value.astype(jnp.bfloat16)
    return first, (value - first.astype(jnp.float32)).astype(jnp.bfloat16)


def dot_right(value, table):
    rows = value.shape[0]
    first, second = split(value)
    wide = jnp.dot(jnp.concatenate([first, second], axis=0), table[0], preferred_element_type=jnp.float32)
    return wide[:rows] + (wide[rows:] + jnp.dot(first, table[1], preferred_element_type=jnp.float32))


def dot_left(table, value):
    rows = table.shape[0] // 2
    first, second = split(value)
    wide = jnp.dot(table, first, preferred_element_type=jnp.float32)
    return wide[:rows] + (wide[rows:] + jnp.dot(table[:rows], second, preferred_element_type=jnp.float32))


def cmul(a, b):
    return (a[0] * b[0] - a[1] * b[1], a[0] * b[1] + a[1] * b[0])


def csqr(a):
    cross = a[0] * a[1]
    return ((a[0] - a[1]) * (a[0] + a[1]), cross + cross)


def cpow(a, count):
    result = None
    while count:
        if count & 1:
            result = a if result is None else cmul(result, a)
        count >>= 1
        if count:
            a = csqr(a)
    return result


def cadd(a, b):
    return (a[0] + b[0], a[1] + b[1])


def csub(a, b):
    return (a[0] - b[0], a[1] - b[1])


def cscale(a, scale):
    return (a[0] * scale, a[1] * scale)


def cmore(total, factor, term):
    return cadd(total, cmul(factor, term))


def cinv(a):
    scale = 1.0 / (a[0] * a[0] + a[1] * a[1])
    return (a[0] * scale, -a[1] * scale)


def cone(a):
    return (1.0 - a[0], -a[1])


def cpick(cond, a, b):
    return (jnp.where(cond, a[0], b[0]), jnp.where(cond, a[1], b[1]))


def rows_at(start, rows):
    if isinstance(start, int):
        return pl.ds(start, rows)
    return pl.ds(pl.multiple_of(start, 8), rows)


def load(ref, base, short, row, rows):
    return (ref[rows_at(base + row, rows), :], ref[rows_at(base + short + row, rows), :])


def store(ref, base, short, row, rows, value):
    ref[rows_at(base + row, rows), :] = value[0]
    ref[rows_at(base + short + row, rows), :] = value[1]


def each_strip(count, rows, body):
    def step(i, carry):
        body(pl.multiple_of(i * rows, rows))
        return carry

    steps = count // rows
    lax.fori_loop(0, steps, step, 0, unroll=min(steps, 4))


def squares_of(a):
    return a[0] * a[0] + a[1] * a[1]


def conduct_kernel(table_ref, ids_ref, out_ref):
    planes = ids_ref.shape[0]
    ids = ids_ref[...]
    cells = jnp.zeros(ids.shape, jnp.float32)
    for layer in range(table_ref.shape[0]):
        cells = jnp.where(ids == layer, table_ref[layer], cells)
    out_ref[...] = jnp.zeros_like(out_ref)
    out_ref[pl.ds(0, planes), :] = cells
    out_ref[pl.ds(TAG - 1, 1), :] = jnp.sum(cells, axis=0, keepdims=True)


def add_kernel(one_ref, two_ref, out_ref):
    out_ref[...] = one_ref[...] + two_ref[...]


def fill_tag(out_ref, planes, own_ref, below_ref, above_ref, *part_refs):
    start = out_ref.shape[0] - TAG
    for n, ref in enumerate((own_ref, below_ref, above_ref)):
        out_ref[pl.ds(start + n * planes, planes), :] = ref[pl.ds(0, planes), :]
    total = part_refs[0][pl.ds(TAG - 1, 1), :]
    for ref in part_refs[1:]:
        total = total + ref[pl.ds(TAG - 1, 1), :]
    out_ref[pl.ds(start + TAG - 1, 1), :] = total


def tag_of(ref):
    return ref[pl.ds(ref.shape[0] - TAG, TAG), :]


def find_numbers(cells_total, shift_ref, part_refs, numbers_ref):
    total = None
    for ref in part_refs:
        row = ref[pl.ds(ref.shape[0] - 1, 1), :]
        total = row if total is None else total + row
    inv = (1.0 / (jnp.sum(total, axis=1, keepdims=True) * (1.0 / cells_total)))[0, 0]
    numbers_ref[0] = shift_ref[0] * inv
    numbers_ref[1] = shift_ref[1] * inv
    numbers_ref[2] = relax * inv
    numbers_ref[3] = 0.5 * relax * inv
    numbers_ref[4] = shift_ref[0]
    numbers_ref[5] = shift_ref[1]


def faces_kernel(planes, blocks, flags_ref, *refs):
    part_refs, (faces_ref, padded_ref, below_ref, above_ref) = refs[:GROUP], refs[GROUP:]
    z, member = flags_ref[2], flags_ref[3]
    _, count, width = faces_ref.shape
    for d, ref in enumerate(part_refs):
        tag = tag_of(ref)
        place = member ^ d
        for p in range(planes):
            padded_ref[pl.ds(8 + place * planes + p, 1), :] = tag[p : p + 1]
        below_ref[pl.ds(place, 1), :] = tag[2 * planes - 1 : 2 * planes]
        above_ref[pl.ds(place, 1), :] = tag[2 * planes : 2 * planes + 1]
    cells = padded_ref[pl.ds(8, count), :]
    padded_ref[pl.ds(7, 1), :] = jnp.where(z == 0, cells[0:1], below_ref[pl.ds(GROUP - 1, 1), :])
    padded_ref[pl.ds(8 + count, 1), :] = jnp.where(
        z == blocks - 1, cells[count - 1 : count], above_ref[pl.ds(0, 1), :]
    )
    lane = lax.broadcasted_iota(jnp.int32, cells.shape, 1)
    last, first = lane == width - 1, lane == 0
    right = 0.5 * (cells + pltpu.roll(cells, width - 1, 1))
    left = 0.5 * (cells + pltpu.roll(cells, 1, 1))
    low = 0.5 * (cells + padded_ref[pl.ds(7, count), :])
    high = 0.5 * (cells + padded_ref[pl.ds(9, count), :])
    faces_ref[0] = jnp.where(last, cells, right) + jnp.where(first, cells, left) + (low + high)
    faces_ref[1] = cells
    faces_ref[2] = jnp.where(last, 0.0, right)
    faces_ref[3] = jnp.where(first, 0.0, left)
    faces_ref[4] = low
    faces_ref[5] = high


def forward_kernel(distance, tags_count, flags_ref, source_ref, wave_ref, *refs):
    tag_refs, out_refs, stage_ref = refs[:tags_count], refs[tags_count:-1], refs[-1]
    planes = source_ref.shape[1]
    q = flags_ref[0] ^ distance
    sign = (1 - 2 * (q & 1)).astype(jnp.float32)
    turn_re = jnp.where(q == 0, 1.0, jnp.where(q == 2, -1.0, 0.0))
    turn_im = jnp.where(q == 1, 1.0, jnp.where(q == 3, -1.0, 0.0))
    rows = stage_ref.shape[1] // (HALVES * CHUNKS)
    for p in range(planes):
        parts = [[source_ref[c, p, i] for i in range(RADIX)] for c in range(2)]
        even = [parts[c][0] + sign * parts[c][2] for c in range(2)]
        odd = [parts[c][1] + sign * parts[c][3] for c in range(2)]
        mixed = jnp.concatenate(
            [
                even[0] + (turn_re * odd[0] + turn_im * odd[1]),
                even[1] + (turn_re * odd[1] - turn_im * odd[0]),
            ],
            axis=0,
        )
        stage_ref[p] = dot_left(wave_ref[q], mixed)
        for n in range(HALVES):
            h = flags_ref[1] ^ n
            for t in range(CHUNKS):
                out_refs[n * CHUNKS + t][pl.ds(p * rows, rows), :] = stage_ref[
                    p, rows_at((h * CHUNKS + t) * rows, rows), :
                ]
    for ref in out_refs if tags_count else ():
        fill_tag(ref, planes, *tag_refs)


def tagged_kernel(planes, count, *refs):
    for ref, out_ref in zip(refs[:count], refs[-count:]):
        rows = ref.shape[0] - TAG
        out_ref[pl.ds(0, rows), :] = ref[pl.ds(0, rows), :]
        fill_tag(out_ref, planes, *refs[count:-count])


def backward_kernel(planes, cells, flags_ref, wave_ref, *refs):
    arrays, (out_ref, norms_ref, mixed_ref, stage_ref) = refs[:-4], refs[-4:]
    rows = (arrays[0].shape[0] - TAG) // planes
    came = {}
    for (t, d), ref in zip(ANSWERS, arrays):
        for n in range(CHUNKS if d in JOINT else 1):
            came[d, n if d in JOINT else t] = ref.at[pl.ds(n * planes * rows, planes * rows)]
    short = rows * CHUNKS * HALVES // 2
    total = None
    for ref in arrays:
        tag = tag_of(ref)
        total = tag if total is None else total + tag
    for d in range(RADIX):
        q = flags_ref[0] ^ d
        for p in range(planes):
            for n in range(HALVES):
                h = flags_ref[1] ^ n
                for t in range(CHUNKS):
                    stage_ref[d, p, rows_at((h * CHUNKS + t) * rows, rows), :] = came[d + RADIX * n, t][
                        pl.ds(p * rows, rows), :
                    ]
            mixed_ref[p, q] = dot_left(wave_ref[q], stage_ref[d, p])
    for p in range(planes):

        def strip(row):
            zero, one, two, three = [load(mixed_ref.at[p, q], 0, short, row, 8) for q in range(RADIX)]
            even, odd = cadd(zero, two), cadd(one, three)
            even_d, odd_d = csub(zero, two), csub(one, three)
            parts = (
                cadd(even, odd),
                (even_d[0] - odd_d[1], even_d[1] + odd_d[0]),
                csub(even, odd),
                (even_d[0] + odd_d[1], even_d[1] - odd_d[0]),
            )
            for i in range(RADIX):
                for c in range(2):
                    out_ref[c, p, rows_at(i * short + row, 8), :] = parts[i][c]

        each_strip(short, 8, strip)
    norms = jnp.sqrt(jnp.sum(total, axis=1, keepdims=True) * (1.0 / cells))
    for n in range(norms_ref.shape[0]):
        norms_ref[n] = norms[n, 0]


def decay_root(h):
    sq = (h[0] + 0.25 * (h[0] * h[0] - h[1] * h[1]), h[1] + 0.5 * h[0] * h[1])
    size = jnp.sqrt(squares_of(sq))
    root_re = jnp.sqrt(0.5 * (size + sq[0]))
    root = (root_re, 0.5 * sq[1] / root_re)
    return cinv((1.0 + 0.5 * h[0] + root[0], 0.5 * h[1] + root[1])), root


def two_powers(power, z, stacks):
    low = high = None
    bit = 0
    while (1 << bit) < stacks:
        taken = ((z >> bit) & 1) == 1
        if low is None:
            one = (jnp.ones_like(power[0]), jnp.zeros_like(power[0]))
            low, high = cpick(taken, power, one), cpick(taken, one, power)
        else:
            grown = cmul(cpick(taken, low, high), power)
            low, high = cpick(taken, grown, low), cpick(taken, high, grown)
        power = csqr(power)
        bit += 1
    return low, high


def sums_of(planes, rho, cross_f, cross_b):
    ahead = planes[0]
    for a in planes[1:]:
        ahead = cmore(a, rho, ahead)
    behind = planes[-1]
    for a in planes[-2::-1]:
        behind = cmore(a, rho, behind)
    return csub(ahead, cmul(cross_f, behind)), csub(behind, cmul(cross_b, ahead))


def sine_rows(source_ref, target_ref, sine_ref, count):
    sine = (sine_ref[0], sine_ref[1])
    rows = max(n for n in range(16, 641, 16) if count % n == 0)
    for i in range(0, count, rows):
        target_ref[pl.ds(i, rows), :] = dot_right(source_ref[pl.ds(i, rows), :], sine)


def fill_give(z, rows, sums_ref, give_refs):
    for ref in give_refs:
        ref[pl.ds(0, rows), :] = sums_ref[rows_at((z & 1) * rows, rows), :]
        ref[pl.ds(rows, TAG), :] = sums_ref[pl.ds(2 * rows, TAG), :]


def start_kernel(
    chunk, planes, blocks, cells_total, flags_ref, numbers_ref, wave_eig_ref, sine_eig_ref, sine_ref, *refs,
):
    part_refs, (field_ref, modes_ref, base_ref, sums_ref), give_refs = refs[:GROUP], refs[GROUP : GROUP + 4], refs[GROUP + 4 :]
    if chunk == 0:
        shift_ref, numbers_ref, give_refs = numbers_ref, give_refs[-1], give_refs[:-1]
        find_numbers(cells_total, shift_ref, part_refs, numbers_ref)
    q, h, z, member = [flags_ref[n] for n in range(4)]
    rows = base_ref.shape[1]
    part = rows * planes
    short = rows // 2
    count = GROUP * planes
    first_row = (h * CHUNKS + chunk) * short
    for d, ref in enumerate(part_refs):
        field_ref[rows_at((member ^ d) * part, part), :] = ref[pl.ds(0, part), :]
    sine_rows(field_ref, modes_ref, sine_ref, count * rows)
    h_re, h_im = numbers_ref[0], numbers_ref[1]
    sine_eig = sine_eig_ref[...]

    def strip(i, total):
        row = pl.multiple_of(i * 8, 8)
        eigen = wave_eig_ref[q, rows_at(first_row + row, 8), :] + sine_eig
        rho, _ = decay_root((eigen + h_re, jnp.full_like(eigen, h_im)))
        block = cpow(rho, count)
        next_one = cmul(block, rho)
        low, high = two_powers(csqr(block), z, blocks)
        cross_f, cross_b = cmul(next_one, low), cmul(next_one, high)
        for n, value in enumerate((rho, cross_f, cross_b, block, low, high)):
            store(base_ref.at[n], 0, short, row, 8, value)
        found = [load(modes_ref, l * rows, short, row, 8) for l in range(count)]
        ahead, behind = sums_of(found, rho, cross_f, cross_b)
        store(sums_ref, 0, short, row, 8, ahead)
        store(sums_ref, rows, short, row, 8, behind)
        for l in range(count):
            total = total + squares_of(load(field_ref, l * rows, short, row, 8))
        return total

    total = lax.fori_loop(
        0, short // 8, strip, jnp.zeros((8, field_ref.shape[1]), jnp.float32), unroll=2
    )
    sums_ref[pl.ds(2 * rows, TAG), :] = jnp.zeros((TAG, field_ref.shape[1]), jnp.float32)
    sums_ref[pl.ds(2 * rows, 1), :] = jnp.sum(total, axis=0, keepdims=True)
    fill_give(z, rows, sums_ref, give_refs)


def factors_kernel(
    chunk, count, levels, flags_ref, numbers_ref, wave_eig_ref, sine_eig_ref, base_ref, out_ref,
):
    q, h_part, z = flags_ref[0], flags_ref[1], flags_ref[2]
    short = base_ref.shape[1] // 2
    h_re, h_im, scale = numbers_ref[0], numbers_ref[1], numbers_ref[3]
    sine_eig = sine_eig_ref[...]

    def strip(row):
        eigen = wave_eig_ref[q, rows_at((h_part * CHUNKS + chunk) * short + row, 8), :] + sine_eig
        h = (eigen + h_re, jnp.full_like(eigen, h_im))
        rho, _, _, block, low, high = [load(base_ref.at[n], 0, short, row, 8) for n in range(6)]
        half_gap = csub((1.0 + 0.5 * h[0], 0.5 * h[1]), rho)
        wide = cmul(csqr(block), csqr(rho))
        low_w, high_w = cmul(low, wide), cmul(high, wide)
        whole = cscale(cinv(cmul(half_gap, cone(cmul(low, high_w)))), scale)
        turned = cmul(rho, whole)
        values = [
            cmul(cone(high_w), whole), cmul(cone(low), turned),
            cmul(cone(high), turned), cmul(cone(low_w), whole),
        ]
        pivot = (2.0 + h[0], h[1])
        inverse = cinv(pivot)
        values.append(inverse)
        for _ in range(count - 1):
            inverse = cinv(csub(pivot, inverse))
            values.append(inverse)
        near = far = None
        power = block
        for level in range(1, levels):
            taken = ((z >> (level - 1)) & 1) == 1
            if near is None:
                one = (jnp.ones_like(power[0]), jnp.zeros_like(power[0]))
                near, far = cpick(taken, power, one), cpick(taken, one, power)
            else:
                grown = cmul(cpick(taken, near, far), power)
                near, far = cpick(taken, grown, near), cpick(taken, far, grown)
            power = csqr(power)
            values.append(cpick(((z >> level) & 1) == 1, near, far))
        for n, value in enumerate(values):
            store(out_ref.at[n], 0, short, row, 8, value)

    each_strip(short, 8, strip)


def join_kernel(level, levels, flags_ref, sums_ref, came_ref, base_ref, out_ref):
    z = flags_ref[2]
    short = base_ref.shape[1] // 2
    rows = 2 * short
    above = ((z >> level) & 1) == 1
    last = level + 2 == levels
    upper = ((z >> (level + 1)) & 1) == 1

    def strip(row):
        block = load(base_ref.at[3], 0, short, row, 8)
        for _ in range(level):
            block = csqr(block)
        ahead, behind = load(sums_ref, 0, short, row, 8), load(sums_ref, rows, short, row, 8)
        ahead_c, behind_c = load(came_ref, 0, short, row, 8), load(came_ref, rows, short, row, 8)
        joined = cmore(cpick(above, ahead, ahead_c), block, cpick(above, ahead_c, ahead))
        joined_b = cmore(cpick(above, behind_c, behind), block, cpick(above, behind, behind_c))
        if last:
            store(out_ref, 0, short, row, 8, cpick(upper, joined_b, joined))
        else:
            store(out_ref, 0, short, row, 8, joined)
            store(out_ref, rows, short, row, 8, joined_b)

    each_strip(short, 8, strip)
    out_ref[pl.ds(out_ref.shape[0] - TAG, TAG), :] = (
        sums_ref[pl.ds(2 * rows, TAG), :] + came_ref[pl.ds(2 * rows, TAG), :]
    )


def solved(count, levels, z, scale, modes_ref, sums_ref, came_refs, base_ref, factors_ref, row):
    short = base_ref.shape[1] // 2
    rows = 2 * short

    def factor(n):
        return load(factors_ref.at[n], 0, short, row, 8)

    enter_f = enter_b = None
    for level in range(levels):
        above = ((z >> level) & 1) == 1
        base = 0 if level == levels - 1 else jnp.where(above, 0, rows)
        came = load(came_refs[level], base, short, row, 8)
        if level:
            came = cmul(factor(4 + count + level - 1), came)
        nought = (jnp.zeros_like(came[0]), jnp.zeros_like(came[0]))
        now_f, now_b = cpick(above, came, nought), cpick(above, nought, came)
        enter_f = now_f if enter_f is None else cadd(enter_f, now_f)
        enter_b = now_b if enter_b is None else cadd(enter_b, now_b)
    block = load(base_ref.at[3], 0, short, row, 8)
    all_f = cmore(load(sums_ref, 0, short, row, 8), block, enter_f)
    all_b = cmore(load(sums_ref, rows, short, row, 8), block, enter_b)
    below = cmore(cmul(factor(0), enter_f), factor(1), all_b)
    above = cmore(cmul(factor(3), enter_b), factor(2), all_f)
    planes = [cscale(load(modes_ref, l * rows, short, row, 8), scale) for l in range(count)]
    planes[0] = cadd(planes[0], below)
    planes[-1] = cadd(planes[-1], above)
    for l in range(1, count):
        planes[l] = cmore(planes[l], factor(4 + l - 1), planes[l - 1])
    planes[-1] = cmul(factor(4 + count - 1), planes[-1])
    for l in range(count - 2, -1, -1):
        planes[l] = cmul(factor(4 + l), cadd(planes[l], planes[l + 1]))
    return below, planes, above


def middle_kernel(
    chunk, count, levels, flags_ref, numbers_ref, wave_eig_ref, sine_ref, faces_ref, field_ref,
    modes_ref, base_ref, factors_ref, sums_ref, *refs,
):
    came_refs, (found_ref, next_ref, next_sums_ref) = refs[:levels], refs[levels : levels + 3]
    give_refs, work_ref = refs[levels + 3 : -1], refs[-1]
    q, h, z = flags_ref[0], flags_ref[1], flags_ref[2]
    scale, s_re, s_im = numbers_ref[2], numbers_ref[4], numbers_ref[5]
    short = base_ref.shape[1] // 2
    rows = 2 * short
    width = base_ref.shape[2]

    def solve(row):
        below, planes, above = solved(
            count, levels, z, scale, modes_ref, sums_ref, came_refs, base_ref, factors_ref, row
        )
        store(work_ref, 0, short, row, 8, below)
        store(work_ref, (count + 1) * rows, short, row, 8, above)
        for l in range(count):
            store(work_ref, (l + 1) * rows, short, row, 8, planes[l])
            store(found_ref, l * rows, short, row, 8, planes[l])

    each_strip(short, 8, solve)
    sine_rows(work_ref, work_ref, sine_ref, (count + 2) * rows)

    def residual(i, total):
        row = pl.multiple_of(i * 8, 8)
        eigen = wave_eig_ref[q, rows_at((h * CHUNKS + chunk) * short + row, 8), :]
        under = load(work_ref, 0, short, row, 8)
        here = load(work_ref, rows, short, row, 8)
        for l in range(count):
            over = load(work_ref, (l + 2) * rows, short, row, 8)
            diag, cell, right, left, low, high = [faces_ref[n, pl.ds(l, 1), :] for n in range(6)]
            diag = s_re + (diag + cell * eigen)
            value = []
            for c in range(2):
                v = diag * here[c] - right * pltpu.roll(here[c], width - 1, 1)
                v = v - left * pltpu.roll(here[c], 1, 1)
                value.append(v - (low * under[c] + high * over[c]))
            value = (value[0] - s_im * here[1], value[1] + s_im * here[0])
            value = csub(load(field_ref, l * rows, short, row, 8), value)
            total = total + squares_of(value)
            store(work_ref, l * rows, short, row, 8, value)
            under, here = here, over
        return total

    total = lax.fori_loop(0, short // 8, residual, jnp.zeros((8, width), jnp.float32), unroll=2)
    sine_rows(work_ref, next_ref, sine_ref, count * rows)

    def sums(row):
        rho, cross_f, cross_b = [load(base_ref.at[n], 0, short, row, 8) for n in range(3)]
        planes = [load(next_ref, l * rows, short, row, 8) for l in range(count)]
        ahead, behind = sums_of(planes, rho, cross_f, cross_b)
        store(next_sums_ref, 0, short, row, 8, ahead)
        store(next_sums_ref, rows, short, row, 8, behind)

    each_strip(short, 8, sums)
    next_sums_ref[pl.ds(2 * rows, TAG), :] = sums_ref[pl.ds(2 * rows, TAG), :]
    next_sums_ref[pl.ds(2 * rows + 1, 1), :] = jnp.sum(total, axis=0, keepdims=True)
    fill_give(z, rows, next_sums_ref, give_refs)


def end_kernel(
    count, levels, flags_ref, numbers_ref, sine_ref, found_ref, modes_ref, base_ref,
    factors_ref, sums_ref, *refs,
):
    came_refs, out_refs, work_ref = refs[:levels], refs[-1 - GROUP : -1], refs[-1]
    before_refs = refs[levels + (levels > 1) : -1 - GROUP]
    z, member = flags_ref[2], flags_ref[3]
    scale = numbers_ref[2]
    short = base_ref.shape[1] // 2
    rows = 2 * short

    def solve(row):
        _, planes, _ = solved(
            count, levels, z, scale, modes_ref, sums_ref, came_refs, base_ref, factors_ref, row
        )
        for l in range(count):
            before = load(found_ref, l * rows, short, row, 8)
            store(work_ref, l * rows, short, row, 8, cadd(before, planes[l]))

    each_strip(short, 8, solve)
    sine_rows(work_ref, work_ref, sine_ref, count * rows)
    part = count // GROUP * rows
    tag_refs = (refs[levels] if levels > 1 else sums_ref, came_refs[-1])
    tag = None
    for ref in tag_refs:
        part_tag = ref[pl.ds(ref.shape[0] - TAG, TAG), :]
        tag = part_tag if tag is None else tag + part_tag
    for d in range(GROUP):
        start, whole = 0, tag
        if d in JOINT:
            held = len(before_refs) // len(JOINT)
            for ref in before_refs[JOINT.index(d) * held : (JOINT.index(d) + 1) * held]:
                out_refs[d][pl.ds(start, part), :] = ref[pl.ds(0, part), :]
                start, whole = start + part, whole + tag_of(ref)
        out_refs[d][pl.ds(start, part), :] = work_ref[rows_at((member ^ d) * part, part), :]
        out_refs[d][pl.ds(start + part, TAG), :] = whole


smem = pl.BlockSpec(memory_space=pltpu.SMEM)
vmem = pl.BlockSpec(memory_space=pltpu.VMEM)
unread = pl.BlockSpec(memory_space=pl.ANY)


def call(kernel, scalars, arrays, outs, scratch=(), flops=0, after=()):
    out_shape = [jax.ShapeDtypeStruct(shape, jnp.float32) for shape in outs]
    head = len(scalars) + len(arrays)

    def run(*refs):
        kernel(*refs[:head], *refs[head + len(after) :])

    moved = sum(a.size * a.dtype.itemsize for a in arrays) + sum(4 * int(np.prod(s)) for s in outs)
    held = moved + sum(4 * int(np.prod(s)) for s in scratch)
    return pl.pallas_call(
        run,
        out_shape=out_shape,
        in_specs=[smem] * len(scalars) + [vmem] * len(arrays) + [unread] * len(after),
        out_specs=[smem if len(shape) == 1 else vmem for shape in outs],
        scratch_shapes=[pltpu.VMEM(shape, jnp.float32) for shape in scratch],
        compiler_params=pltpu.CompilerParams(vmem_limit_bytes=held + 4 * 2**20),
        cost_estimate=pl.CostEstimate(flops=flops, bytes_accessed=moved, transcendentals=0),
    )(*scalars, *arrays, *after)


def pair_up(array, groups, flip):
    return lax.ppermute(array, "gz", [(i, i ^ flip) for i in range(groups)])


def step_by(array, groups, distance):
    return lax.ppermute(
        array, "gz", [(i, i + distance) for i in range(groups) if 0 <= i + distance < groups]
    )


def body(source, layer_ids, conduct_table, shift):
    planes, length_x, length_y = source.shape[1:]
    groups = lax.axis_size("gz")
    blocks = groups // GROUP
    levels = blocks.bit_length() - 1
    count = GROUP * planes
    length_z = planes * groups
    full = length_x // RADIX
    short = full // (HALVES * CHUNKS)
    rows = 2 * short
    if blocks < 2 or groups != GROUP << levels or planes > 2 or short % 8 or length_x != RADIX * full:
        raise ValueError("unsupported layout")
    me = lax.axis_index("gz")
    member = me % GROUP
    flags = jnp.stack([member % RADIX, member // RADIX, me // GROUP, member]).astype(jnp.int32)

    wave = wave_tables(length_x)
    wave_f = jnp.asarray(np.concatenate(two_terms(wave), axis=1))
    wave_b = jnp.asarray(np.concatenate(two_terms(np.swapaxes(wave, 1, 2) / length_x), axis=1))
    sine = jnp.asarray(two_terms(sine_table(length_y)))
    wave_eig = np.broadcast_to(wave_eigen(length_x)[:, :, None], (RADIX, full, length_y))
    wave_eig = jnp.asarray(np.ascontiguousarray(wave_eig).astype(np.float32))
    sine_eig = jnp.asarray(np.tile(sine_eigen(length_y)[None, :], (8, 1)).astype(np.float32))

    chunks = range(CHUNKS)
    row_block = (TAG, length_y)
    block = (count * rows, length_y)
    sums_block = (2 * rows + TAG, length_y)
    single = (rows + TAG, length_y)
    part = (planes * rows + TAG, length_y)
    parts = (CHUNKS * planes * rows + TAG, length_y)
    gives = [single] if levels == 1 else []
    dots = 6 * length_y * length_y

    (cells,) = call(conduct_kernel, [conduct_table], [layer_ids], [row_block])
    if levels == 1:
        below = above = pair_up(cells, groups, GROUP)
        totals = [cells, below]
    else:
        below = step_by(cells, groups, GROUP)
        above = step_by(cells, groups, -GROUP)
        total = cells
        for level in range(levels):
            (total,) = call(add_kernel, [], [total, pair_up(total, groups, GROUP << level)], [row_block])
        totals = [total]

    parted = source.reshape(2, planes, RADIX, full, length_y)
    spectra = {}
    placed = [cells]
    tags = [cells, below, above, *totals]
    for d in (2, 3, 0, 1):
        early = d == 2
        made = call(
            functools.partial(forward_kernel, d, 0 if early else len(tags)), [flags],
            [parted, wave_f, *([] if early else tags)], [part] * (HALVES * CHUNKS),
            scratch=[(planes, 2 * full, length_y)], flops=planes * 2 * full * dots, after=placed,
        )
        if early:
            made = call(
                functools.partial(tagged_kernel, planes, len(made)), [], [*made, *tags], [part] * len(made),
            )
        placed = made[:1]
        for n in range(HALVES):
            for t in chunks:
                spectra[d + RADIX * n, t] = made[n * CHUNKS + t]
    for t in chunks:
        for d in (6, 2, 4, 7, 3, 5, 1):
            if t == 0 or d not in JOINT:
                spectra[d, t] = pair_up(spectra[d, t], groups, d)

    state = [{} for _ in chunks]

    def exchange(st, after):
        sums, give = st["sums"][0], st["sums"][-1]
        st["came"], st["tags"] = [], []
        for level in range(levels):
            st["came"].append(pair_up(give, groups, GROUP << level))
            if level + 1 < levels:
                shape = single if level + 2 == levels else sums_block
                (give,) = call(
                    functools.partial(join_kernel, level, levels), [flags], [sums, st["came"][-1], st["base"]],
                    [shape], after=after,
                )
                sums = give
                st["tags"] = [give[-TAG:]]

    def start(t, after):
        st = state[t]
        outs = [block, block, (6, rows, length_y), sums_block, *gives]
        made = call(
            functools.partial(start_kernel, t, planes, blocks, length_y * length_z),
            [flags, state[0]["numbers"] if t else shift],
            [wave_eig, sine_eig, sine] + [spectra[d, t] for d in range(GROUP)],
            outs if t else [*outs, (6,)], flops=count * rows * dots, after=after,
        )
        if not t:
            *made, st["numbers"] = made
        st["field"], st["modes"], st["base"], *st["sums"] = made
        exchange(st, [])
        return [st["sums"][-1]]

    def faces(t, after):
        state[t]["faces"] = call(
            functools.partial(faces_kernel, planes, blocks), [flags], [spectra[d, 0] for d in range(GROUP)],
            [(6, count, length_y)], scratch=[(count + 16, length_y), row_block, row_block], after=after,
        )[0]
        return [state[t]["faces"]]

    def factors(t, after):
        st = state[t]
        (st["factors"],) = call(
            functools.partial(factors_kernel, t, count, levels), [flags, state[0]["numbers"]],
            [wave_eig, sine_eig, st["base"]], [(4 + count + levels - 1, rows, length_y)], after=after,
        )
        return [st["factors"]]

    def middle(t, after):
        st = state[t]
        st["found"], st["modes"], *st["sums"] = call(
            functools.partial(middle_kernel, t, count, levels), [flags, state[0]["numbers"]],
            [wave_eig, sine, state[0]["faces"], st["field"], st["modes"], st["base"], st["factors"], st["sums"][0], *st["came"]],
            [block, block, sums_block, *gives], scratch=[((count + 2) * rows, length_y)],
            flops=(2 * count + 2) * rows * dots, after=after,
        )
        exchange(st, [])
        return [st["sums"][-1]]

    def end(t, after):
        st = state[t]
        last = t == CHUNKS - 1
        before = [state[u]["made"][d] for d in JOINT for u in range(t)] if last else []
        st["made"] = call(
            functools.partial(end_kernel, count, levels), [flags, state[0]["numbers"]],
            [sine, st["found"], st["modes"], st["base"], st["factors"], st["sums"][0], *st["came"], *st["tags"], *before],
            [parts if last and d in JOINT else part for d in range(GROUP)],
            scratch=[block], flops=count * rows * dots, after=after,
        )
        st["answers"] = {d: st["made"][d] for d in SENDS[t]}
        return [st["made"][0]]

    def held(array, after):
        return lax.optimization_barrier((array, *after))[0]

    def answer(t, distances):
        answers = state[t]["answers"]
        for d in distances:
            answers[d] = pair_up(answers[d], groups, d)

    placed = []
    for step in (start, faces, factors):
        placed = step(0, placed)
    for d in JOINT:
        spectra[d, 1] = pair_up(held(spectra[d, 1], placed), groups, d)
    for step, t in ((middle, 0), (start, 1), (factors, 1), (end, 0)):
        placed = step(t, placed)
    answer(0, SENDS[0][:-1])
    placed = middle(1, placed)
    end(1, [*placed, *[state[0]["answers"][d] for d in SENDS[0][:2]]])
    answer(1, SENDS[1][:-1])
    return call(
        functools.partial(backward_kernel, planes, length_x * length_x * length_y * length_z),
        [flags], [wave_b] + [state[t]["answers"][d] for t, d in ANSWERS],
        [(2, planes, length_x, length_y), (2,)],
        scratch=[(planes, RADIX, 2 * full, length_y), (RADIX, planes, 2 * full, length_y)],
        flops=planes * RADIX * 2 * full * dots,
    )


def solution(mesh):
    placed = (P(None, ("node", "gz"), None, None), P(("node", "gz"), None), P(), P("node"))
    return jax.shard_map(
        body,
        mesh=mesh,
        in_specs=placed,
        out_specs=(P(None, ("node", "gz"), None, None), P("node")),
        check_vma=False,
    )
```

```python
import functools

import jax
import jax.numpy as jnp
import ml_dtypes
import numpy as np
from jax import lax
from jax.experimental import pallas as pl
from jax.experimental.pallas import tpu as pltpu
from jax.sharding import PartitionSpec as P

RADIX = 4
HALVES = 2
GROUP = RADIX * HALVES
CHUNKS = 2
SENDS = ((6, 7, 2, 3, 4, 0), (6, 2, 7, 3, 4, 5, 1, 0))
ANSWERS = tuple((t, d) for t in range(CHUNKS) for d in SENDS[t])
JOINT = (5, 1)
TAG = 8

relax = 0.6


def sine_table(length):
    indices = np.arange(1, length + 1)
    product = indices[:, None] * indices[None, :] % (2 * (length + 1))
    return np.sqrt(2.0 / (length + 1)) * np.sin(np.pi / (length + 1) * product)


def sine_eigen(length):
    indices = np.arange(1, length + 1)
    return 4.0 * np.sin(np.pi / (2 * (length + 1)) * indices) ** 2


def wave_numbers(length):
    return RADIX * np.arange(length // RADIX)[None, :] + np.arange(RADIX)[:, None]


def wave_eigen(length):
    return 4.0 * np.sin(np.pi / length * wave_numbers(length)) ** 2


def wave_tables(length):
    waves = wave_numbers(length)
    short = length // RADIX
    product = waves[:, :, None] * np.arange(short)[None, None, :] % length
    angles = 2.0 * np.pi / length * product
    cos_t, sin_t = np.cos(angles), np.sin(angles)
    pieces = HALVES * CHUNKS
    top = np.concatenate([cos_t, sin_t], axis=2).reshape(RADIX, pieces, short // pieces, 2 * short)
    low = np.concatenate([-sin_t, cos_t], axis=2).reshape(RADIX, pieces, short // pieces, 2 * short)
    return np.concatenate([top, low], axis=2).reshape(RADIX, 2 * short, 2 * short)


def two_terms(table):
    first = table.astype(ml_dtypes.bfloat16)
    return np.stack([first, (table - first.astype(np.float64)).astype(ml_dtypes.bfloat16)])


def split(value):
    first = value.astype(jnp.bfloat16)
    return first, (value - first.astype(jnp.float32)).astype(jnp.bfloat16)


def dot_right(value, table):
    rows = value.shape[0]
    first, second = split(value)
    wide = jnp.dot(jnp.concatenate([first, second], axis=0), table[0], preferred_element_type=jnp.float32)
    return wide[:rows] + (wide[rows:] + jnp.dot(first, table[1], preferred_element_type=jnp.float32))


def dot_left(table, value):
    rows = table.shape[0] // 2
    first, second = split(value)
    wide = jnp.dot(table, first, preferred_element_type=jnp.float32)
    return wide[:rows] + (wide[rows:] + jnp.dot(table[:rows], second, preferred_element_type=jnp.float32))


def cmul(a, b):
    return (a[0] * b[0] - a[1] * b[1], a[0] * b[1] + a[1] * b[0])


def csqr(a):
    cross = a[0] * a[1]
    return ((a[0] - a[1]) * (a[0] + a[1]), cross + cross)


def cpow(a, count):
    result = None
    while count:
        if count & 1:
            result = a if result is None else cmul(result, a)
        count >>= 1
        if count:
            a = csqr(a)
    return result


def cadd(a, b):
    return (a[0] + b[0], a[1] + b[1])


def csub(a, b):
    return (a[0] - b[0], a[1] - b[1])


def cscale(a, scale):
    return (a[0] * scale, a[1] * scale)


def cmore(total, factor, term):
    return cadd(total, cmul(factor, term))


def cinv(a):
    scale = 1.0 / (a[0] * a[0] + a[1] * a[1])
    return (a[0] * scale, -a[1] * scale)


def cone(a):
    return (1.0 - a[0], -a[1])


def cpick(cond, a, b):
    return (jnp.where(cond, a[0], b[0]), jnp.where(cond, a[1], b[1]))


def rows_at(start, rows):
    if isinstance(start, int):
        return pl.ds(start, rows)
    return pl.ds(pl.multiple_of(start, 8), rows)


def load(ref, base, short, row, rows):
    return (ref[rows_at(base + row, rows), :], ref[rows_at(base + short + row, rows), :])


def store(ref, base, short, row, rows, value):
    ref[rows_at(base + row, rows), :] = value[0]
    ref[rows_at(base + short + row, rows), :] = value[1]


def each_strip(count, rows, body):
    def step(i, carry):
        body(pl.multiple_of(i * rows, rows))
        return carry

    steps = count // rows
    lax.fori_loop(0, steps, step, 0, unroll=min(steps, 4))


def squares_of(a):
    return a[0] * a[0] + a[1] * a[1]


def conduct_kernel(table_ref, ids_ref, out_ref):
    planes = ids_ref.shape[0]
    ids = ids_ref[...]
    cells = jnp.zeros(ids.shape, jnp.float32)
    for layer in range(table_ref.shape[0]):
        cells = jnp.where(ids == layer, table_ref[layer], cells)
    out_ref[...] = jnp.zeros_like(out_ref)
    out_ref[pl.ds(0, planes), :] = cells
    out_ref[pl.ds(TAG - 1, 1), :] = jnp.sum(cells, axis=0, keepdims=True)


def add_kernel(one_ref, two_ref, out_ref):
    out_ref[...] = one_ref[...] + two_ref[...]


def fill_tag(out_ref, planes, own_ref, below_ref, above_ref, *part_refs):
    start = out_ref.shape[0] - TAG
    for n, ref in enumerate((own_ref, below_ref, above_ref)):
        out_ref[pl.ds(start + n * planes, planes), :] = ref[pl.ds(0, planes), :]
    total = part_refs[0][pl.ds(TAG - 1, 1), :]
    for ref in part_refs[1:]:
        total = total + ref[pl.ds(TAG - 1, 1), :]
    out_ref[pl.ds(start + TAG - 1, 1), :] = total


def tag_of(ref):
    return ref[pl.ds(ref.shape[0] - TAG, TAG), :]


def find_numbers(cells_total, shift_ref, part_refs, numbers_ref):
    total = None
    for ref in part_refs:
        row = ref[pl.ds(ref.shape[0] - 1, 1), :]
        total = row if total is None else total + row
    inv = (1.0 / (jnp.sum(total, axis=1, keepdims=True) * (1.0 / cells_total)))[0, 0]
    numbers_ref[0] = shift_ref[0] * inv
    numbers_ref[1] = shift_ref[1] * inv
    numbers_ref[2] = relax * inv
    numbers_ref[3] = 0.5 * relax * inv
    numbers_ref[4] = shift_ref[0]
    numbers_ref[5] = shift_ref[1]


def faces_kernel(planes, blocks, flags_ref, *refs):
    part_refs, (faces_ref, padded_ref, below_ref, above_ref) = refs[:GROUP], refs[GROUP:]
    z, member = flags_ref[2], flags_ref[3]
    _, count, width = faces_ref.shape
    for d, ref in enumerate(part_refs):
        tag = tag_of(ref)
        place = member ^ d
        for p in range(planes):
            padded_ref[pl.ds(8 + place * planes + p, 1), :] = tag[p : p + 1]
        below_ref[pl.ds(place, 1), :] = tag[2 * planes - 1 : 2 * planes]
        above_ref[pl.ds(place, 1), :] = tag[2 * planes : 2 * planes + 1]
    cells = padded_ref[pl.ds(8, count), :]
    padded_ref[pl.ds(7, 1), :] = jnp.where(z == 0, cells[0:1], below_ref[pl.ds(GROUP - 1, 1), :])
    padded_ref[pl.ds(8 + count, 1), :] = jnp.where(
        z == blocks - 1, cells[count - 1 : count], above_ref[pl.ds(0, 1), :]
    )
    lane = lax.broadcasted_iota(jnp.int32, cells.shape, 1)
    last, first = lane == width - 1, lane == 0
    right = 0.5 * (cells + pltpu.roll(cells, width - 1, 1))
    left = 0.5 * (cells + pltpu.roll(cells, 1, 1))
    low = 0.5 * (cells + padded_ref[pl.ds(7, count), :])
    high = 0.5 * (cells + padded_ref[pl.ds(9, count), :])
    faces_ref[0] = jnp.where(last, cells, right) + jnp.where(first, cells, left) + (low + high)
    faces_ref[1] = cells
    faces_ref[2] = jnp.where(last, 0.0, right)
    faces_ref[3] = jnp.where(first, 0.0, left)
    faces_ref[4] = low
    faces_ref[5] = high


def forward_kernel(distance, tags_count, flags_ref, source_ref, wave_ref, *refs):
    tag_refs, out_refs, stage_ref = refs[:tags_count], refs[tags_count:-1], refs[-1]
    planes = source_ref.shape[1]
    q = flags_ref[0] ^ distance
    sign = (1 - 2 * (q & 1)).astype(jnp.float32)
    turn_re = jnp.where(q == 0, 1.0, jnp.where(q == 2, -1.0, 0.0))
    turn_im = jnp.where(q == 1, 1.0, jnp.where(q == 3, -1.0, 0.0))
    rows = stage_ref.shape[1] // (HALVES * CHUNKS)
    for p in range(planes):
        parts = [[source_ref[c, p, i] for i in range(RADIX)] for c in range(2)]
        even = [parts[c][0] + sign * parts[c][2] for c in range(2)]
        odd = [parts[c][1] + sign * parts[c][3] for c in range(2)]
        mixed = jnp.concatenate(
            [
                even[0] + (turn_re * odd[0] + turn_im * odd[1]),
                even[1] + (turn_re * odd[1] - turn_im * odd[0]),
            ],
            axis=0,
        )
        stage_ref[p] = dot_left(wave_ref[q], mixed)
        for n in range(HALVES):
            h = flags_ref[1] ^ n
            for t in range(CHUNKS):
                out_refs[n * CHUNKS + t][pl.ds(p * rows, rows), :] = stage_ref[
                    p, rows_at((h * CHUNKS + t) * rows, rows), :
                ]
    for ref in out_refs if tags_count else ():
        fill_tag(ref, planes, *tag_refs)


def tagged_kernel(planes, count, *refs):
    for ref, out_ref in zip(refs[:count], refs[-count:]):
        rows = ref.shape[0] - TAG
        out_ref[pl.ds(0, rows), :] = ref[pl.ds(0, rows), :]
        fill_tag(out_ref, planes, *refs[count:-count])


def backward_kernel(planes, cells, flags_ref, wave_ref, *refs):
    arrays, (out_ref, norms_ref, mixed_ref, stage_ref) = refs[:-4], refs[-4:]
    rows = (arrays[0].shape[0] - TAG) // planes
    came = {}
    for (t, d), ref in zip(ANSWERS, arrays):
        for n in range(CHUNKS if d in JOINT else 1):
            came[d, n if d in JOINT else t] = ref.at[pl.ds(n * planes * rows, planes * rows)]
    short = rows * CHUNKS * HALVES // 2
    total = None
    for ref in arrays:
        tag = tag_of(ref)
        total = tag if total is None else total + tag
    for d in range(RADIX):
        q = flags_ref[0] ^ d
        for p in range(planes):
            for n in range(HALVES):
                h = flags_ref[1] ^ n
                for t in range(CHUNKS):
                    stage_ref[d, p, rows_at((h * CHUNKS + t) * rows, rows), :] = came[d + RADIX * n, t][
                        pl.ds(p * rows, rows), :
                    ]
            mixed_ref[p, q] = dot_left(wave_ref[q], stage_ref[d, p])
    for p in range(planes):

        def strip(row):
            zero, one, two, three = [load(mixed_ref.at[p, q], 0, short, row, 8) for q in range(RADIX)]
            even, odd = cadd(zero, two), cadd(one, three)
            even_d, odd_d = csub(zero, two), csub(one, three)
            parts = (
                cadd(even, odd),
                (even_d[0] - odd_d[1], even_d[1] + odd_d[0]),
                csub(even, odd),
                (even_d[0] + odd_d[1], even_d[1] - odd_d[0]),
            )
            for i in range(RADIX):
                for c in range(2):
                    out_ref[c, p, rows_at(i * short + row, 8), :] = parts[i][c]

        each_strip(short, 8, strip)
    norms = jnp.sqrt(jnp.sum(total, axis=1, keepdims=True) * (1.0 / cells))
    for n in range(norms_ref.shape[0]):
        norms_ref[n] = norms[n, 0]


def decay_root(h):
    sq = (h[0] + 0.25 * (h[0] * h[0] - h[1] * h[1]), h[1] + 0.5 * h[0] * h[1])
    size = jnp.sqrt(squares_of(sq))
    root_re = jnp.sqrt(0.5 * (size + sq[0]))
    root = (root_re, 0.5 * sq[1] / root_re)
    return cinv((1.0 + 0.5 * h[0] + root[0], 0.5 * h[1] + root[1])), root


def two_powers(power, z, stacks):
    low = high = None
    bit = 0
    while (1 << bit) < stacks:
        taken = ((z >> bit) & 1) == 1
        if low is None:
            one = (jnp.ones_like(power[0]), jnp.zeros_like(power[0]))
            low, high = cpick(taken, power, one), cpick(taken, one, power)
        else:
            grown = cmul(cpick(taken, low, high), power)
            low, high = cpick(taken, grown, low), cpick(taken, high, grown)
        power = csqr(power)
        bit += 1
    return low, high


def sums_of(planes, rho, cross_f, cross_b):
    ahead = planes[0]
    for a in planes[1:]:
        ahead = cmore(a, rho, ahead)
    behind = planes[-1]
    for a in planes[-2::-1]:
        behind = cmore(a, rho, behind)
    return csub(ahead, cmul(cross_f, behind)), csub(behind, cmul(cross_b, ahead))


def sine_rows(source_ref, target_ref, sine_ref, count):
    sine = (sine_ref[0], sine_ref[1])
    rows = max(n for n in range(16, 641, 16) if count % n == 0)
    for i in range(0, count, rows):
        target_ref[pl.ds(i, rows), :] = dot_right(source_ref[pl.ds(i, rows), :], sine)


def fill_give(z, rows, sums_ref, give_refs):
    for ref in give_refs:
        ref[pl.ds(0, rows), :] = sums_ref[rows_at((z & 1) * rows, rows), :]
        ref[pl.ds(rows, TAG), :] = sums_ref[pl.ds(2 * rows, TAG), :]


def start_kernel(
    chunk, planes, blocks, cells_total, flags_ref, numbers_ref, wave_eig_ref, sine_eig_ref, sine_ref, *refs,
):
    part_refs, (field_ref, modes_ref, base_ref, sums_ref), give_refs = refs[:GROUP], refs[GROUP : GROUP + 4], refs[GROUP + 4 :]
    if chunk == 0:
        shift_ref, numbers_ref, give_refs = numbers_ref, give_refs[-1], give_refs[:-1]
        find_numbers(cells_total, shift_ref, part_refs, numbers_ref)
    q, h, z, member = [flags_ref[n] for n in range(4)]
    rows = base_ref.shape[1]
    part = rows * planes
    short = rows // 2
    count = GROUP * planes
    first_row = (h * CHUNKS + chunk) * short
    for d, ref in enumerate(part_refs):
        field_ref[rows_at((member ^ d) * part, part), :] = ref[pl.ds(0, part), :]
    sine_rows(field_ref, modes_ref, sine_ref, count * rows)
    h_re, h_im = numbers_ref[0], numbers_ref[1]
    sine_eig = sine_eig_ref[...]

    def strip(i, total):
        row = pl.multiple_of(i * 8, 8)
        eigen = wave_eig_ref[q, rows_at(first_row + row, 8), :] + sine_eig
        rho, _ = decay_root((eigen + h_re, jnp.full_like(eigen, h_im)))
        block = cpow(rho, count)
        next_one = cmul(block, rho)
        low, high = two_powers(csqr(block), z, blocks)
        cross_f, cross_b = cmul(next_one, low), cmul(next_one, high)
        for n, value in enumerate((rho, cross_f, cross_b, block, low, high)):
            store(base_ref.at[n], 0, short, row, 8, value)
        found = [load(modes_ref, l * rows, short, row, 8) for l in range(count)]
        ahead, behind = sums_of(found, rho, cross_f, cross_b)
        store(sums_ref, 0, short, row, 8, ahead)
        store(sums_ref, rows, short, row, 8, behind)
        for l in range(count):
            total = total + squares_of(load(field_ref, l * rows, short, row, 8))
        return total

    total = lax.fori_loop(
        0, short // 8, strip, jnp.zeros((8, field_ref.shape[1]), jnp.float32), unroll=2
    )
    sums_ref[pl.ds(2 * rows, TAG), :] = jnp.zeros((TAG, field_ref.shape[1]), jnp.float32)
    sums_ref[pl.ds(2 * rows, 1), :] = jnp.sum(total, axis=0, keepdims=True)
    fill_give(z, rows, sums_ref, give_refs)


def factors_kernel(
    chunk, count, levels, flags_ref, numbers_ref, wave_eig_ref, sine_eig_ref, base_ref, out_ref,
):
    q, h_part, z = flags_ref[0], flags_ref[1], flags_ref[2]
    short = base_ref.shape[1] // 2
    h_re, h_im, scale = numbers_ref[0], numbers_ref[1], numbers_ref[3]
    sine_eig = sine_eig_ref[...]

    def strip(row):
        eigen = wave_eig_ref[q, rows_at((h_part * CHUNKS + chunk) * short + row, 8), :] + sine_eig
        h = (eigen + h_re, jnp.full_like(eigen, h_im))
        rho, _, _, block, low, high = [load(base_ref.at[n], 0, short, row, 8) for n in range(6)]
        half_gap = csub((1.0 + 0.5 * h[0], 0.5 * h[1]), rho)
        wide = cmul(csqr(block), csqr(rho))
        low_w, high_w = cmul(low, wide), cmul(high, wide)
        whole = cscale(cinv(cmul(half_gap, cone(cmul(low, high_w)))), scale)
        turned = cmul(rho, whole)
        values = [
            cmul(cone(high_w), whole), cmul(cone(low), turned),
            cmul(cone(high), turned), cmul(cone(low_w), whole),
        ]
        pivot = (2.0 + h[0], h[1])
        inverse = cinv(pivot)
        values.append(inverse)
        for _ in range(count - 1):
            inverse = cinv(csub(pivot, inverse))
            values.append(inverse)
        near = far = None
        power = block
        for level in range(1, levels):
            taken = ((z >> (level - 1)) & 1) == 1
            if near is None:
                one = (jnp.ones_like(power[0]), jnp.zeros_like(power[0]))
                near, far = cpick(taken, power, one), cpick(taken, one, power)
            else:
                grown = cmul(cpick(taken, near, far), power)
                near, far = cpick(taken, grown, near), cpick(taken, far, grown)
            power = csqr(power)
            values.append(cpick(((z >> level) & 1) == 1, near, far))
        for n, value in enumerate(values):
            store(out_ref.at[n], 0, short, row, 8, value)

    each_strip(short, 8, strip)


def join_kernel(level, levels, flags_ref, sums_ref, came_ref, base_ref, out_ref):
    z = flags_ref[2]
    short = base_ref.shape[1] // 2
    rows = 2 * short
    above = ((z >> level) & 1) == 1
    last = level + 2 == levels
    upper = ((z >> (level + 1)) & 1) == 1

    def strip(row):
        block = load(base_ref.at[3], 0, short, row, 8)
        for _ in range(level):
            block = csqr(block)
        ahead, behind = load(sums_ref, 0, short, row, 8), load(sums_ref, rows, short, row, 8)
        ahead_c, behind_c = load(came_ref, 0, short, row, 8), load(came_ref, rows, short, row, 8)
        joined = cmore(cpick(above, ahead, ahead_c), block, cpick(above, ahead_c, ahead))
        joined_b = cmore(cpick(above, behind_c, behind), block, cpick(above, behind, behind_c))
        if last:
            store(out_ref, 0, short, row, 8, cpick(upper, joined_b, joined))
        else:
            store(out_ref, 0, short, row, 8, joined)
            store(out_ref, rows, short, row, 8, joined_b)

    each_strip(short, 8, strip)
    out_ref[pl.ds(out_ref.shape[0] - TAG, TAG), :] = (
        sums_ref[pl.ds(2 * rows, TAG), :] + came_ref[pl.ds(2 * rows, TAG), :]
    )


def solved(count, levels, z, scale, modes_ref, sums_ref, came_refs, base_ref, factors_ref, row):
    short = base_ref.shape[1] // 2
    rows = 2 * short

    def factor(n):
        return load(factors_ref.at[n], 0, short, row, 8)

    enter_f = enter_b = None
    for level in range(levels):
        above = ((z >> level) & 1) == 1
        base = 0 if level == levels - 1 else jnp.where(above, 0, rows)
        came = load(came_refs[level], base, short, row, 8)
        if level:
            came = cmul(factor(4 + count + level - 1), came)
        nought = (jnp.zeros_like(came[0]), jnp.zeros_like(came[0]))
        now_f, now_b = cpick(above, came, nought), cpick(above, nought, came)
        enter_f = now_f if enter_f is None else cadd(enter_f, now_f)
        enter_b = now_b if enter_b is None else cadd(enter_b, now_b)
    block = load(base_ref.at[3], 0, short, row, 8)
    all_f = cmore(load(sums_ref, 0, short, row, 8), block, enter_f)
    all_b = cmore(load(sums_ref, rows, short, row, 8), block, enter_b)
    below = cmore(cmul(factor(0), enter_f), factor(1), all_b)
    above = cmore(cmul(factor(3), enter_b), factor(2), all_f)
    planes = [cscale(load(modes_ref, l * rows, short, row, 8), scale) for l in range(count)]
    planes[0] = cadd(planes[0], below)
    planes[-1] = cadd(planes[-1], above)
    for l in range(1, count):
        planes[l] = cmore(planes[l], factor(4 + l - 1), planes[l - 1])
    planes[-1] = cmul(factor(4 + count - 1), planes[-1])
    for l in range(count - 2, -1, -1):
        planes[l] = cmul(factor(4 + l), cadd(planes[l], planes[l + 1]))
    return below, planes, above


def middle_kernel(
    chunk, count, levels, flags_ref, numbers_ref, wave_eig_ref, sine_ref, faces_ref, field_ref,
    modes_ref, base_ref, factors_ref, sums_ref, *refs,
):
    came_refs, (found_ref, next_ref, next_sums_ref) = refs[:levels], refs[levels : levels + 3]
    give_refs, work_ref = refs[levels + 3 : -1], refs[-1]
    q, h, z = flags_ref[0], flags_ref[1], flags_ref[2]
    scale, s_re, s_im = numbers_ref[2], numbers_ref[4], numbers_ref[5]
    short = base_ref.shape[1] // 2
    rows = 2 * short
    width = base_ref.shape[2]

    def solve(row):
        below, planes, above = solved(
            count, levels, z, scale, modes_ref, sums_ref, came_refs, base_ref, factors_ref, row
        )
        store(work_ref, 0, short, row, 8, below)
        store(work_ref, (count + 1) * rows, short, row, 8, above)
        for l in range(count):
            store(work_ref, (l + 1) * rows, short, row, 8, planes[l])
            store(found_ref, l * rows, short, row, 8, planes[l])

    each_strip(short, 8, solve)
    sine_rows(work_ref, work_ref, sine_ref, (count + 2) * rows)

    def residual(i, total):
        row = pl.multiple_of(i * 8, 8)
        eigen = wave_eig_ref[q, rows_at((h * CHUNKS + chunk) * short + row, 8), :]
        under = load(work_ref, 0, short, row, 8)
        here = load(work_ref, rows, short, row, 8)
        for l in range(count):
            over = load(work_ref, (l + 2) * rows, short, row, 8)
            diag, cell, right, left, low, high = [faces_ref[n, pl.ds(l, 1), :] for n in range(6)]
            diag = s_re + (diag + cell * eigen)
            value = []
            for c in range(2):
                v = diag * here[c] - right * pltpu.roll(here[c], width - 1, 1)
                v = v - left * pltpu.roll(here[c], 1, 1)
                value.append(v - (low * under[c] + high * over[c]))
            value = (value[0] - s_im * here[1], value[1] + s_im * here[0])
            value = csub(load(field_ref, l * rows, short, row, 8), value)
            total = total + squares_of(value)
            store(work_ref, l * rows, short, row, 8, value)
            under, here = here, over
        return total

    total = lax.fori_loop(0, short // 8, residual, jnp.zeros((8, width), jnp.float32), unroll=2)
    sine_rows(work_ref, next_ref, sine_ref, count * rows)

    def sums(row):
        rho, cross_f, cross_b = [load(base_ref.at[n], 0, short, row, 8) for n in range(3)]
        planes = [load(next_ref, l * rows, short, row, 8) for l in range(count)]
        ahead, behind = sums_of(planes, rho, cross_f, cross_b)
        store(next_sums_ref, 0, short, row, 8, ahead)
        store(next_sums_ref, rows, short, row, 8, behind)

    each_strip(short, 8, sums)
    next_sums_ref[pl.ds(2 * rows, TAG), :] = sums_ref[pl.ds(2 * rows, TAG), :]
    next_sums_ref[pl.ds(2 * rows + 1, 1), :] = jnp.sum(total, axis=0, keepdims=True)
    fill_give(z, rows, next_sums_ref, give_refs)


def end_kernel(
    count, levels, flags_ref, numbers_ref, sine_ref, found_ref, modes_ref, base_ref,
    factors_ref, sums_ref, *refs,
):
    came_refs, out_refs, work_ref = refs[:levels], refs[-1 - GROUP : -1], refs[-1]
    before_refs = refs[levels + (levels > 1) : -1 - GROUP]
    z, member = flags_ref[2], flags_ref[3]
    scale = numbers_ref[2]
    short = base_ref.shape[1] // 2
    rows = 2 * short

    def solve(row):
        _, planes, _ = solved(
            count, levels, z, scale, modes_ref, sums_ref, came_refs, base_ref, factors_ref, row
        )
        for l in range(count):
            before = load(found_ref, l * rows, short, row, 8)
            store(work_ref, l * rows, short, row, 8, cadd(before, planes[l]))

    each_strip(short, 8, solve)
    sine_rows(work_ref, work_ref, sine_ref, count * rows)
    part = count // GROUP * rows
    tag_refs = (refs[levels] if levels > 1 else sums_ref, came_refs[-1])
    tag = None
    for ref in tag_refs:
        part_tag = ref[pl.ds(ref.shape[0] - TAG, TAG), :]
        tag = part_tag if tag is None else tag + part_tag
    for d in range(GROUP):
        start, whole = 0, tag
        if d in JOINT:
            held = len(before_refs) // len(JOINT)
            for ref in before_refs[JOINT.index(d) * held : (JOINT.index(d) + 1) * held]:
                out_refs[d][pl.ds(start, part), :] = ref[pl.ds(0, part), :]
                start, whole = start + part, whole + tag_of(ref)
        out_refs[d][pl.ds(start, part), :] = work_ref[rows_at((member ^ d) * part, part), :]
        out_refs[d][pl.ds(start + part, TAG), :] = whole


smem = pl.BlockSpec(memory_space=pltpu.SMEM)
vmem = pl.BlockSpec(memory_space=pltpu.VMEM)
unread = pl.BlockSpec(memory_space=pl.ANY)


def call(kernel, scalars, arrays, outs, scratch=(), flops=0, after=()):
    out_shape = [jax.ShapeDtypeStruct(shape, jnp.float32) for shape in outs]
    head = len(scalars) + len(arrays)

    def run(*refs):
        kernel(*refs[:head], *refs[head + len(after) :])

    moved = sum(a.size * a.dtype.itemsize for a in arrays) + sum(4 * int(np.prod(s)) for s in outs)
    held = moved + sum(4 * int(np.prod(s)) for s in scratch)
    return pl.pallas_call(
        run,
        out_shape=out_shape,
        in_specs=[smem] * len(scalars) + [vmem] * len(arrays) + [unread] * len(after),
        out_specs=[smem if len(shape) == 1 else vmem for shape in outs],
        scratch_shapes=[pltpu.VMEM(shape, jnp.float32) for shape in scratch],
        compiler_params=pltpu.CompilerParams(vmem_limit_bytes=held + 4 * 2**20),
        cost_estimate=pl.CostEstimate(flops=flops, bytes_accessed=moved, transcendentals=0),
    )(*scalars, *arrays, *after)


def pair_up(array, groups, flip):
    return lax.ppermute(array, "gz", [(i, i ^ flip) for i in range(groups)])


def step_by(array, groups, distance):
    return lax.ppermute(
        array, "gz", [(i, i + distance) for i in range(groups) if 0 <= i + distance < groups]
    )


def body(source, layer_ids, conduct_table, shift):
    planes, length_x, length_y = source.shape[1:]
    groups = lax.axis_size("gz")
    blocks = groups // GROUP
    levels = blocks.bit_length() - 1
    count = GROUP * planes
    length_z = planes * groups
    full = length_x // RADIX
    short = full // (HALVES * CHUNKS)
    rows = 2 * short
    if blocks < 2 or groups != GROUP << levels or planes > 2 or short % 8 or length_x != RADIX * full:
        raise ValueError("unsupported layout")
    me = lax.axis_index("gz")
    member = me % GROUP
    flags = jnp.stack([member % RADIX, member // RADIX, me // GROUP, member]).astype(jnp.int32)

    wave = wave_tables(length_x)
    wave_f = jnp.asarray(np.concatenate(two_terms(wave), axis=1))
    wave_b = jnp.asarray(np.concatenate(two_terms(np.swapaxes(wave, 1, 2) / length_x), axis=1))
    sine = jnp.asarray(two_terms(sine_table(length_y)))
    wave_eig = np.broadcast_to(wave_eigen(length_x)[:, :, None], (RADIX, full, length_y))
    wave_eig = jnp.asarray(np.ascontiguousarray(wave_eig).astype(np.float32))
    sine_eig = jnp.asarray(np.tile(sine_eigen(length_y)[None, :], (8, 1)).astype(np.float32))

    chunks = range(CHUNKS)
    row_block = (TAG, length_y)
    block = (count * rows, length_y)
    sums_block = (2 * rows + TAG, length_y)
    single = (rows + TAG, length_y)
    part = (planes * rows + TAG, length_y)
    parts = (CHUNKS * planes * rows + TAG, length_y)
    gives = [single] if levels == 1 else []
    dots = 6 * length_y * length_y

    (cells,) = call(conduct_kernel, [conduct_table], [layer_ids], [row_block])
    if levels == 1:
        below = above = pair_up(cells, groups, GROUP)
        totals = [cells, below]
    else:
        below = step_by(cells, groups, GROUP)
        above = step_by(cells, groups, -GROUP)
        total = cells
        for level in range(levels):
            (total,) = call(add_kernel, [], [total, pair_up(total, groups, GROUP << level)], [row_block])
        totals = [total]

    parted = source.reshape(2, planes, RADIX, full, length_y)
    spectra = {}
    placed = [cells]
    tags = [cells, below, above, *totals]
    for d in (2, 0, 3, 1):
        early = d == 2
        made = call(
            functools.partial(forward_kernel, d, 0 if early else len(tags)), [flags],
            [parted, wave_f, *([] if early else tags)], [part] * (HALVES * CHUNKS),
            scratch=[(planes, 2 * full, length_y)], flops=planes * 2 * full * dots, after=placed,
        )
        if early:
            made = call(
                functools.partial(tagged_kernel, planes, len(made)), [], [*made, *tags], [part] * len(made),
            )
        placed = made[:1]
        for n in range(HALVES):
            for t in chunks:
                spectra[d + RADIX * n, t] = made[n * CHUNKS + t]
    for t in chunks:
        for d in (6, 2, 4, 7, 3, 5, 1):
            if t == 0 or d not in JOINT:
                spectra[d, t] = pair_up(spectra[d, t], groups, d)

    state = [{} for _ in chunks]

    def exchange(st, after):
        sums, give = st["sums"][0], st["sums"][-1]
        st["came"], st["tags"] = [], []
        for level in range(levels):
            st["came"].append(pair_up(give, groups, GROUP << level))
            if level + 1 < levels:
                shape = single if level + 2 == levels else sums_block
                (give,) = call(
                    functools.partial(join_kernel, level, levels), [flags], [sums, st["came"][-1], st["base"]],
                    [shape], after=after,
                )
                sums = give
                st["tags"] = [give[-TAG:]]

    def start(t, after):
        st = state[t]
        outs = [block, block, (6, rows, length_y), sums_block, *gives]
        made = call(
            functools.partial(start_kernel, t, planes, blocks, length_y * length_z),
            [flags, state[0]["numbers"] if t else shift],
            [wave_eig, sine_eig, sine] + [spectra[d, t] for d in range(GROUP)],
            outs if t else [*outs, (6,)], flops=count * rows * dots, after=after,
        )
        if not t:
            *made, st["numbers"] = made
        st["field"], st["modes"], st["base"], *st["sums"] = made
        exchange(st, [])
        return [st["sums"][-1]]

    def faces(t, after):
        state[t]["faces"] = call(
            functools.partial(faces_kernel, planes, blocks), [flags], [spectra[d, 0] for d in range(GROUP)],
            [(6, count, length_y)], scratch=[(count + 16, length_y), row_block, row_block], after=after,
        )[0]
        return [state[t]["faces"]]

    def factors(t, after):
        st = state[t]
        (st["factors"],) = call(
            functools.partial(factors_kernel, t, count, levels), [flags, state[0]["numbers"]],
            [wave_eig, sine_eig, st["base"]], [(4 + count + levels - 1, rows, length_y)], after=after,
        )
        return [st["factors"]]

    def middle(t, after):
        st = state[t]
        st["found"], st["modes"], *st["sums"] = call(
            functools.partial(middle_kernel, t, count, levels), [flags, state[0]["numbers"]],
            [wave_eig, sine, state[0]["faces"], st["field"], st["modes"], st["base"], st["factors"], st["sums"][0], *st["came"]],
            [block, block, sums_block, *gives], scratch=[((count + 2) * rows, length_y)],
            flops=(2 * count + 2) * rows * dots, after=after,
        )
        exchange(st, [])
        return [st["sums"][-1]]

    def end(t, after):
        st = state[t]
        last = t == CHUNKS - 1
        before = [state[u]["made"][d] for d in JOINT for u in range(t)] if last else []
        st["made"] = call(
            functools.partial(end_kernel, count, levels), [flags, state[0]["numbers"]],
            [sine, st["found"], st["modes"], st["base"], st["factors"], st["sums"][0], *st["came"], *st["tags"], *before],
            [parts if last and d in JOINT else part for d in range(GROUP)],
            scratch=[block], flops=count * rows * dots, after=after,
        )
        st["answers"] = {d: st["made"][d] for d in SENDS[t]}
        return [st["made"][0]]

    def held(array, after):
        return lax.optimization_barrier((array, *after))[0]

    def answer(t, distances):
        answers = state[t]["answers"]
        for d in distances:
            answers[d] = pair_up(answers[d], groups, d)

    placed = []
    for step in (start, faces, factors):
        placed = step(0, placed)
    for d in JOINT:
        spectra[d, 1] = pair_up(held(spectra[d, 1], placed), groups, d)
    for step, t in ((middle, 0), (start, 1), (factors, 1), (end, 0)):
        placed = step(t, placed)
    answer(0, SENDS[0][:-1])
    placed = middle(1, placed)
    end(1, [*placed, *[state[0]["answers"][d] for d in SENDS[0][:2]]])
    answer(1, SENDS[1][:-1])
    return call(
        functools.partial(backward_kernel, planes, length_x * length_x * length_y * length_z),
        [flags], [wave_b] + [state[t]["answers"][d] for t, d in ANSWERS],
        [(2, planes, length_x, length_y), (2,)],
        scratch=[(planes, RADIX, 2 * full, length_y), (RADIX, planes, 2 * full, length_y)],
        flops=planes * RADIX * 2 * full * dots,
    )


def solution(mesh):
    placed = (P(None, ("node", "gz"), None, None), P(("node", "gz"), None), P(), P("node"))
    return jax.shard_map(
        body,
        mesh=mesh,
        in_specs=placed,
        out_specs=(P(None, ("node", "gz"), None, None), P("node")),
        check_vma=False,
    )
```
